32 devices in a mesh: role: 2 (over x), seq: 8 (over z, core), head: 2 (over y).
Axes of the slice: x: 2, y: 2, z: 4, core: 2. Of those that a mesh axis runs over, the one named last changes fastest.
Arguments:
- hidden_rows: bfloat16 [3072, 5120], P('seq'), may hold values from -6 to 6
- gen_weight: bfloat16 [5120, 5120], P(None, ('role', 'head')), may hold values from -0.078125 to 0.078125
- noise: bfloat16 [3072, 5120], P('seq'), may hold values from -6 to 6
- timesteps: int32 [48], P('seq'), may hold values from 20 to 979
- qkv_weight: bfloat16 [2, 5120, 9216], P('role', 'seq', 'head'), may hold values from -0.078125 to 0.078125
- out_weight: bfloat16 [2, 3072, 5120], P('role', 'head'), may hold values from -0.109375 to 0.109375
- qk_gain: float32 [2, 2, 24], P('role', None, 'head'), may hold values from 0.6 to 9
- block_keys: int32 [24, 48, 8], P('head', 'seq'), may hold values from 0 to 47, as said below
- block_count: int32 [24, 48], P('head', 'seq'), may hold values from 1 to 8, as said below
Outputs:
- score_grad: float32 [3072, 5120], P('seq', ('role', 'head'))
The draws below stay inside these ranges and needn't reach their ends.
Inputs may be any that keep to these rules, and one draw needn't show every extreme that they name: `block_keys`: entry 0 of each list is the query block itself; the entries of one list are distinct. For each head, all entries of the lists of one index of seq name at most 2 distinct blocks of any other index of seq, and every index names exactly 2 blocks of the next index. `block_count`: in every draw the lists of some sequence shards are all full, those of others shorter.
All inputs are finite; a program needn't handle non-finite values.
Results may differ from the reference program's by a relative error of at most 0.018.
The reference program's roundings to bfloat16 on the way count: a program that leaves them out, or rounds other values in their place, can miss the bound.
Values may be sent and summed in bfloat16 or wider, within the bound.
No kernel may reach another device: no remote copies, remote signals or barrier semaphores. Data moves between devices by JAX's collectives and lax.ppermute only.
A program may use at most 192 MiB of HBM per device.

```python
import math
import jax
import jax.numpy as jnp
from jax import lax

D = 5120
HEADS = 24
HEAD_DIM = 128
BLOCK = 64
KMAX = 8
TOK_DEV = 384
TOKENS = 3072
BLOCKS = 48
CAP = 2


def draw_qk_gain(key, part):
    upper = math.log(2.2)
    return jnp.exp(jax.random.uniform(key, (2, 2, HEADS), jnp.float32, math.log(0.6), upper))


def pair_lists(key):
    blocks = TOKENS // BLOCK
    shard_blocks = TOK_DEV // BLOCK
    shards = TOKENS // TOK_DEV
    width = shard_blocks + shards * CAP
    elig_scores = jax.random.randint(jax.random.fold_in(key, 17), (HEADS, shards, shards, shard_blocks), 0, 1 << 20)
    elig_rank = elig_scores * shard_blocks + lax.broadcasted_iota(jnp.int32, (HEADS, shards, shards, shard_blocks), 3)
    owner_grid = lax.broadcasted_iota(jnp.int32, (HEADS, shards, shards, CAP), 2)
    eligible = lax.top_k(elig_rank, CAP)[1].astype(jnp.int32) + owner_grid * shard_blocks
    own_blocks = lax.broadcasted_iota(jnp.int32, (HEADS, shards, shard_blocks), 1) * shard_blocks + lax.broadcasted_iota(jnp.int32, (HEADS, shards, shard_blocks), 2)
    candidates = jnp.concatenate([own_blocks, eligible.reshape(HEADS, shards, shards * CAP)], axis=2)
    dest_grid = lax.broadcasted_iota(jnp.int32, (HEADS, shards, shards, CAP), 1)
    remote_ok = (owner_grid != dest_grid).reshape(HEADS, shards, shards * CAP)
    next_one = (owner_grid == (dest_grid + 1) % shards).reshape(HEADS, shards, shards * CAP)
    valid = jnp.concatenate([jnp.ones((HEADS, shards, shard_blocks), bool), remote_ok], axis=2)
    forced = jnp.concatenate([jnp.zeros((HEADS, shards, shard_blocks), bool), next_one], axis=2)
    cand_b = jnp.repeat(candidates, shard_blocks, axis=1)
    valid_b = jnp.repeat(valid, shard_blocks, axis=1)
    forced_b = jnp.repeat(forced, shard_blocks, axis=1)
    anchor_b = lax.broadcasted_iota(jnp.int32, (HEADS, blocks, width), 1)
    valid_b = jnp.logical_and(valid_b, cand_b != anchor_b)
    first_b = anchor_b % shard_blocks == 0
    forced_b = jnp.logical_and(forced_b, first_b)
    pick_scores = jax.random.randint(jax.random.fold_in(key, 23), (HEADS, blocks, width), 0, 1 << 20)
    pick_scores = pick_scores * width + lax.broadcasted_iota(jnp.int32, (HEADS, blocks, width), 2)
    pick_scores = jnp.where(forced_b, pick_scores + (1 << 28), pick_scores)
    pick_scores = jnp.where(valid_b, pick_scores, -1)
    picked = lax.top_k(pick_scores, KMAX - 1)[1].astype(jnp.int32)
    chosen = jnp.take_along_axis(cand_b, picked, axis=2)
    anchor = lax.broadcasted_iota(jnp.int32, (HEADS, blocks, 1), 1)
    key_list = jnp.concatenate([anchor, chosen], axis=2).astype(jnp.int32)
    heavy = jax.random.randint(jax.random.fold_in(key, 29), (shards,), 0, 3) == 0
    heavy = jnp.logical_or(heavy, lax.broadcasted_iota(jnp.int32, (shards,), 0) == 0)
    shard_of = lax.broadcasted_iota(jnp.int32, (blocks,), 0) // shard_blocks
    heavy_blocks = jnp.any(jnp.logical_and(shard_of[:, None] == lax.broadcasted_iota(jnp.int32, (blocks, shards), 1), heavy[None, :]), axis=1)
    light = jax.random.randint(jax.random.fold_in(key, 31), (HEADS, blocks), 1, KMAX // 2 + 1)
    counts = jnp.where(heavy_blocks[None, :], KMAX, light).astype(jnp.int32)
    return (key_list, counts)


def draw_block_keys(key, part):
    return pair_lists(key)[0]


def draw_block_count(key, part):
    return pair_lists(key)[1]


def touch_ends(entries, stream_key, least, largest):
    shape = entries.shape
    spot = [jax.random.randint(jax.random.fold_in(stream_key, axis), (), 0, shape[axis]) for axis in range(len(shape))]
    entries = entries.at[tuple(spot)].set(least)
    longest = shape.index(max(shape))
    spot[longest] = (spot[longest] + 1) % shape[longest]
    return entries.at[tuple(spot)].set(largest)


def steps_of(key, dims, cuts, least, high):
    gain, own = 1.0, jax.random.fold_in(key, 6)
    for dim, blocks in cuts:
        steps = jnp.exp(jax.random.uniform(jax.random.fold_in(own, dim), (blocks,), jnp.float32, least / len(cuts), high / len(cuts)))
        gain = gain * jnp.repeat(steps, dims[dim] // blocks).reshape([-1 if axis == dim else 1 for axis in range(len(dims))])
    return gain


def gaussian(stream_key, dims, scale, limit, cuts=(), held_as=jnp.bfloat16):
    result = jax.random.normal(stream_key, dims, jnp.float32) * scale
    if len(cuts) > 0:
        result = steps_of(stream_key, dims, cuts, -0.22, 0.18) * result
    return jnp.clip(result, min=-limit, max=limit).astype(held_as)


def setup_inputs(seed: int = 0) -> dict:
    streams_of = jax.random.split(jax.random.key(seed), 10)
    return {
        "hidden_rows": gaussian(streams_of[0], (TOKENS, D), 1.0, 6.0, ((0, 8),)),
        "gen_weight": gaussian(streams_of[1], (D, D), D ** -0.5, 0.078125, ((1, 4),)),
        "noise": gaussian(streams_of[2], (TOKENS, D), 1.0, 6.0, ((0, 8),)),
        "timesteps": touch_ends(jax.random.randint(streams_of[3], (BLOCKS,), 20, 980), jax.random.fold_in(streams_of[3], 1), 20, 979).astype(jnp.int32),
        "qkv_weight": gaussian(streams_of[4], (2, D, 3 * HEADS * HEAD_DIM), D ** -0.5, 0.078125, ((0, 2), (1, 8), (2, 2))),
        "out_weight": gaussian(streams_of[5], (2, HEADS * HEAD_DIM, D), (HEADS * HEAD_DIM) ** -0.5, 0.109375, ((0, 2), (1, 2))),
        "qk_gain": draw_qk_gain(jax.random.fold_in(streams_of[9], 71), 0),
        "block_keys": draw_block_keys(jax.random.fold_in(streams_of[9], 71), 0),
        "block_count": draw_block_count(jax.random.fold_in(streams_of[9], 71), 0),
    }


def rms_rows(values):
    return values * lax.rsqrt(lax.optimization_barrier(jnp.mean(values * values, axis=-1, keepdims=True)) + 1e-06)

def block_attention(operands):
    queries, key_table, value_table, key_list, key_count = operands
    picked_keys = key_table[key_list]
    picked_values = value_table[key_list]
    scale = 1.0 / math.sqrt(HEAD_DIM)
    scores = jnp.einsum('nqe,nkbe->nqkb', queries.astype(jnp.float32), picked_keys.astype(jnp.float32)) * scale
    live = jnp.arange(KMAX)[None, :] < key_count[:, None]
    scores = jnp.where(live[:, None, :, None], scores, -jnp.inf)
    highest = lax.optimization_barrier(jnp.max(scores, axis=(2, 3), keepdims=True))
    raised = jnp.exp(scores - highest)
    summed = lax.optimization_barrier(jnp.sum(raised, axis=(2, 3), keepdims=True))
    weights = (raised / summed).astype(jnp.bfloat16)
    mixed = jnp.einsum('nqkb,nkbe->nqe', weights.astype(jnp.float32), picked_values.astype(jnp.float32))
    return mixed.astype(jnp.bfloat16)

def section_output(normed, weight_one, out_one, gain_one, block_keys, block_count):
    projected = jnp.dot(normed, weight_one, preferred_element_type=jnp.float32)
    projected = projected.reshape(TOKENS, HEADS, 3, HEAD_DIM)
    queries = (rms_rows(projected[:, :, 0]) * gain_one[0][None, :, None]).astype(jnp.bfloat16)
    key_rows = (rms_rows(projected[:, :, 1]) * gain_one[1][None, :, None]).astype(jnp.bfloat16)
    value_rows = projected[:, :, 2].astype(jnp.bfloat16)

    def by_head(array):
        return array.reshape(BLOCKS, BLOCK, HEADS, HEAD_DIM).transpose(2, 0, 1, 3)
    attended = lax.map(block_attention, (by_head(queries), by_head(key_rows), by_head(value_rows), block_keys, block_count))
    attended = attended.transpose(1, 2, 0, 3).reshape(TOKENS, HEADS * HEAD_DIM)
    return jnp.dot(attended, out_one, preferred_element_type=jnp.float32)

def reference(hidden_rows, gen_weight, noise, timesteps, qkv_weight, out_weight, qk_gain, block_keys, block_count):
    generated = jnp.dot(hidden_rows, gen_weight, preferred_element_type=jnp.float32).astype(jnp.bfloat16)
    angle_rows = jnp.repeat(timesteps.astype(jnp.float32) * (math.pi / 2000.0), BLOCK)[:, None]
    noisy = jnp.cos(angle_rows) * generated.astype(jnp.float32) + jnp.sin(angle_rows) * noise.astype(jnp.float32)
    normed = rms_rows(noisy).astype(jnp.bfloat16)
    real_term = section_output(normed, qkv_weight[0], out_weight[0], qk_gain[0], block_keys, block_count)
    fake_term = section_output(normed, qkv_weight[1], out_weight[1], qk_gain[1], block_keys, block_count)
    return fake_term - real_term
```

```python
import math

import jax
import jax.numpy as jnp
from jax import lax
from jax.experimental import pallas as pl
from jax.experimental.pallas import tpu as pltpu
from jax.sharding import Mesh
from jax.sharding import PartitionSpec as P

HEAD_DIM = 128
BLOCK = 64
KMAX = 8
CAP = 2


def rms_rows(values):
    return values * lax.rsqrt(jnp.mean(values * values, axis=-1, keepdims=True) + 1e-06)


def block_attention(queries, key_table, value_table, key_list, key_count):
    picked_keys = key_table[key_list]
    picked_values = value_table[key_list]
    scale = 1.0 / math.sqrt(HEAD_DIM)
    scores = (
        jnp.einsum("nqe,nkbe->nqkb", queries, picked_keys, preferred_element_type=jnp.float32)
        * scale
    )
    live = lax.broadcasted_iota(jnp.int32, (key_list.shape[0], KMAX), 1) < key_count[:, None]
    scores = jnp.where(live[:, None, :, None], scores, -jnp.inf)
    highest = jnp.max(scores, axis=(2, 3), keepdims=True)
    raised = jnp.exp(scores - highest)
    summed = jnp.sum(raised, axis=(2, 3), keepdims=True)
    weights = (raised / summed).astype(jnp.bfloat16)
    mixed = jnp.einsum("nqkb,nkbe->nqe", weights, picked_values, preferred_element_type=jnp.float32)
    return mixed.astype(jnp.bfloat16)


def pick_blocks(table, wanted):
    return table[wanted]


def per_device_by_tokens(
    hidden_rows,
    gen_weight,
    noise,
    timesteps,
    qkv_weight,
    out_weight,
    qk_gain,
    block_keys,
    block_count,
):
    generated = jnp.dot(hidden_rows, gen_weight, preferred_element_type=jnp.float32).astype(
        jnp.bfloat16
    )
    forked = lax.all_gather(generated, ("role", "head"), axis=1, tiled=True)
    row_count = forked.shape[0]
    width = forked.shape[1]
    local_blocks = timesteps.shape[0]
    angle_blocks = (timesteps.astype(jnp.float32) * (math.pi / 2000.0))[:, None, None]
    noisy = jnp.cos(angle_blocks) * forked.astype(jnp.float32).reshape(local_blocks, BLOCK, width)
    noisy = noisy + jnp.sin(angle_blocks) * noise.astype(jnp.float32).reshape(
        local_blocks, BLOCK, width
    )
    normed = rms_rows(noisy).reshape(row_count, width).astype(jnp.bfloat16)
    weight_here = qkv_weight[0]
    projected = jnp.dot(
        normed,
        lax.all_gather(weight_here, "seq", axis=0, tiled=True),
        preferred_element_type=jnp.float32,
    )
    heads_here = projected.shape[1] // (3 * HEAD_DIM)
    head_parts = projected.reshape(row_count, heads_here, 3, HEAD_DIM)
    gain_here = qk_gain[0]
    queries = (rms_rows(head_parts[:, :, 0]) * gain_here[0][None, :, None]).astype(jnp.bfloat16)
    key_local = (rms_rows(head_parts[:, :, 1]) * gain_here[1][None, :, None]).astype(jnp.bfloat16)
    value_local = head_parts[:, :, 2].astype(jnp.bfloat16)
    query_table = queries.reshape(local_blocks, BLOCK, heads_here, HEAD_DIM).transpose(2, 0, 1, 3)
    shard_count = lax.axis_size("seq")
    shard_here = lax.axis_index("seq")
    all_blocks = shard_count * local_blocks
    key_heads = key_local.reshape(local_blocks, BLOCK, heads_here, HEAD_DIM).transpose(2, 0, 1, 3)
    value_heads = value_local.reshape(local_blocks, BLOCK, heads_here, HEAD_DIM).transpose(
        2, 0, 1, 3
    )
    block_ids = lax.broadcasted_iota(jnp.int32, (1, 1, 1, all_blocks), 3)
    matches = block_keys[:, :, :, None] == block_ids
    remote = block_ids // local_blocks != shard_here
    needed = jnp.any(jnp.logical_and(matches, remote), axis=(1, 2))
    needed = needed.reshape(heads_here, shard_count, local_blocks)
    slot_of = jnp.cumsum(needed.astype(jnp.int32), axis=2) - 1
    slot_ids = lax.broadcasted_iota(jnp.int32, (1, 1, 1, CAP), 3)
    within_ids = lax.broadcasted_iota(jnp.int32, (1, 1, local_blocks, 1), 2)
    chosen_slot = jnp.logical_and(needed[..., None], slot_of[..., None] == slot_ids)
    requests = jnp.sum(jnp.where(chosen_slot, within_ids, 0), axis=2)
    asked = lax.all_to_all(
        requests.transpose(1, 0, 2), "seq", split_axis=0, concat_axis=0, tiled=True
    )
    sent_keys = jax.vmap(pick_blocks, in_axes=(0, 1), out_axes=1)(key_heads, asked)
    sent_values = jax.vmap(pick_blocks, in_axes=(0, 1), out_axes=1)(value_heads, asked)
    got_keys, got_values = (
        lax.all_to_all(sent_keys, "seq", split_axis=0, concat_axis=0, tiled=True),
        lax.all_to_all(sent_values, "seq", split_axis=0, concat_axis=0, tiled=True),
    )
    fetched_keys = got_keys.transpose(1, 0, 2, 3, 4).reshape(
        heads_here, shard_count * CAP, BLOCK, HEAD_DIM
    )
    fetched_values = got_values.transpose(1, 0, 2, 3, 4).reshape(
        heads_here, shard_count * CAP, BLOCK, HEAD_DIM
    )
    key_table = jnp.concatenate([key_heads, fetched_keys], axis=1)
    value_table = jnp.concatenate([value_heads, fetched_values], axis=1)
    local_ids = lax.broadcasted_iota(jnp.int32, (1, shard_count, local_blocks), 2)
    owner_grid = lax.broadcasted_iota(jnp.int32, (1, shard_count, local_blocks), 1)
    position = jnp.where(
        owner_grid == shard_here, local_ids, local_blocks + owner_grid * CAP + slot_of
    )
    position = position.reshape(heads_here, all_blocks)
    key_lists = jnp.sum(jnp.where(matches, position[:, None, None, :], 0), axis=3)
    attended = jax.vmap(block_attention)(
        query_table, key_table, value_table, key_lists, block_count
    )
    attended = attended.transpose(1, 2, 0, 3).reshape(row_count, heads_here * HEAD_DIM)
    contribution = jnp.dot(attended, out_weight[0], preferred_element_type=jnp.float32)
    signed = (2.0 * lax.axis_index("role").astype(jnp.float32) - 1.0) * contribution
    return lax.psum_scatter(
        signed.astype(jnp.bfloat16), ("role", "head"), scatter_dimension=1, tiled=True
    ).astype(jnp.float32)


VMEM_BYTES = 56 * 1024 * 1024
CORES = 2


def whole_in_vmem():
    return pl.BlockSpec(memory_space=pltpu.VMEM)


def in_hbm():
    return pl.BlockSpec(memory_space=pl.ANY)


def in_smem():
    return pl.BlockSpec(memory_space=pltpu.SMEM)


def project_heads(places, gains, rounds, weight_own, weight_other):
    slabs, depth, columns = weight_own.shape
    tokens, features = rounds[0][0].shape
    half = rounds[0][3].shape[0]
    heads = columns // (3 * HEAD_DIM)
    pieces = [piece for one in rounds for piece in one]
    per_round = len(rounds[0])
    dtype = weight_own.dtype

    def body(places_ref, gains_ref, own_ref, other_ref, *refs):
        piece_refs = refs[: len(pieces)]
        query_ref, kv_ref = refs[len(pieces) : len(pieces) + 2]
        table, rows, weight_sems, row_sems = refs[len(pieces) + 2 :]
        core = places_ref[4]
        weight_copies = []
        for slab in range(slabs):
            for side, ref in enumerate((own_ref, other_ref)):
                place = core if side == 0 else 1 - core
                copy = pltpu.make_async_copy(
                    ref.at[slab], table.at[slab, place], weight_sems.at[slab, side]
                )
                copy.start()
                weight_copies.append(copy)
        row_copies = []
        for turn in range(len(rounds)):
            for which in range(per_round):
                ref = piece_refs[turn * per_round + which]
                if which < 3:
                    target = rows.at[turn, which]
                else:
                    target = rows.at[turn, 3, pl.ds((which - 3) * half, half)]
                copy = pltpu.make_async_copy(ref, target, row_sems.at[turn, which])
                copy.start()
                row_copies.append(copy)
        for copy in weight_copies:
            copy.wait()
        for turn in range(len(rounds)):
            for which in range(per_round):
                row_copies[turn * per_round + which].wait()
            total = None
            for which in range(4):
                weight = table[places_ref[which]].reshape(CORES * depth, columns)
                part = jnp.dot(rows[turn, which], weight, preferred_element_type=jnp.float32)
                total = part if total is None else total + part
            for head in range(heads):
                at = 3 * head * HEAD_DIM
                for part in range(2):
                    block = total[:, at + part * HEAD_DIM : at + (part + 1) * HEAD_DIM]
                    normal = rms_rows(block) * gains_ref[part, head]
                    if part == 0:
                        query_ref[head, turn] = normal.astype(dtype)
                    else:
                        kv_ref[head, 0, turn] = normal.astype(dtype)
                block = total[:, at + 2 * HEAD_DIM : at + 3 * HEAD_DIM]
                kv_ref[head, 1, turn] = block.astype(dtype)

    return pl.pallas_call(
        body,
        in_specs=[in_smem(), in_smem(), in_hbm(), in_hbm()] + [in_hbm()] * len(pieces),
        out_specs=(whole_in_vmem(), whole_in_vmem()),
        out_shape=(
            jax.ShapeDtypeStruct((heads, len(rounds), tokens, HEAD_DIM), dtype),
            jax.ShapeDtypeStruct((heads, 2, len(rounds), tokens, HEAD_DIM), dtype),
        ),
        scratch_shapes=[
            pltpu.VMEM((slabs, CORES, depth, columns), dtype),
            pltpu.VMEM((len(rounds), 4, tokens, features), dtype),
            pltpu.SemaphoreType.DMA((slabs, 2)),
            pltpu.SemaphoreType.DMA((len(rounds), per_round)),
        ],
        compiler_params=pltpu.CompilerParams(vmem_limit_bytes=VMEM_BYTES),
        name="project_heads",
    )(places, gains, weight_own, weight_other, *pieces)


def attend(key_slots, counts, query_slots, queries, kv_own, kv_other):
    blocks = queries.shape[0]
    most = key_slots.shape[1]
    scale = 1.0 / math.sqrt(HEAD_DIM)
    together = 4 if blocks % 4 == 0 else 1

    def body(slots_ref, counts_ref, from_ref, query_ref, own_ref, other_ref, out_ref, table, sems):
        copies = []
        for side, ref in enumerate((own_ref, other_ref)):
            for part in range(2):
                copy = pltpu.make_async_copy(
                    ref.at[part], table.at[part, pl.ds(side * blocks, blocks)], sems.at[side, part]
                )
                copy.start()
                copies.append(copy)
        for copy in copies:
            copy.wait()

        def step(at, carry):
            for inner in range(together):
                block = at * together + inner
                slots = [slots_ref[block, entry] for entry in range(most)]
                keys = jnp.concatenate([table[0, slot] for slot in slots], axis=0)
                values = jnp.concatenate([table[1, slot] for slot in slots], axis=0)
                scores = (
                    lax.dot_general(
                        query_ref[from_ref[block]],
                        keys,
                        (((1,), (1,)), ((), ())),
                        preferred_element_type=jnp.float32,
                    )
                    * scale
                )
                column = lax.broadcasted_iota(jnp.int32, scores.shape, 1)
                scores = jnp.where(column < counts_ref[block] * BLOCK, scores, -jnp.inf)
                highest = jnp.max(scores, axis=1, keepdims=True)
                raised = jnp.exp(scores - highest)
                summed = jnp.sum(raised, axis=1, keepdims=True)
                weights = (raised / summed).astype(values.dtype)
                mixed = jnp.dot(weights, values, preferred_element_type=jnp.float32)
                out_ref[block] = mixed.astype(out_ref.dtype)
            return carry

        lax.fori_loop(0, blocks // together, step, 0)

    return pl.pallas_call(
        body,
        in_specs=[in_smem(), in_smem(), in_smem(), whole_in_vmem(), in_hbm(), in_hbm()],
        out_specs=whole_in_vmem(),
        out_shape=jax.ShapeDtypeStruct(queries.shape, queries.dtype),
        scratch_shapes=[
            pltpu.VMEM((2, CORES * blocks, BLOCK, HEAD_DIM), queries.dtype),
            pltpu.SemaphoreType.DMA((2, 2)),
        ],
        compiler_params=pltpu.CompilerParams(vmem_limit_bytes=VMEM_BYTES),
        name="attend",
    )(key_slots, counts, query_slots, queries, kv_own, kv_other)


def out_blocks(which, sign, attended, out_weight, dtype, steps):
    groups, tokens, _ = attended[0].shape
    count = len(attended)
    depth, features = out_weight.shape
    wanted = which.shape[0]
    width = features // steps
    split = 1 if (width // 2) % HEAD_DIM else 2
    tile = width // split

    def body(which_ref, sign_ref, *refs):
        parts, weight_ref, out_ref, joined = refs[:count], refs[count], refs[count + 1], refs[count + 2]

        @pl.when(jnp.logical_and(pl.program_id(0) == 0, pl.program_id(1) == 0))
        def _():
            for group in range(groups):
                for chunk in range(count):
                    at = (group * count + chunk) * HEAD_DIM
                    joined[:, at : at + HEAD_DIM] = parts[chunk][group]

        total = jnp.dot(joined[...], weight_ref[...], preferred_element_type=jnp.float32)
        out_ref[0] = (total * sign_ref[0].astype(jnp.float32)).astype(dtype)

    return pl.pallas_call(
        body,
        grid_spec=pltpu.PrefetchScalarGridSpec(
            num_scalar_prefetch=2,
            grid=(wanted, split),
            in_specs=[pl.BlockSpec((groups, tokens, HEAD_DIM), lambda i, k, w, s: (0, 0, 0))] * count
            + [pl.BlockSpec((depth, tile), lambda i, k, w, s: (0, w[i] * split + k))],
            out_specs=pl.BlockSpec((1, tokens, tile), lambda i, k, w, s: (i, 0, k)),
            scratch_shapes=[pltpu.VMEM((tokens, depth), attended[0].dtype)],
        ),
        out_shape=jax.ShapeDtypeStruct((wanted, tokens, width), dtype),
        compiler_params=pltpu.CompilerParams(vmem_limit_bytes=VMEM_BYTES),
        name="out_blocks",
    )(which, sign, *attended, out_weight)


def per_device_by_heads(
    hidden_rows,
    gen_weight,
    noise,
    timesteps,
    qkv_weight,
    out_weight,
    qk_gain,
    block_keys,
    block_count,
):
    role, head = lax.axis_index("role"), lax.axis_index("head")
    chip, core = lax.axis_index("chip"), lax.axis_index("core")
    chips = lax.axis_size("chip")
    local_heads, local_blocks, most = block_keys.shape
    heads = local_heads // chips
    tokens = hidden_rows.shape[0]
    width = hidden_rows.shape[1]
    features = gen_weight.shape[1]
    all_blocks = chips * local_blocks
    swap = [(0, 1), (1, 0)]
    ring = [(at, (at + 1) % chips) for at in range(chips)]

    def exchange(array):
        return lax.all_to_all(array, "chip", split_axis=0, concat_axis=0, tiled=True)

    weight_rows = qkv_weight.shape[1]
    by_chip = qkv_weight[0].reshape(weight_rows, chips, heads, 3 * HEAD_DIM)
    weights_own = [exchange(by_chip[:, :, at].transpose(1, 0, 2)) for at in range(heads)]
    weights_other = [lax.ppermute(one, "core", swap) for one in weights_own]

    mine = role * lax.axis_size("head") + head
    generated = jnp.dot(hidden_rows, gen_weight, preferred_element_type=jnp.float32).astype(
        jnp.bfloat16
    )
    angle_blocks = (timesteps.astype(jnp.float32) * (math.pi / 2000.0))[:, None, None]
    noise_here = lax.dynamic_slice_in_dim(noise, mine * features, features, axis=1)
    noisy = jnp.cos(angle_blocks) * generated.astype(jnp.float32).reshape(
        local_blocks, BLOCK, features
    )
    noisy = noisy + jnp.sin(angle_blocks) * noise_here.astype(jnp.float32).reshape(
        local_blocks, BLOCK, features
    )
    squares = jnp.sum(noisy * noisy, axis=-1)
    squares = squares + lax.ppermute(squares, "role", swap)
    squares = squares + lax.ppermute(squares, "head", swap)
    normed = (noisy * lax.rsqrt(squares / width + 1e-06)[:, :, None]).astype(jnp.bfloat16)
    normed = normed.reshape(tokens, features)

    shards = [normed]
    for _ in range(chips - 1):
        shards.append(lax.ppermute(shards[-1], "chip", ring))
    rounds = []
    for shard in shards:
        over_role = lax.ppermute(shard, "role", swap)
        over_head = lax.ppermute(shard, "head", swap)
        first = lax.ppermute(over_head[: tokens // 2], "role", swap)
        second = lax.ppermute(over_role[tokens // 2 :], "head", swap)
        rounds.append((shard, over_role, over_head, first, second))

    lists = jnp.concatenate([block_keys, block_count[:, :, None]], axis=2)
    lists = exchange(lists.reshape(chips, heads, local_blocks, most + 1))
    lists = lists.transpose(1, 0, 2, 3).reshape(heads, all_blocks, most + 1)
    owner = lists[:, :, :most] // local_blocks
    turn = (chip - owner // CORES) % chips
    far = (owner % CORES != core).astype(jnp.int32)
    key_slots = far * all_blocks + turn * local_blocks + lists[:, :, :most] % local_blocks
    counts = lists[:, :, most]
    spot = jnp.arange(all_blocks, dtype=jnp.int32)
    query_slots = (chip - spot // local_blocks) % chips * local_blocks + spot % local_blocks

    sides = lax.axis_size("head")
    peers = jnp.stack(
        [
            role * sides + head,
            (1 - role) * sides + head,
            role * sides + 1 - head,
            (1 - role) * sides + 1 - head,
        ]
    ).astype(jnp.int32)
    places = jnp.concatenate([peers, core[None].astype(jnp.int32)])
    gains = lax.dynamic_slice_in_dim(qk_gain[0], chip * heads, heads, axis=1)

    attended = []
    for at in range(heads):
        queries, kv = project_heads(
            places, gains[:, at : at + 1], rounds, weights_own[at], weights_other[at]
        )
        kv = kv.reshape(2, all_blocks, BLOCK, HEAD_DIM)
        kv_other = lax.ppermute(kv, "core", swap)
        mixed = attend(
            key_slots[at],
            counts[at],
            query_slots,
            queries.reshape(all_blocks, BLOCK, HEAD_DIM),
            kv,
            kv_other,
        )
        attended.append(exchange(mixed.reshape(chips, tokens, HEAD_DIM)))

    sign = (2 * role - 1).astype(jnp.int32)[None]
    blocks = sides * lax.axis_size("role")
    diagonal = out_blocks(peers[3:4], sign, attended, out_weight[0], jnp.bfloat16, blocks)
    sides_two = out_blocks(peers[1:3], sign, attended, out_weight[0], jnp.bfloat16, blocks)
    own = out_blocks(peers[0:1], sign, attended, out_weight[0], jnp.float32, blocks)
    far_swap = [(0, 3), (1, 2), (2, 1), (3, 0)]
    from_diagonal = lax.ppermute(diagonal[0], ("role", "head"), far_swap)
    from_role = lax.ppermute(sides_two[0], "role", swap)
    from_head = lax.ppermute(sides_two[1], "head", swap)
    return own[0] + (
        from_role.astype(jnp.float32)
        + from_head.astype(jnp.float32)
        + from_diagonal.astype(jnp.float32)
    )


def splits_heads(mesh, qkv_weight, hidden_rows):
    role, seq, head = (mesh.shape[name] for name in ("role", "seq", "head"))
    if role != 2 or head != 2 or seq % CORES != 0:
        return False
    chips = seq // CORES
    heads = qkv_weight.shape[2] // (3 * HEAD_DIM * head)
    width = hidden_rows.shape[1]
    tokens = hidden_rows.shape[0] // seq
    return (
        heads % chips == 0
        and chips == role * head
        and width % (role * head * 256) == 0
        and width % (seq * 16) == 0
        and tokens % (2 * BLOCK) == 0
    )


def solution(mesh):
    def call(*arrays):
        if splits_heads(mesh, arrays[4], arrays[0]):
            per_device = per_device_by_heads
            seq = ("chip", "core")
            shape = mesh.devices.shape
            names = mesh.axis_names
            at = names.index("seq")
            layout = Mesh(
                mesh.devices.reshape(shape[:at] + (shape[at] // CORES, CORES) + shape[at + 1 :]),
                names[:at] + seq + names[at + 1 :],
            )
        else:
            per_device = per_device_by_tokens
            seq = "seq"
            layout = mesh
        placed = (
            P(seq, None),
            P(None, ("role", "head")),
            P(seq, None),
            P(seq),
            P("role", seq, "head"),
            P("role", "head", None),
            P("role", None, "head"),
            P("head", seq, None),
            P("head", seq),
        )
        return jax.shard_map(
            per_device,
            mesh=layout,
            in_specs=placed,
            out_specs=P(seq, ("role", "head")),
            check_vma=False,
        )(*arrays)

    return call
```

```python
import math

import jax
import jax.numpy as jnp
from jax import lax
from jax.experimental import pallas as pl
from jax.experimental.pallas import tpu as pltpu
from jax.sharding import Mesh
from jax.sharding import PartitionSpec as P

HEAD_DIM = 128
BLOCK = 64
KMAX = 8
CAP = 2


def rms_rows(values):
    return values * lax.rsqrt(jnp.mean(values * values, axis=-1, keepdims=True) + 1e-06)


def block_attention(queries, key_table, value_table, key_list, key_count):
    picked_keys = key_table[key_list]
    picked_values = value_table[key_list]
    scale = 1.0 / math.sqrt(HEAD_DIM)
    scores = (
        jnp.einsum("nqe,nkbe->nqkb", queries, picked_keys, preferred_element_type=jnp.float32)
        * scale
    )
    live = lax.broadcasted_iota(jnp.int32, (key_list.shape[0], KMAX), 1) < key_count[:, None]
    scores = jnp.where(live[:, None, :, None], scores, -jnp.inf)
    highest = jnp.max(scores, axis=(2, 3), keepdims=True)
    raised = jnp.exp(scores - highest)
    summed = jnp.sum(raised, axis=(2, 3), keepdims=True)
    weights = (raised / summed).astype(jnp.bfloat16)
    mixed = jnp.einsum("nqkb,nkbe->nqe", weights, picked_values, preferred_element_type=jnp.float32)
    return mixed.astype(jnp.bfloat16)


def pick_blocks(table, wanted):
    return table[wanted]


def per_device_by_tokens(
    hidden_rows,
    gen_weight,
    noise,
    timesteps,
    qkv_weight,
    out_weight,
    qk_gain,
    block_keys,
    block_count,
):
    generated = jnp.dot(hidden_rows, gen_weight, preferred_element_type=jnp.float32).astype(
        jnp.bfloat16
    )
    forked = lax.all_gather(generated, ("role", "head"), axis=1, tiled=True)
    row_count = forked.shape[0]
    width = forked.shape[1]
    local_blocks = timesteps.shape[0]
    angle_blocks = (timesteps.astype(jnp.float32) * (math.pi / 2000.0))[:, None, None]
    noisy = jnp.cos(angle_blocks) * forked.astype(jnp.float32).reshape(local_blocks, BLOCK, width)
    noisy = noisy + jnp.sin(angle_blocks) * noise.astype(jnp.float32).reshape(
        local_blocks, BLOCK, width
    )
    normed = rms_rows(noisy).reshape(row_count, width).astype(jnp.bfloat16)
    weight_here = qkv_weight[0]
    projected = jnp.dot(
        normed,
        lax.all_gather(weight_here, "seq", axis=0, tiled=True),
        preferred_element_type=jnp.float32,
    )
    heads_here = projected.shape[1] // (3 * HEAD_DIM)
    head_parts = projected.reshape(row_count, heads_here, 3, HEAD_DIM)
    gain_here = qk_gain[0]
    queries = (rms_rows(head_parts[:, :, 0]) * gain_here[0][None, :, None]).astype(jnp.bfloat16)
    key_local = (rms_rows(head_parts[:, :, 1]) * gain_here[1][None, :, None]).astype(jnp.bfloat16)
    value_local = head_parts[:, :, 2].astype(jnp.bfloat16)
    query_table = queries.reshape(local_blocks, BLOCK, heads_here, HEAD_DIM).transpose(2, 0, 1, 3)
    shard_count = lax.axis_size("seq")
    shard_here = lax.axis_index("seq")
    all_blocks = shard_count * local_blocks
    key_heads = key_local.reshape(local_blocks, BLOCK, heads_here, HEAD_DIM).transpose(2, 0, 1, 3)
    value_heads = value_local.reshape(local_blocks, BLOCK, heads_here, HEAD_DIM).transpose(
        2, 0, 1, 3
    )
    block_ids = lax.broadcasted_iota(jnp.int32, (1, 1, 1, all_blocks), 3)
    matches = block_keys[:, :, :, None] == block_ids
    remote = block_ids // local_blocks != shard_here
    needed = jnp.any(jnp.logical_and(matches, remote), axis=(1, 2))
    needed = needed.reshape(heads_here, shard_count, local_blocks)
    slot_of = jnp.cumsum(needed.astype(jnp.int32), axis=2) - 1
    slot_ids = lax.broadcasted_iota(jnp.int32, (1, 1, 1, CAP), 3)
    within_ids = lax.broadcasted_iota(jnp.int32, (1, 1, local_blocks, 1), 2)
    chosen_slot = jnp.logical_and(needed[..., None], slot_of[..., None] == slot_ids)
    requests = jnp.sum(jnp.where(chosen_slot, within_ids, 0), axis=2)
    asked = lax.all_to_all(
        requests.transpose(1, 0, 2), "seq", split_axis=0, concat_axis=0, tiled=True
    )
    sent_keys = jax.vmap(pick_blocks, in_axes=(0, 1), out_axes=1)(key_heads, asked)
    sent_values = jax.vmap(pick_blocks, in_axes=(0, 1), out_axes=1)(value_heads, asked)
    got_keys, got_values = (
        lax.all_to_all(sent_keys, "seq", split_axis=0, concat_axis=0, tiled=True),
        lax.all_to_all(sent_values, "seq", split_axis=0, concat_axis=0, tiled=True),
    )
    fetched_keys = got_keys.transpose(1, 0, 2, 3, 4).reshape(
        heads_here, shard_count * CAP, BLOCK, HEAD_DIM
    )
    fetched_values = got_values.transpose(1, 0, 2, 3, 4).reshape(
        heads_here, shard_count * CAP, BLOCK, HEAD_DIM
    )
    key_table = jnp.concatenate([key_heads, fetched_keys], axis=1)
    value_table = jnp.concatenate([value_heads, fetched_values], axis=1)
    local_ids = lax.broadcasted_iota(jnp.int32, (1, shard_count, local_blocks), 2)
    owner_grid = lax.broadcasted_iota(jnp.int32, (1, shard_count, local_blocks), 1)
    position = jnp.where(
        owner_grid == shard_here, local_ids, local_blocks + owner_grid * CAP + slot_of
    )
    position = position.reshape(heads_here, all_blocks)
    key_lists = jnp.sum(jnp.where(matches, position[:, None, None, :], 0), axis=3)
    attended = jax.vmap(block_attention)(
        query_table, key_table, value_table, key_lists, block_count
    )
    attended = attended.transpose(1, 2, 0, 3).reshape(row_count, heads_here * HEAD_DIM)
    contribution = jnp.dot(attended, out_weight[0], preferred_element_type=jnp.float32)
    signed = (2.0 * lax.axis_index("role").astype(jnp.float32) - 1.0) * contribution
    return lax.psum_scatter(
        signed.astype(jnp.bfloat16), ("role", "head"), scatter_dimension=1, tiled=True
    ).astype(jnp.float32)


VMEM_BYTES = 56 * 1024 * 1024
CORES = 2


def whole_in_vmem():
    return pl.BlockSpec(memory_space=pltpu.VMEM)


def in_hbm():
    return pl.BlockSpec(memory_space=pl.ANY)


def in_smem():
    return pl.BlockSpec(memory_space=pltpu.SMEM)


def cut_columns(weight, chips, first, heads, chip_heads):
    rows = weight.shape[0]
    wide = 3 * HEAD_DIM

    def body(weight_ref, out_ref, sems):
        copies = []
        for chip in range(chips):
            at = (chip * chip_heads + first) * wide
            copy = pltpu.make_async_copy(
                weight_ref.at[:, pl.ds(at, heads * wide)], out_ref.at[chip], sems.at[chip]
            )
            copy.start()
            copies.append(copy)
        for copy in copies:
            copy.wait()

    return pl.pallas_call(
        body,
        in_specs=[in_hbm()],
        out_specs=in_hbm(),
        out_shape=jax.ShapeDtypeStruct((chips, rows, heads * wide), weight.dtype),
        scratch_shapes=[pltpu.SemaphoreType.DMA((chips,))],
        name="cut_columns",
    )(weight)


def project_heads(places, gains, rounds, weight_own, weight_other):
    slabs, depth, columns = weight_own.shape
    tokens, features = rounds[0][0].shape
    half = rounds[0][3].shape[0]
    heads = columns // (3 * HEAD_DIM)
    pieces = [piece for one in rounds for piece in one]
    per_round = len(rounds[0])
    turns = len(rounds)
    dtype = weight_own.dtype
    width = CORES * slabs * depth
    pair = 2 if turns % 2 == 0 else 1

    def body(places_ref, gains_ref, own_ref, other_ref, *refs):
        piece_refs = refs[: len(pieces)]
        query_ref, kv_ref = refs[len(pieces) : len(pieces) + 2]
        table, rows, weight_sems, row_sems = refs[len(pieces) + 2 :]
        core = places_ref[4]
        weight_copies = []
        for slab in range(slabs):
            for side, ref in enumerate((own_ref, other_ref)):
                place = core if side == 0 else 1 - core
                copy = pltpu.make_async_copy(
                    ref.at[places_ref[slab]], table.at[slab, place], weight_sems.at[slab, side]
                )
                copy.start()
                weight_copies.append(copy)
        row_copies = []
        for turn in range(turns):
            for which in range(per_round):
                ref = piece_refs[turn * per_round + which]
                column = min(which, 3) * features
                first = turn * tokens + max(which - 3, 0) * half
                count = tokens if which < 3 else half
                copy = pltpu.make_async_copy(
                    ref,
                    rows.at[pl.ds(first, count), pl.ds(column, features)],
                    row_sems.at[turn, which],
                )
                copy.start()
                row_copies.append(copy)
        for copy in weight_copies:
            copy.wait()
        for begin in range(0, turns, pair):
            for copy in row_copies[begin * per_round : (begin + pair) * per_round]:
                copy.wait()
            total = jnp.dot(
                rows[begin * tokens : (begin + pair) * tokens],
                table[...].reshape(width, columns),
                preferred_element_type=jnp.float32,
            )
            for turn in range(pair):
                for head in range(heads):
                    at = 3 * head * HEAD_DIM
                    here = total[turn * tokens : (turn + 1) * tokens]
                    for part in range(2):
                        block = here[:, at + part * HEAD_DIM : at + (part + 1) * HEAD_DIM]
                        normal = (rms_rows(block) * gains_ref[part, head]).astype(dtype)
                        if part == 0:
                            query_ref[head, begin + turn] = normal
                        else:
                            kv_ref[head, 0, begin + turn] = normal
                    block = here[:, at + 2 * HEAD_DIM : at + 3 * HEAD_DIM]
                    kv_ref[head, 1, begin + turn] = block.astype(dtype)

    return pl.pallas_call(
        body,
        in_specs=[in_smem(), in_smem(), in_hbm(), in_hbm()] + [in_hbm()] * len(pieces),
        out_specs=(whole_in_vmem(), whole_in_vmem()),
        out_shape=(
            jax.ShapeDtypeStruct((heads, turns, tokens, HEAD_DIM), dtype),
            jax.ShapeDtypeStruct((heads, 2, turns, tokens, HEAD_DIM), dtype),
        ),
        scratch_shapes=[
            pltpu.VMEM((slabs, CORES, depth, columns), dtype),
            pltpu.VMEM((turns * tokens, 4 * features), dtype),
            pltpu.SemaphoreType.DMA((slabs, 2)),
            pltpu.SemaphoreType.DMA((turns, per_round)),
        ],
        compiler_params=pltpu.CompilerParams(vmem_limit_bytes=VMEM_BYTES),
        name="project_heads",
    )(places, gains, weight_own, weight_other, *pieces)


def attend(key_slots, counts, query_slots, group_most, queries, kv_own, kv_other):
    heads, blocks, most = key_slots.shape
    groups = group_most.shape[1]
    together = blocks // groups
    parts = len(queries)
    sizes = [one.shape[1] for one in queries]
    starts = [sum(sizes[:at]) for at in range(parts)]
    scale = 1.0 / math.sqrt(HEAD_DIM)
    dtype = queries[0].dtype

    def body(slots_ref, counts_ref, from_ref, most_ref, *refs):
        query_refs = refs[:parts]
        own_refs = refs[parts : 2 * parts]
        other_refs = refs[2 * parts : 3 * parts]
        out_ref, query_table, table, query_sems, sems = refs[3 * parts :]
        copies = []
        for at in range(parts):
            span = pl.ds(starts[at], sizes[at])
            copies.append(
                pltpu.make_async_copy(query_refs[at], query_table.at[:, span], query_sems.at[at])
            )
            for side, ref in enumerate((own_refs[at], other_refs[at])):
                span = pl.ds(side * blocks + starts[at], sizes[at])
                copies.append(pltpu.make_async_copy(ref, table.at[:, :, span], sems.at[at, side]))
        for copy in copies:
            copy.start()
        for copy in copies:
            copy.wait()

        def run(head, group, listed):
            for inner in range(together):
                block = group * together + inner
                slots = [slots_ref[head, block, entry] for entry in range(listed)]
                keys = jnp.concatenate([table[head, 0, slot] for slot in slots], axis=0)
                values = jnp.concatenate([table[head, 1, slot] for slot in slots], axis=0)
                scores = (
                    lax.dot_general(
                        query_table[head, from_ref[block]],
                        keys,
                        (((1,), (1,)), ((), ())),
                        preferred_element_type=jnp.float32,
                    )
                    * scale
                )
                column = lax.broadcasted_iota(jnp.int32, scores.shape, 1)
                scores = jnp.where(column < counts_ref[head, block] * BLOCK, scores, -jnp.inf)
                highest = jnp.max(scores, axis=1, keepdims=True)
                raised = jnp.exp(scores - highest)
                summed = jnp.sum(raised, axis=1, keepdims=True)
                weights = (raised * (1.0 / summed)).astype(dtype)
                mixed = jnp.dot(weights, values, preferred_element_type=jnp.float32)
                out_ref[head, block] = mixed.astype(dtype)

        def step(at, carry):
            head, group = at // groups, at % groups
            few = most_ref[head, group] <= most // 2

            @pl.when(few)
            def _():
                run(head, group, most // 2)

            @pl.when(jnp.logical_not(few))
            def _():
                run(head, group, most)

            return carry

        lax.fori_loop(0, heads * groups, step, 0)

    return pl.pallas_call(
        body,
        in_specs=[in_smem()] * 4 + [in_hbm()] * (3 * parts),
        out_specs=whole_in_vmem(),
        out_shape=jax.ShapeDtypeStruct((heads, blocks, BLOCK, HEAD_DIM), dtype),
        scratch_shapes=[
            pltpu.VMEM((heads, blocks, BLOCK, HEAD_DIM), dtype),
            pltpu.VMEM((heads, 2, CORES * blocks, BLOCK, HEAD_DIM), dtype),
            pltpu.SemaphoreType.DMA((parts,)),
            pltpu.SemaphoreType.DMA((parts, 2)),
        ],
        compiler_params=pltpu.CompilerParams(vmem_limit_bytes=VMEM_BYTES),
        name="attend",
    )(key_slots, counts, query_slots, group_most, *queries, *kv_own, *kv_other)


def out_blocks(which, sign, attended, out_weight, dtype, blocks):
    groups, _, tokens, _ = attended[0].shape
    sizes = [one.shape[1] for one in attended]
    count = len(attended)
    depth, features = out_weight.shape
    width = features // blocks

    def body(which_ref, sign_ref, *refs):
        parts, weight_ref, out_ref = refs[:count], refs[count], refs[count + 1]
        columns = []
        for group in range(groups):
            for chunk in range(count):
                for head in range(sizes[chunk]):
                    columns.append(parts[chunk][group, head])
        joined = jnp.concatenate(columns, axis=1)
        total = jnp.dot(joined, weight_ref[...], preferred_element_type=jnp.float32)
        out_ref[...] = (total * sign_ref[0].astype(jnp.float32)).astype(dtype)

    return pl.pallas_call(
        body,
        grid_spec=pltpu.PrefetchScalarGridSpec(
            num_scalar_prefetch=2,
            grid=(1,),
            in_specs=[pl.BlockSpec(one.shape, lambda i, w, s: (0, 0, 0, 0)) for one in attended]
            + [pl.BlockSpec((depth, width), lambda i, w, s: (0, w[0]))],
            out_specs=pl.BlockSpec((tokens, width), lambda i, w, s: (0, 0)),
        ),
        out_shape=jax.ShapeDtypeStruct((tokens, width), dtype),
        compiler_params=pltpu.CompilerParams(vmem_limit_bytes=VMEM_BYTES),
        name="out_blocks",
    )(which, sign, *attended, out_weight)


def chunk_sizes(heads):
    last = max(1, heads // 3)
    return [heads - last, last] if heads > last else [heads]


def per_device_by_heads(
    hidden_rows,
    gen_weight,
    noise,
    timesteps,
    qkv_weight,
    out_weight,
    qk_gain,
    block_keys,
    block_count,
):
    role, head = lax.axis_index("role"), lax.axis_index("head")
    chip, core = lax.axis_index("chip"), lax.axis_index("core")
    chips = lax.axis_size("chip")
    local_heads, local_blocks, most = block_keys.shape
    heads = local_heads // chips
    tokens = hidden_rows.shape[0]
    width = hidden_rows.shape[1]
    features = gen_weight.shape[1]
    all_blocks = chips * local_blocks
    swap = [(0, 1), (1, 0)]
    ring = [(at, (at + 1) % chips) for at in range(chips)]

    def exchange(array):
        return lax.all_to_all(array, "chip", split_axis=0, concat_axis=0, tiled=True)

    chunks = chunk_sizes(heads)
    weight_here = qkv_weight[0]
    cuts = [
        cut_columns(weight_here, chips, sum(chunks[:at]), chunks[at], heads)
        for at in range(len(chunks))
    ]
    weights_own = [exchange(cuts[0])]

    mine = role * lax.axis_size("head") + head
    generated = jnp.dot(hidden_rows, gen_weight, preferred_element_type=jnp.float32)
    generated = lax.reduce_precision(generated, 8, 7)
    angle_blocks = (timesteps.astype(jnp.float32) * (math.pi / 2000.0))[:, None, None]
    noise_here = lax.dynamic_slice_in_dim(noise, mine * features, features, axis=1)
    noisy = jnp.cos(angle_blocks) * generated.reshape(local_blocks, BLOCK, features)
    noisy = noisy + jnp.sin(angle_blocks) * noise_here.astype(jnp.float32).reshape(
        local_blocks, BLOCK, features
    )
    squares = jnp.sum(noisy * noisy, axis=-1)
    squares = squares + lax.ppermute(squares, "role", swap)
    squares = squares + lax.ppermute(squares, "head", swap)
    normed = (noisy * lax.rsqrt(squares / width + 1e-06)[:, :, None]).astype(jnp.bfloat16)
    normed = normed.reshape(tokens, features)
    for cut in cuts[1:]:
        held, _ = lax.optimization_barrier((cut, normed))
        weights_own.append(exchange(held))
    weights_other = [lax.ppermute(one, "core", swap) for one in weights_own]

    shards = [normed]
    for _ in range(chips - 1):
        shards.append(lax.ppermute(shards[-1], "chip", ring))
    rounds = []
    for shard in shards:
        over_role = lax.ppermute(shard, "role", swap)
        over_head = lax.ppermute(shard, "head", swap)
        first = lax.ppermute(over_head[: tokens // 2], "role", swap)
        second = lax.ppermute(over_role[tokens // 2 :], "head", swap)
        rounds.append((shard, over_role, over_head, first, second))

    lists = jnp.concatenate([block_keys, block_count[:, :, None]], axis=2)
    lists = lax.all_gather(lists, "chip", axis=1, tiled=True)
    lists = lax.dynamic_slice_in_dim(lists, chip * heads, heads, axis=0)
    owner = lists[:, :, :most] // local_blocks
    turn = (chip - owner // CORES) % chips
    far = (owner % CORES != core).astype(jnp.int32)
    key_slots = far * all_blocks + turn * local_blocks + lists[:, :, :most] % local_blocks
    counts = lists[:, :, most]
    group_most = jnp.max(counts.reshape(heads, chips, local_blocks), axis=2)
    spot = jnp.arange(all_blocks, dtype=jnp.int32)
    query_slots = (chip - spot // local_blocks) % chips * local_blocks + spot % local_blocks

    sides = lax.axis_size("head")
    peers = jnp.stack(
        [
            role * sides + head,
            (1 - role) * sides + head,
            role * sides + 1 - head,
            (1 - role) * sides + 1 - head,
        ]
    ).astype(jnp.int32)
    places = jnp.concatenate([peers, core[None].astype(jnp.int32)])
    gains = lax.dynamic_slice_in_dim(qk_gain[0], chip * heads, heads, axis=1)

    attended = []
    held_places = places
    for at, size in enumerate(chunks):
        span = slice(sum(chunks[:at]), sum(chunks[: at + 1]))
        last = at == len(chunks) - 1
        parts = [rounds] if last else [rounds[: chips // 2], rounds[chips // 2 :]]
        queries, kv_own, kv_other = [], [], []
        for part in parts:
            query, kv = project_heads(
                held_places, gains[:, span], part, weights_own[at], weights_other[at]
            )
            here = len(part) * local_blocks
            queries.append(query.reshape(size, here, BLOCK, HEAD_DIM))
            kv_own.append(kv.reshape(size, 2, here, BLOCK, HEAD_DIM))
            kv_other.append(lax.ppermute(kv_own[-1], "core", swap))
            held_places, _ = lax.optimization_barrier((places, kv))
        mixed = attend(
            key_slots[span],
            counts[span],
            query_slots,
            group_most[span],
            queries,
            kv_own,
            kv_other,
        )
        mixed = mixed.reshape(size, chips, tokens, HEAD_DIM).transpose(1, 0, 2, 3)
        attended.append(exchange(mixed))

    sign = (2 * role - 1).astype(jnp.int32)[None]
    blocks = sides * lax.axis_size("role")

    def block_of(at, dtype):
        return out_blocks(peers[at : at + 1], sign, attended, out_weight[0], dtype, blocks)

    far_swap = [(0, 3), (1, 2), (2, 1), (3, 0)]
    from_diagonal = lax.ppermute(block_of(3, jnp.bfloat16), ("role", "head"), far_swap)
    from_role = lax.ppermute(block_of(1, jnp.bfloat16), "role", swap)
    from_head = lax.ppermute(block_of(2, jnp.bfloat16), "head", swap)
    return block_of(0, jnp.float32) + (
        from_role.astype(jnp.float32)
        + from_head.astype(jnp.float32)
        + from_diagonal.astype(jnp.float32)
    )


def splits_heads(mesh, qkv_weight, hidden_rows):
    role, seq, head = (mesh.shape[name] for name in ("role", "seq", "head"))
    if role != 2 or head != 2 or seq % CORES != 0:
        return False
    chips = seq // CORES
    heads = qkv_weight.shape[2] // (3 * HEAD_DIM * head)
    width = hidden_rows.shape[1]
    tokens = hidden_rows.shape[0] // seq
    return (
        heads % chips == 0
        and chips == role * head
        and width % (role * head * 256) == 0
        and width % (seq * 16) == 0
        and tokens % (2 * BLOCK) == 0
    )


def solution(mesh):
    def call(*arrays):
        if splits_heads(mesh, arrays[4], arrays[0]):
            per_device = per_device_by_heads
            seq = ("chip", "core")
            shape = mesh.devices.shape
            names = mesh.axis_names
            at = names.index("seq")
            layout = Mesh(
                mesh.devices.reshape(shape[:at] + (shape[at] // CORES, CORES) + shape[at + 1 :]),
                names[:at] + seq + names[at + 1 :],
            )
        else:
            per_device = per_device_by_tokens
            seq = "seq"
            layout = mesh
        placed = (
            P(seq, None),
            P(None, ("role", "head")),
            P(seq, None),
            P(seq),
            P("role", seq, "head"),
            P("role", "head", None),
            P("role", None, "head"),
            P("head", seq, None),
            P("head", seq),
        )
        return jax.shard_map(
            per_device,
            mesh=layout,
            in_specs=placed,
            out_specs=P(seq, ("role", "head")),
            check_vma=False,
        )(*arrays)

    return call
```

```python
import math

import jax
import jax.numpy as jnp
from jax import lax
from jax.experimental import pallas as pl
from jax.experimental.pallas import tpu as pltpu
from jax.sharding import Mesh
from jax.sharding import PartitionSpec as P

HEAD_DIM = 128
BLOCK = 64
KMAX = 8
CAP = 2


def rms_rows(values):
    return values * lax.rsqrt(jnp.mean(values * values, axis=-1, keepdims=True) + 1e-06)


def block_attention(queries, key_table, value_table, key_list, key_count):
    picked_keys = key_table[key_list]
    picked_values = value_table[key_list]
    scale = 1.0 / math.sqrt(HEAD_DIM)
    scores = (
        jnp.einsum("nqe,nkbe->nqkb", queries, picked_keys, preferred_element_type=jnp.float32)
        * scale
    )
    live = lax.broadcasted_iota(jnp.int32, (key_list.shape[0], KMAX), 1) < key_count[:, None]
    scores = jnp.where(live[:, None, :, None], scores, -jnp.inf)
    highest = jnp.max(scores, axis=(2, 3), keepdims=True)
    raised = jnp.exp(scores - highest)
    summed = jnp.sum(raised, axis=(2, 3), keepdims=True)
    weights = (raised / summed).astype(jnp.bfloat16)
    mixed = jnp.einsum("nqkb,nkbe->nqe", weights, picked_values, preferred_element_type=jnp.float32)
    return mixed.astype(jnp.bfloat16)


def pick_blocks(table, wanted):
    return table[wanted]


def per_device_by_tokens(
    hidden_rows,
    gen_weight,
    noise,
    timesteps,
    qkv_weight,
    out_weight,
    qk_gain,
    block_keys,
    block_count,
):
    generated = jnp.dot(hidden_rows, gen_weight, preferred_element_type=jnp.float32).astype(
        jnp.bfloat16
    )
    forked = lax.all_gather(generated, ("role", "head"), axis=1, tiled=True)
    row_count = forked.shape[0]
    width = forked.shape[1]
    local_blocks = timesteps.shape[0]
    angle_blocks = (timesteps.astype(jnp.float32) * (math.pi / 2000.0))[:, None, None]
    noisy = jnp.cos(angle_blocks) * forked.astype(jnp.float32).reshape(local_blocks, BLOCK, width)
    noisy = noisy + jnp.sin(angle_blocks) * noise.astype(jnp.float32).reshape(
        local_blocks, BLOCK, width
    )
    normed = rms_rows(noisy).reshape(row_count, width).astype(jnp.bfloat16)
    weight_here = qkv_weight[0]
    projected = jnp.dot(
        normed,
        lax.all_gather(weight_here, "seq", axis=0, tiled=True),
        preferred_element_type=jnp.float32,
    )
    heads_here = projected.shape[1] // (3 * HEAD_DIM)
    head_parts = projected.reshape(row_count, heads_here, 3, HEAD_DIM)
    gain_here = qk_gain[0]
    queries = (rms_rows(head_parts[:, :, 0]) * gain_here[0][None, :, None]).astype(jnp.bfloat16)
    key_local = (rms_rows(head_parts[:, :, 1]) * gain_here[1][None, :, None]).astype(jnp.bfloat16)
    value_local = head_parts[:, :, 2].astype(jnp.bfloat16)
    query_table = queries.reshape(local_blocks, BLOCK, heads_here, HEAD_DIM).transpose(2, 0, 1, 3)
    shard_count = lax.axis_size("seq")
    shard_here = lax.axis_index("seq")
    all_blocks = shard_count * local_blocks
    key_heads = key_local.reshape(local_blocks, BLOCK, heads_here, HEAD_DIM).transpose(2, 0, 1, 3)
    value_heads = value_local.reshape(local_blocks, BLOCK, heads_here, HEAD_DIM).transpose(
        2, 0, 1, 3
    )
    block_ids = lax.broadcasted_iota(jnp.int32, (1, 1, 1, all_blocks), 3)
    matches = block_keys[:, :, :, None] == block_ids
    remote = block_ids // local_blocks != shard_here
    needed = jnp.any(jnp.logical_and(matches, remote), axis=(1, 2))
    needed = needed.reshape(heads_here, shard_count, local_blocks)
    slot_of = jnp.cumsum(needed.astype(jnp.int32), axis=2) - 1
    slot_ids = lax.broadcasted_iota(jnp.int32, (1, 1, 1, CAP), 3)
    within_ids = lax.broadcasted_iota(jnp.int32, (1, 1, local_blocks, 1), 2)
    chosen_slot = jnp.logical_and(needed[..., None], slot_of[..., None] == slot_ids)
    requests = jnp.sum(jnp.where(chosen_slot, within_ids, 0), axis=2)
    asked = lax.all_to_all(
        requests.transpose(1, 0, 2), "seq", split_axis=0, concat_axis=0, tiled=True
    )
    sent_keys = jax.vmap(pick_blocks, in_axes=(0, 1), out_axes=1)(key_heads, asked)
    sent_values = jax.vmap(pick_blocks, in_axes=(0, 1), out_axes=1)(value_heads, asked)
    got_keys, got_values = (
        lax.all_to_all(sent_keys, "seq", split_axis=0, concat_axis=0, tiled=True),
        lax.all_to_all(sent_values, "seq", split_axis=0, concat_axis=0, tiled=True),
    )
    fetched_keys = got_keys.transpose(1, 0, 2, 3, 4).reshape(
        heads_here, shard_count * CAP, BLOCK, HEAD_DIM
    )
    fetched_values = got_values.transpose(1, 0, 2, 3, 4).reshape(
        heads_here, shard_count * CAP, BLOCK, HEAD_DIM
    )
    key_table = jnp.concatenate([key_heads, fetched_keys], axis=1)
    value_table = jnp.concatenate([value_heads, fetched_values], axis=1)
    local_ids = lax.broadcasted_iota(jnp.int32, (1, shard_count, local_blocks), 2)
    owner_grid = lax.broadcasted_iota(jnp.int32, (1, shard_count, local_blocks), 1)
    position = jnp.where(
        owner_grid == shard_here, local_ids, local_blocks + owner_grid * CAP + slot_of
    )
    position = position.reshape(heads_here, all_blocks)
    key_lists = jnp.sum(jnp.where(matches, position[:, None, None, :], 0), axis=3)
    attended = jax.vmap(block_attention)(
        query_table, key_table, value_table, key_lists, block_count
    )
    attended = attended.transpose(1, 2, 0, 3).reshape(row_count, heads_here * HEAD_DIM)
    contribution = jnp.dot(attended, out_weight[0], preferred_element_type=jnp.float32)
    signed = (2.0 * lax.axis_index("role").astype(jnp.float32) - 1.0) * contribution
    return lax.psum_scatter(
        signed.astype(jnp.bfloat16), ("role", "head"), scatter_dimension=1, tiled=True
    ).astype(jnp.float32)


VMEM_BYTES = 56 * 1024 * 1024
CORES = 2


def whole_in_vmem():
    return pl.BlockSpec(memory_space=pltpu.VMEM)


def in_hbm():
    return pl.BlockSpec(memory_space=pl.ANY)


def in_smem():
    return pl.BlockSpec(memory_space=pltpu.SMEM)


def cut_columns(weight, chips, head):
    rows, columns = weight.shape
    wide = 3 * HEAD_DIM
    chip_heads = columns // (chips * wide)

    def body(weight_ref, out_ref):
        out_ref[0] = weight_ref[...]

    return pl.pallas_call(
        body,
        grid=(chips,),
        in_specs=[pl.BlockSpec((rows, wide), lambda chip: (0, chip * chip_heads + head))],
        out_specs=pl.BlockSpec((1, rows, wide), lambda chip: (chip, 0, 0)),
        out_shape=jax.ShapeDtypeStruct((chips, rows, wide), weight.dtype),
        name="cut_columns",
    )(weight)


def project_heads(places, gains, rounds, weights_own, weights_other):
    heads = len(weights_own)
    slabs, depth, columns = weights_own[0].shape
    tokens, features = rounds[0][0].shape
    pieces = [piece for one in rounds for piece in one]
    turns = len(rounds)
    dtype = weights_own[0].dtype

    def body(places_ref, gains_ref, *refs):
        own_refs, other_refs = refs[:heads], refs[heads : 2 * heads]
        piece_refs = refs[2 * heads : 2 * heads + len(pieces)]
        query_ref, kv_ref = refs[2 * heads + len(pieces) : 2 * heads + len(pieces) + 2]
        table, rows, total, weight_sems, row_sems = refs[2 * heads + len(pieces) + 2 :]
        core = places_ref[slabs]
        copies = []
        for slab in range(slabs):
            here = []
            for head in range(heads):
                for side, ref in enumerate((own_refs[head], other_refs[head])):
                    place = core if side == 0 else 1 - core
                    here.append(
                        pltpu.make_async_copy(
                            ref.at[places_ref[slab]],
                            table.at[slab, place, :, pl.ds(head * columns, columns)],
                            weight_sems.at[slab, head, side],
                        )
                    )
            for turn in range(turns):
                here.append(
                    pltpu.make_async_copy(
                        piece_refs[turn * slabs + slab],
                        rows.at[slab, pl.ds(turn * tokens, tokens)],
                        row_sems.at[slab, turn],
                    )
                )
            for copy in here:
                copy.start()
            copies.append(here)
        for slab in range(slabs):
            for copy in copies[slab]:
                copy.wait()
            part = jnp.dot(
                rows[slab],
                table[slab].reshape(CORES * depth, heads * columns),
                preferred_element_type=jnp.float32,
            )
            if slab == 0:
                total[...] = part
            elif slab < slabs - 1:
                total[...] += part
            else:
                part = total[...] + part
        for turn in range(turns):
            here = part[turn * tokens : (turn + 1) * tokens]
            for head in range(heads):
                at = head * columns
                for which in range(2):
                    block = here[:, at + which * HEAD_DIM : at + (which + 1) * HEAD_DIM]
                    normal = (rms_rows(block) * gains_ref[which, head]).astype(dtype)
                    if which == 0:
                        query_ref[head, turn] = normal
                    else:
                        kv_ref[head, 0, turn] = normal
                block = here[:, at + 2 * HEAD_DIM : at + 3 * HEAD_DIM]
                kv_ref[head, 1, turn] = block.astype(dtype)

    return pl.pallas_call(
        body,
        in_specs=[in_smem(), in_smem()] + [in_hbm()] * (2 * heads + len(pieces)),
        out_specs=(whole_in_vmem(), whole_in_vmem()),
        out_shape=(
            jax.ShapeDtypeStruct((heads, turns, tokens, HEAD_DIM), dtype),
            jax.ShapeDtypeStruct((heads, 2, turns, tokens, HEAD_DIM), dtype),
        ),
        scratch_shapes=[
            pltpu.VMEM((slabs, CORES, depth, heads * columns), dtype),
            pltpu.VMEM((slabs, turns * tokens, features), dtype),
            pltpu.VMEM((turns * tokens, heads * columns), jnp.float32),
            pltpu.SemaphoreType.DMA((slabs, heads, 2)),
            pltpu.SemaphoreType.DMA((slabs, turns)),
        ],
        compiler_params=pltpu.CompilerParams(vmem_limit_bytes=VMEM_BYTES),
        name="project_heads",
    )(places, gains, *weights_own, *weights_other, *pieces)


def attend(key_slots, counts, query_slots, group_most, queries, kv_own, kv_other):
    heads, blocks, most = key_slots.shape
    groups = group_most.shape[1]
    together = blocks // groups
    parts = len(queries)
    sizes = [one.shape[1] for one in queries]
    starts = [sum(sizes[:at]) for at in range(parts)]
    scale = 1.0 / math.sqrt(HEAD_DIM)
    dtype = queries[0].dtype

    def body(slots_ref, counts_ref, from_ref, most_ref, *refs):
        query_refs = refs[:parts]
        own_refs = refs[parts : 2 * parts]
        other_refs = refs[2 * parts : 3 * parts]
        out_ref, query_table, table, query_sems, sems = refs[3 * parts :]
        copies = []
        for at in range(parts):
            span = pl.ds(starts[at], sizes[at])
            copies.append(
                pltpu.make_async_copy(query_refs[at], query_table.at[:, span], query_sems.at[at])
            )
            for side, ref in enumerate((own_refs[at], other_refs[at])):
                span = pl.ds(side * blocks + starts[at], sizes[at])
                copies.append(pltpu.make_async_copy(ref, table.at[:, :, span], sems.at[at, side]))
        for copy in copies:
            copy.start()
        for copy in copies:
            copy.wait()

        def run(head, group, listed, batch):
            for first in range(0, together, batch):
                spots = [group * together + at for at in range(first, min(first + batch, together))]
                slots = [[slots_ref[head, at, entry] for entry in range(listed)] for at in spots]
                scores = []
                for at, listing in zip(spots, slots):
                    keys = jnp.concatenate([table[head, 0, slot] for slot in listing], axis=0)
                    scores.append(
                        lax.dot_general(
                            query_table[head, from_ref[at]],
                            keys,
                            (((1,), (1,)), ((), ())),
                            preferred_element_type=jnp.float32,
                        )
                    )
                column = lax.broadcasted_iota(jnp.int32, (1, listed * BLOCK), 1)
                scores = [
                    jnp.where(column < counts_ref[head, at] * BLOCK, one * scale, -jnp.inf)
                    for at, one in zip(spots, scores)
                ]
                highest = [jnp.max(one, axis=1, keepdims=True) for one in scores]
                raised = [jnp.exp(one - top) for one, top in zip(scores, highest)]
                inverse = [1.0 / jnp.sum(one, axis=1, keepdims=True) for one in raised]
                weights = [(one * by).astype(dtype) for one, by in zip(raised, inverse)]
                mixed = []
                for one, listing in zip(weights, slots):
                    values = jnp.concatenate([table[head, 1, slot] for slot in listing], axis=0)
                    mixed.append(jnp.dot(one, values, preferred_element_type=jnp.float32))
                for at, one in zip(spots, mixed):
                    out_ref[head, at] = one.astype(dtype)

        def step(at, carry):
            head, group = at // groups, at % groups
            few = most_ref[head, group] <= most // 2

            @pl.when(few)
            def _():
                run(head, group, most // 2, 6)

            @pl.when(jnp.logical_not(few))
            def _():
                run(head, group, most, 3)

            return carry

        lax.fori_loop(0, heads * groups, step, 0)

    return pl.pallas_call(
        body,
        in_specs=[in_smem()] * 4 + [in_hbm()] * (3 * parts),
        out_specs=whole_in_vmem(),
        out_shape=jax.ShapeDtypeStruct((heads, blocks, BLOCK, HEAD_DIM), dtype),
        scratch_shapes=[
            pltpu.VMEM((heads, blocks, BLOCK, HEAD_DIM), dtype),
            pltpu.VMEM((heads, 2, CORES * blocks, BLOCK, HEAD_DIM), dtype),
            pltpu.SemaphoreType.DMA((parts,)),
            pltpu.SemaphoreType.DMA((parts, 2)),
        ],
        compiler_params=pltpu.CompilerParams(vmem_limit_bytes=VMEM_BYTES),
        name="attend",
    )(key_slots, counts, query_slots, group_most, *queries, *kv_own, *kv_other)


def out_blocks(which, sign, attended, out_weight, dtype, blocks):
    groups, _, tokens, _ = attended[0].shape
    sizes = [one.shape[1] for one in attended]
    count = len(attended)
    depth, features = out_weight.shape
    width = features // blocks
    tile = 2 * HEAD_DIM
    steps = width // tile

    def body(which_ref, sign_ref, *refs):
        parts, weight_ref, out_ref = refs[:count], refs[count], refs[count + 1]
        columns = []
        for group in range(groups):
            for chunk in range(count):
                for head in range(sizes[chunk]):
                    columns.append(parts[chunk][group, head])
        joined = jnp.concatenate(columns, axis=1)
        total = jnp.dot(joined, weight_ref[...], preferred_element_type=jnp.float32)
        out_ref[...] = (total * sign_ref[0].astype(jnp.float32)).astype(dtype)

    return pl.pallas_call(
        body,
        grid_spec=pltpu.PrefetchScalarGridSpec(
            num_scalar_prefetch=2,
            grid=(steps,),
            in_specs=[pl.BlockSpec(one.shape, lambda i, w, s: (0, 0, 0, 0)) for one in attended]
            + [pl.BlockSpec((depth, tile), lambda i, w, s: (0, w[0] * steps + i))],
            out_specs=pl.BlockSpec((tokens, tile), lambda i, w, s: (0, i)),
        ),
        out_shape=jax.ShapeDtypeStruct((tokens, width), dtype),
        compiler_params=pltpu.CompilerParams(vmem_limit_bytes=VMEM_BYTES),
        name="out_blocks",
    )(which, sign, *attended, out_weight)


def chunk_sizes(heads):
    last = max(1, heads // 3)
    return [heads - last, last] if heads > last else [heads]


def per_device_by_heads(
    hidden_rows,
    gen_weight,
    noise,
    timesteps,
    qkv_weight,
    out_weight,
    qk_gain,
    block_keys,
    block_count,
):
    role, head = lax.axis_index("role"), lax.axis_index("head")
    chip, core = lax.axis_index("chip"), lax.axis_index("core")
    chips = lax.axis_size("chip")
    local_heads, local_blocks, most = block_keys.shape
    heads = local_heads // chips
    tokens = hidden_rows.shape[0]
    width = hidden_rows.shape[1]
    features = gen_weight.shape[1]
    all_blocks = chips * local_blocks
    swap = [(0, 1), (1, 0)]
    upward = [(at, (at + 1) % chips) for at in range(chips)]
    downward = [((at + 1) % chips, at) for at in range(chips)]

    def turn_of(behind):
        return jnp.where(behind <= chips // 2, jnp.maximum(2 * behind - 1, 0), 2 * (chips - behind))

    def exchange(array):
        return lax.all_to_all(array, "chip", split_axis=0, concat_axis=0, tiled=True)

    weight_here = qkv_weight[0]
    cuts = [cut_columns(weight_here, chips, at) for at in range(heads)]
    weights_own = [exchange(cuts[0])]

    mine = role * lax.axis_size("head") + head
    generated = jnp.dot(hidden_rows, gen_weight, preferred_element_type=jnp.float32)
    generated = lax.reduce_precision(generated, 8, 7)
    angle_blocks = (timesteps.astype(jnp.float32) * (math.pi / 2000.0))[:, None, None]
    noise_here = lax.dynamic_slice_in_dim(noise, mine * features, features, axis=1)
    noisy = jnp.cos(angle_blocks) * generated.reshape(local_blocks, BLOCK, features)
    noisy = noisy + jnp.sin(angle_blocks) * noise_here.astype(jnp.float32).reshape(
        local_blocks, BLOCK, features
    )
    squares = jnp.sum(noisy * noisy, axis=-1)
    squares = squares + lax.ppermute(squares, "role", swap)
    squares = squares + lax.ppermute(squares, "head", swap)
    normed = (noisy * lax.rsqrt(squares / width + 1e-06)[:, :, None]).astype(jnp.bfloat16)
    normed = normed.reshape(tokens, features)

    shards = [normed]
    up = down = normed
    for at in range(1, chips):
        if at % 2 == 1:
            up = lax.ppermute(up, "chip", upward)
            shards.append(up)
        else:
            down = lax.ppermute(down, "chip", downward)
            shards.append(down)
    rounds = []
    for at, shard in enumerate(shards):
        over_role = lax.ppermute(shard, "role", swap)
        over_head = lax.ppermute(shard, "head", swap)
        if at % 2 == 0:
            diagonal = lax.ppermute(over_head, "role", swap)
        else:
            diagonal = lax.ppermute(over_role, "head", swap)
        rounds.append((shard, over_role, over_head, diagonal))

    lists = jnp.concatenate([block_keys, block_count[:, :, None]], axis=2)
    lists, _ = lax.optimization_barrier((lists, normed))
    lists = lax.all_gather(lists, "chip", axis=1, tiled=True)
    lists = lax.dynamic_slice_in_dim(lists, chip * heads, heads, axis=0)

    for at in range(1, heads):
        if at == 1:
            held, _ = lax.optimization_barrier((cuts[at], (lists, shards[1:3])))
        else:
            held, _ = lax.optimization_barrier((cuts[at], weights_own[-1]))
        weights_own.append(exchange(held))
    weights_other = [lax.ppermute(one, "core", swap) for one in weights_own]

    owner = lists[:, :, :most] // local_blocks
    turn = turn_of((chip - owner // CORES) % chips)
    far = (owner % CORES != core).astype(jnp.int32)
    key_slots = far * all_blocks + turn * local_blocks + lists[:, :, :most] % local_blocks
    counts = lists[:, :, most]
    group_most = jnp.max(counts.reshape(heads, chips, local_blocks), axis=2)
    spot = jnp.arange(all_blocks, dtype=jnp.int32)
    query_slots = turn_of((chip - spot // local_blocks) % chips)
    query_slots = query_slots * local_blocks + spot % local_blocks

    sides = lax.axis_size("head")
    peers = jnp.stack(
        [
            role * sides + head,
            (1 - role) * sides + head,
            role * sides + 1 - head,
            (1 - role) * sides + 1 - head,
        ]
    ).astype(jnp.int32)
    places = jnp.concatenate([peers, core[None].astype(jnp.int32)])
    gains = lax.dynamic_slice_in_dim(qk_gain[0], chip * heads, heads, axis=1)

    attended = []
    held_places = places
    chunks = chunk_sizes(heads)
    for at, size in enumerate(chunks):
        span = slice(sum(chunks[:at]), sum(chunks[: at + 1]))
        last = at == len(chunks) - 1
        parts = [rounds] if last else [rounds[:-1], rounds[-1:]]
        queries, kv_own, kv_other = [], [], []
        for part in parts:
            query, kv = project_heads(
                held_places, gains[:, span], part, weights_own[span], weights_other[span]
            )
            here = len(part) * local_blocks
            queries.append(query.reshape(size, here, BLOCK, HEAD_DIM))
            kv_own.append(kv.reshape(size, 2, here, BLOCK, HEAD_DIM))
            kv_other.append(lax.ppermute(kv_own[-1], "core", swap))
            held_places, _ = lax.optimization_barrier((places, kv))
        mixed = attend(
            key_slots[span],
            counts[span],
            query_slots,
            group_most[span],
            queries,
            kv_own,
            kv_other,
        )
        held_places, _ = lax.optimization_barrier((places, mixed))
        mixed = mixed.reshape(size, chips, tokens, HEAD_DIM).transpose(1, 0, 2, 3)
        attended.append(exchange(mixed))

    sign = (2 * role - 1).astype(jnp.int32)[None]
    blocks = sides * lax.axis_size("role")

    def block_of(at, dtype):
        return out_blocks(peers[at : at + 1], sign, attended, out_weight[0], dtype, blocks)

    far_swap = [(0, 3), (1, 2), (2, 1), (3, 0)]
    from_diagonal = lax.ppermute(block_of(3, jnp.bfloat16), ("role", "head"), far_swap)
    from_role = lax.ppermute(block_of(1, jnp.bfloat16), "role", swap)
    from_head = lax.ppermute(block_of(2, jnp.bfloat16), "head", swap)
    return block_of(0, jnp.float32) + (
        from_role.astype(jnp.float32)
        + from_head.astype(jnp.float32)
        + from_diagonal.astype(jnp.float32)
    )


def splits_heads(mesh, qkv_weight, hidden_rows):
    role, seq, head = (mesh.shape[name] for name in ("role", "seq", "head"))
    if role != 2 or head != 2 or seq % CORES != 0:
        return False
    chips = seq // CORES
    heads = qkv_weight.shape[2] // (3 * HEAD_DIM * head)
    width = hidden_rows.shape[1]
    tokens = hidden_rows.shape[0] // seq
    return (
        heads % chips == 0
        and chips == role * head
        and width % (role * head * 256) == 0
        and width % (seq * 16) == 0
        and tokens % (2 * BLOCK) == 0
    )


def solution(mesh):
    def call(*arrays):
        if splits_heads(mesh, arrays[4], arrays[0]):
            per_device = per_device_by_heads
            seq = ("chip", "core")
            shape = mesh.devices.shape
            names = mesh.axis_names
            at = names.index("seq")
            layout = Mesh(
                mesh.devices.reshape(shape[:at] + (shape[at] // CORES, CORES) + shape[at + 1 :]),
                names[:at] + seq + names[at + 1 :],
            )
        else:
            per_device = per_device_by_tokens
            seq = "seq"
            layout = mesh
        placed = (
            P(seq, None),
            P(None, ("role", "head")),
            P(seq, None),
            P(seq),
            P("role", seq, "head"),
            P("role", "head", None),
            P("role", None, "head"),
            P("head", seq, None),
            P("head", seq),
        )
        return jax.shard_map(
            per_device,
            mesh=layout,
            in_specs=placed,
            out_specs=P(seq, ("role", "head")),
            check_vma=False,
        )(*arrays)

    return call
```

```python
import math

import jax
import jax.numpy as jnp
from jax import lax
from jax.experimental import pallas as pl
from jax.experimental.pallas import tpu as pltpu
from jax.sharding import Mesh
from jax.sharding import PartitionSpec as P

HEAD_DIM = 128
BLOCK = 64
KMAX = 8
CAP = 2


def rms_rows(values):
    return values * lax.rsqrt(jnp.mean(values * values, axis=-1, keepdims=True) + 1e-06)


def block_attention(queries, key_table, value_table, key_list, key_count):
    picked_keys = key_table[key_list]
    picked_values = value_table[key_list]
    scale = 1.0 / math.sqrt(HEAD_DIM)
    scores = (
        jnp.einsum("nqe,nkbe->nqkb", queries, picked_keys, preferred_element_type=jnp.float32)
        * scale
    )
    live = lax.broadcasted_iota(jnp.int32, (key_list.shape[0], KMAX), 1) < key_count[:, None]
    scores = jnp.where(live[:, None, :, None], scores, -jnp.inf)
    highest = jnp.max(scores, axis=(2, 3), keepdims=True)
    raised = jnp.exp(scores - highest)
    summed = jnp.sum(raised, axis=(2, 3), keepdims=True)
    weights = (raised / summed).astype(jnp.bfloat16)
    mixed = jnp.einsum("nqkb,nkbe->nqe", weights, picked_values, preferred_element_type=jnp.float32)
    return mixed.astype(jnp.bfloat16)


def pick_blocks(table, wanted):
    return table[wanted]


def per_device_by_tokens(
    hidden_rows,
    gen_weight,
    noise,
    timesteps,
    qkv_weight,
    out_weight,
    qk_gain,
    block_keys,
    block_count,
):
    generated = jnp.dot(hidden_rows, gen_weight, preferred_element_type=jnp.float32).astype(
        jnp.bfloat16
    )
    forked = lax.all_gather(generated, ("role", "head"), axis=1, tiled=True)
    row_count = forked.shape[0]
    width = forked.shape[1]
    local_blocks = timesteps.shape[0]
    angle_blocks = (timesteps.astype(jnp.float32) * (math.pi / 2000.0))[:, None, None]
    noisy = jnp.cos(angle_blocks) * forked.astype(jnp.float32).reshape(local_blocks, BLOCK, width)
    noisy = noisy + jnp.sin(angle_blocks) * noise.astype(jnp.float32).reshape(
        local_blocks, BLOCK, width
    )
    normed = rms_rows(noisy).reshape(row_count, width).astype(jnp.bfloat16)
    weight_here = qkv_weight[0]
    projected = jnp.dot(
        normed,
        lax.all_gather(weight_here, "seq", axis=0, tiled=True),
        preferred_element_type=jnp.float32,
    )
    heads_here = projected.shape[1] // (3 * HEAD_DIM)
    head_parts = projected.reshape(row_count, heads_here, 3, HEAD_DIM)
    gain_here = qk_gain[0]
    queries = (rms_rows(head_parts[:, :, 0]) * gain_here[0][None, :, None]).astype(jnp.bfloat16)
    key_local = (rms_rows(head_parts[:, :, 1]) * gain_here[1][None, :, None]).astype(jnp.bfloat16)
    value_local = head_parts[:, :, 2].astype(jnp.bfloat16)
    query_table = queries.reshape(local_blocks, BLOCK, heads_here, HEAD_DIM).transpose(2, 0, 1, 3)
    shard_count = lax.axis_size("seq")
    shard_here = lax.axis_index("seq")
    all_blocks = shard_count * local_blocks
    key_heads = key_local.reshape(local_blocks, BLOCK, heads_here, HEAD_DIM).transpose(2, 0, 1, 3)
    value_heads = value_local.reshape(local_blocks, BLOCK, heads_here, HEAD_DIM).transpose(
        2, 0, 1, 3
    )
    block_ids = lax.broadcasted_iota(jnp.int32, (1, 1, 1, all_blocks), 3)
    matches = block_keys[:, :, :, None] == block_ids
    remote = block_ids // local_blocks != shard_here
    needed = jnp.any(jnp.logical_and(matches, remote), axis=(1, 2))
    needed = needed.reshape(heads_here, shard_count, local_blocks)
    slot_of = jnp.cumsum(needed.astype(jnp.int32), axis=2) - 1
    slot_ids = lax.broadcasted_iota(jnp.int32, (1, 1, 1, CAP), 3)
    within_ids = lax.broadcasted_iota(jnp.int32, (1, 1, local_blocks, 1), 2)
    chosen_slot = jnp.logical_and(needed[..., None], slot_of[..., None] == slot_ids)
    requests = jnp.sum(jnp.where(chosen_slot, within_ids, 0), axis=2)
    asked = lax.all_to_all(
        requests.transpose(1, 0, 2), "seq", split_axis=0, concat_axis=0, tiled=True
    )
    sent_keys = jax.vmap(pick_blocks, in_axes=(0, 1), out_axes=1)(key_heads, asked)
    sent_values = jax.vmap(pick_blocks, in_axes=(0, 1), out_axes=1)(value_heads, asked)
    got_keys, got_values = (
        lax.all_to_all(sent_keys, "seq", split_axis=0, concat_axis=0, tiled=True),
        lax.all_to_all(sent_values, "seq", split_axis=0, concat_axis=0, tiled=True),
    )
    fetched_keys = got_keys.transpose(1, 0, 2, 3, 4).reshape(
        heads_here, shard_count * CAP, BLOCK, HEAD_DIM
    )
    fetched_values = got_values.transpose(1, 0, 2, 3, 4).reshape(
        heads_here, shard_count * CAP, BLOCK, HEAD_DIM
    )
    key_table = jnp.concatenate([key_heads, fetched_keys], axis=1)
    value_table = jnp.concatenate([value_heads, fetched_values], axis=1)
    local_ids = lax.broadcasted_iota(jnp.int32, (1, shard_count, local_blocks), 2)
    owner_grid = lax.broadcasted_iota(jnp.int32, (1, shard_count, local_blocks), 1)
    position = jnp.where(
        owner_grid == shard_here, local_ids, local_blocks + owner_grid * CAP + slot_of
    )
    position = position.reshape(heads_here, all_blocks)
    key_lists = jnp.sum(jnp.where(matches, position[:, None, None, :], 0), axis=3)
    attended = jax.vmap(block_attention)(
        query_table, key_table, value_table, key_lists, block_count
    )
    attended = attended.transpose(1, 2, 0, 3).reshape(row_count, heads_here * HEAD_DIM)
    contribution = jnp.dot(attended, out_weight[0], preferred_element_type=jnp.float32)
    signed = (2.0 * lax.axis_index("role").astype(jnp.float32) - 1.0) * contribution
    return lax.psum_scatter(
        signed.astype(jnp.bfloat16), ("role", "head"), scatter_dimension=1, tiled=True
    ).astype(jnp.float32)


VMEM_BYTES = 56 * 1024 * 1024
CORES = 2


def whole_in_vmem():
    return pl.BlockSpec(memory_space=pltpu.VMEM)


def in_hbm():
    return pl.BlockSpec(memory_space=pl.ANY)


def in_smem():
    return pl.BlockSpec(memory_space=pltpu.SMEM)


def cut_columns(weight, chips, head):
    rows, columns = weight.shape
    wide = 3 * HEAD_DIM
    chip_heads = columns // (chips * wide)

    def body(weight_ref, out_ref):
        out_ref[0] = weight_ref[...]

    return pl.pallas_call(
        body,
        grid=(chips,),
        in_specs=[pl.BlockSpec((rows, wide), lambda chip: (0, chip * chip_heads + head))],
        out_specs=pl.BlockSpec((1, rows, wide), lambda chip: (chip, 0, 0)),
        out_shape=jax.ShapeDtypeStruct((chips, rows, wide), weight.dtype),
        name="cut_columns",
    )(weight)


def project_heads(places, gains, rounds, weights_own, weights_other):
    heads = len(weights_own)
    slabs, depth, columns = weights_own[0].shape
    tokens, features = rounds[0][0].shape
    pieces = [piece for one in rounds for piece in one]
    turns = len(rounds)
    per_round = len(rounds[0])
    half = tokens // 2
    dtype = weights_own[0].dtype

    def body(places_ref, gains_ref, *refs):
        own_refs, other_refs = refs[:heads], refs[heads : 2 * heads]
        piece_refs = refs[2 * heads : 2 * heads + len(pieces)]
        query_ref, kv_ref = refs[2 * heads + len(pieces) : 2 * heads + len(pieces) + 2]
        table, rows, total, weight_sems, row_sems = refs[2 * heads + len(pieces) + 2 :]
        core = places_ref[slabs]
        copies = []
        for slab in range(slabs):
            here = []
            for head in range(heads):
                for side, ref in enumerate((own_refs[head], other_refs[head])):
                    place = core if side == 0 else 1 - core
                    here.append(
                        pltpu.make_async_copy(
                            ref.at[places_ref[slab]],
                            table.at[slab, place, :, pl.ds(head * columns, columns)],
                            weight_sems.at[slab, head, side],
                        )
                    )
            for turn in range(turns):
                for which in [slab] if slab < slabs - 1 else [slab, slab + 1]:
                    first = turn * tokens + max(which - slabs + 1, 0) * half
                    count = tokens if slab < slabs - 1 else half
                    here.append(
                        pltpu.make_async_copy(
                            piece_refs[turn * per_round + which],
                            rows.at[slab, pl.ds(first, count)],
                            row_sems.at[which, turn],
                        )
                    )
            for copy in here:
                copy.start()
            copies.append(here)
        for slab in range(slabs):
            for copy in copies[slab]:
                copy.wait()
            part = jnp.dot(
                rows[slab],
                table[slab].reshape(CORES * depth, heads * columns),
                preferred_element_type=jnp.float32,
            )
            if slab == 0:
                total[...] = part
            elif slab < slabs - 1:
                total[...] += part
            else:
                part = total[...] + part
        for turn in range(turns):
            here = part[turn * tokens : (turn + 1) * tokens]
            for head in range(heads):
                at = head * columns
                for which in range(2):
                    block = here[:, at + which * HEAD_DIM : at + (which + 1) * HEAD_DIM]
                    normal = (rms_rows(block) * gains_ref[which, head]).astype(dtype)
                    if which == 0:
                        query_ref[head, turn] = normal
                    else:
                        kv_ref[head, 0, turn] = normal
                block = here[:, at + 2 * HEAD_DIM : at + 3 * HEAD_DIM]
                kv_ref[head, 1, turn] = block.astype(dtype)

    return pl.pallas_call(
        body,
        in_specs=[in_smem(), in_smem()] + [in_hbm()] * (2 * heads + len(pieces)),
        out_specs=(whole_in_vmem(), whole_in_vmem()),
        out_shape=(
            jax.ShapeDtypeStruct((heads, turns, tokens, HEAD_DIM), dtype),
            jax.ShapeDtypeStruct((heads, 2, turns, tokens, HEAD_DIM), dtype),
        ),
        scratch_shapes=[
            pltpu.VMEM((slabs, CORES, depth, heads * columns), dtype),
            pltpu.VMEM((slabs, turns * tokens, features), dtype),
            pltpu.VMEM((turns * tokens, heads * columns), jnp.float32),
            pltpu.SemaphoreType.DMA((slabs, heads, 2)),
            pltpu.SemaphoreType.DMA((per_round, turns)),
        ],
        compiler_params=pltpu.CompilerParams(vmem_limit_bytes=VMEM_BYTES),
        name="project_heads",
    )(places, gains, *weights_own, *weights_other, *pieces)


def attend(key_slots, counts, query_slots, group_most, queries, kv_own, kv_other):
    heads, blocks, most = key_slots.shape
    groups = group_most.shape[1]
    together = blocks // groups
    parts = len(queries)
    sizes = [one.shape[1] for one in queries]
    starts = [sum(sizes[:at]) for at in range(parts)]
    scale = 1.0 / math.sqrt(HEAD_DIM)
    dtype = queries[0].dtype

    def body(slots_ref, counts_ref, from_ref, most_ref, *refs):
        query_refs = refs[:parts]
        own_refs = refs[parts : 2 * parts]
        other_refs = refs[2 * parts : 3 * parts]
        out_ref, query_table, table, query_sems, sems = refs[3 * parts :]
        copies = []
        for at in range(parts):
            span = pl.ds(starts[at], sizes[at])
            copies.append(
                pltpu.make_async_copy(query_refs[at], query_table.at[:, span], query_sems.at[at])
            )
            for side, ref in enumerate((own_refs[at], other_refs[at])):
                span = pl.ds(side * blocks + starts[at], sizes[at])
                copies.append(pltpu.make_async_copy(ref, table.at[:, :, span], sems.at[at, side]))
        for copy in copies:
            copy.start()
        for copy in copies:
            copy.wait()

        def run(head, group, listed, batch):
            for first in range(0, together, batch):
                spots = [group * together + at for at in range(first, min(first + batch, together))]
                slots = [[slots_ref[head, at, entry] for entry in range(listed)] for at in spots]
                scores = []
                for at, listing in zip(spots, slots):
                    keys = jnp.concatenate([table[head, 0, slot] for slot in listing], axis=0)
                    scores.append(
                        lax.dot_general(
                            query_table[head, from_ref[at]],
                            keys,
                            (((1,), (1,)), ((), ())),
                            preferred_element_type=jnp.float32,
                        )
                    )
                column = lax.broadcasted_iota(jnp.int32, (1, listed * BLOCK), 1)
                scores = [
                    jnp.where(column < counts_ref[head, at] * BLOCK, one * scale, -jnp.inf)
                    for at, one in zip(spots, scores)
                ]
                highest = [jnp.max(one, axis=1, keepdims=True) for one in scores]
                raised = [jnp.exp(one - top) for one, top in zip(scores, highest)]
                inverse = [1.0 / jnp.sum(one, axis=1, keepdims=True) for one in raised]
                weights = [(one * by).astype(dtype) for one, by in zip(raised, inverse)]
                mixed = []
                for one, listing in zip(weights, slots):
                    values = jnp.concatenate([table[head, 1, slot] for slot in listing], axis=0)
                    mixed.append(jnp.dot(one, values, preferred_element_type=jnp.float32))
                for at, one in zip(spots, mixed):
                    out_ref[head, at] = one.astype(dtype)

        def step(at, carry):
            head, group = at // groups, at % groups
            few = most_ref[head, group] <= most // 2

            @pl.when(few)
            def _():
                run(head, group, most // 2, 6)

            @pl.when(jnp.logical_not(few))
            def _():
                run(head, group, most, 3)

            return carry

        lax.fori_loop(0, heads * groups, step, 0)

    return pl.pallas_call(
        body,
        in_specs=[in_smem()] * 4 + [in_hbm()] * (3 * parts),
        out_specs=whole_in_vmem(),
        out_shape=jax.ShapeDtypeStruct((heads, blocks, BLOCK, HEAD_DIM), dtype),
        scratch_shapes=[
            pltpu.VMEM((heads, blocks, BLOCK, HEAD_DIM), dtype),
            pltpu.VMEM((heads, 2, CORES * blocks, BLOCK, HEAD_DIM), dtype),
            pltpu.SemaphoreType.DMA((parts,)),
            pltpu.SemaphoreType.DMA((parts, 2)),
        ],
        compiler_params=pltpu.CompilerParams(vmem_limit_bytes=VMEM_BYTES),
        name="attend",
    )(key_slots, counts, query_slots, group_most, *queries, *kv_own, *kv_other)


def out_blocks(which, sign, attended, out_weight, dtypes, blocks):
    groups, _, tokens, _ = attended[0].shape
    sizes = [one.shape[1] for one in attended]
    count = len(attended)
    depth, features = out_weight.shape
    width = features // blocks
    wanted = len(dtypes)

    def body(which_ref, sign_ref, *refs):
        parts, weight_ref, out_refs = refs[:count], refs[count], refs[count + 1 :]
        columns = []
        for group in range(groups):
            for chunk in range(count):
                for head in range(sizes[chunk]):
                    columns.append(parts[chunk][group, head])
        joined = jnp.concatenate(columns, axis=1)
        total = jnp.dot(joined, weight_ref[...], preferred_element_type=jnp.float32)
        total = total * sign_ref[0].astype(jnp.float32)
        for at in range(wanted):

            @pl.when(pl.program_id(0) == at)
            def _(at=at):
                out_refs[at][...] = total.astype(dtypes[at])

    return pl.pallas_call(
        body,
        grid_spec=pltpu.PrefetchScalarGridSpec(
            num_scalar_prefetch=2,
            grid=(wanted,),
            in_specs=[pl.BlockSpec(one.shape, lambda i, w, s: (0, 0, 0, 0)) for one in attended]
            + [pl.BlockSpec((depth, width), lambda i, w, s: (0, w[i]))],
            out_specs=[pl.BlockSpec((tokens, width), lambda i, w, s: (0, 0))] * wanted,
        ),
        out_shape=[jax.ShapeDtypeStruct((tokens, width), dtype) for dtype in dtypes],
        compiler_params=pltpu.CompilerParams(vmem_limit_bytes=VMEM_BYTES),
        name="out_blocks",
    )(which, sign, *attended, out_weight)


def nearest(chips):
    order = [
        sorted((at for at in range(chips) if at != here), key=lambda at: (abs(at - here), at))
        for here in range(chips)
    ]
    turns = [
        [0 if at == here else order[here].index(at) + 1 for at in range(chips)]
        for here in range(chips)
    ]
    return order, turns


def chunk_sizes(heads):
    last = max(1, heads // 3)
    return [heads - last, last] if heads > last else [heads]


def per_device_by_heads(
    hidden_rows,
    gen_weight,
    noise,
    timesteps,
    qkv_weight,
    out_weight,
    qk_gain,
    block_keys,
    block_count,
):
    role, head = lax.axis_index("role"), lax.axis_index("head")
    chip, core = lax.axis_index("chip"), lax.axis_index("core")
    chips = lax.axis_size("chip")
    local_heads, local_blocks, most = block_keys.shape
    heads = local_heads // chips
    tokens = hidden_rows.shape[0]
    width = hidden_rows.shape[1]
    features = gen_weight.shape[1]
    all_blocks = chips * local_blocks
    swap = [(0, 1), (1, 0)]
    order, turns = nearest(chips)
    turn_here = jnp.asarray(turns, dtype=jnp.int32)[chip]

    def pick(index, options):
        picked = options[0]
        for at in range(1, len(options)):
            picked = jnp.where(index == at, options[at], picked)
        return picked

    def turn_of(other):
        return pick(other, [turn_here[at] for at in range(chips)])

    def exchange(array):
        return lax.all_to_all(array, "chip", split_axis=0, concat_axis=0, tiled=True)

    weight_here = qkv_weight[0]
    cuts = [cut_columns(weight_here, chips, at) for at in range(heads)]
    hidden_rows, cuts[0] = lax.optimization_barrier((hidden_rows, cuts[0]))
    weights_own = [exchange(cuts[0])]

    mine = role * lax.axis_size("head") + head
    generated = jnp.dot(hidden_rows, gen_weight, preferred_element_type=jnp.float32)
    generated = lax.reduce_precision(generated, 8, 7)
    angle_blocks = (timesteps.astype(jnp.float32) * (math.pi / 2000.0))[:, None, None]
    noise_here = lax.dynamic_slice_in_dim(noise, mine * features, features, axis=1)
    noisy = jnp.cos(angle_blocks) * generated.reshape(local_blocks, BLOCK, features)
    noisy = noisy + jnp.sin(angle_blocks) * noise_here.astype(jnp.float32).reshape(
        local_blocks, BLOCK, features
    )
    squares = jnp.sum(noisy * noisy, axis=-1)
    squares = squares + lax.ppermute(squares, "role", swap)
    squares = squares + lax.ppermute(squares, "head", swap)
    normed = (noisy * lax.rsqrt(squares / width + 1e-06)[:, :, None]).astype(jnp.bfloat16)
    normed = normed.reshape(tokens, features)

    lists = jnp.concatenate([block_keys, block_count[:, :, None]], axis=2)
    half = tokens // 2
    rounds = []
    straight = None
    shard, up, down = normed, normed, normed
    ups, downs = [None], [None]
    gathered = [lists]
    for phase in range(chips + 1):
        sent = {}
        if phase < chips:
            sent["role"] = lax.ppermute(shard, "role", swap)
            sent["head"] = lax.ppermute(shard, "head", swap)
        if straight is not None:
            sent["first"] = lax.ppermute(straight[2][:half], "role", swap)
            sent["second"] = lax.ppermute(straight[1][half:], "head", swap)
        step = phase + 1
        if step < chips:
            sent["up"] = lax.ppermute(
                up, "chip", [(at, at + 1) for at in range(step - 1, chips - 1)]
            )
            sent["down"] = lax.ppermute(
                down, "chip", [(at + 1, at) for at in range(chips - step)]
            )
        if phase == 1:
            for shift in range(1, chips):
                pairs = [(at, (at + shift) % chips) for at in range(chips)]
                sent["lists" + str(shift)] = lax.ppermute(lists, "chip", pairs)
        if phase == 0:
            sent["weights"] = weights_own.pop()
        sent, (shard, straight) = lax.optimization_barrier((sent, (shard, straight)))
        if phase == 0:
            weights_own.append(sent["weights"])
        if phase == 1:
            gathered += [sent["lists" + str(shift)] for shift in range(1, chips)]
        if straight is not None:
            rounds.append(straight + (sent["first"], sent["second"]))
        if phase < chips:
            straight = (shard, sent["role"], sent["head"])
        if step < chips:
            up, down = sent["up"], sent["down"]
            ups.append(up)
            downs.append(down)
            options = []
            for here in range(chips):
                source = order[here][step - 1]
                options.append(ups[here - source] if source < here else downs[source - here])
            shard = pick(chip, options)
        if phase % 2 == 0 and len(weights_own) < heads:
            held, _ = lax.optimization_barrier((cuts[len(weights_own)], sent))
            weights_own.append(exchange(held))
    while len(weights_own) < heads:
        weights_own.append(exchange(cuts[len(weights_own)]))
    weights_other = [lax.ppermute(one, "core", swap) for one in weights_own]

    gathered = [lax.dynamic_slice_in_dim(one, chip * heads, heads, axis=0) for one in gathered]
    lists = jnp.concatenate(
        [pick((chip - at) % chips, gathered) for at in range(chips)], axis=1
    )
    owner = lists[:, :, :most] // local_blocks
    turn = turn_of(owner // CORES)
    far = (owner % CORES != core).astype(jnp.int32)
    key_slots = far * all_blocks + turn * local_blocks + lists[:, :, :most] % local_blocks
    counts = lists[:, :, most]
    group_most = jnp.max(counts.reshape(heads, chips, local_blocks), axis=2)
    spot = jnp.arange(all_blocks, dtype=jnp.int32)
    query_slots = turn_of(spot // local_blocks)
    query_slots = query_slots * local_blocks + spot % local_blocks

    sides = lax.axis_size("head")
    peers = jnp.stack(
        [
            role * sides + head,
            (1 - role) * sides + head,
            role * sides + 1 - head,
            (1 - role) * sides + 1 - head,
        ]
    ).astype(jnp.int32)
    places = jnp.concatenate([peers, core[None].astype(jnp.int32)])
    gains = lax.dynamic_slice_in_dim(qk_gain[0], chip * heads, heads, axis=1)

    attended = []
    held_places = places
    chunks = chunk_sizes(heads)
    for at, size in enumerate(chunks):
        span = slice(sum(chunks[:at]), sum(chunks[: at + 1]))
        last = at == len(chunks) - 1
        parts = [rounds] if last else [rounds[:-1], rounds[-1:]]
        queries, kv_own, kv_other = [], [], []
        for part in parts:
            query, kv = project_heads(
                held_places, gains[:, span], part, weights_own[span], weights_other[span]
            )
            here = len(part) * local_blocks
            queries.append(query.reshape(size, here, BLOCK, HEAD_DIM))
            kv_own.append(kv.reshape(size, 2, here, BLOCK, HEAD_DIM))
            kv_other.append(lax.ppermute(kv_own[-1], "core", swap))
            held_places, _ = lax.optimization_barrier((places, kv))
        mixed = attend(
            key_slots[span],
            counts[span],
            query_slots,
            group_most[span],
            queries,
            kv_own,
            kv_other,
        )
        held_places, _ = lax.optimization_barrier((places, mixed))
        mixed = mixed.reshape(size, chips, tokens, HEAD_DIM).transpose(1, 0, 2, 3)
        attended.append(exchange(mixed))

    sign = (2 * role - 1).astype(jnp.int32)[None]
    blocks = sides * lax.axis_size("role")

    def blocks_of(first, second, dtypes):
        which = jnp.stack([peers[first], peers[second]])
        return out_blocks(which, sign, attended, out_weight[0], dtypes, blocks)

    far_swap = [(0, 3), (1, 2), (2, 1), (3, 0)]
    diagonal, over_head = blocks_of(3, 2, (jnp.bfloat16, jnp.bfloat16))
    over_role, own = blocks_of(1, 0, (jnp.bfloat16, jnp.float32))
    from_diagonal = lax.ppermute(diagonal, ("role", "head"), far_swap)
    from_head = lax.ppermute(over_head, "head", swap)
    from_role = lax.ppermute(over_role, "role", swap)
    return own + (
        from_role.astype(jnp.float32)
        + from_head.astype(jnp.float32)
        + from_diagonal.astype(jnp.float32)
    )


def splits_heads(mesh, qkv_weight, hidden_rows):
    role, seq, head = (mesh.shape[name] for name in ("role", "seq", "head"))
    if role != 2 or head != 2 or seq % CORES != 0:
        return False
    chips = seq // CORES
    heads = qkv_weight.shape[2] // (3 * HEAD_DIM * head)
    width = hidden_rows.shape[1]
    tokens = hidden_rows.shape[0] // seq
    return (
        heads % chips == 0
        and chips == role * head
        and width % (role * head * 256) == 0
        and width % (seq * 16) == 0
        and tokens % (2 * BLOCK) == 0
    )


def solution(mesh):
    def call(*arrays):
        if splits_heads(mesh, arrays[4], arrays[0]):
            per_device = per_device_by_heads
            seq = ("chip", "core")
            shape = mesh.devices.shape
            names = mesh.axis_names
            at = names.index("seq")
            layout = Mesh(
                mesh.devices.reshape(shape[:at] + (shape[at] // CORES, CORES) + shape[at + 1 :]),
                names[:at] + seq + names[at + 1 :],
            )
        else:
            per_device = per_device_by_tokens
            seq = "seq"
            layout = mesh
        placed = (
            P(seq, None),
            P(None, ("role", "head")),
            P(seq, None),
            P(seq),
            P("role", seq, "head"),
            P("role", "head", None),
            P("role", None, "head"),
            P("head", seq, None),
            P("head", seq),
        )
        return jax.shard_map(
            per_device,
            mesh=layout,
            in_specs=placed,
            out_specs=P(seq, ("role", "head")),
            check_vma=False,
        )(*arrays)

    return call
```

```python
import math

import jax
import jax.numpy as jnp
from jax import lax
from jax.experimental import pallas as pl
from jax.experimental.pallas import tpu as pltpu
from jax.sharding import Mesh
from jax.sharding import PartitionSpec as P

HEAD_DIM = 128
BLOCK = 64
KMAX = 8
CAP = 2


def rms_rows(values):
    return values * lax.rsqrt(jnp.mean(values * values, axis=-1, keepdims=True) + 1e-06)


def block_attention(queries, key_table, value_table, key_list, key_count):
    picked_keys = key_table[key_list]
    picked_values = value_table[key_list]
    scale = 1.0 / math.sqrt(HEAD_DIM)
    scores = (
        jnp.einsum("nqe,nkbe->nqkb", queries, picked_keys, preferred_element_type=jnp.float32)
        * scale
    )
    live = lax.broadcasted_iota(jnp.int32, (key_list.shape[0], KMAX), 1) < key_count[:, None]
    scores = jnp.where(live[:, None, :, None], scores, -jnp.inf)
    highest = jnp.max(scores, axis=(2, 3), keepdims=True)
    raised = jnp.exp(scores - highest)
    summed = jnp.sum(raised, axis=(2, 3), keepdims=True)
    weights = (raised / summed).astype(jnp.bfloat16)
    mixed = jnp.einsum("nqkb,nkbe->nqe", weights, picked_values, preferred_element_type=jnp.float32)
    return mixed.astype(jnp.bfloat16)


def pick_blocks(table, wanted):
    return table[wanted]


def per_device_by_tokens(
    hidden_rows,
    gen_weight,
    noise,
    timesteps,
    qkv_weight,
    out_weight,
    qk_gain,
    block_keys,
    block_count,
):
    generated = jnp.dot(hidden_rows, gen_weight, preferred_element_type=jnp.float32).astype(
        jnp.bfloat16
    )
    forked = lax.all_gather(generated, ("role", "head"), axis=1, tiled=True)
    row_count = forked.shape[0]
    width = forked.shape[1]
    local_blocks = timesteps.shape[0]
    angle_blocks = (timesteps.astype(jnp.float32) * (math.pi / 2000.0))[:, None, None]
    noisy = jnp.cos(angle_blocks) * forked.astype(jnp.float32).reshape(local_blocks, BLOCK, width)
    noisy = noisy + jnp.sin(angle_blocks) * noise.astype(jnp.float32).reshape(
        local_blocks, BLOCK, width
    )
    normed = rms_rows(noisy).reshape(row_count, width).astype(jnp.bfloat16)
    weight_here = qkv_weight[0]
    projected = jnp.dot(
        normed,
        lax.all_gather(weight_here, "seq", axis=0, tiled=True),
        preferred_element_type=jnp.float32,
    )
    heads_here = projected.shape[1] // (3 * HEAD_DIM)
    head_parts = projected.reshape(row_count, heads_here, 3, HEAD_DIM)
    gain_here = qk_gain[0]
    queries = (rms_rows(head_parts[:, :, 0]) * gain_here[0][None, :, None]).astype(jnp.bfloat16)
    key_local = (rms_rows(head_parts[:, :, 1]) * gain_here[1][None, :, None]).astype(jnp.bfloat16)
    value_local = head_parts[:, :, 2].astype(jnp.bfloat16)
    query_table = queries.reshape(local_blocks, BLOCK, heads_here, HEAD_DIM).transpose(2, 0, 1, 3)
    shard_count = lax.axis_size("seq")
    shard_here = lax.axis_index("seq")
    all_blocks = shard_count * local_blocks
    key_heads = key_local.reshape(local_blocks, BLOCK, heads_here, HEAD_DIM).transpose(2, 0, 1, 3)
    value_heads = value_local.reshape(local_blocks, BLOCK, heads_here, HEAD_DIM).transpose(
        2, 0, 1, 3
    )
    block_ids = lax.broadcasted_iota(jnp.int32, (1, 1, 1, all_blocks), 3)
    matches = block_keys[:, :, :, None] == block_ids
    remote = block_ids // local_blocks != shard_here
    needed = jnp.any(jnp.logical_and(matches, remote), axis=(1, 2))
    needed = needed.reshape(heads_here, shard_count, local_blocks)
    slot_of = jnp.cumsum(needed.astype(jnp.int32), axis=2) - 1
    slot_ids = lax.broadcasted_iota(jnp.int32, (1, 1, 1, CAP), 3)
    within_ids = lax.broadcasted_iota(jnp.int32, (1, 1, local_blocks, 1), 2)
    chosen_slot = jnp.logical_and(needed[..., None], slot_of[..., None] == slot_ids)
    requests = jnp.sum(jnp.where(chosen_slot, within_ids, 0), axis=2)
    asked = lax.all_to_all(
        requests.transpose(1, 0, 2), "seq", split_axis=0, concat_axis=0, tiled=True
    )
    sent_keys = jax.vmap(pick_blocks, in_axes=(0, 1), out_axes=1)(key_heads, asked)
    sent_values = jax.vmap(pick_blocks, in_axes=(0, 1), out_axes=1)(value_heads, asked)
    got_keys, got_values = (
        lax.all_to_all(sent_keys, "seq", split_axis=0, concat_axis=0, tiled=True),
        lax.all_to_all(sent_values, "seq", split_axis=0, concat_axis=0, tiled=True),
    )
    fetched_keys = got_keys.transpose(1, 0, 2, 3, 4).reshape(
        heads_here, shard_count * CAP, BLOCK, HEAD_DIM
    )
    fetched_values = got_values.transpose(1, 0, 2, 3, 4).reshape(
        heads_here, shard_count * CAP, BLOCK, HEAD_DIM
    )
    key_table = jnp.concatenate([key_heads, fetched_keys], axis=1)
    value_table = jnp.concatenate([value_heads, fetched_values], axis=1)
    local_ids = lax.broadcasted_iota(jnp.int32, (1, shard_count, local_blocks), 2)
    owner_grid = lax.broadcasted_iota(jnp.int32, (1, shard_count, local_blocks), 1)
    position = jnp.where(
        owner_grid == shard_here, local_ids, local_blocks + owner_grid * CAP + slot_of
    )
    position = position.reshape(heads_here, all_blocks)
    key_lists = jnp.sum(jnp.where(matches, position[:, None, None, :], 0), axis=3)
    attended = jax.vmap(block_attention)(
        query_table, key_table, value_table, key_lists, block_count
    )
    attended = attended.transpose(1, 2, 0, 3).reshape(row_count, heads_here * HEAD_DIM)
    contribution = jnp.dot(attended, out_weight[0], preferred_element_type=jnp.float32)
    signed = (2.0 * lax.axis_index("role").astype(jnp.float32) - 1.0) * contribution
    return lax.psum_scatter(
        signed.astype(jnp.bfloat16), ("role", "head"), scatter_dimension=1, tiled=True
    ).astype(jnp.float32)


VMEM_BYTES = 56 * 1024 * 1024
CORES = 2


def whole_in_vmem():
    return pl.BlockSpec(memory_space=pltpu.VMEM)


def in_hbm():
    return pl.BlockSpec(memory_space=pl.ANY)


def in_smem():
    return pl.BlockSpec(memory_space=pltpu.SMEM)


def cut_columns(weight, chips, head):
    rows, columns = weight.shape
    wide = 3 * HEAD_DIM
    chip_heads = columns // (chips * wide)

    def body(weight_ref, out_ref):
        out_ref[0] = weight_ref[...]

    return pl.pallas_call(
        body,
        grid=(chips,),
        in_specs=[pl.BlockSpec((rows, wide), lambda chip: (0, chip * chip_heads + head))],
        out_specs=pl.BlockSpec((1, rows, wide), lambda chip: (chip, 0, 0)),
        out_shape=jax.ShapeDtypeStruct((chips, rows, wide), weight.dtype),
        name="cut_columns",
    )(weight)


def project_heads(places, gains, rounds, weights_own, weights_other):
    heads = len(weights_own)
    slabs, depth, columns = weights_own[0].shape
    tokens, features = rounds[0][0].shape
    pieces = [piece for one in rounds for piece in one]
    turns = len(rounds)
    per_round = len(rounds[0])
    half = tokens // 2
    dtype = weights_own[0].dtype

    def body(places_ref, gains_ref, *refs):
        own_refs, other_refs = refs[:heads], refs[heads : 2 * heads]
        piece_refs = refs[2 * heads : 2 * heads + len(pieces)]
        query_ref, kv_ref = refs[2 * heads + len(pieces) : 2 * heads + len(pieces) + 2]
        table, rows, total, weight_sems, row_sems = refs[2 * heads + len(pieces) + 2 :]
        core = places_ref[slabs]
        copies = []
        for slab in range(slabs):
            here = []
            for head in range(heads):
                for side, ref in enumerate((own_refs[head], other_refs[head])):
                    place = core if side == 0 else 1 - core
                    here.append(
                        pltpu.make_async_copy(
                            ref.at[places_ref[slab]],
                            table.at[slab, place, :, pl.ds(head * columns, columns)],
                            weight_sems.at[slab, head, side],
                        )
                    )
            for turn in range(turns):
                for which in [slab] if slab < slabs - 1 else [slab, slab + 1]:
                    first = turn * tokens + max(which - slabs + 1, 0) * half
                    count = tokens if slab < slabs - 1 else half
                    here.append(
                        pltpu.make_async_copy(
                            piece_refs[turn * per_round + which],
                            rows.at[slab, pl.ds(first, count)],
                            row_sems.at[which, turn],
                        )
                    )
            for copy in here:
                copy.start()
            copies.append(here)
        for slab in range(slabs):
            for copy in copies[slab]:
                copy.wait()
            part = jnp.dot(
                rows[slab],
                table[slab].reshape(CORES * depth, heads * columns),
                preferred_element_type=jnp.float32,
            )
            if slab == 0:
                total[...] = part
            elif slab < slabs - 1:
                total[...] += part
            else:
                part = total[...] + part
        for turn in range(turns):
            here = part[turn * tokens : (turn + 1) * tokens]
            for head in range(heads):
                at = head * columns
                for which in range(2):
                    block = here[:, at + which * HEAD_DIM : at + (which + 1) * HEAD_DIM]
                    normal = (rms_rows(block) * gains_ref[which, head]).astype(dtype)
                    if which == 0:
                        query_ref[head, turn] = normal
                    else:
                        kv_ref[head, 0, turn] = normal
                block = here[:, at + 2 * HEAD_DIM : at + 3 * HEAD_DIM]
                kv_ref[head, 1, turn] = block.astype(dtype)

    return pl.pallas_call(
        body,
        in_specs=[in_smem(), in_smem()] + [in_hbm()] * (2 * heads + len(pieces)),
        out_specs=(whole_in_vmem(), whole_in_vmem()),
        out_shape=(
            jax.ShapeDtypeStruct((heads, turns, tokens, HEAD_DIM), dtype),
            jax.ShapeDtypeStruct((heads, 2, turns, tokens, HEAD_DIM), dtype),
        ),
        scratch_shapes=[
            pltpu.VMEM((slabs, CORES, depth, heads * columns), dtype),
            pltpu.VMEM((slabs, turns * tokens, features), dtype),
            pltpu.VMEM((turns * tokens, heads * columns), jnp.float32),
            pltpu.SemaphoreType.DMA((slabs, heads, 2)),
            pltpu.SemaphoreType.DMA((per_round, turns)),
        ],
        compiler_params=pltpu.CompilerParams(vmem_limit_bytes=VMEM_BYTES),
        name="project_heads",
    )(places, gains, *weights_own, *weights_other, *pieces)


def attend(key_slots, counts, query_slots, group_most, queries, kv_own, kv_other):
    heads, blocks, most = key_slots.shape
    groups = group_most.shape[1]
    together = blocks // groups
    parts = len(queries)
    sizes = [one.shape[1] for one in queries]
    starts = [sum(sizes[:at]) for at in range(parts)]
    scale = 1.0 / math.sqrt(HEAD_DIM)
    dtype = queries[0].dtype

    def body(slots_ref, counts_ref, from_ref, most_ref, *refs):
        query_refs = refs[:parts]
        own_refs = refs[parts : 2 * parts]
        other_refs = refs[2 * parts : 3 * parts]
        out_ref, query_table, table, query_sems, sems = refs[3 * parts :]
        copies = []
        for at in range(parts):
            span = pl.ds(starts[at], sizes[at])
            copies.append(
                pltpu.make_async_copy(query_refs[at], query_table.at[:, span], query_sems.at[at])
            )
            for side, ref in enumerate((own_refs[at], other_refs[at])):
                span = pl.ds(side * blocks + starts[at], sizes[at])
                copies.append(pltpu.make_async_copy(ref, table.at[:, :, span], sems.at[at, side]))
        for copy in copies:
            copy.start()
        for copy in copies:
            copy.wait()

        def run(head, group, listed, batch):
            for first in range(0, together, batch):
                spots = [group * together + at for at in range(first, min(first + batch, together))]
                slots = [[slots_ref[head, at, entry] for entry in range(listed)] for at in spots]
                scores = []
                for at, listing in zip(spots, slots):
                    keys = jnp.concatenate([table[head, 0, slot] for slot in listing], axis=0)
                    scores.append(
                        lax.dot_general(
                            query_table[head, from_ref[at]],
                            keys,
                            (((1,), (1,)), ((), ())),
                            preferred_element_type=jnp.float32,
                        )
                    )
                column = lax.broadcasted_iota(jnp.int32, (1, listed * BLOCK), 1)
                scores = [
                    jnp.where(column < counts_ref[head, at] * BLOCK, one * scale, -jnp.inf)
                    for at, one in zip(spots, scores)
                ]
                highest = [jnp.max(one, axis=1, keepdims=True) for one in scores]
                raised = [jnp.exp(one - top) for one, top in zip(scores, highest)]
                inverse = [1.0 / jnp.sum(one, axis=1, keepdims=True) for one in raised]
                weights = [(one * by).astype(dtype) for one, by in zip(raised, inverse)]
                mixed = []
                for one, listing in zip(weights, slots):
                    values = jnp.concatenate([table[head, 1, slot] for slot in listing], axis=0)
                    mixed.append(jnp.dot(one, values, preferred_element_type=jnp.float32))
                for at, one in zip(spots, mixed):
                    out_ref[head, at] = one.astype(dtype)

        def step(at, carry):
            head, group = at // groups, at % groups
            few = most_ref[head, group] <= most // 2

            @pl.when(few)
            def _():
                run(head, group, most // 2, 6)

            @pl.when(jnp.logical_not(few))
            def _():
                run(head, group, most, 3)

            return carry

        lax.fori_loop(0, heads * groups, step, 0)

    return pl.pallas_call(
        body,
        in_specs=[in_smem()] * 4 + [in_hbm()] * (3 * parts),
        out_specs=whole_in_vmem(),
        out_shape=jax.ShapeDtypeStruct((heads, blocks, BLOCK, HEAD_DIM), dtype),
        scratch_shapes=[
            pltpu.VMEM((heads, blocks, BLOCK, HEAD_DIM), dtype),
            pltpu.VMEM((heads, 2, CORES * blocks, BLOCK, HEAD_DIM), dtype),
            pltpu.SemaphoreType.DMA((parts,)),
            pltpu.SemaphoreType.DMA((parts, 2)),
        ],
        compiler_params=pltpu.CompilerParams(vmem_limit_bytes=VMEM_BYTES),
        name="attend",
    )(key_slots, counts, query_slots, group_most, *queries, *kv_own, *kv_other)


def out_blocks(which, sign, attended, out_weight, dtypes, blocks):
    groups, _, tokens, _ = attended[0].shape
    sizes = [one.shape[1] for one in attended]
    count = len(attended)
    depth, features = out_weight.shape
    width = features // blocks
    wanted = len(dtypes)

    def body(which_ref, sign_ref, *refs):
        parts, weight_ref, out_refs = refs[:count], refs[count], refs[count + 1 :]
        columns = []
        for group in range(groups):
            for chunk in range(count):
                for head in range(sizes[chunk]):
                    columns.append(parts[chunk][group, head])
        joined = jnp.concatenate(columns, axis=1)
        total = jnp.dot(joined, weight_ref[...], preferred_element_type=jnp.float32)
        total = total * sign_ref[0].astype(jnp.float32)
        for at in range(wanted):

            @pl.when(pl.program_id(0) == at)
            def _(at=at):
                out_refs[at][...] = total.astype(dtypes[at])

    return pl.pallas_call(
        body,
        grid_spec=pltpu.PrefetchScalarGridSpec(
            num_scalar_prefetch=2,
            grid=(wanted,),
            in_specs=[pl.BlockSpec(one.shape, lambda i, w, s: (0, 0, 0, 0)) for one in attended]
            + [pl.BlockSpec((depth, width), lambda i, w, s: (0, w[i]))],
            out_specs=[pl.BlockSpec((tokens, width), lambda i, w, s: (0, 0))] * wanted,
        ),
        out_shape=[jax.ShapeDtypeStruct((tokens, width), dtype) for dtype in dtypes],
        compiler_params=pltpu.CompilerParams(vmem_limit_bytes=VMEM_BYTES),
        name="out_blocks",
    )(which, sign, *attended, out_weight)


def nearest(chips):
    order = [
        sorted((at for at in range(chips) if at != here), key=lambda at: (abs(at - here), at))
        for here in range(chips)
    ]
    turns = [
        [0 if at == here else order[here].index(at) + 1 for at in range(chips)]
        for here in range(chips)
    ]
    return order, turns


def chunk_sizes(heads):
    last = max(1, heads // 3)
    return [heads - last, last] if heads > last else [heads]


def per_device_by_heads(
    hidden_rows,
    gen_weight,
    noise,
    timesteps,
    qkv_weight,
    out_weight,
    qk_gain,
    block_keys,
    block_count,
):
    role, head = lax.axis_index("role"), lax.axis_index("head")
    chip, core = lax.axis_index("chip"), lax.axis_index("core")
    chips = lax.axis_size("chip")
    local_heads, local_blocks, most = block_keys.shape
    heads = local_heads // chips
    tokens = hidden_rows.shape[0]
    width = hidden_rows.shape[1]
    features = gen_weight.shape[1]
    all_blocks = chips * local_blocks
    swap = [(0, 1), (1, 0)]
    order, turns = nearest(chips)
    turn_here = jnp.asarray(turns, dtype=jnp.int32)[chip]

    def pick(index, options):
        picked = options[0]
        for at in range(1, len(options)):
            picked = jnp.where(index == at, options[at], picked)
        return picked

    def turn_of(other):
        return pick(other, [turn_here[at] for at in range(chips)])

    def exchange(array):
        return lax.all_to_all(array, "chip", split_axis=0, concat_axis=0, tiled=True)

    weight_here = qkv_weight[0]
    cuts = [cut_columns(weight_here, chips, at) for at in range(heads)]
    hidden_rows, cuts[0] = lax.optimization_barrier((hidden_rows, cuts[0]))
    weights_own = [exchange(cuts[0])]

    mine = role * lax.axis_size("head") + head
    generated = jnp.dot(hidden_rows, gen_weight, preferred_element_type=jnp.float32)
    generated = lax.reduce_precision(generated, 8, 7)
    angle_blocks = (timesteps.astype(jnp.float32) * (math.pi / 2000.0))[:, None, None]
    noise_here = lax.dynamic_slice_in_dim(noise, mine * features, features, axis=1)
    noisy = jnp.cos(angle_blocks) * generated.reshape(local_blocks, BLOCK, features)
    noisy = noisy + jnp.sin(angle_blocks) * noise_here.astype(jnp.float32).reshape(
        local_blocks, BLOCK, features
    )
    squares = jnp.sum(noisy * noisy, axis=-1)
    squares = squares + lax.ppermute(squares, "role", swap)
    squares = squares + lax.ppermute(squares, "head", swap)
    normed = (noisy * lax.rsqrt(squares / width + 1e-06)[:, :, None]).astype(jnp.bfloat16)
    normed = normed.reshape(tokens, features)

    lists = jnp.concatenate([block_keys, block_count[:, :, None]], axis=2)
    half = tokens // 2
    rounds = []
    straight = None
    shard, up, down = normed, normed, normed
    ups, downs = [None], [None]
    gathered = [lists]
    late = None
    for phase in range(chips + 1):
        sent = {}
        if phase < chips:
            sent["role"] = lax.ppermute(shard, "role", swap)
            sent["head"] = lax.ppermute(shard, "head", swap)
        diagonal = None
        if straight is not None:
            diagonal = straight + (
                lax.ppermute(straight[2][:half], "role", swap),
                lax.ppermute(straight[1][half:], "head", swap),
            )
        step = phase + 1
        if step < chips:
            sent["up"] = lax.ppermute(
                up, "chip", [(at, at + 1) for at in range(step - 1, chips - 1)]
            )
            sent["down"] = lax.ppermute(
                down, "chip", [(at + 1, at) for at in range(chips - step)]
            )
        if phase == chips - 1:
            for shift in range(1, chips):
                pairs = [(at, (at + shift) % chips) for at in range(chips)]
                gathered.append(lax.ppermute(lists, "chip", pairs))
        if phase == 0:
            sent["weights"] = weights_own.pop()
        if phase < chips:
            sent, shard, late = lax.optimization_barrier((sent, shard, late))
        if phase == 0:
            weights_own.append(sent["weights"])
        if late is not None:
            rounds.append(late)
        late = diagonal
        if phase < chips:
            straight = (shard, sent["role"], sent["head"])
        if step < chips:
            up, down = sent["up"], sent["down"]
            ups.append(up)
            downs.append(down)
            options = []
            for here in range(chips):
                source = order[here][step - 1]
                options.append(ups[here - source] if source < here else downs[source - here])
            shard = pick(chip, options)
        if 1 <= phase < chips - 1 and len(weights_own) < heads:
            held, _ = lax.optimization_barrier((cuts[len(weights_own)], sent))
            weights_own.append(exchange(held))
    rounds.append(late)
    while len(weights_own) < heads:
        weights_own.append(exchange(cuts[len(weights_own)]))
    weights_other = [lax.ppermute(one, "core", swap) for one in weights_own]

    gathered = [lax.dynamic_slice_in_dim(one, chip * heads, heads, axis=0) for one in gathered]
    lists = jnp.concatenate(
        [pick((chip - at) % chips, gathered) for at in range(chips)], axis=1
    )
    owner = lists[:, :, :most] // local_blocks
    turn = turn_of(owner // CORES)
    far = (owner % CORES != core).astype(jnp.int32)
    key_slots = far * all_blocks + turn * local_blocks + lists[:, :, :most] % local_blocks
    counts = lists[:, :, most]
    group_most = jnp.max(counts.reshape(heads, chips, local_blocks), axis=2)
    spot = jnp.arange(all_blocks, dtype=jnp.int32)
    query_slots = turn_of(spot // local_blocks)
    query_slots = query_slots * local_blocks + spot % local_blocks

    sides = lax.axis_size("head")
    peers = jnp.stack(
        [
            role * sides + head,
            (1 - role) * sides + head,
            role * sides + 1 - head,
            (1 - role) * sides + 1 - head,
        ]
    ).astype(jnp.int32)
    places = jnp.concatenate([peers, core[None].astype(jnp.int32)])
    gains = lax.dynamic_slice_in_dim(qk_gain[0], chip * heads, heads, axis=1)

    chunks = chunk_sizes(heads)
    spans = [slice(sum(chunks[:at]), sum(chunks[: at + 1])) for at in range(len(chunks))]
    middle = (chips + 1) // 2
    projected = [([], [], []) for _ in chunks]
    tables = (key_slots, counts, query_slots, group_most)
    held_places, tables = lax.optimization_barrier((places, tables))
    key_slots, counts, query_slots, group_most = tables
    for part in (rounds[:middle], rounds[middle:]):
        for span, size, (queries, kv_own, kv_other) in zip(spans, chunks, projected):
            query, kv = project_heads(
                held_places, gains[:, span], part, weights_own[span], weights_other[span]
            )
            here = len(part) * local_blocks
            queries.append(query.reshape(size, here, BLOCK, HEAD_DIM))
            kv_own.append(kv.reshape(size, 2, here, BLOCK, HEAD_DIM))
            kv_other.append(lax.ppermute(kv_own[-1], "core", swap))
            held_places, _ = lax.optimization_barrier((places, kv))
    attended = []
    held = counts
    for span, size, (queries, kv_own, kv_other) in zip(spans, chunks, projected):
        mixed = attend(
            key_slots[span], held[span], query_slots, group_most[span], queries, kv_own, kv_other
        )
        held, _ = lax.optimization_barrier((counts, mixed))
        mixed = mixed.reshape(size, chips, tokens, HEAD_DIM).transpose(1, 0, 2, 3)
        attended.append(exchange(mixed))

    sign = (2 * role - 1).astype(jnp.int32)[None]
    blocks = sides * lax.axis_size("role")

    def blocks_of(first, second, dtypes):
        which = jnp.stack([peers[first], peers[second]])
        return out_blocks(which, sign, attended, out_weight[0], dtypes, blocks)

    far_swap = [(0, 3), (1, 2), (2, 1), (3, 0)]
    diagonal, over_head = blocks_of(3, 2, (jnp.bfloat16, jnp.bfloat16))
    over_role, own = blocks_of(1, 0, (jnp.bfloat16, jnp.float32))
    from_diagonal = lax.ppermute(diagonal, ("role", "head"), far_swap)
    from_head = lax.ppermute(over_head, "head", swap)
    from_role = lax.ppermute(over_role, "role", swap)
    return own + (
        from_role.astype(jnp.float32)
        + from_head.astype(jnp.float32)
        + from_diagonal.astype(jnp.float32)
    )


def splits_heads(mesh, qkv_weight, hidden_rows):
    role, seq, head = (mesh.shape[name] for name in ("role", "seq", "head"))
    if role != 2 or head != 2 or seq % CORES != 0:
        return False
    chips = seq // CORES
    heads = qkv_weight.shape[2] // (3 * HEAD_DIM * head)
    width = hidden_rows.shape[1]
    tokens = hidden_rows.shape[0] // seq
    return (
        heads % chips == 0
        and chips == role * head
        and width % (role * head * 256) == 0
        and width % (seq * 16) == 0
        and tokens % (2 * BLOCK) == 0
    )


def solution(mesh):
    def call(*arrays):
        if splits_heads(mesh, arrays[4], arrays[0]):
            per_device = per_device_by_heads
            seq = ("chip", "core")
            shape = mesh.devices.shape
            names = mesh.axis_names
            at = names.index("seq")
            layout = Mesh(
                mesh.devices.reshape(shape[:at] + (shape[at] // CORES, CORES) + shape[at + 1 :]),
                names[:at] + seq + names[at + 1 :],
            )
        else:
            per_device = per_device_by_tokens
            seq = "seq"
            layout = mesh
        placed = (
            P(seq, None),
            P(None, ("role", "head")),
            P(seq, None),
            P(seq),
            P("role", seq, "head"),
            P("role", "head", None),
            P("role", None, "head"),
            P("head", seq, None),
            P("head", seq),
        )
        return jax.shard_map(
            per_device,
            mesh=layout,
            in_specs=placed,
            out_specs=P(seq, ("role", "head")),
            check_vma=False,
        )(*arrays)

    return call
```

```python
import math

import jax
import jax.numpy as jnp
from jax import lax
from jax.experimental import pallas as pl
from jax.experimental.pallas import tpu as pltpu
from jax.sharding import Mesh
from jax.sharding import PartitionSpec as P

HEAD_DIM = 128
BLOCK = 64
KMAX = 8
CAP = 2


def rms_rows(values):
    return values * lax.rsqrt(jnp.mean(values * values, axis=-1, keepdims=True) + 1e-06)


def block_attention(queries, key_table, value_table, key_list, key_count):
    picked_keys = key_table[key_list]
    picked_values = value_table[key_list]
    scale = 1.0 / math.sqrt(HEAD_DIM)
    scores = (
        jnp.einsum("nqe,nkbe->nqkb", queries, picked_keys, preferred_element_type=jnp.float32)
        * scale
    )
    live = lax.broadcasted_iota(jnp.int32, (key_list.shape[0], KMAX), 1) < key_count[:, None]
    scores = jnp.where(live[:, None, :, None], scores, -jnp.inf)
    highest = jnp.max(scores, axis=(2, 3), keepdims=True)
    raised = jnp.exp(scores - highest)
    summed = jnp.sum(raised, axis=(2, 3), keepdims=True)
    weights = (raised / summed).astype(jnp.bfloat16)
    mixed = jnp.einsum("nqkb,nkbe->nqe", weights, picked_values, preferred_element_type=jnp.float32)
    return mixed.astype(jnp.bfloat16)


def pick_blocks(table, wanted):
    return table[wanted]


def per_device_by_tokens(
    hidden_rows,
    gen_weight,
    noise,
    timesteps,
    qkv_weight,
    out_weight,
    qk_gain,
    block_keys,
    block_count,
):
    generated = jnp.dot(hidden_rows, gen_weight, preferred_element_type=jnp.float32).astype(
        jnp.bfloat16
    )
    forked = lax.all_gather(generated, ("role", "head"), axis=1, tiled=True)
    row_count = forked.shape[0]
    width = forked.shape[1]
    local_blocks = timesteps.shape[0]
    angle_blocks = (timesteps.astype(jnp.float32) * (math.pi / 2000.0))[:, None, None]
    noisy = jnp.cos(angle_blocks) * forked.astype(jnp.float32).reshape(local_blocks, BLOCK, width)
    noisy = noisy + jnp.sin(angle_blocks) * noise.astype(jnp.float32).reshape(
        local_blocks, BLOCK, width
    )
    normed = rms_rows(noisy).reshape(row_count, width).astype(jnp.bfloat16)
    weight_here = qkv_weight[0]
    projected = jnp.dot(
        normed,
        lax.all_gather(weight_here, "seq", axis=0, tiled=True),
        preferred_element_type=jnp.float32,
    )
    heads_here = projected.shape[1] // (3 * HEAD_DIM)
    head_parts = projected.reshape(row_count, heads_here, 3, HEAD_DIM)
    gain_here = qk_gain[0]
    queries = (rms_rows(head_parts[:, :, 0]) * gain_here[0][None, :, None]).astype(jnp.bfloat16)
    key_local = (rms_rows(head_parts[:, :, 1]) * gain_here[1][None, :, None]).astype(jnp.bfloat16)
    value_local = head_parts[:, :, 2].astype(jnp.bfloat16)
    query_table = queries.reshape(local_blocks, BLOCK, heads_here, HEAD_DIM).transpose(2, 0, 1, 3)
    shard_count = lax.axis_size("seq")
    shard_here = lax.axis_index("seq")
    all_blocks = shard_count * local_blocks
    key_heads = key_local.reshape(local_blocks, BLOCK, heads_here, HEAD_DIM).transpose(2, 0, 1, 3)
    value_heads = value_local.reshape(local_blocks, BLOCK, heads_here, HEAD_DIM).transpose(
        2, 0, 1, 3
    )
    block_ids = lax.broadcasted_iota(jnp.int32, (1, 1, 1, all_blocks), 3)
    matches = block_keys[:, :, :, None] == block_ids
    remote = block_ids // local_blocks != shard_here
    needed = jnp.any(jnp.logical_and(matches, remote), axis=(1, 2))
    needed = needed.reshape(heads_here, shard_count, local_blocks)
    slot_of = jnp.cumsum(needed.astype(jnp.int32), axis=2) - 1
    slot_ids = lax.broadcasted_iota(jnp.int32, (1, 1, 1, CAP), 3)
    within_ids = lax.broadcasted_iota(jnp.int32, (1, 1, local_blocks, 1), 2)
    chosen_slot = jnp.logical_and(needed[..., None], slot_of[..., None] == slot_ids)
    requests = jnp.sum(jnp.where(chosen_slot, within_ids, 0), axis=2)
    asked = lax.all_to_all(
        requests.transpose(1, 0, 2), "seq", split_axis=0, concat_axis=0, tiled=True
    )
    sent_keys = jax.vmap(pick_blocks, in_axes=(0, 1), out_axes=1)(key_heads, asked)
    sent_values = jax.vmap(pick_blocks, in_axes=(0, 1), out_axes=1)(value_heads, asked)
    got_keys, got_values = (
        lax.all_to_all(sent_keys, "seq", split_axis=0, concat_axis=0, tiled=True),
        lax.all_to_all(sent_values, "seq", split_axis=0, concat_axis=0, tiled=True),
    )
    fetched_keys = got_keys.transpose(1, 0, 2, 3, 4).reshape(
        heads_here, shard_count * CAP, BLOCK, HEAD_DIM
    )
    fetched_values = got_values.transpose(1, 0, 2, 3, 4).reshape(
        heads_here, shard_count * CAP, BLOCK, HEAD_DIM
    )
    key_table = jnp.concatenate([key_heads, fetched_keys], axis=1)
    value_table = jnp.concatenate([value_heads, fetched_values], axis=1)
    local_ids = lax.broadcasted_iota(jnp.int32, (1, shard_count, local_blocks), 2)
    owner_grid = lax.broadcasted_iota(jnp.int32, (1, shard_count, local_blocks), 1)
    position = jnp.where(
        owner_grid == shard_here, local_ids, local_blocks + owner_grid * CAP + slot_of
    )
    position = position.reshape(heads_here, all_blocks)
    key_lists = jnp.sum(jnp.where(matches, position[:, None, None, :], 0), axis=3)
    attended = jax.vmap(block_attention)(
        query_table, key_table, value_table, key_lists, block_count
    )
    attended = attended.transpose(1, 2, 0, 3).reshape(row_count, heads_here * HEAD_DIM)
    contribution = jnp.dot(attended, out_weight[0], preferred_element_type=jnp.float32)
    signed = (2.0 * lax.axis_index("role").astype(jnp.float32) - 1.0) * contribution
    return lax.psum_scatter(
        signed.astype(jnp.bfloat16), ("role", "head"), scatter_dimension=1, tiled=True
    ).astype(jnp.float32)


VMEM_BYTES = 56 * 1024 * 1024
CORES = 2


def whole_in_vmem():
    return pl.BlockSpec(memory_space=pltpu.VMEM)


def in_hbm():
    return pl.BlockSpec(memory_space=pl.ANY)


def in_smem():
    return pl.BlockSpec(memory_space=pltpu.SMEM)


def cut_columns(weight, chips, head):
    rows, columns = weight.shape
    wide = 3 * HEAD_DIM
    chip_heads = columns // (chips * wide)

    def body(weight_ref, out_ref):
        out_ref[0] = weight_ref[...]

    return pl.pallas_call(
        body,
        grid=(chips,),
        in_specs=[pl.BlockSpec((rows, wide), lambda chip: (0, chip * chip_heads + head))],
        out_specs=pl.BlockSpec((1, rows, wide), lambda chip: (chip, 0, 0)),
        out_shape=jax.ShapeDtypeStruct((chips, rows, wide), weight.dtype),
        name="cut_columns",
    )(weight)


def project_heads(places, gains, rounds, weights_own, weights_other):
    heads = len(weights_own)
    slabs, depth, columns = weights_own[0].shape
    tokens, features = rounds[0][0].shape
    pieces = [piece for one in rounds for piece in one]
    turns = len(rounds)
    per_round = len(rounds[0])
    half = tokens // 2
    joint = 2 if slabs % 2 == 0 else 1
    dtype = weights_own[0].dtype

    def body(places_ref, gains_ref, *refs):
        own_refs, other_refs = refs[:heads], refs[heads : 2 * heads]
        piece_refs = refs[2 * heads : 2 * heads + len(pieces)]
        query_ref, kv_ref = refs[2 * heads + len(pieces) : 2 * heads + len(pieces) + 2]
        table, rows, weight_sems, row_sems = refs[2 * heads + len(pieces) + 2 :]
        core = places_ref[slabs]
        copies = []
        for slab in range(slabs):
            here = []
            for head in range(heads):
                for side, ref in enumerate((own_refs[head], other_refs[head])):
                    place = core if side == 0 else 1 - core
                    here.append(
                        pltpu.make_async_copy(
                            ref.at[places_ref[slab]],
                            table.at[
                                slab // joint,
                                slab % joint,
                                place,
                                :,
                                pl.ds(head * columns, columns),
                            ],
                            weight_sems.at[slab, head, side],
                        )
                    )
            for turn in range(turns):
                for which in [slab] if slab < slabs - 1 else [slab, slab + 1]:
                    first = turn * tokens + max(which - slabs + 1, 0) * half
                    count = tokens if slab < slabs - 1 else half
                    here.append(
                        pltpu.make_async_copy(
                            piece_refs[turn * per_round + which],
                            rows.at[
                                slab // joint,
                                pl.ds(first, count),
                                pl.ds(slab % joint * features, features),
                            ],
                            row_sems.at[which, turn],
                        )
                    )
            for copy in here:
                copy.start()
            copies.append(here)
        total = None
        for group in range(slabs // joint):
            for slab in range(group * joint, (group + 1) * joint):
                for copy in copies[slab]:
                    copy.wait()
            part = jnp.dot(
                rows[group],
                table[group].reshape(joint * CORES * depth, heads * columns),
                preferred_element_type=jnp.float32,
            )
            total = part if total is None else total + part
        for turn in range(turns):
            here = total[turn * tokens : (turn + 1) * tokens]
            for head in range(heads):
                at = head * columns
                for which in range(2):
                    block = here[:, at + which * HEAD_DIM : at + (which + 1) * HEAD_DIM]
                    normal = (rms_rows(block) * gains_ref[which, head]).astype(dtype)
                    if which == 0:
                        query_ref[head, turn] = normal
                    else:
                        kv_ref[head, 0, turn] = normal
                block = here[:, at + 2 * HEAD_DIM : at + 3 * HEAD_DIM]
                kv_ref[head, 1, turn] = block.astype(dtype)

    return pl.pallas_call(
        body,
        in_specs=[in_smem(), in_smem()] + [in_hbm()] * (2 * heads + len(pieces)),
        out_specs=(whole_in_vmem(), whole_in_vmem()),
        out_shape=(
            jax.ShapeDtypeStruct((heads, turns, tokens, HEAD_DIM), dtype),
            jax.ShapeDtypeStruct((heads, 2, turns, tokens, HEAD_DIM), dtype),
        ),
        scratch_shapes=[
            pltpu.VMEM((slabs // joint, joint, CORES, depth, heads * columns), dtype),
            pltpu.VMEM((slabs // joint, turns * tokens, joint * features), dtype),
            pltpu.SemaphoreType.DMA((slabs, heads, 2)),
            pltpu.SemaphoreType.DMA((per_round, turns)),
        ],
        compiler_params=pltpu.CompilerParams(vmem_limit_bytes=VMEM_BYTES),
        name="project_heads",
    )(places, gains, *weights_own, *weights_other, *pieces)


def attend(first_head, heads, key_slots, counts, query_slots, group_most, parts):
    _, blocks, most = key_slots.shape
    groups = group_most.shape[1]
    together = blocks // groups
    scale = 1.0 / math.sqrt(HEAD_DIM)
    dtype = parts[0][4].dtype
    arrays = [array for part in parts for array in part[4:]]

    def body(slots_ref, counts_ref, from_ref, most_ref, *refs):
        out_ref, query_table, table, sems = refs[len(arrays) :]
        copies = []
        for at, (head, size, block, span, _, _, _) in enumerate(parts):
            query_part, own_part, other_part = refs[3 * at : 3 * at + 3]
            rows = pl.ds(head, size)
            copies.append(
                pltpu.make_async_copy(
                    query_part, query_table.at[rows, pl.ds(block, span)], sems.at[at, 0]
                )
            )
            for side, ref in enumerate((own_part, other_part)):
                place = pl.ds(side * blocks + block, span)
                copies.append(
                    pltpu.make_async_copy(ref, table.at[rows, :, place], sems.at[at, 1 + side])
                )
        for copy in copies:
            copy.start()
        for copy in copies:
            copy.wait()

        def run(head, group, listed, batch):
            for first in range(0, together, batch):
                spots = [group * together + at for at in range(first, min(first + batch, together))]
                slots = [[slots_ref[first_head + head, at, entry] for entry in range(listed)] for at in spots]
                scores = []
                for at, listing in zip(spots, slots):
                    keys = jnp.concatenate([table[head, 0, slot] for slot in listing], axis=0)
                    scores.append(
                        lax.dot_general(
                            query_table[head, from_ref[at]],
                            keys,
                            (((1,), (1,)), ((), ())),
                            preferred_element_type=jnp.float32,
                        )
                    )
                column = lax.broadcasted_iota(jnp.int32, (1, listed * BLOCK), 1)
                scores = [
                    jnp.where(column < counts_ref[first_head + head, at] * BLOCK, one * scale, -jnp.inf)
                    for at, one in zip(spots, scores)
                ]
                highest = [jnp.max(one, axis=1, keepdims=True) for one in scores]
                raised = [jnp.exp(one - top) for one, top in zip(scores, highest)]
                inverse = [1.0 / jnp.sum(one, axis=1, keepdims=True) for one in raised]
                weights = [(one * by).astype(dtype) for one, by in zip(raised, inverse)]
                mixed = []
                for one, listing in zip(weights, slots):
                    values = jnp.concatenate([table[head, 1, slot] for slot in listing], axis=0)
                    mixed.append(jnp.dot(one, values, preferred_element_type=jnp.float32))
                for at, one in enumerate(mixed):
                    out_ref[group, head, first + at] = one.astype(dtype)

        def step(at, carry):
            head, group = at // groups, at % groups
            few = most_ref[first_head + head, group] <= most // 2

            @pl.when(few)
            def _():
                run(head, group, most // 2, 6)

            @pl.when(jnp.logical_not(few))
            def _():
                run(head, group, most, 3)

            return carry

        lax.fori_loop(0, heads * groups, step, 0)

    return pl.pallas_call(
        body,
        in_specs=[in_smem()] * 4 + [in_hbm()] * len(arrays),
        out_specs=whole_in_vmem(),
        out_shape=jax.ShapeDtypeStruct((groups, heads, together, BLOCK, HEAD_DIM), dtype),
        scratch_shapes=[
            pltpu.VMEM((heads, blocks, BLOCK, HEAD_DIM), dtype),
            pltpu.VMEM((heads, 2, CORES * blocks, BLOCK, HEAD_DIM), dtype),
            pltpu.SemaphoreType.DMA((len(parts), 3)),
        ],
        compiler_params=pltpu.CompilerParams(vmem_limit_bytes=VMEM_BYTES),
        name="attend",
    )(key_slots, counts, query_slots, group_most, *arrays)


def out_blocks(which, sign, attended, place, out_weight, blocks, dtypes, before=None, skip=0):
    groups, heads, tokens, _ = attended.shape
    depth, features = out_weight.shape
    width = features // blocks
    wanted = which.shape[0]
    rows = heads * HEAD_DIM
    weight = out_weight.reshape(groups, depth // groups, features)
    stacked = len(dtypes) == 1 and wanted > 1

    def body(which_ref, sign_ref, mixed_ref, weight_ref, *refs):
        out_refs = refs if before is None else refs[1:]
        joined = jnp.concatenate(
            [mixed_ref[group, head] for group in range(groups) for head in range(heads)], axis=1
        )
        total = jnp.dot(
            joined,
            weight_ref[...].reshape(groups * rows, width),
            preferred_element_type=jnp.float32,
        )
        total = total * sign_ref[0].astype(jnp.float32)
        if before is not None:
            total = total + refs[0][0]
        if stacked:
            out_refs[0][0] = total.astype(dtypes[0])
        else:
            for at in range(wanted):

                @pl.when(pl.program_id(0) == at)
                def _(at=at):
                    out_refs[at][...] = total.astype(dtypes[at])

    in_specs = [
        pl.BlockSpec(attended.shape, lambda i, w, s: (0, 0, 0, 0)),
        pl.BlockSpec((groups, rows, width), lambda i, w, s: (0, place, w[i])),
    ]
    operands = [attended, weight]
    if before is not None:
        in_specs.append(pl.BlockSpec((1, tokens, width), lambda i, w, s: (i + skip, 0, 0)))
        operands.append(before)
    if stacked:
        out_specs = [pl.BlockSpec((1, tokens, width), lambda i, w, s: (i, 0, 0))]
        out_shape = [jax.ShapeDtypeStruct((wanted, tokens, width), dtypes[0])]
    else:
        out_specs = [pl.BlockSpec((tokens, width), lambda i, w, s: (0, 0))] * wanted
        out_shape = [jax.ShapeDtypeStruct((tokens, width), dtype) for dtype in dtypes]
    return pl.pallas_call(
        body,
        grid_spec=pltpu.PrefetchScalarGridSpec(
            num_scalar_prefetch=2, grid=(wanted,), in_specs=in_specs, out_specs=out_specs
        ),
        out_shape=out_shape,
        compiler_params=pltpu.CompilerParams(vmem_limit_bytes=VMEM_BYTES),
        name="out_blocks",
    )(which, sign, *operands)


def nearest(chips):
    order = [
        sorted((at for at in range(chips) if at != here), key=lambda at: (abs(at - here), at))
        for here in range(chips)
    ]
    turns = [
        [0 if at == here else order[here].index(at) + 1 for at in range(chips)]
        for here in range(chips)
    ]
    return order, turns


def chunk_sizes(heads):
    last = heads // 3 if heads % 3 == 0 else 1
    return [heads - last, last] if heads > last else [heads]


def per_device_by_heads(
    hidden_rows,
    gen_weight,
    noise,
    timesteps,
    qkv_weight,
    out_weight,
    qk_gain,
    block_keys,
    block_count,
):
    role, head = lax.axis_index("role"), lax.axis_index("head")
    chip, core = lax.axis_index("chip"), lax.axis_index("core")
    chips = lax.axis_size("chip")
    local_heads, local_blocks, most = block_keys.shape
    heads = local_heads // chips
    tokens = hidden_rows.shape[0]
    width = hidden_rows.shape[1]
    features = gen_weight.shape[1]
    all_blocks = chips * local_blocks
    swap = [(0, 1), (1, 0)]
    order, turns = nearest(chips)
    turn_here = jnp.asarray(turns, dtype=jnp.int32)[chip]

    def pick(index, options):
        picked = options[0]
        for at in range(1, len(options)):
            picked = jnp.where(index == at, options[at], picked)
        return picked

    def turn_of(other):
        return pick(other, [turn_here[at] for at in range(chips)])

    def exchange(array):
        return lax.all_to_all(array, "chip", split_axis=0, concat_axis=0, tiled=True)

    weight_here = qkv_weight[0]
    cuts = [cut_columns(weight_here, chips, at) for at in range(heads)]
    hidden_rows, cuts[0] = lax.optimization_barrier((hidden_rows, cuts[0]))
    weights_own = [exchange(cuts[0])]

    mine = role * lax.axis_size("head") + head
    generated = jnp.dot(hidden_rows, gen_weight, preferred_element_type=jnp.float32)
    generated = lax.reduce_precision(generated, 8, 7)
    angle_blocks = (timesteps.astype(jnp.float32) * (math.pi / 2000.0))[:, None, None]
    noise_here = lax.dynamic_slice_in_dim(noise, mine * features, features, axis=1)
    noisy = jnp.cos(angle_blocks) * generated.reshape(local_blocks, BLOCK, features)
    noisy = noisy + jnp.sin(angle_blocks) * noise_here.astype(jnp.float32).reshape(
        local_blocks, BLOCK, features
    )
    squares = jnp.sum(noisy * noisy, axis=-1)
    squares = squares + lax.ppermute(squares, "role", swap)
    squares = squares + lax.ppermute(squares, "head", swap)
    normed = (noisy * lax.rsqrt(squares / width + 1e-06)[:, :, None]).astype(jnp.bfloat16)
    normed = normed.reshape(tokens, features)

    lists = jnp.concatenate([block_keys, block_count[:, :, None]], axis=2)
    half = tokens // 2
    rounds = []
    straight = None
    shard, up, down = normed, normed, normed
    ups, downs = [None], [None]
    gathered = [lists]
    late = None
    for phase in range(chips + 1):
        sent = {}
        if phase < chips:
            sent["role"] = lax.ppermute(shard, "role", swap)
            sent["head"] = lax.ppermute(shard, "head", swap)
        diagonal = None
        if straight is not None:
            diagonal = straight + (
                lax.ppermute(straight[2][:half], "role", swap),
                lax.ppermute(straight[1][half:], "head", swap),
            )
        step = phase + 1
        if step < chips:
            sent["up"] = lax.ppermute(
                up, "chip", [(at, at + 1) for at in range(step - 1, chips - 1)]
            )
            sent["down"] = lax.ppermute(
                down, "chip", [(at + 1, at) for at in range(chips - step)]
            )
        if phase == 0:
            for shift in range(1, chips):
                pairs = [(at, (at + shift) % chips) for at in range(chips)]
                sent["lists" + str(shift)] = lax.ppermute(lists, "chip", pairs)
            sent["weights"] = weights_own.pop()
        if phase < chips:
            sent, shard, late = lax.optimization_barrier((sent, shard, late))
        if phase == 0:
            weights_own.append(sent["weights"])
            gathered += [sent["lists" + str(shift)] for shift in range(1, chips)]
        if late is not None:
            rounds.append(late)
        late = diagonal
        if phase < chips:
            straight = (shard, sent["role"], sent["head"])
        if step < chips:
            up, down = sent["up"], sent["down"]
            ups.append(up)
            downs.append(down)
            options = []
            for here in range(chips):
                source = order[here][step - 1]
                options.append(ups[here - source] if source < here else downs[source - here])
            shard = pick(chip, options)
        if phase == chips - 2 and len(weights_own) < heads:
            cuts[1:], _ = lax.optimization_barrier((cuts[1:], sent))
            for cut in cuts[1:]:
                held, _ = lax.optimization_barrier((cut, weights_own[-1]))
                weights_own.append(exchange(held))
    rounds.append(late)
    while len(weights_own) < heads:
        weights_own.append(exchange(cuts[len(weights_own)]))
    weights_other = [lax.ppermute(one, "core", swap) for one in weights_own]

    gathered = [lax.dynamic_slice_in_dim(one, chip * heads, heads, axis=0) for one in gathered]
    lists = jnp.concatenate(
        [pick((chip - at) % chips, gathered) for at in range(chips)], axis=1
    )
    owner = lists[:, :, :most] // local_blocks
    turn = turn_of(owner // CORES)
    far = (owner % CORES != core).astype(jnp.int32)
    key_slots = far * all_blocks + turn * local_blocks + lists[:, :, :most] % local_blocks
    counts = lists[:, :, most]
    group_most = jnp.max(counts.reshape(heads, chips, local_blocks), axis=2)
    spot = jnp.arange(all_blocks, dtype=jnp.int32)
    query_slots = turn_of(spot // local_blocks)
    query_slots = query_slots * local_blocks + spot % local_blocks

    sides = lax.axis_size("head")
    peers = jnp.stack(
        [
            role * sides + head,
            (1 - role) * sides + head,
            role * sides + 1 - head,
            (1 - role) * sides + 1 - head,
        ]
    ).astype(jnp.int32)
    places = jnp.concatenate([peers, core[None].astype(jnp.int32)])
    gains = lax.dynamic_slice_in_dim(qk_gain[0], chip * heads, heads, axis=1)

    chunks = chunk_sizes(heads)
    spans = [slice(sum(chunks[:at]), sum(chunks[: at + 1])) for at in range(len(chunks))]
    middle = (chips + 1) // 2
    tables = (key_slots, counts, query_slots, group_most)
    held_places, tables = lax.optimization_barrier((places, tables))
    key_slots, counts, query_slots, group_most = tables
    parts = [[] for _ in chunks]

    def project(chunk, first, size, begin, end, places):
        at = spans[chunk].start + first
        span = slice(at, at + size)
        query, kv = project_heads(
            places, gains[:, span], rounds[begin:end], weights_own[span], weights_other[span]
        )
        here = (end - begin) * local_blocks
        kv = kv.reshape(size, 2, here, BLOCK, HEAD_DIM)
        kv_other = lax.ppermute(kv, "core", swap)
        query = query.reshape(size, here, BLOCK, HEAD_DIM)
        parts[chunk].append((first, size, begin * local_blocks, here, query, kv, kv_other))
        return lax.optimization_barrier((places, kv))[0]

    attended = []
    for chunk, size in enumerate(chunks):
        if chunk == 0:
            for at in range(size):
                held_places = project(0, at, 1, 0, middle, held_places)
            held_places = project(0, 0, size, middle, chips, held_places)
        else:
            held_places = project(chunk, 0, size, 0, chips, held_places)
        mixed = attend(
            spans[chunk].start, size, key_slots, counts, query_slots, group_most, parts[chunk]
        )
        held_places, mixed = lax.optimization_barrier((held_places, mixed))
        mixed = mixed.reshape(chips, size, tokens, HEAD_DIM)
        if attended:
            mixed, attended = lax.optimization_barrier((mixed, attended))
        attended.append(exchange(mixed))

    sign = (2 * role - 1).astype(jnp.int32)[None]
    blocks = sides * lax.axis_size("role")
    which = jnp.stack([peers[3], peers[2], peers[1], peers[0]])
    before = None
    for chunk, size in enumerate(chunks[:-1]):
        before = out_blocks(
            which, sign, attended[chunk], spans[chunk].start // size, out_weight[0], blocks,
            (jnp.float32,), before,
        )[0]
    place = spans[-1].start // chunks[-1]
    (diagonal,) = out_blocks(
        which[:1], sign, attended[-1], place, out_weight[0], blocks, (jnp.bfloat16,), before
    )
    over_head, over_role, own = out_blocks(
        which[1:], sign, attended[-1], place, out_weight[0], blocks,
        (jnp.bfloat16, jnp.bfloat16, jnp.float32), before, 1,
    )
    far_swap = [(0, 3), (1, 2), (2, 1), (3, 0)]
    from_diagonal = lax.ppermute(diagonal, ("role", "head"), far_swap)
    from_head = lax.ppermute(over_head, "head", swap)
    from_role = lax.ppermute(over_role, "role", swap)
    return own + (
        from_role.astype(jnp.float32)
        + from_head.astype(jnp.float32)
        + from_diagonal.astype(jnp.float32)
    )


def splits_heads(mesh, qkv_weight, hidden_rows):
    role, seq, head = (mesh.shape[name] for name in ("role", "seq", "head"))
    if role != 2 or head != 2 or seq % CORES != 0:
        return False
    chips = seq // CORES
    heads = qkv_weight.shape[2] // (3 * HEAD_DIM * head)
    width = hidden_rows.shape[1]
    tokens = hidden_rows.shape[0] // seq
    return (
        heads % chips == 0
        and chips == role * head
        and width % (role * head * 256) == 0
        and width % (seq * 16) == 0
        and tokens % (2 * BLOCK) == 0
    )


def solution(mesh):
    def call(*arrays):
        if splits_heads(mesh, arrays[4], arrays[0]):
            per_device = per_device_by_heads
            seq = ("chip", "core")
            shape = mesh.devices.shape
            names = mesh.axis_names
            at = names.index("seq")
            layout = Mesh(
                mesh.devices.reshape(shape[:at] + (shape[at] // CORES, CORES) + shape[at + 1 :]),
                names[:at] + seq + names[at + 1 :],
            )
        else:
            per_device = per_device_by_tokens
            seq = "seq"
            layout = mesh
        placed = (
            P(seq, None),
            P(None, ("role", "head")),
            P(seq, None),
            P(seq),
            P("role", seq, "head"),
            P("role", "head", None),
            P("role", None, "head"),
            P("head", seq, None),
            P("head", seq),
        )
        return jax.shard_map(
            per_device,
            mesh=layout,
            in_specs=placed,
            out_specs=P(seq, ("role", "head")),
            check_vma=False,
        )(*arrays)

    return call
```

```python
import math

import jax
import jax.numpy as jnp
from jax import lax
from jax.experimental import pallas as pl
from jax.experimental.pallas import tpu as pltpu
from jax.sharding import Mesh
from jax.sharding import PartitionSpec as P

HEAD_DIM = 128
BLOCK = 64
KMAX = 8
CAP = 2


def rms_rows(values):
    return values * lax.rsqrt(jnp.mean(values * values, axis=-1, keepdims=True) + 1e-06)


def block_attention(queries, key_table, value_table, key_list, key_count):
    picked_keys = key_table[key_list]
    picked_values = value_table[key_list]
    scale = 1.0 / math.sqrt(HEAD_DIM)
    scores = (
        jnp.einsum("nqe,nkbe->nqkb", queries, picked_keys, preferred_element_type=jnp.float32)
        * scale
    )
    live = lax.broadcasted_iota(jnp.int32, (key_list.shape[0], KMAX), 1) < key_count[:, None]
    scores = jnp.where(live[:, None, :, None], scores, -jnp.inf)
    highest = jnp.max(scores, axis=(2, 3), keepdims=True)
    raised = jnp.exp(scores - highest)
    summed = jnp.sum(raised, axis=(2, 3), keepdims=True)
    weights = (raised / summed).astype(jnp.bfloat16)
    mixed = jnp.einsum("nqkb,nkbe->nqe", weights, picked_values, preferred_element_type=jnp.float32)
    return mixed.astype(jnp.bfloat16)


def pick_blocks(table, wanted):
    return table[wanted]


def per_device_by_tokens(
    hidden_rows,
    gen_weight,
    noise,
    timesteps,
    qkv_weight,
    out_weight,
    qk_gain,
    block_keys,
    block_count,
):
    generated = jnp.dot(hidden_rows, gen_weight, preferred_element_type=jnp.float32).astype(
        jnp.bfloat16
    )
    forked = lax.all_gather(generated, ("role", "head"), axis=1, tiled=True)
    row_count = forked.shape[0]
    width = forked.shape[1]
    local_blocks = timesteps.shape[0]
    angle_blocks = (timesteps.astype(jnp.float32) * (math.pi / 2000.0))[:, None, None]
    noisy = jnp.cos(angle_blocks) * forked.astype(jnp.float32).reshape(local_blocks, BLOCK, width)
    noisy = noisy + jnp.sin(angle_blocks) * noise.astype(jnp.float32).reshape(
        local_blocks, BLOCK, width
    )
    normed = rms_rows(noisy).reshape(row_count, width).astype(jnp.bfloat16)
    weight_here = qkv_weight[0]
    projected = jnp.dot(
        normed,
        lax.all_gather(weight_here, "seq", axis=0, tiled=True),
        preferred_element_type=jnp.float32,
    )
    heads_here = projected.shape[1] // (3 * HEAD_DIM)
    head_parts = projected.reshape(row_count, heads_here, 3, HEAD_DIM)
    gain_here = qk_gain[0]
    queries = (rms_rows(head_parts[:, :, 0]) * gain_here[0][None, :, None]).astype(jnp.bfloat16)
    key_local = (rms_rows(head_parts[:, :, 1]) * gain_here[1][None, :, None]).astype(jnp.bfloat16)
    value_local = head_parts[:, :, 2].astype(jnp.bfloat16)
    query_table = queries.reshape(local_blocks, BLOCK, heads_here, HEAD_DIM).transpose(2, 0, 1, 3)
    shard_count = lax.axis_size("seq")
    shard_here = lax.axis_index("seq")
    all_blocks = shard_count * local_blocks
    key_heads = key_local.reshape(local_blocks, BLOCK, heads_here, HEAD_DIM).transpose(2, 0, 1, 3)
    value_heads = value_local.reshape(local_blocks, BLOCK, heads_here, HEAD_DIM).transpose(
        2, 0, 1, 3
    )
    block_ids = lax.broadcasted_iota(jnp.int32, (1, 1, 1, all_blocks), 3)
    matches = block_keys[:, :, :, None] == block_ids
    remote = block_ids // local_blocks != shard_here
    needed = jnp.any(jnp.logical_and(matches, remote), axis=(1, 2))
    needed = needed.reshape(heads_here, shard_count, local_blocks)
    slot_of = jnp.cumsum(needed.astype(jnp.int32), axis=2) - 1
    slot_ids = lax.broadcasted_iota(jnp.int32, (1, 1, 1, CAP), 3)
    within_ids = lax.broadcasted_iota(jnp.int32, (1, 1, local_blocks, 1), 2)
    chosen_slot = jnp.logical_and(needed[..., None], slot_of[..., None] == slot_ids)
    requests = jnp.sum(jnp.where(chosen_slot, within_ids, 0), axis=2)
    asked = lax.all_to_all(
        requests.transpose(1, 0, 2), "seq", split_axis=0, concat_axis=0, tiled=True
    )
    sent_keys = jax.vmap(pick_blocks, in_axes=(0, 1), out_axes=1)(key_heads, asked)
    sent_values = jax.vmap(pick_blocks, in_axes=(0, 1), out_axes=1)(value_heads, asked)
    got_keys, got_values = (
        lax.all_to_all(sent_keys, "seq", split_axis=0, concat_axis=0, tiled=True),
        lax.all_to_all(sent_values, "seq", split_axis=0, concat_axis=0, tiled=True),
    )
    fetched_keys = got_keys.transpose(1, 0, 2, 3, 4).reshape(
        heads_here, shard_count * CAP, BLOCK, HEAD_DIM
    )
    fetched_values = got_values.transpose(1, 0, 2, 3, 4).reshape(
        heads_here, shard_count * CAP, BLOCK, HEAD_DIM
    )
    key_table = jnp.concatenate([key_heads, fetched_keys], axis=1)
    value_table = jnp.concatenate([value_heads, fetched_values], axis=1)
    local_ids = lax.broadcasted_iota(jnp.int32, (1, shard_count, local_blocks), 2)
    owner_grid = lax.broadcasted_iota(jnp.int32, (1, shard_count, local_blocks), 1)
    position = jnp.where(
        owner_grid == shard_here, local_ids, local_blocks + owner_grid * CAP + slot_of
    )
    position = position.reshape(heads_here, all_blocks)
    key_lists = jnp.sum(jnp.where(matches, position[:, None, None, :], 0), axis=3)
    attended = jax.vmap(block_attention)(
        query_table, key_table, value_table, key_lists, block_count
    )
    attended = attended.transpose(1, 2, 0, 3).reshape(row_count, heads_here * HEAD_DIM)
    contribution = jnp.dot(attended, out_weight[0], preferred_element_type=jnp.float32)
    signed = (2.0 * lax.axis_index("role").astype(jnp.float32) - 1.0) * contribution
    return lax.psum_scatter(
        signed.astype(jnp.bfloat16), ("role", "head"), scatter_dimension=1, tiled=True
    ).astype(jnp.float32)


VMEM_BYTES = 56 * 1024 * 1024
CORES = 2


def whole_in_vmem():
    return pl.BlockSpec(memory_space=pltpu.VMEM)


def in_hbm():
    return pl.BlockSpec(memory_space=pl.ANY)


def in_smem():
    return pl.BlockSpec(memory_space=pltpu.SMEM)


def cut_columns(weight, chips, head, extra=None):
    rows, columns = weight.shape
    wide = 3 * HEAD_DIM
    chip_heads = columns // (chips * wide)
    more = 0 if extra is None else extra.shape[1]

    def body(weight_ref, *refs):
        out_ref = refs[-1]
        out_ref[0, :rows] = weight_ref[...]
        if more:
            out_ref[0, rows:] = refs[0][0]

    in_specs = [pl.BlockSpec((rows, wide), lambda chip: (0, chip * chip_heads + head))]
    operands = [weight]
    if more:
        in_specs.append(pl.BlockSpec((1, more, wide), lambda chip: (chip, 0, 0)))
        operands.append(extra)
    return pl.pallas_call(
        body,
        grid=(chips,),
        in_specs=in_specs,
        out_specs=pl.BlockSpec((1, rows + more, wide), lambda chip: (chip, 0, 0)),
        out_shape=jax.ShapeDtypeStruct((chips, rows + more, wide), weight.dtype),
        name="cut_columns",
    )(*operands)


def project_heads(places, gains, rounds, depth, weights_own, weights_other):
    heads = len(weights_own)
    slabs, _, columns = weights_own[0].shape
    tokens, features = rounds[0][0].shape
    pieces = [piece for one in rounds for piece in one]
    turns = len(rounds)
    most = max(len(one) for one in rounds)
    joint = 2 if slabs % 2 == 0 else 1
    dtype = weights_own[0].dtype

    def body(places_ref, gains_ref, *refs):
        own_refs, other_refs = refs[:heads], refs[heads : 2 * heads]
        piece_refs = refs[2 * heads : 2 * heads + len(pieces)]
        query_ref, kv_ref = refs[2 * heads + len(pieces) : 2 * heads + len(pieces) + 2]
        table, rows, weight_sems, row_sems = refs[2 * heads + len(pieces) + 2 :]
        core = places_ref[slabs]
        copies = []
        for slab in range(slabs):
            here = []
            for head in range(heads):
                for side, ref in enumerate((own_refs[head], other_refs[head])):
                    place = core if side == 0 else 1 - core
                    here.append(
                        pltpu.make_async_copy(
                            ref.at[places_ref[slab], pl.ds(0, depth)],
                            table.at[
                                slab // joint,
                                slab % joint,
                                place,
                                :,
                                pl.ds(head * columns, columns),
                            ],
                            weight_sems.at[slab, head, side],
                        )
                    )
            at = 0
            for turn in range(turns):
                first = turn * tokens
                for which in range(len(rounds[turn])):
                    if min(which, slabs - 1) == slab:
                        count = rounds[turn][which].shape[0]
                        here.append(
                            pltpu.make_async_copy(
                                piece_refs[at],
                                rows.at[
                                    slab // joint,
                                    pl.ds(first, count),
                                    pl.ds(slab % joint * features, features),
                                ],
                                row_sems.at[which, turn],
                            )
                        )
                        first += count
                    at += 1
            for copy in here:
                copy.start()
            copies.append(here)
        total = None
        for group in range(slabs // joint):
            for slab in range(group * joint, (group + 1) * joint):
                for copy in copies[slab]:
                    copy.wait()
            part = jnp.dot(
                rows[group],
                table[group].reshape(joint * CORES * depth, heads * columns),
                preferred_element_type=jnp.float32,
            )
            total = part if total is None else total + part
        for turn in range(turns):
            here = total[turn * tokens : (turn + 1) * tokens]
            for head in range(heads):
                at = head * columns
                for which in range(2):
                    block = here[:, at + which * HEAD_DIM : at + (which + 1) * HEAD_DIM]
                    normal = (rms_rows(block) * gains_ref[which, head]).astype(dtype)
                    if which == 0:
                        query_ref[head, turn] = normal
                    else:
                        kv_ref[head, 0, turn] = normal
                block = here[:, at + 2 * HEAD_DIM : at + 3 * HEAD_DIM]
                kv_ref[head, 1, turn] = block.astype(dtype)

    return pl.pallas_call(
        body,
        in_specs=[in_smem(), in_smem()] + [in_hbm()] * (2 * heads + len(pieces)),
        out_specs=(whole_in_vmem(), whole_in_vmem()),
        out_shape=(
            jax.ShapeDtypeStruct((heads, turns, tokens, HEAD_DIM), dtype),
            jax.ShapeDtypeStruct((heads, 2, turns, tokens, HEAD_DIM), dtype),
        ),
        scratch_shapes=[
            pltpu.VMEM((slabs // joint, joint, CORES, depth, heads * columns), dtype),
            pltpu.VMEM((slabs // joint, turns * tokens, joint * features), dtype),
            pltpu.SemaphoreType.DMA((slabs, heads, 2)),
            pltpu.SemaphoreType.DMA((most, turns)),
        ],
        compiler_params=pltpu.CompilerParams(vmem_limit_bytes=VMEM_BYTES),
        name="project_heads",
    )(places, gains, *weights_own, *weights_other, *pieces)


def attend(first_head, heads, key_slots, counts, query_slots, group_most, parts):
    _, blocks, most = key_slots.shape
    groups = group_most.shape[1]
    together = blocks // groups
    scale = 1.0 / math.sqrt(HEAD_DIM)
    dtype = parts[0][4].dtype
    arrays = [array for part in parts for array in part[4:]]

    def body(slots_ref, counts_ref, from_ref, most_ref, *refs):
        out_ref, query_table, table, sems = refs[len(arrays) :]
        copies = []
        for at, (head, size, block, span, _, _, _) in enumerate(parts):
            query_part, own_part, other_part = refs[3 * at : 3 * at + 3]
            rows = pl.ds(head, size)
            copies.append(
                pltpu.make_async_copy(
                    query_part, query_table.at[rows, pl.ds(block, span)], sems.at[at, 0]
                )
            )
            for side, ref in enumerate((own_part, other_part)):
                place = pl.ds(side * blocks + block, span)
                copies.append(
                    pltpu.make_async_copy(ref, table.at[rows, :, place], sems.at[at, 1 + side])
                )
        for copy in copies:
            copy.start()
        for copy in copies:
            copy.wait()

        def run(head, group, listed, batch):
            for first in range(0, together, batch):
                spots = [group * together + at for at in range(first, min(first + batch, together))]
                slots = [[slots_ref[first_head + head, at, entry] for entry in range(listed)] for at in spots]
                scores = []
                for at, listing in zip(spots, slots):
                    keys = jnp.concatenate([table[head, 0, slot] for slot in listing], axis=0)
                    scores.append(
                        lax.dot_general(
                            query_table[head, from_ref[at]],
                            keys,
                            (((1,), (1,)), ((), ())),
                            preferred_element_type=jnp.float32,
                        )
                    )
                column = lax.broadcasted_iota(jnp.int32, (1, listed * BLOCK), 1)
                scores = [
                    jnp.where(column < counts_ref[first_head + head, at] * BLOCK, one * scale, -jnp.inf)
                    for at, one in zip(spots, scores)
                ]
                highest = [jnp.max(one, axis=1, keepdims=True) for one in scores]
                raised = [jnp.exp(one - top) for one, top in zip(scores, highest)]
                inverse = [1.0 / jnp.sum(one, axis=1, keepdims=True) for one in raised]
                weights = [(one * by).astype(dtype) for one, by in zip(raised, inverse)]
                mixed = []
                for one, listing in zip(weights, slots):
                    values = jnp.concatenate([table[head, 1, slot] for slot in listing], axis=0)
                    mixed.append(jnp.dot(one, values, preferred_element_type=jnp.float32))
                for at, one in enumerate(mixed):
                    out_ref[group, head, first + at] = one.astype(dtype)

        def step(at, carry):
            head, group = at // groups, at % groups
            few = most_ref[first_head + head, group] <= most // 2

            @pl.when(few)
            def _():
                run(head, group, most // 2, 6)

            @pl.when(jnp.logical_not(few))
            def _():
                run(head, group, most, 3)

            return carry

        lax.fori_loop(0, heads * groups, step, 0)

    return pl.pallas_call(
        body,
        in_specs=[in_smem()] * 4 + [in_hbm()] * len(arrays),
        out_specs=whole_in_vmem(),
        out_shape=jax.ShapeDtypeStruct((groups, heads, together, BLOCK, HEAD_DIM), dtype),
        scratch_shapes=[
            pltpu.VMEM((heads, blocks, BLOCK, HEAD_DIM), dtype),
            pltpu.VMEM((heads, 2, CORES * blocks, BLOCK, HEAD_DIM), dtype),
            pltpu.SemaphoreType.DMA((len(parts), 3)),
        ],
        compiler_params=pltpu.CompilerParams(vmem_limit_bytes=VMEM_BYTES),
        name="attend",
    )(key_slots, counts, query_slots, group_most, *arrays)


def out_blocks(which, sign, attended, place, out_weight, blocks, dtypes, before=None, skip=0):
    groups, heads, tokens, _ = attended.shape
    depth, features = out_weight.shape
    width = features // blocks
    wanted = which.shape[0]
    rows = heads * HEAD_DIM
    weight = out_weight.reshape(groups, depth // groups, features)
    stacked = len(dtypes) == 1 and wanted > 1

    def body(which_ref, sign_ref, mixed_ref, weight_ref, *refs):
        out_refs = refs if before is None else refs[1:]
        joined = jnp.concatenate(
            [mixed_ref[group, head] for group in range(groups) for head in range(heads)], axis=1
        )
        total = jnp.dot(
            joined,
            weight_ref[...].reshape(groups * rows, width),
            preferred_element_type=jnp.float32,
        )
        total = total * sign_ref[0].astype(jnp.float32)
        if before is not None:
            total = total + refs[0][0]
        if stacked:
            out_refs[0][0] = total.astype(dtypes[0])
        else:
            for at in range(wanted):

                @pl.when(pl.program_id(0) == at)
                def _(at=at):
                    out_refs[at][...] = total.astype(dtypes[at])

    in_specs = [
        pl.BlockSpec(attended.shape, lambda i, w, s: (0, 0, 0, 0)),
        pl.BlockSpec((groups, rows, width), lambda i, w, s: (0, place, w[i])),
    ]
    operands = [attended, weight]
    if before is not None:
        in_specs.append(pl.BlockSpec((1, tokens, width), lambda i, w, s: (i + skip, 0, 0)))
        operands.append(before)
    if stacked:
        out_specs = [pl.BlockSpec((1, tokens, width), lambda i, w, s: (i, 0, 0))]
        out_shape = [jax.ShapeDtypeStruct((wanted, tokens, width), dtypes[0])]
    else:
        out_specs = [pl.BlockSpec((tokens, width), lambda i, w, s: (0, 0))] * wanted
        out_shape = [jax.ShapeDtypeStruct((tokens, width), dtype) for dtype in dtypes]
    return pl.pallas_call(
        body,
        grid_spec=pltpu.PrefetchScalarGridSpec(
            num_scalar_prefetch=2, grid=(wanted,), in_specs=in_specs, out_specs=out_specs
        ),
        out_shape=out_shape,
        compiler_params=pltpu.CompilerParams(vmem_limit_bytes=VMEM_BYTES),
        name="out_blocks",
    )(which, sign, *operands)


def nearest(chips):
    order = [
        sorted((at for at in range(chips) if at != here), key=lambda at: (abs(at - here), at))
        for here in range(chips)
    ]
    turns = [
        [0 if at == here else order[here].index(at) + 1 for at in range(chips)]
        for here in range(chips)
    ]
    return order, turns


def chunk_sizes(heads):
    last = heads // 3 if heads % 3 == 0 else 1
    return [heads - last, last] if heads > last else [heads]


def per_device_by_heads(
    hidden_rows,
    gen_weight,
    noise,
    timesteps,
    qkv_weight,
    out_weight,
    qk_gain,
    block_keys,
    block_count,
):
    role, head = lax.axis_index("role"), lax.axis_index("head")
    chip, core = lax.axis_index("chip"), lax.axis_index("core")
    chips = lax.axis_size("chip")
    local_heads, local_blocks, most = block_keys.shape
    heads = local_heads // chips
    tokens = hidden_rows.shape[0]
    width = hidden_rows.shape[1]
    features = gen_weight.shape[1]
    all_blocks = chips * local_blocks
    swap = [(0, 1), (1, 0)]
    far_swap = [(0, 3), (1, 2), (2, 1), (3, 0)]
    order, turns = nearest(chips)
    turn_here = jnp.asarray(turns, dtype=jnp.int32)[chip]

    def pick(index, options):
        picked = options[0]
        for at in range(1, len(options)):
            picked = jnp.where(index == at, options[at], picked)
        return picked

    def turn_of(other):
        return pick(other, [turn_here[at] for at in range(chips)])

    def exchange(array):
        return lax.all_to_all(array, "chip", split_axis=0, concat_axis=0, tiled=True)

    weight_here = qkv_weight[0]
    depth = weight_here.shape[0]
    wide = 3 * HEAD_DIM
    lists = jnp.concatenate([block_keys, block_count[:, :, None]], axis=2)
    lists = lists.reshape(chips, -1).astype(jnp.bfloat16)
    listed = lists.shape[1]
    spare = -(-listed // (16 * wide)) * 16
    lists = jnp.pad(lists, ((0, 0), (0, spare * wide - listed))).reshape(chips, spare, wide)
    cuts = [
        cut_columns(weight_here, chips, at, lists if at == 0 else None) for at in range(heads)
    ]
    hidden_rows, cuts[0] = lax.optimization_barrier((hidden_rows, cuts[0]))
    weights_own = [exchange(cuts[0])]
    weights_other = []

    mine = role * lax.axis_size("head") + head
    generated = jnp.dot(hidden_rows, gen_weight, preferred_element_type=jnp.float32)
    generated = lax.reduce_precision(generated, 8, 7)
    angle_blocks = (timesteps.astype(jnp.float32) * (math.pi / 2000.0))[:, None, None]
    noise_here = lax.dynamic_slice_in_dim(noise, mine * features, features, axis=1)
    noisy = jnp.cos(angle_blocks) * generated.reshape(local_blocks, BLOCK, features)
    noisy = noisy + jnp.sin(angle_blocks) * noise_here.astype(jnp.float32).reshape(
        local_blocks, BLOCK, features
    )
    squares = jnp.sum(noisy * noisy, axis=-1)
    squares = squares + lax.ppermute(squares, "role", swap)
    squares = squares + lax.ppermute(squares, "head", swap)
    normed = (noisy * lax.rsqrt(squares / width + 1e-06)[:, :, None]).astype(jnp.bfloat16)
    normed = normed.reshape(tokens, features)

    def tables_of(lists):
        lists = lists.reshape(chips, spare * wide)[:, :listed].astype(jnp.int32)
        lists = lists.reshape(chips, heads, local_blocks, most + 1).transpose(1, 0, 2, 3)
        lists = lists.reshape(heads, all_blocks, most + 1)
        owner = lists[:, :, :most] // local_blocks
        turn = turn_of(owner // CORES)
        far = (owner % CORES != core).astype(jnp.int32)
        key_slots = far * all_blocks + turn * local_blocks + lists[:, :, :most] % local_blocks
        counts = lists[:, :, most]
        group_most = jnp.max(counts.reshape(heads, chips, local_blocks), axis=2)
        spot = jnp.arange(all_blocks, dtype=jnp.int32)
        query_slots = turn_of(spot // local_blocks)
        query_slots = query_slots * local_blocks + spot % local_blocks

        return key_slots, counts, query_slots, group_most

    sides = lax.axis_size("head")
    peers = jnp.stack(
        [
            role * sides + head,
            (1 - role) * sides + head,
            role * sides + 1 - head,
            (1 - role) * sides + 1 - head,
        ]
    ).astype(jnp.int32)
    places = jnp.concatenate([peers, core[None].astype(jnp.int32)])
    gains = lax.dynamic_slice_in_dim(qk_gain[0], chip * heads, heads, axis=1)

    chunks = chunk_sizes(heads)
    spans = [slice(sum(chunks[:at]), sum(chunks[: at + 1])) for at in range(len(chunks))]
    parts = [[] for _ in chunks]

    def project(chunk, first, size, begin, some, places):
        at = spans[chunk].start + first
        span = slice(at, at + size)
        query, kv = project_heads(
            places, gains[:, span], some, depth, weights_own[span], weights_other[span]
        )
        here = len(some) * local_blocks
        kv = kv.reshape(size, 2, here, BLOCK, HEAD_DIM)
        kv_other = lax.ppermute(kv, "core", swap)
        query = query.reshape(size, here, BLOCK, HEAD_DIM)
        parts[chunk].append((first, size, begin * local_blocks, here, query, kv, kv_other))
        return lax.optimization_barrier((places, kv))[0]

    half = tokens // 2
    rounds = []
    straight = None
    shard, up, down = normed, normed, normed
    ups, downs = [None], [None]
    late = None
    for phase in range(chips):
        sent = {}
        sent["role"] = lax.ppermute(shard, "role", swap)
        sent["head"] = lax.ppermute(shard, "head", swap)
        diagonal = None
        if straight is not None:
            diagonal = straight + (
                lax.ppermute(straight[2][:half], "role", swap),
                lax.ppermute(straight[1][half:], "head", swap),
            )
        step = phase + 1
        if step < chips:
            sent["up"] = lax.ppermute(
                up, "chip", [(at, at + 1) for at in range(step - 1, chips - 1)]
            )
            sent["down"] = lax.ppermute(
                down, "chip", [(at + 1, at) for at in range(chips - step)]
            )
        else:
            sent["far"] = lax.ppermute(shard, ("role", "head"), far_swap)
        if phase == 0:
            sent["weights"] = weights_own.pop()
        if phase == 1:
            sent["weights"] = lax.ppermute(weights_own[0], "core", swap)
        if step == chips:
            early = rounds + [late]
            tables = tables_of(weights_own[0][:, depth:])
            held_places, tables = lax.optimization_barrier((places, tables))
            held_places = project(0, 0, 1, 0, early, held_places)
            sent["places"] = held_places
            sent["diagonal"] = diagonal
        sent, shard, late = lax.optimization_barrier((sent, shard, late))
        if phase == 0:
            weights_own.append(sent["weights"])
        if phase == 1:
            weights_other.append(sent["weights"])
        if step == chips:
            held_places, diagonal = sent["places"], sent["diagonal"]
        if late is not None:
            rounds.append(late)
        late = diagonal
        straight = (shard, sent["role"], sent["head"])
        if step < chips:
            up, down = sent["up"], sent["down"]
            ups.append(up)
            downs.append(down)
            options = []
            for here in range(chips):
                source = order[here][step - 1]
                options.append(ups[here - source] if source < here else downs[source - here])
            shard = pick(chip, options)
        if phase >= chips - 2 and len(weights_own) < heads:
            held, _ = lax.optimization_barrier((cuts[len(weights_own)], sent))
            weights_own.append(exchange(held))
            if step == chips:
                weights_other += [lax.ppermute(one, "core", swap) for one in weights_own[1:]]
    rounds.append(late)
    rounds.append(straight + (sent["far"],))
    while len(weights_own) < heads:
        weights_own.append(exchange(cuts[len(weights_own)]))
    for at in range(len(weights_other), heads):
        weights_other.append(lax.ppermute(weights_own[at], "core", swap))

    attended = []
    for chunk, size in enumerate(chunks):
        if chunk == 0:
            for at in range(1, size):
                held_places = project(0, at, 1, 0, early, held_places)
            held_places = project(0, 0, size, len(early), rounds[len(early) :], held_places)
        else:
            held_places = project(chunk, 0, size, 0, rounds, held_places)
        mixed = attend(spans[chunk].start, size, *tables, parts[chunk])
        held_places, mixed = lax.optimization_barrier((held_places, mixed))
        mixed = mixed.reshape(chips, size, tokens, HEAD_DIM)
        if attended:
            mixed, attended = lax.optimization_barrier((mixed, attended))
        attended.append(exchange(mixed))

    sign = (2 * role - 1).astype(jnp.int32)[None]
    blocks = sides * lax.axis_size("role")
    which = jnp.stack([peers[3], peers[2], peers[1], peers[0]])
    before = None
    for chunk, size in enumerate(chunks[:-1]):
        before = out_blocks(
            which, sign, attended[chunk], spans[chunk].start // size, out_weight[0], blocks,
            (jnp.float32,), before,
        )[0]
    place = spans[-1].start // chunks[-1]
    (diagonal,) = out_blocks(
        which[:1], sign, attended[-1], place, out_weight[0], blocks, (jnp.bfloat16,), before
    )
    over_head, over_role, own = out_blocks(
        which[1:], sign, attended[-1], place, out_weight[0], blocks,
        (jnp.bfloat16, jnp.bfloat16, jnp.float32), before, 1,
    )
    from_diagonal = lax.ppermute(diagonal, ("role", "head"), far_swap)
    from_head = lax.ppermute(over_head, "head", swap)
    from_role = lax.ppermute(over_role, "role", swap)
    return own + (
        from_role.astype(jnp.float32)
        + from_head.astype(jnp.float32)
        + from_diagonal.astype(jnp.float32)
    )


def splits_heads(mesh, qkv_weight, hidden_rows):
    role, seq, head = (mesh.shape[name] for name in ("role", "seq", "head"))
    if role != 2 or head != 2 or seq % CORES != 0:
        return False
    chips = seq // CORES
    heads = qkv_weight.shape[2] // (3 * HEAD_DIM * head)
    width = hidden_rows.shape[1]
    tokens = hidden_rows.shape[0] // seq
    return (
        heads % chips == 0
        and chips == role * head
        and width % (role * head * 256) == 0
        and width % (seq * 16) == 0
        and tokens % (2 * BLOCK) == 0
        and hidden_rows.shape[0] // BLOCK <= 256
    )


def solution(mesh):
    def call(*arrays):
        if splits_heads(mesh, arrays[4], arrays[0]):
            per_device = per_device_by_heads
            seq = ("chip", "core")
            shape = mesh.devices.shape
            names = mesh.axis_names
            at = names.index("seq")
            layout = Mesh(
                mesh.devices.reshape(shape[:at] + (shape[at] // CORES, CORES) + shape[at + 1 :]),
                names[:at] + seq + names[at + 1 :],
            )
        else:
            per_device = per_device_by_tokens
            seq = "seq"
            layout = mesh
        placed = (
            P(seq, None),
            P(None, ("role", "head")),
            P(seq, None),
            P(seq),
            P("role", seq, "head"),
            P("role", "head", None),
            P("role", None, "head"),
            P("head", seq, None),
            P("head", seq),
        )
        return jax.shard_map(
            per_device,
            mesh=layout,
            in_specs=placed,
            out_specs=P(seq, ("role", "head")),
            check_vma=False,
        )(*arrays)

    return call
```

```python
import math

import jax
import jax.numpy as jnp
from jax import lax
from jax.experimental import pallas as pl
from jax.experimental.pallas import tpu as pltpu
from jax.sharding import Mesh
from jax.sharding import PartitionSpec as P

HEAD_DIM = 128
BLOCK = 64
KMAX = 8
CAP = 2


def rms_rows(values):
    return values * lax.rsqrt(jnp.mean(values * values, axis=-1, keepdims=True) + 1e-06)


def block_attention(queries, key_table, value_table, key_list, key_count):
    picked_keys = key_table[key_list]
    picked_values = value_table[key_list]
    scale = 1.0 / math.sqrt(HEAD_DIM)
    scores = (
        jnp.einsum("nqe,nkbe->nqkb", queries, picked_keys, preferred_element_type=jnp.float32)
        * scale
    )
    live = lax.broadcasted_iota(jnp.int32, (key_list.shape[0], KMAX), 1) < key_count[:, None]
    scores = jnp.where(live[:, None, :, None], scores, -jnp.inf)
    highest = jnp.max(scores, axis=(2, 3), keepdims=True)
    raised = jnp.exp(scores - highest)
    summed = jnp.sum(raised, axis=(2, 3), keepdims=True)
    weights = (raised / summed).astype(jnp.bfloat16)
    mixed = jnp.einsum("nqkb,nkbe->nqe", weights, picked_values, preferred_element_type=jnp.float32)
    return mixed.astype(jnp.bfloat16)


def pick_blocks(table, wanted):
    return table[wanted]


def per_device_by_tokens(
    hidden_rows,
    gen_weight,
    noise,
    timesteps,
    qkv_weight,
    out_weight,
    qk_gain,
    block_keys,
    block_count,
):
    generated = jnp.dot(hidden_rows, gen_weight, preferred_element_type=jnp.float32).astype(
        jnp.bfloat16
    )
    forked = lax.all_gather(generated, ("role", "head"), axis=1, tiled=True)
    row_count = forked.shape[0]
    width = forked.shape[1]
    local_blocks = timesteps.shape[0]
    angle_blocks = (timesteps.astype(jnp.float32) * (math.pi / 2000.0))[:, None, None]
    noisy = jnp.cos(angle_blocks) * forked.astype(jnp.float32).reshape(local_blocks, BLOCK, width)
    noisy = noisy + jnp.sin(angle_blocks) * noise.astype(jnp.float32).reshape(
        local_blocks, BLOCK, width
    )
    normed = rms_rows(noisy).reshape(row_count, width).astype(jnp.bfloat16)
    weight_here = qkv_weight[0]
    projected = jnp.dot(
        normed,
        lax.all_gather(weight_here, "seq", axis=0, tiled=True),
        preferred_element_type=jnp.float32,
    )
    heads_here = projected.shape[1] // (3 * HEAD_DIM)
    head_parts = projected.reshape(row_count, heads_here, 3, HEAD_DIM)
    gain_here = qk_gain[0]
    queries = (rms_rows(head_parts[:, :, 0]) * gain_here[0][None, :, None]).astype(jnp.bfloat16)
    key_local = (rms_rows(head_parts[:, :, 1]) * gain_here[1][None, :, None]).astype(jnp.bfloat16)
    value_local = head_parts[:, :, 2].astype(jnp.bfloat16)
    query_table = queries.reshape(local_blocks, BLOCK, heads_here, HEAD_DIM).transpose(2, 0, 1, 3)
    shard_count = lax.axis_size("seq")
    shard_here = lax.axis_index("seq")
    all_blocks = shard_count * local_blocks
    key_heads = key_local.reshape(local_blocks, BLOCK, heads_here, HEAD_DIM).transpose(2, 0, 1, 3)
    value_heads = value_local.reshape(local_blocks, BLOCK, heads_here, HEAD_DIM).transpose(
        2, 0, 1, 3
    )
    block_ids = lax.broadcasted_iota(jnp.int32, (1, 1, 1, all_blocks), 3)
    matches = block_keys[:, :, :, None] == block_ids
    remote = block_ids // local_blocks != shard_here
    needed = jnp.any(jnp.logical_and(matches, remote), axis=(1, 2))
    needed = needed.reshape(heads_here, shard_count, local_blocks)
    slot_of = jnp.cumsum(needed.astype(jnp.int32), axis=2) - 1
    slot_ids = lax.broadcasted_iota(jnp.int32, (1, 1, 1, CAP), 3)
    within_ids = lax.broadcasted_iota(jnp.int32, (1, 1, local_blocks, 1), 2)
    chosen_slot = jnp.logical_and(needed[..., None], slot_of[..., None] == slot_ids)
    requests = jnp.sum(jnp.where(chosen_slot, within_ids, 0), axis=2)
    asked = lax.all_to_all(
        requests.transpose(1, 0, 2), "seq", split_axis=0, concat_axis=0, tiled=True
    )
    sent_keys = jax.vmap(pick_blocks, in_axes=(0, 1), out_axes=1)(key_heads, asked)
    sent_values = jax.vmap(pick_blocks, in_axes=(0, 1), out_axes=1)(value_heads, asked)
    got_keys, got_values = (
        lax.all_to_all(sent_keys, "seq", split_axis=0, concat_axis=0, tiled=True),
        lax.all_to_all(sent_values, "seq", split_axis=0, concat_axis=0, tiled=True),
    )
    fetched_keys = got_keys.transpose(1, 0, 2, 3, 4).reshape(
        heads_here, shard_count * CAP, BLOCK, HEAD_DIM
    )
    fetched_values = got_values.transpose(1, 0, 2, 3, 4).reshape(
        heads_here, shard_count * CAP, BLOCK, HEAD_DIM
    )
    key_table = jnp.concatenate([key_heads, fetched_keys], axis=1)
    value_table = jnp.concatenate([value_heads, fetched_values], axis=1)
    local_ids = lax.broadcasted_iota(jnp.int32, (1, shard_count, local_blocks), 2)
    owner_grid = lax.broadcasted_iota(jnp.int32, (1, shard_count, local_blocks), 1)
    position = jnp.where(
        owner_grid == shard_here, local_ids, local_blocks + owner_grid * CAP + slot_of
    )
    position = position.reshape(heads_here, all_blocks)
    key_lists = jnp.sum(jnp.where(matches, position[:, None, None, :], 0), axis=3)
    attended = jax.vmap(block_attention)(
        query_table, key_table, value_table, key_lists, block_count
    )
    attended = attended.transpose(1, 2, 0, 3).reshape(row_count, heads_here * HEAD_DIM)
    contribution = jnp.dot(attended, out_weight[0], preferred_element_type=jnp.float32)
    signed = (2.0 * lax.axis_index("role").astype(jnp.float32) - 1.0) * contribution
    return lax.psum_scatter(
        signed.astype(jnp.bfloat16), ("role", "head"), scatter_dimension=1, tiled=True
    ).astype(jnp.float32)


VMEM_BYTES = 56 * 1024 * 1024
CORES = 2


def whole_in_vmem():
    return pl.BlockSpec(memory_space=pltpu.VMEM)


def in_hbm():
    return pl.BlockSpec(memory_space=pl.ANY)


def in_smem():
    return pl.BlockSpec(memory_space=pltpu.SMEM)


def cut_columns(weight, chips, head, extra=None):
    rows, columns = weight.shape
    wide = 3 * HEAD_DIM
    chip_heads = columns // (chips * wide)
    more = 0 if extra is None else extra.shape[1]

    def body(weight_ref, *refs):
        out_ref = refs[-1]
        out_ref[0, :rows] = weight_ref[...]
        if more:
            out_ref[0, rows:] = refs[0][0]

    in_specs = [pl.BlockSpec((rows, wide), lambda chip: (0, chip * chip_heads + head))]
    operands = [weight]
    if more:
        in_specs.append(pl.BlockSpec((1, more, wide), lambda chip: (chip, 0, 0)))
        operands.append(extra)
    return pl.pallas_call(
        body,
        grid=(chips,),
        in_specs=in_specs,
        out_specs=pl.BlockSpec((1, rows + more, wide), lambda chip: (chip, 0, 0)),
        out_shape=jax.ShapeDtypeStruct((chips, rows + more, wide), weight.dtype),
        name="cut_columns",
    )(*operands)


def project_heads(places, gains, rounds, depth, weights_own, weights_other):
    heads = len(weights_own)
    slabs, _, columns = weights_own[0].shape
    tokens, features = rounds[0][0].shape
    pieces = [piece for one in rounds for piece in one]
    turns = len(rounds)
    most = max(len(one) for one in rounds)
    joint = 2 if slabs % 2 == 0 else 1
    dtype = weights_own[0].dtype

    def body(places_ref, gains_ref, *refs):
        own_refs, other_refs = refs[:heads], refs[heads : 2 * heads]
        piece_refs = refs[2 * heads : 2 * heads + len(pieces)]
        query_ref, kv_ref = refs[2 * heads + len(pieces) : 2 * heads + len(pieces) + 2]
        table, rows, weight_sems, row_sems = refs[2 * heads + len(pieces) + 2 :]
        core = places_ref[slabs]
        copies = []
        for slab in range(slabs):
            here = []
            for head in range(heads):
                for side, ref in enumerate((own_refs[head], other_refs[head])):
                    place = core if side == 0 else 1 - core
                    here.append(
                        pltpu.make_async_copy(
                            ref.at[places_ref[slab], pl.ds(0, depth)],
                            table.at[
                                slab // joint,
                                slab % joint,
                                place,
                                :,
                                pl.ds(head * columns, columns),
                            ],
                            weight_sems.at[slab, head, side],
                        )
                    )
            at = 0
            for turn in range(turns):
                first = turn * tokens
                for which in range(len(rounds[turn])):
                    if min(which, slabs - 1) == slab:
                        count = rounds[turn][which].shape[0]
                        here.append(
                            pltpu.make_async_copy(
                                piece_refs[at],
                                rows.at[
                                    slab // joint,
                                    pl.ds(first, count),
                                    pl.ds(slab % joint * features, features),
                                ],
                                row_sems.at[which, turn],
                            )
                        )
                        first += count
                    at += 1
            for copy in here:
                copy.start()
            copies.append(here)
        total = None
        for group in range(slabs // joint):
            for slab in range(group * joint, (group + 1) * joint):
                for copy in copies[slab]:
                    copy.wait()
            part = jnp.dot(
                rows[group],
                table[group].reshape(joint * CORES * depth, heads * columns),
                preferred_element_type=jnp.float32,
            )
            total = part if total is None else total + part
        for turn in range(turns):
            here = total[turn * tokens : (turn + 1) * tokens]
            for head in range(heads):
                at = head * columns
                for which in range(2):
                    block = here[:, at + which * HEAD_DIM : at + (which + 1) * HEAD_DIM]
                    normal = (rms_rows(block) * gains_ref[which, head]).astype(dtype)
                    if which == 0:
                        query_ref[head, turn] = normal
                    else:
                        kv_ref[head, 0, turn] = normal
                block = here[:, at + 2 * HEAD_DIM : at + 3 * HEAD_DIM]
                kv_ref[head, 1, turn] = block.astype(dtype)

    return pl.pallas_call(
        body,
        in_specs=[in_smem(), in_smem()] + [in_hbm()] * (2 * heads + len(pieces)),
        out_specs=(whole_in_vmem(), whole_in_vmem()),
        out_shape=(
            jax.ShapeDtypeStruct((heads, turns, tokens, HEAD_DIM), dtype),
            jax.ShapeDtypeStruct((heads, 2, turns, tokens, HEAD_DIM), dtype),
        ),
        scratch_shapes=[
            pltpu.VMEM((slabs // joint, joint, CORES, depth, heads * columns), dtype),
            pltpu.VMEM((slabs // joint, turns * tokens, joint * features), dtype),
            pltpu.SemaphoreType.DMA((slabs, heads, 2)),
            pltpu.SemaphoreType.DMA((most, turns)),
        ],
        compiler_params=pltpu.CompilerParams(vmem_limit_bytes=VMEM_BYTES),
        name="project_heads",
    )(places, gains, *weights_own, *weights_other, *pieces)


def attend(first_head, heads, key_slots, counts, query_slots, group_most, parts):
    _, blocks, most = key_slots.shape
    groups = group_most.shape[1]
    together = blocks // groups
    scale = 1.0 / math.sqrt(HEAD_DIM)
    dtype = parts[0][4].dtype
    arrays = [array for part in parts for array in part[4:]]

    def body(slots_ref, counts_ref, from_ref, most_ref, *refs):
        out_ref, query_table, table, sems = refs[len(arrays) :]
        copies = []
        for at, (head, size, block, span, _, _, _) in enumerate(parts):
            query_part, own_part, other_part = refs[3 * at : 3 * at + 3]
            rows = pl.ds(head, size)
            copies.append(
                pltpu.make_async_copy(
                    query_part, query_table.at[rows, pl.ds(block, span)], sems.at[at, 0]
                )
            )
            for side, ref in enumerate((own_part, other_part)):
                place = pl.ds(side * blocks + block, span)
                copies.append(
                    pltpu.make_async_copy(ref, table.at[rows, :, place], sems.at[at, 1 + side])
                )
        for copy in copies:
            copy.start()
        for copy in copies:
            copy.wait()

        def run(head, group, listed, batch):
            for first in range(0, together, batch):
                spots = [group * together + at for at in range(first, min(first + batch, together))]
                slots = [[slots_ref[first_head + head, at, entry] for entry in range(listed)] for at in spots]
                scores = []
                for at, listing in zip(spots, slots):
                    keys = jnp.concatenate([table[head, 0, slot] for slot in listing], axis=0)
                    scores.append(
                        lax.dot_general(
                            query_table[head, from_ref[at]],
                            keys,
                            (((1,), (1,)), ((), ())),
                            preferred_element_type=jnp.float32,
                        )
                    )
                column = lax.broadcasted_iota(jnp.int32, (1, listed * BLOCK), 1)
                scores = [
                    jnp.where(column < counts_ref[first_head + head, at] * BLOCK, one * scale, -jnp.inf)
                    for at, one in zip(spots, scores)
                ]
                highest = [jnp.max(one, axis=1, keepdims=True) for one in scores]
                raised = [jnp.exp(one - top) for one, top in zip(scores, highest)]
                inverse = [1.0 / jnp.sum(one, axis=1, keepdims=True) for one in raised]
                weights = [(one * by).astype(dtype) for one, by in zip(raised, inverse)]
                mixed = []
                for one, listing in zip(weights, slots):
                    values = jnp.concatenate([table[head, 1, slot] for slot in listing], axis=0)
                    mixed.append(jnp.dot(one, values, preferred_element_type=jnp.float32))
                for at, one in enumerate(mixed):
                    out_ref[group, head, first + at] = one.astype(dtype)

        def step(at, carry):
            head, group = at // groups, at % groups
            few = most_ref[first_head + head, group] <= most // 2

            @pl.when(few)
            def _():
                run(head, group, most // 2, 6)

            @pl.when(jnp.logical_not(few))
            def _():
                run(head, group, most, 3)

            return carry

        lax.fori_loop(0, heads * groups, step, 0)

    return pl.pallas_call(
        body,
        in_specs=[in_smem()] * 4 + [in_hbm()] * len(arrays),
        out_specs=whole_in_vmem(),
        out_shape=jax.ShapeDtypeStruct((groups, heads, together, BLOCK, HEAD_DIM), dtype),
        scratch_shapes=[
            pltpu.VMEM((heads, blocks, BLOCK, HEAD_DIM), dtype),
            pltpu.VMEM((heads, 2, CORES * blocks, BLOCK, HEAD_DIM), dtype),
            pltpu.SemaphoreType.DMA((len(parts), 3)),
        ],
        compiler_params=pltpu.CompilerParams(vmem_limit_bytes=VMEM_BYTES),
        name="attend",
    )(key_slots, counts, query_slots, group_most, *arrays)


def out_blocks(which, sign, attended, place, out_weight, blocks, dtypes, before=None, skip=0):
    groups, heads, tokens, _ = attended.shape
    depth, features = out_weight.shape
    width = features // blocks
    wanted = which.shape[0]
    rows = heads * HEAD_DIM
    weight = out_weight.reshape(groups, depth // groups, features)
    stacked = len(dtypes) == 1 and wanted > 1

    def body(which_ref, sign_ref, mixed_ref, weight_ref, *refs):
        out_refs = refs if before is None else refs[1:]
        joined = jnp.concatenate(
            [mixed_ref[group, head] for group in range(groups) for head in range(heads)], axis=1
        )
        total = jnp.dot(
            joined,
            weight_ref[...].reshape(groups * rows, width),
            preferred_element_type=jnp.float32,
        )
        total = total * sign_ref[0].astype(jnp.float32)
        if before is not None:
            total = total + refs[0][0]
        if stacked:
            out_refs[0][0] = total.astype(dtypes[0])
        else:
            for at in range(wanted):

                @pl.when(pl.program_id(0) == at)
                def _(at=at):
                    out_refs[at][...] = total.astype(dtypes[at])

    in_specs = [
        pl.BlockSpec(attended.shape, lambda i, w, s: (0, 0, 0, 0)),
        pl.BlockSpec((groups, rows, width), lambda i, w, s: (0, place, w[i])),
    ]
    operands = [attended, weight]
    if before is not None:
        in_specs.append(pl.BlockSpec((1, tokens, width), lambda i, w, s: (i + skip, 0, 0)))
        operands.append(before)
    if stacked:
        out_specs = [pl.BlockSpec((1, tokens, width), lambda i, w, s: (i, 0, 0))]
        out_shape = [jax.ShapeDtypeStruct((wanted, tokens, width), dtypes[0])]
    else:
        out_specs = [pl.BlockSpec((tokens, width), lambda i, w, s: (0, 0))] * wanted
        out_shape = [jax.ShapeDtypeStruct((tokens, width), dtype) for dtype in dtypes]
    return pl.pallas_call(
        body,
        grid_spec=pltpu.PrefetchScalarGridSpec(
            num_scalar_prefetch=2, grid=(wanted,), in_specs=in_specs, out_specs=out_specs
        ),
        out_shape=out_shape,
        compiler_params=pltpu.CompilerParams(vmem_limit_bytes=VMEM_BYTES),
        name="out_blocks",
    )(which, sign, *operands)


def nearest(chips):
    order = [
        sorted((at for at in range(chips) if at != here), key=lambda at: (abs(at - here), at))
        for here in range(chips)
    ]
    turns = [
        [0 if at == here else order[here].index(at) + 1 for at in range(chips)]
        for here in range(chips)
    ]
    return order, turns


def chunk_sizes(heads):
    last = heads // 3 if heads % 3 == 0 else 1
    return [heads - last, last] if heads > last else [heads]


def per_device_by_heads(
    hidden_rows,
    gen_weight,
    noise,
    timesteps,
    qkv_weight,
    out_weight,
    qk_gain,
    block_keys,
    block_count,
):
    role, head = lax.axis_index("role"), lax.axis_index("head")
    chip, core = lax.axis_index("chip"), lax.axis_index("core")
    chips = lax.axis_size("chip")
    local_heads, local_blocks, most = block_keys.shape
    heads = local_heads // chips
    tokens = hidden_rows.shape[0]
    width = hidden_rows.shape[1]
    features = gen_weight.shape[1]
    all_blocks = chips * local_blocks
    swap = [(0, 1), (1, 0)]
    far_swap = [(0, 3), (1, 2), (2, 1), (3, 0)]
    order, turns = nearest(chips)
    turn_here = jnp.asarray(turns, dtype=jnp.int32)[chip]

    def pick(index, options):
        picked = options[0]
        for at in range(1, len(options)):
            picked = jnp.where(index == at, options[at], picked)
        return picked

    def turn_of(other):
        return pick(other, [turn_here[at] for at in range(chips)])

    def exchange(array):
        return lax.all_to_all(array, "chip", split_axis=0, concat_axis=0, tiled=True)

    weight_here = qkv_weight[0]
    depth = weight_here.shape[0]
    wide = 3 * HEAD_DIM
    lists = jnp.concatenate([block_keys, block_count[:, :, None]], axis=2)
    lists = lists.reshape(chips, -1).astype(jnp.bfloat16)
    listed = lists.shape[1]
    spare = -(-listed // (16 * wide)) * 16
    lists = jnp.pad(lists, ((0, 0), (0, spare * wide - listed))).reshape(chips, spare, wide)
    cuts = [
        cut_columns(weight_here, chips, at, lists if at == 0 else None) for at in range(heads)
    ]
    hidden_rows, cuts[0] = lax.optimization_barrier((hidden_rows, cuts[0]))
    weights_own = [exchange(cuts[0])]
    weights_other = []

    mine = role * lax.axis_size("head") + head
    generated = jnp.dot(hidden_rows, gen_weight, preferred_element_type=jnp.float32)
    generated = lax.reduce_precision(generated, 8, 7)
    angle_blocks = (timesteps.astype(jnp.float32) * (math.pi / 2000.0))[:, None, None]
    noise_here = lax.dynamic_slice_in_dim(noise, mine * features, features, axis=1)
    noisy = jnp.cos(angle_blocks) * generated.reshape(local_blocks, BLOCK, features)
    noisy = noisy + jnp.sin(angle_blocks) * noise_here.astype(jnp.float32).reshape(
        local_blocks, BLOCK, features
    )
    squares = jnp.sum(noisy * noisy, axis=-1)
    squares = squares + lax.ppermute(squares, "role", swap)
    squares = squares + lax.ppermute(squares, "head", swap)
    normed = (noisy * lax.rsqrt(squares / width + 1e-06)[:, :, None]).astype(jnp.bfloat16)
    normed = normed.reshape(tokens, features)

    def tables_of(lists):
        lists = lists.reshape(chips, spare * wide)[:, :listed].astype(jnp.int32)
        lists = lists.reshape(chips, heads, local_blocks, most + 1).transpose(1, 0, 2, 3)
        lists = lists.reshape(heads, all_blocks, most + 1)
        owner = lists[:, :, :most] // local_blocks
        turn = turn_of(owner // CORES)
        far = (owner % CORES != core).astype(jnp.int32)
        key_slots = far * all_blocks + turn * local_blocks + lists[:, :, :most] % local_blocks
        counts = lists[:, :, most]
        group_most = jnp.max(counts.reshape(heads, chips, local_blocks), axis=2)
        spot = jnp.arange(all_blocks, dtype=jnp.int32)
        query_slots = turn_of(spot // local_blocks)
        query_slots = query_slots * local_blocks + spot % local_blocks

        return key_slots, counts, query_slots, group_most

    sides = lax.axis_size("head")
    peers = jnp.stack(
        [
            role * sides + head,
            (1 - role) * sides + head,
            role * sides + 1 - head,
            (1 - role) * sides + 1 - head,
        ]
    ).astype(jnp.int32)
    places = jnp.concatenate([peers, core[None].astype(jnp.int32)])
    gains = lax.dynamic_slice_in_dim(qk_gain[0], chip * heads, heads, axis=1)

    chunks = chunk_sizes(heads)
    spans = [slice(sum(chunks[:at]), sum(chunks[: at + 1])) for at in range(len(chunks))]
    parts = [[] for _ in chunks]

    def project(chunk, first, size, begin, some, places):
        at = spans[chunk].start + first
        span = slice(at, at + size)
        query, kv = project_heads(
            places, gains[:, span], some, depth, weights_own[span], weights_other[span]
        )
        here = len(some) * local_blocks
        kv = kv.reshape(size, 2, here, BLOCK, HEAD_DIM)
        kv_other = lax.ppermute(kv, "core", swap)
        query = query.reshape(size, here, BLOCK, HEAD_DIM)
        parts[chunk].append((first, size, begin * local_blocks, here, query, kv, kv_other))
        return lax.optimization_barrier((places, kv))[0]

    half = tokens // 2
    rounds = []
    straight = None
    shard, up, down = normed, normed, normed
    ups, downs = [None], [None]
    for phase in range(chips):
        step = phase + 1
        sent = {}
        sent["role"] = lax.ppermute(shard, "role", swap)
        sent["head"] = lax.ppermute(shard, "head", swap)
        if straight is not None:
            sent["first"] = lax.ppermute(straight[2][:half], "role", swap)
            sent["second"] = lax.ppermute(straight[1][half:], "head", swap)
        if step < chips:
            sent["up"] = lax.ppermute(
                up, "chip", [(at, at + 1) for at in range(step - 1, chips - 1)]
            )
            sent["down"] = lax.ppermute(
                down, "chip", [(at + 1, at) for at in range(chips - step)]
            )
        else:
            sent["far"] = lax.ppermute(shard, ("role", "head"), far_swap)
        if phase == 0:
            sent["weights"] = weights_own.pop()
            sent["cuts"] = cuts[1:]
        if phase == 1:
            sent["weights"] = lax.ppermute(weights_own[0], "core", swap)
            sent["places"] = places
            sent["gains"] = gains
        if step == chips:
            early = list(rounds)
            tables = tables_of(weights_own[0][:, depth:])
            held_places, tables = lax.optimization_barrier((places, tables))
            sent["places"] = project(0, 0, 1, 0, early, held_places)
            if len(weights_own) < heads:
                held, _ = lax.optimization_barrier(
                    (cuts[len(weights_own)], (sent["role"], sent["head"]))
                )
                weights_own.append(exchange(held))
        if step == chips - 1 and len(weights_own) < heads - 1:
            for cut in cuts[len(weights_own) : heads - 1]:
                held, _ = lax.optimization_barrier((cut, (sent["up"], sent["down"])))
                weights_own.append(exchange(held))
        sent, shard = lax.optimization_barrier((sent, shard))
        if phase == 0:
            weights_own.append(sent["weights"])
            cuts[1:] = sent["cuts"]
        if phase == 1:
            weights_other.append(sent["weights"])
            places, gains = sent["places"], sent["gains"]
        if straight is not None:
            rounds.append(straight + (sent["first"], sent["second"]))
        if step == chips:
            held_places = sent["places"]
        straight = (shard, sent["role"], sent["head"])
        if step < chips:
            up, down = sent["up"], sent["down"]
            ups.append(up)
            downs.append(down)
            options = []
            for here in range(chips):
                source = order[here][step - 1]
                options.append(ups[here - source] if source < here else downs[source - here])
            shard = pick(chip, options)
    rounds.append(straight + (sent["far"],))
    for at in range(len(weights_other), heads - 1):
        weights_other.append(lax.ppermute(weights_own[at], "core", swap))

    attended = []
    for chunk, size in enumerate(chunks):
        if chunk == 0:
            for at in range(1, size):
                held_places = project(0, at, 1, 0, early, held_places)
            held_places = project(0, 0, size, len(early), rounds[len(early) :], held_places)
            for at in range(len(weights_other), heads):
                weights_own[at], held_places = lax.optimization_barrier(
                    (weights_own[at], held_places)
                )
                weights_other.append(lax.ppermute(weights_own[at], "core", swap))
        else:
            held_places = project(chunk, 0, size, 0, rounds, held_places)
        mixed = attend(spans[chunk].start, size, *tables, parts[chunk])
        held_places, mixed = lax.optimization_barrier((held_places, mixed))
        mixed = mixed.reshape(chips, size, tokens, HEAD_DIM)
        if attended:
            mixed, attended = lax.optimization_barrier((mixed, attended))
        attended.append(exchange(mixed))

    sign = (2 * role - 1).astype(jnp.int32)[None]
    blocks = sides * lax.axis_size("role")
    which = jnp.stack([peers[3], peers[2], peers[1], peers[0]])
    before = None
    for chunk, size in enumerate(chunks[:-1]):
        before = out_blocks(
            which, sign, attended[chunk], spans[chunk].start // size, out_weight[0], blocks,
            (jnp.float32,), before,
        )[0]
    place = spans[-1].start // chunks[-1]
    (diagonal,) = out_blocks(
        which[:1], sign, attended[-1], place, out_weight[0], blocks, (jnp.bfloat16,), before
    )
    over_head, over_role, own = out_blocks(
        which[1:], sign, attended[-1], place, out_weight[0], blocks,
        (jnp.bfloat16, jnp.bfloat16, jnp.float32), before, 1,
    )
    from_diagonal = lax.ppermute(diagonal, ("role", "head"), far_swap)
    from_head = lax.ppermute(over_head, "head", swap)
    from_role = lax.ppermute(over_role, "role", swap)
    return own + (
        from_role.astype(jnp.float32)
        + from_head.astype(jnp.float32)
        + from_diagonal.astype(jnp.float32)
    )


def splits_heads(mesh, qkv_weight, hidden_rows):
    role, seq, head = (mesh.shape[name] for name in ("role", "seq", "head"))
    if role != 2 or head != 2 or seq % CORES != 0:
        return False
    chips = seq // CORES
    heads = qkv_weight.shape[2] // (3 * HEAD_DIM * head)
    width = hidden_rows.shape[1]
    tokens = hidden_rows.shape[0] // seq
    return (
        heads % chips == 0
        and chips == role * head
        and width % (role * head * 256) == 0
        and width % (seq * 16) == 0
        and tokens % (2 * BLOCK) == 0
        and hidden_rows.shape[0] // BLOCK <= 256
    )


def solution(mesh):
    def call(*arrays):
        if splits_heads(mesh, arrays[4], arrays[0]):
            per_device = per_device_by_heads
            seq = ("chip", "core")
            shape = mesh.devices.shape
            names = mesh.axis_names
            at = names.index("seq")
            layout = Mesh(
                mesh.devices.reshape(shape[:at] + (shape[at] // CORES, CORES) + shape[at + 1 :]),
                names[:at] + seq + names[at + 1 :],
            )
        else:
            per_device = per_device_by_tokens
            seq = "seq"
            layout = mesh
        placed = (
            P(seq, None),
            P(None, ("role", "head")),
            P(seq, None),
            P(seq),
            P("role", seq, "head"),
            P("role", "head", None),
            P("role", None, "head"),
            P("head", seq, None),
            P("head", seq),
        )
        return jax.shard_map(
            per_device,
            mesh=layout,
            in_specs=placed,
            out_specs=P(seq, ("role", "head")),
            check_vma=False,
        )(*arrays)

    return call
```

```python
import math

import jax
import jax.numpy as jnp
from jax import lax
from jax.experimental import pallas as pl
from jax.experimental.pallas import tpu as pltpu
from jax.sharding import Mesh
from jax.sharding import PartitionSpec as P

HEAD_DIM = 128
BLOCK = 64
KMAX = 8
CAP = 2


def rms_rows(values):
    return values * lax.rsqrt(jnp.mean(values * values, axis=-1, keepdims=True) + 1e-06)


def block_attention(queries, key_table, value_table, key_list, key_count):
    picked_keys = key_table[key_list]
    picked_values = value_table[key_list]
    scale = 1.0 / math.sqrt(HEAD_DIM)
    scores = (
        jnp.einsum("nqe,nkbe->nqkb", queries, picked_keys, preferred_element_type=jnp.float32)
        * scale
    )
    live = lax.broadcasted_iota(jnp.int32, (key_list.shape[0], KMAX), 1) < key_count[:, None]
    scores = jnp.where(live[:, None, :, None], scores, -jnp.inf)
    highest = jnp.max(scores, axis=(2, 3), keepdims=True)
    raised = jnp.exp(scores - highest)
    summed = jnp.sum(raised, axis=(2, 3), keepdims=True)
    weights = (raised / summed).astype(jnp.bfloat16)
    mixed = jnp.einsum("nqkb,nkbe->nqe", weights, picked_values, preferred_element_type=jnp.float32)
    return mixed.astype(jnp.bfloat16)


def pick_blocks(table, wanted):
    return table[wanted]


def per_device_by_tokens(
    hidden_rows,
    gen_weight,
    noise,
    timesteps,
    qkv_weight,
    out_weight,
    qk_gain,
    block_keys,
    block_count,
):
    generated = jnp.dot(hidden_rows, gen_weight, preferred_element_type=jnp.float32).astype(
        jnp.bfloat16
    )
    forked = lax.all_gather(generated, ("role", "head"), axis=1, tiled=True)
    row_count = forked.shape[0]
    width = forked.shape[1]
    local_blocks = timesteps.shape[0]
    angle_blocks = (timesteps.astype(jnp.float32) * (math.pi / 2000.0))[:, None, None]
    noisy = jnp.cos(angle_blocks) * forked.astype(jnp.float32).reshape(local_blocks, BLOCK, width)
    noisy = noisy + jnp.sin(angle_blocks) * noise.astype(jnp.float32).reshape(
        local_blocks, BLOCK, width
    )
    normed = rms_rows(noisy).reshape(row_count, width).astype(jnp.bfloat16)
    weight_here = qkv_weight[0]
    projected = jnp.dot(
        normed,
        lax.all_gather(weight_here, "seq", axis=0, tiled=True),
        preferred_element_type=jnp.float32,
    )
    heads_here = projected.shape[1] // (3 * HEAD_DIM)
    head_parts = projected.reshape(row_count, heads_here, 3, HEAD_DIM)
    gain_here = qk_gain[0]
    queries = (rms_rows(head_parts[:, :, 0]) * gain_here[0][None, :, None]).astype(jnp.bfloat16)
    key_local = (rms_rows(head_parts[:, :, 1]) * gain_here[1][None, :, None]).astype(jnp.bfloat16)
    value_local = head_parts[:, :, 2].astype(jnp.bfloat16)
    query_table = queries.reshape(local_blocks, BLOCK, heads_here, HEAD_DIM).transpose(2, 0, 1, 3)
    shard_count = lax.axis_size("seq")
    shard_here = lax.axis_index("seq")
    all_blocks = shard_count * local_blocks
    key_heads = key_local.reshape(local_blocks, BLOCK, heads_here, HEAD_DIM).transpose(2, 0, 1, 3)
    value_heads = value_local.reshape(local_blocks, BLOCK, heads_here, HEAD_DIM).transpose(
        2, 0, 1, 3
    )
    block_ids = lax.broadcasted_iota(jnp.int32, (1, 1, 1, all_blocks), 3)
    matches = block_keys[:, :, :, None] == block_ids
    remote = block_ids // local_blocks != shard_here
    needed = jnp.any(jnp.logical_and(matches, remote), axis=(1, 2))
    needed = needed.reshape(heads_here, shard_count, local_blocks)
    slot_of = jnp.cumsum(needed.astype(jnp.int32), axis=2) - 1
    slot_ids = lax.broadcasted_iota(jnp.int32, (1, 1, 1, CAP), 3)
    within_ids = lax.broadcasted_iota(jnp.int32, (1, 1, local_blocks, 1), 2)
    chosen_slot = jnp.logical_and(needed[..., None], slot_of[..., None] == slot_ids)
    requests = jnp.sum(jnp.where(chosen_slot, within_ids, 0), axis=2)
    asked = lax.all_to_all(
        requests.transpose(1, 0, 2), "seq", split_axis=0, concat_axis=0, tiled=True
    )
    sent_keys = jax.vmap(pick_blocks, in_axes=(0, 1), out_axes=1)(key_heads, asked)
    sent_values = jax.vmap(pick_blocks, in_axes=(0, 1), out_axes=1)(value_heads, asked)
    got_keys, got_values = (
        lax.all_to_all(sent_keys, "seq", split_axis=0, concat_axis=0, tiled=True),
        lax.all_to_all(sent_values, "seq", split_axis=0, concat_axis=0, tiled=True),
    )
    fetched_keys = got_keys.transpose(1, 0, 2, 3, 4).reshape(
        heads_here, shard_count * CAP, BLOCK, HEAD_DIM
    )
    fetched_values = got_values.transpose(1, 0, 2, 3, 4).reshape(
        heads_here, shard_count * CAP, BLOCK, HEAD_DIM
    )
    key_table = jnp.concatenate([key_heads, fetched_keys], axis=1)
    value_table = jnp.concatenate([value_heads, fetched_values], axis=1)
    local_ids = lax.broadcasted_iota(jnp.int32, (1, shard_count, local_blocks), 2)
    owner_grid = lax.broadcasted_iota(jnp.int32, (1, shard_count, local_blocks), 1)
    position = jnp.where(
        owner_grid == shard_here, local_ids, local_blocks + owner_grid * CAP + slot_of
    )
    position = position.reshape(heads_here, all_blocks)
    key_lists = jnp.sum(jnp.where(matches, position[:, None, None, :], 0), axis=3)
    attended = jax.vmap(block_attention)(
        query_table, key_table, value_table, key_lists, block_count
    )
    attended = attended.transpose(1, 2, 0, 3).reshape(row_count, heads_here * HEAD_DIM)
    contribution = jnp.dot(attended, out_weight[0], preferred_element_type=jnp.float32)
    signed = (2.0 * lax.axis_index("role").astype(jnp.float32) - 1.0) * contribution
    return lax.psum_scatter(
        signed.astype(jnp.bfloat16), ("role", "head"), scatter_dimension=1, tiled=True
    ).astype(jnp.float32)


VMEM_BYTES = 56 * 1024 * 1024
CORES = 2


def whole_in_vmem():
    return pl.BlockSpec(memory_space=pltpu.VMEM)


def in_hbm():
    return pl.BlockSpec(memory_space=pl.ANY)


def in_smem():
    return pl.BlockSpec(memory_space=pltpu.SMEM)


def cut_columns(weight, chips, head, extra=None):
    rows, columns = weight.shape
    wide = 3 * HEAD_DIM
    chip_heads = columns // (chips * wide)
    more = 0 if extra is None else extra.shape[1]

    def body(weight_ref, *refs):
        out_ref = refs[-1]
        out_ref[0, :rows] = weight_ref[...]
        if more:
            out_ref[0, rows:] = refs[0][0]

    in_specs = [pl.BlockSpec((rows, wide), lambda chip: (0, chip * chip_heads + head))]
    operands = [weight]
    if more:
        in_specs.append(pl.BlockSpec((1, more, wide), lambda chip: (chip, 0, 0)))
        operands.append(extra)
    return pl.pallas_call(
        body,
        grid=(chips,),
        in_specs=in_specs,
        out_specs=pl.BlockSpec((1, rows + more, wide), lambda chip: (chip, 0, 0)),
        out_shape=jax.ShapeDtypeStruct((chips, rows + more, wide), weight.dtype),
        name="cut_columns",
    )(*operands)


def project_heads(places, gains, rounds, depth, weights_own, weights_other):
    heads = len(weights_own)
    slabs, _, columns = weights_own[0].shape
    tokens, features = rounds[0][0].shape
    pieces = [piece for one in rounds for piece in one]
    turns = len(rounds)
    most = max(len(one) for one in rounds)
    joint = 2 if slabs % 2 == 0 else 1
    dtype = weights_own[0].dtype

    def body(places_ref, gains_ref, *refs):
        own_refs, other_refs = refs[:heads], refs[heads : 2 * heads]
        piece_refs = refs[2 * heads : 2 * heads + len(pieces)]
        query_ref, kv_ref = refs[2 * heads + len(pieces) : 2 * heads + len(pieces) + 2]
        table, rows, weight_sems, row_sems = refs[2 * heads + len(pieces) + 2 :]
        core = places_ref[slabs]
        copies = []
        for slab in range(slabs):
            here = []
            for head in range(heads):
                for side, ref in enumerate((own_refs[head], other_refs[head])):
                    place = core if side == 0 else 1 - core
                    here.append(
                        pltpu.make_async_copy(
                            ref.at[places_ref[slab], pl.ds(0, depth)],
                            table.at[
                                slab // joint,
                                slab % joint,
                                place,
                                :,
                                pl.ds(head * columns, columns),
                            ],
                            weight_sems.at[slab, head, side],
                        )
                    )
            at = 0
            for turn in range(turns):
                first = turn * tokens
                for which in range(len(rounds[turn])):
                    if min(which, slabs - 1) == slab:
                        count = rounds[turn][which].shape[0]
                        here.append(
                            pltpu.make_async_copy(
                                piece_refs[at],
                                rows.at[
                                    slab // joint,
                                    pl.ds(first, count),
                                    pl.ds(slab % joint * features, features),
                                ],
                                row_sems.at[which, turn],
                            )
                        )
                        first += count
                    at += 1
            for copy in here:
                copy.start()
            copies.append(here)
        total = None
        for group in range(slabs // joint):
            for slab in range(group * joint, (group + 1) * joint):
                for copy in copies[slab]:
                    copy.wait()
            part = jnp.dot(
                rows[group],
                table[group].reshape(joint * CORES * depth, heads * columns),
                preferred_element_type=jnp.float32,
            )
            total = part if total is None else total + part
        for turn in range(turns):
            here = total[turn * tokens : (turn + 1) * tokens]
            for head in range(heads):
                at = head * columns
                for which in range(2):
                    block = here[:, at + which * HEAD_DIM : at + (which + 1) * HEAD_DIM]
                    normal = (rms_rows(block) * gains_ref[which, head]).astype(dtype)
                    if which == 0:
                        query_ref[head, turn] = normal
                    else:
                        kv_ref[head, 0, turn] = normal
                block = here[:, at + 2 * HEAD_DIM : at + 3 * HEAD_DIM]
                kv_ref[head, 1, turn] = block.astype(dtype)

    return pl.pallas_call(
        body,
        in_specs=[in_smem(), in_smem()] + [in_hbm()] * (2 * heads + len(pieces)),
        out_specs=(whole_in_vmem(), whole_in_vmem()),
        out_shape=(
            jax.ShapeDtypeStruct((heads, turns, tokens, HEAD_DIM), dtype),
            jax.ShapeDtypeStruct((heads, 2, turns, tokens, HEAD_DIM), dtype),
        ),
        scratch_shapes=[
            pltpu.VMEM((slabs // joint, joint, CORES, depth, heads * columns), dtype),
            pltpu.VMEM((slabs // joint, turns * tokens, joint * features), dtype),
            pltpu.SemaphoreType.DMA((slabs, heads, 2)),
            pltpu.SemaphoreType.DMA((most, turns)),
        ],
        compiler_params=pltpu.CompilerParams(vmem_limit_bytes=VMEM_BYTES),
        name="project_heads",
    )(places, gains, *weights_own, *weights_other, *pieces)


def attend(first_head, heads, key_slots, counts, query_slots, group_most, parts):
    _, blocks, most = key_slots.shape
    groups = group_most.shape[1]
    together = blocks // groups
    scale = 1.0 / math.sqrt(HEAD_DIM)
    dtype = parts[0][4].dtype
    arrays = [array for part in parts for array in part[4:]]

    def body(slots_ref, counts_ref, from_ref, most_ref, *refs):
        out_ref, query_table, table, sems = refs[len(arrays) :]
        copies = []
        for at, (head, size, block, span, _, _, _) in enumerate(parts):
            query_part, own_part, other_part = refs[3 * at : 3 * at + 3]
            rows = pl.ds(head, size)
            copies.append(
                pltpu.make_async_copy(
                    query_part, query_table.at[rows, pl.ds(block, span)], sems.at[at, 0]
                )
            )
            for side, ref in enumerate((own_part, other_part)):
                place = pl.ds(side * blocks + block, span)
                copies.append(
                    pltpu.make_async_copy(ref, table.at[rows, :, place], sems.at[at, 1 + side])
                )
        for copy in copies:
            copy.start()
        for copy in copies:
            copy.wait()

        def run(head, group, listed, batch):
            for first in range(0, together, batch):
                spots = [group * together + at for at in range(first, min(first + batch, together))]
                slots = [[slots_ref[first_head + head, at, entry] for entry in range(listed)] for at in spots]
                scores = []
                for at, listing in zip(spots, slots):
                    keys = jnp.concatenate([table[head, 0, slot] for slot in listing], axis=0)
                    scores.append(
                        lax.dot_general(
                            query_table[head, from_ref[at]],
                            keys,
                            (((1,), (1,)), ((), ())),
                            preferred_element_type=jnp.float32,
                        )
                    )
                column = lax.broadcasted_iota(jnp.int32, (1, listed * BLOCK), 1)
                scores = [
                    jnp.where(column < counts_ref[first_head + head, at] * BLOCK, one * scale, -jnp.inf)
                    for at, one in zip(spots, scores)
                ]
                highest = [jnp.max(one, axis=1, keepdims=True) for one in scores]
                raised = [jnp.exp(one - top) for one, top in zip(scores, highest)]
                inverse = [1.0 / jnp.sum(one, axis=1, keepdims=True) for one in raised]
                weights = [(one * by).astype(dtype) for one, by in zip(raised, inverse)]
                mixed = []
                for one, listing in zip(weights, slots):
                    values = jnp.concatenate([table[head, 1, slot] for slot in listing], axis=0)
                    mixed.append(jnp.dot(one, values, preferred_element_type=jnp.float32))
                for at, one in enumerate(mixed):
                    out_ref[group, head, first + at] = one.astype(dtype)

        def step(at, carry):
            head, group = at // groups, at % groups
            few = most_ref[first_head + head, group] <= most // 2

            @pl.when(few)
            def _():
                run(head, group, most // 2, 6)

            @pl.when(jnp.logical_not(few))
            def _():
                run(head, group, most, 3)

            return carry

        lax.fori_loop(0, heads * groups, step, 0)

    return pl.pallas_call(
        body,
        in_specs=[in_smem()] * 4 + [in_hbm()] * len(arrays),
        out_specs=whole_in_vmem(),
        out_shape=jax.ShapeDtypeStruct((groups, heads, together, BLOCK, HEAD_DIM), dtype),
        scratch_shapes=[
            pltpu.VMEM((heads, blocks, BLOCK, HEAD_DIM), dtype),
            pltpu.VMEM((heads, 2, CORES * blocks, BLOCK, HEAD_DIM), dtype),
            pltpu.SemaphoreType.DMA((len(parts), 3)),
        ],
        compiler_params=pltpu.CompilerParams(vmem_limit_bytes=VMEM_BYTES),
        name="attend",
    )(key_slots, counts, query_slots, group_most, *arrays)


def out_blocks(which, sign, attended, place, out_weight, blocks, dtypes, before=None, skip=0):
    groups, heads, tokens, _ = attended.shape
    depth, features = out_weight.shape
    width = features // blocks
    wanted = which.shape[0]
    rows = heads * HEAD_DIM
    weight = out_weight.reshape(groups, depth // groups, features)
    stacked = len(dtypes) == 1 and wanted > 1

    def body(which_ref, sign_ref, mixed_ref, weight_ref, *refs):
        out_refs = refs if before is None else refs[1:]
        joined = jnp.concatenate(
            [mixed_ref[group, head] for group in range(groups) for head in range(heads)], axis=1
        )
        total = jnp.dot(
            joined,
            weight_ref[...].reshape(groups * rows, width),
            preferred_element_type=jnp.float32,
        )
        total = total * sign_ref[0].astype(jnp.float32)
        if before is not None:
            total = total + refs[0][0]
        if stacked:
            out_refs[0][0] = total.astype(dtypes[0])
        else:
            for at in range(wanted):

                @pl.when(pl.program_id(0) == at)
                def _(at=at):
                    out_refs[at][...] = total.astype(dtypes[at])

    in_specs = [
        pl.BlockSpec(attended.shape, lambda i, w, s: (0, 0, 0, 0)),
        pl.BlockSpec((groups, rows, width), lambda i, w, s: (0, place, w[i])),
    ]
    operands = [attended, weight]
    if before is not None:
        in_specs.append(pl.BlockSpec((1, tokens, width), lambda i, w, s: (i + skip, 0, 0)))
        operands.append(before)
    if stacked:
        out_specs = [pl.BlockSpec((1, tokens, width), lambda i, w, s: (i, 0, 0))]
        out_shape = [jax.ShapeDtypeStruct((wanted, tokens, width), dtypes[0])]
    else:
        out_specs = [pl.BlockSpec((tokens, width), lambda i, w, s: (0, 0))] * wanted
        out_shape = [jax.ShapeDtypeStruct((tokens, width), dtype) for dtype in dtypes]
    return pl.pallas_call(
        body,
        grid_spec=pltpu.PrefetchScalarGridSpec(
            num_scalar_prefetch=2, grid=(wanted,), in_specs=in_specs, out_specs=out_specs
        ),
        out_shape=out_shape,
        compiler_params=pltpu.CompilerParams(vmem_limit_bytes=VMEM_BYTES),
        name="out_blocks",
    )(which, sign, *operands)


def chunk_sizes(heads):
    last = heads // 3 if heads % 3 == 0 else 1
    return [heads - last, last] if heads > last else [heads]


def per_device_by_heads(
    hidden_rows,
    gen_weight,
    noise,
    timesteps,
    qkv_weight,
    out_weight,
    qk_gain,
    block_keys,
    block_count,
):
    role, head = lax.axis_index("role"), lax.axis_index("head")
    chip, core = lax.axis_index("chip"), lax.axis_index("core")
    chips = lax.axis_size("chip")
    local_heads, local_blocks, most = block_keys.shape
    heads = local_heads // chips
    tokens = hidden_rows.shape[0]
    width = hidden_rows.shape[1]
    features = gen_weight.shape[1]
    all_blocks = chips * local_blocks
    swap = [(0, 1), (1, 0)]
    far_swap = [(0, 3), (1, 2), (2, 1), (3, 0)]
    ring = [(at, (at + 1) % chips) for at in range(chips)]

    def turn_of(other):
        return (chip - other) % chips

    def exchange(array):
        return lax.all_to_all(array, "chip", split_axis=0, concat_axis=0, tiled=True)

    weight_here = qkv_weight[0]
    depth = weight_here.shape[0]
    wide = 3 * HEAD_DIM
    lists = jnp.concatenate([block_keys, block_count[:, :, None]], axis=2)
    lists = lists.reshape(chips, -1).astype(jnp.bfloat16)
    listed = lists.shape[1]
    spare = -(-listed // (16 * wide)) * 16
    lists = jnp.pad(lists, ((0, 0), (0, spare * wide - listed))).reshape(chips, spare, wide)
    cuts = [
        cut_columns(weight_here, chips, at, lists if at == 0 else None) for at in range(heads)
    ]
    hidden_rows, cuts[0] = lax.optimization_barrier((hidden_rows, cuts[0]))
    weights_own = [exchange(cuts[0])]
    weights_other = []

    mine = role * lax.axis_size("head") + head
    generated = jnp.dot(hidden_rows, gen_weight, preferred_element_type=jnp.float32)
    generated = lax.reduce_precision(generated, 8, 7)
    angle_blocks = (timesteps.astype(jnp.float32) * (math.pi / 2000.0))[:, None, None]
    noise_here = lax.dynamic_slice_in_dim(noise, mine * features, features, axis=1)
    noisy = jnp.cos(angle_blocks) * generated.reshape(local_blocks, BLOCK, features)
    noisy = noisy + jnp.sin(angle_blocks) * noise_here.astype(jnp.float32).reshape(
        local_blocks, BLOCK, features
    )
    squares = jnp.sum(noisy * noisy, axis=-1)
    squares = squares + lax.ppermute(squares, "role", swap)
    squares = squares + lax.ppermute(squares, "head", swap)
    normed = (noisy * lax.rsqrt(squares / width + 1e-06)[:, :, None]).astype(jnp.bfloat16)
    normed = normed.reshape(tokens, features)

    def tables_of(lists):
        lists = lists.reshape(chips, spare * wide)[:, :listed].astype(jnp.int32)
        lists = lists.reshape(chips, heads, local_blocks, most + 1).transpose(1, 0, 2, 3)
        lists = lists.reshape(heads, all_blocks, most + 1)
        owner = lists[:, :, :most] // local_blocks
        turn = turn_of(owner // CORES)
        far = (owner % CORES != core).astype(jnp.int32)
        key_slots = far * all_blocks + turn * local_blocks + lists[:, :, :most] % local_blocks
        counts = lists[:, :, most]
        group_most = jnp.max(counts.reshape(heads, chips, local_blocks), axis=2)
        spot = jnp.arange(all_blocks, dtype=jnp.int32)
        query_slots = turn_of(spot // local_blocks)
        query_slots = query_slots * local_blocks + spot % local_blocks

        return key_slots, counts, query_slots, group_most

    sides = lax.axis_size("head")
    peers = jnp.stack(
        [
            role * sides + head,
            (1 - role) * sides + head,
            role * sides + 1 - head,
            (1 - role) * sides + 1 - head,
        ]
    ).astype(jnp.int32)
    places = jnp.concatenate([peers, core[None].astype(jnp.int32)])
    gains = lax.dynamic_slice_in_dim(qk_gain[0], chip * heads, heads, axis=1)

    chunks = chunk_sizes(heads)
    spans = [slice(sum(chunks[:at]), sum(chunks[: at + 1])) for at in range(len(chunks))]
    parts = [[] for _ in chunks]

    def project(chunk, first, size, begin, some, places):
        at = spans[chunk].start + first
        span = slice(at, at + size)
        query, kv = project_heads(
            places, gains[:, span], some, depth, weights_own[span], weights_other[span]
        )
        here = len(some) * local_blocks
        kv = kv.reshape(size, 2, here, BLOCK, HEAD_DIM)
        kv_other = lax.ppermute(kv, "core", swap)
        query = query.reshape(size, here, BLOCK, HEAD_DIM)
        parts[chunk].append((first, size, begin * local_blocks, here, query, kv, kv_other))
        return lax.optimization_barrier((places, kv))[0]

    half = tokens // 2
    rounds = []
    straight = None
    shard = normed
    for phase in range(chips + 1):
        step = phase + 1
        sent = {}
        if phase < chips:
            sent["role"] = lax.ppermute(shard, "role", swap)
            sent["head"] = lax.ppermute(shard, "head", swap)
        if straight is not None:
            sent["first"] = lax.ppermute(straight[2][:half], "role", swap)
            sent["second"] = lax.ppermute(straight[1][half:], "head", swap)
        if step < chips:
            sent["next"] = lax.ppermute(shard, "chip", ring)
        if phase == 0:
            sent["weights"] = weights_own.pop()
            sent["cuts"] = cuts[1:]
        if phase == 1:
            sent["places"] = places
            sent["gains"] = gains
        if step == chips:
            weights_other.append(lax.ppermute(weights_own[0], "core", swap))
            early = list(rounds)
            tables = tables_of(weights_own[0][:, depth:])
            held_places, tables = lax.optimization_barrier((places, tables))
            sent["places"] = project(0, 0, 1, 0, early, held_places)
        sent, shard = lax.optimization_barrier((sent, shard))
        if phase == 0:
            weights_own.append(sent["weights"])
            cuts[1:] = sent["cuts"]
        if phase == 1:
            places, gains = sent["places"], sent["gains"]
        if straight is not None:
            rounds.append(straight + (sent["first"], sent["second"]))
        if step == chips:
            held_places = sent["places"]
        if phase < chips:
            straight = (shard, sent["role"], sent["head"])
        if step < chips:
            shard = sent["next"]
        if chips - 2 <= phase and len(weights_own) < heads:
            held, _ = lax.optimization_barrier((cuts[len(weights_own)], sent))
            weights_own.append(exchange(held))
    for at in range(len(weights_other), heads - 1):
        weights_other.append(lax.ppermute(weights_own[at], "core", swap))

    attended = []
    for chunk, size in enumerate(chunks):
        if chunk == 0:
            for at in range(1, size):
                held_places = project(0, at, 1, 0, early, held_places)
            held_places = project(0, 0, size, len(early), rounds[len(early) :], held_places)
            for at in range(len(weights_other), heads):
                weights_own[at], held_places = lax.optimization_barrier(
                    (weights_own[at], held_places)
                )
                weights_other.append(lax.ppermute(weights_own[at], "core", swap))
        else:
            held_places = project(chunk, 0, size, 0, rounds, held_places)
        mixed = attend(spans[chunk].start, size, *tables, parts[chunk])
        held_places, mixed = lax.optimization_barrier((held_places, mixed))
        mixed = mixed.reshape(chips, size, tokens, HEAD_DIM)
        if attended:
            mixed, attended = lax.optimization_barrier((mixed, attended))
        attended.append(exchange(mixed))

    sign = (2 * role - 1).astype(jnp.int32)[None]
    blocks = sides * lax.axis_size("role")
    which = jnp.stack([peers[3], peers[2], peers[1], peers[0]])
    before = None
    for chunk, size in enumerate(chunks[:-1]):
        before = out_blocks(
            which, sign, attended[chunk], spans[chunk].start // size, out_weight[0], blocks,
            (jnp.float32,), before,
        )[0]
    place = spans[-1].start // chunks[-1]
    (diagonal,) = out_blocks(
        which[:1], sign, attended[-1], place, out_weight[0], blocks, (jnp.bfloat16,), before
    )
    over_head, over_role, own = out_blocks(
        which[1:], sign, attended[-1], place, out_weight[0], blocks,
        (jnp.bfloat16, jnp.bfloat16, jnp.float32), before, 1,
    )
    from_diagonal = lax.ppermute(diagonal, ("role", "head"), far_swap)
    from_head = lax.ppermute(over_head, "head", swap)
    from_role = lax.ppermute(over_role, "role", swap)
    return own + (
        from_role.astype(jnp.float32)
        + from_head.astype(jnp.float32)
        + from_diagonal.astype(jnp.float32)
    )


def splits_heads(mesh, qkv_weight, hidden_rows):
    role, seq, head = (mesh.shape[name] for name in ("role", "seq", "head"))
    if role != 2 or head != 2 or seq % CORES != 0:
        return False
    chips = seq // CORES
    heads = qkv_weight.shape[2] // (3 * HEAD_DIM * head)
    width = hidden_rows.shape[1]
    tokens = hidden_rows.shape[0] // seq
    return (
        heads % chips == 0
        and chips == role * head
        and width % (role * head * 256) == 0
        and width % (seq * 16) == 0
        and tokens % (2 * BLOCK) == 0
        and hidden_rows.shape[0] // BLOCK <= 256
    )


def solution(mesh):
    def call(*arrays):
        if splits_heads(mesh, arrays[4], arrays[0]):
            per_device = per_device_by_heads
            seq = ("chip", "core")
            shape = mesh.devices.shape
            names = mesh.axis_names
            at = names.index("seq")
            layout = Mesh(
                mesh.devices.reshape(shape[:at] + (shape[at] // CORES, CORES) + shape[at + 1 :]),
                names[:at] + seq + names[at + 1 :],
            )
        else:
            per_device = per_device_by_tokens
            seq = "seq"
            layout = mesh
        placed = (
            P(seq, None),
            P(None, ("role", "head")),
            P(seq, None),
            P(seq),
            P("role", seq, "head"),
            P("role", "head", None),
            P("role", None, "head"),
            P("head", seq, None),
            P("head", seq),
        )
        return jax.shard_map(
            per_device,
            mesh=layout,
            in_specs=placed,
            out_specs=P(seq, ("role", "head")),
            check_vma=False,
        )(*arrays)

    return call
```

```python
import math

import jax
import jax.numpy as jnp
from jax import lax
from jax.experimental import pallas as pl
from jax.experimental.pallas import tpu as pltpu
from jax.sharding import Mesh
from jax.sharding import PartitionSpec as P

HEAD_DIM = 128
BLOCK = 64
KMAX = 8
CAP = 2


def rms_rows(values):
    return values * lax.rsqrt(jnp.mean(values * values, axis=-1, keepdims=True) + 1e-06)


def block_attention(queries, key_table, value_table, key_list, key_count):
    picked_keys = key_table[key_list]
    picked_values = value_table[key_list]
    scale = 1.0 / math.sqrt(HEAD_DIM)
    scores = (
        jnp.einsum("nqe,nkbe->nqkb", queries, picked_keys, preferred_element_type=jnp.float32)
        * scale
    )
    live = lax.broadcasted_iota(jnp.int32, (key_list.shape[0], KMAX), 1) < key_count[:, None]
    scores = jnp.where(live[:, None, :, None], scores, -jnp.inf)
    highest = jnp.max(scores, axis=(2, 3), keepdims=True)
    raised = jnp.exp(scores - highest)
    summed = jnp.sum(raised, axis=(2, 3), keepdims=True)
    weights = (raised / summed).astype(jnp.bfloat16)
    mixed = jnp.einsum("nqkb,nkbe->nqe", weights, picked_values, preferred_element_type=jnp.float32)
    return mixed.astype(jnp.bfloat16)


def pick_blocks(table, wanted):
    return table[wanted]


def per_device_by_tokens(
    hidden_rows,
    gen_weight,
    noise,
    timesteps,
    qkv_weight,
    out_weight,
    qk_gain,
    block_keys,
    block_count,
):
    generated = jnp.dot(hidden_rows, gen_weight, preferred_element_type=jnp.float32).astype(
        jnp.bfloat16
    )
    forked = lax.all_gather(generated, ("role", "head"), axis=1, tiled=True)
    row_count = forked.shape[0]
    width = forked.shape[1]
    local_blocks = timesteps.shape[0]
    angle_blocks = (timesteps.astype(jnp.float32) * (math.pi / 2000.0))[:, None, None]
    noisy = jnp.cos(angle_blocks) * forked.astype(jnp.float32).reshape(local_blocks, BLOCK, width)
    noisy = noisy + jnp.sin(angle_blocks) * noise.astype(jnp.float32).reshape(
        local_blocks, BLOCK, width
    )
    normed = rms_rows(noisy).reshape(row_count, width).astype(jnp.bfloat16)
    weight_here = qkv_weight[0]
    projected = jnp.dot(
        normed,
        lax.all_gather(weight_here, "seq", axis=0, tiled=True),
        preferred_element_type=jnp.float32,
    )
    heads_here = projected.shape[1] // (3 * HEAD_DIM)
    head_parts = projected.reshape(row_count, heads_here, 3, HEAD_DIM)
    gain_here = qk_gain[0]
    queries = (rms_rows(head_parts[:, :, 0]) * gain_here[0][None, :, None]).astype(jnp.bfloat16)
    key_local = (rms_rows(head_parts[:, :, 1]) * gain_here[1][None, :, None]).astype(jnp.bfloat16)
    value_local = head_parts[:, :, 2].astype(jnp.bfloat16)
    query_table = queries.reshape(local_blocks, BLOCK, heads_here, HEAD_DIM).transpose(2, 0, 1, 3)
    shard_count = lax.axis_size("seq")
    shard_here = lax.axis_index("seq")
    all_blocks = shard_count * local_blocks
    key_heads = key_local.reshape(local_blocks, BLOCK, heads_here, HEAD_DIM).transpose(2, 0, 1, 3)
    value_heads = value_local.reshape(local_blocks, BLOCK, heads_here, HEAD_DIM).transpose(
        2, 0, 1, 3
    )
    block_ids = lax.broadcasted_iota(jnp.int32, (1, 1, 1, all_blocks), 3)
    matches = block_keys[:, :, :, None] == block_ids
    remote = block_ids // local_blocks != shard_here
    needed = jnp.any(jnp.logical_and(matches, remote), axis=(1, 2))
    needed = needed.reshape(heads_here, shard_count, local_blocks)
    slot_of = jnp.cumsum(needed.astype(jnp.int32), axis=2) - 1
    slot_ids = lax.broadcasted_iota(jnp.int32, (1, 1, 1, CAP), 3)
    within_ids = lax.broadcasted_iota(jnp.int32, (1, 1, local_blocks, 1), 2)
    chosen_slot = jnp.logical_and(needed[..., None], slot_of[..., None] == slot_ids)
    requests = jnp.sum(jnp.where(chosen_slot, within_ids, 0), axis=2)
    asked = lax.all_to_all(
        requests.transpose(1, 0, 2), "seq", split_axis=0, concat_axis=0, tiled=True
    )
    sent_keys = jax.vmap(pick_blocks, in_axes=(0, 1), out_axes=1)(key_heads, asked)
    sent_values = jax.vmap(pick_blocks, in_axes=(0, 1), out_axes=1)(value_heads, asked)
    got_keys, got_values = (
        lax.all_to_all(sent_keys, "seq", split_axis=0, concat_axis=0, tiled=True),
        lax.all_to_all(sent_values, "seq", split_axis=0, concat_axis=0, tiled=True),
    )
    fetched_keys = got_keys.transpose(1, 0, 2, 3, 4).reshape(
        heads_here, shard_count * CAP, BLOCK, HEAD_DIM
    )
    fetched_values = got_values.transpose(1, 0, 2, 3, 4).reshape(
        heads_here, shard_count * CAP, BLOCK, HEAD_DIM
    )
    key_table = jnp.concatenate([key_heads, fetched_keys], axis=1)
    value_table = jnp.concatenate([value_heads, fetched_values], axis=1)
    local_ids = lax.broadcasted_iota(jnp.int32, (1, shard_count, local_blocks), 2)
    owner_grid = lax.broadcasted_iota(jnp.int32, (1, shard_count, local_blocks), 1)
    position = jnp.where(
        owner_grid == shard_here, local_ids, local_blocks + owner_grid * CAP + slot_of
    )
    position = position.reshape(heads_here, all_blocks)
    key_lists = jnp.sum(jnp.where(matches, position[:, None, None, :], 0), axis=3)
    attended = jax.vmap(block_attention)(
        query_table, key_table, value_table, key_lists, block_count
    )
    attended = attended.transpose(1, 2, 0, 3).reshape(row_count, heads_here * HEAD_DIM)
    contribution = jnp.dot(attended, out_weight[0], preferred_element_type=jnp.float32)
    signed = (2.0 * lax.axis_index("role").astype(jnp.float32) - 1.0) * contribution
    return lax.psum_scatter(
        signed.astype(jnp.bfloat16), ("role", "head"), scatter_dimension=1, tiled=True
    ).astype(jnp.float32)


VMEM_BYTES = 56 * 1024 * 1024
CORES = 2


def whole_in_vmem():
    return pl.BlockSpec(memory_space=pltpu.VMEM)


def in_hbm():
    return pl.BlockSpec(memory_space=pl.ANY)


def in_smem():
    return pl.BlockSpec(memory_space=pltpu.SMEM)


def cut_columns(weight, chips, head, extra=None):
    rows, columns = weight.shape
    wide = 3 * HEAD_DIM
    chip_heads = columns // (chips * wide)
    more = 0 if extra is None else extra.shape[1]

    def body(weight_ref, *refs):
        out_ref = refs[-1]
        out_ref[0, :rows] = weight_ref[...]
        if more:
            out_ref[0, rows:] = refs[0][0]

    in_specs = [pl.BlockSpec((rows, wide), lambda chip: (0, chip * chip_heads + head))]
    operands = [weight]
    if more:
        in_specs.append(pl.BlockSpec((1, more, wide), lambda chip: (chip, 0, 0)))
        operands.append(extra)
    return pl.pallas_call(
        body,
        grid=(chips,),
        in_specs=in_specs,
        out_specs=pl.BlockSpec((1, rows + more, wide), lambda chip: (chip, 0, 0)),
        out_shape=jax.ShapeDtypeStruct((chips, rows + more, wide), weight.dtype),
        name="cut_columns",
    )(*operands)


def project_heads(places, gains, rounds, depth, weights_own, weights_other):
    heads = len(weights_own)
    slabs, _, columns = weights_own[0].shape
    tokens, features = rounds[0][0].shape
    pieces = [piece for one in rounds for piece in one]
    turns = len(rounds)
    most = max(len(one) for one in rounds)
    joint = 2 if slabs % 2 == 0 else 1
    dtype = weights_own[0].dtype

    def body(places_ref, gains_ref, *refs):
        own_refs, other_refs = refs[:heads], refs[heads : 2 * heads]
        piece_refs = refs[2 * heads : 2 * heads + len(pieces)]
        query_ref, kv_ref = refs[2 * heads + len(pieces) : 2 * heads + len(pieces) + 2]
        table, rows, weight_sems, row_sems = refs[2 * heads + len(pieces) + 2 :]
        core = places_ref[slabs]
        copies = []
        for slab in range(slabs):
            here = []
            for head in range(heads):
                for side, ref in enumerate((own_refs[head], other_refs[head])):
                    place = core if side == 0 else 1 - core
                    here.append(
                        pltpu.make_async_copy(
                            ref.at[places_ref[slab], pl.ds(0, depth)],
                            table.at[
                                slab // joint,
                                slab % joint,
                                place,
                                :,
                                pl.ds(head * columns, columns),
                            ],
                            weight_sems.at[slab, head, side],
                        )
                    )
            at = 0
            for turn in range(turns):
                first = turn * tokens
                for which in range(len(rounds[turn])):
                    if min(which, slabs - 1) == slab:
                        count = rounds[turn][which].shape[0]
                        here.append(
                            pltpu.make_async_copy(
                                piece_refs[at],
                                rows.at[
                                    slab // joint,
                                    pl.ds(first, count),
                                    pl.ds(slab % joint * features, features),
                                ],
                                row_sems.at[which, turn],
                            )
                        )
                        first += count
                    at += 1
            for copy in here:
                copy.start()
            copies.append(here)
        total = None
        for group in range(slabs // joint):
            for slab in range(group * joint, (group + 1) * joint):
                for copy in copies[slab]:
                    copy.wait()
            part = jnp.dot(
                rows[group],
                table[group].reshape(joint * CORES * depth, heads * columns),
                preferred_element_type=jnp.float32,
            )
            total = part if total is None else total + part
        for turn in range(turns):
            here = total[turn * tokens : (turn + 1) * tokens]
            for head in range(heads):
                at = head * columns
                for which in range(2):
                    block = here[:, at + which * HEAD_DIM : at + (which + 1) * HEAD_DIM]
                    normal = (rms_rows(block) * gains_ref[which, head]).astype(dtype)
                    if which == 0:
                        query_ref[head, turn] = normal
                    else:
                        kv_ref[head, 0, turn] = normal
                block = here[:, at + 2 * HEAD_DIM : at + 3 * HEAD_DIM]
                kv_ref[head, 1, turn] = block.astype(dtype)

    return pl.pallas_call(
        body,
        in_specs=[in_smem(), in_smem()] + [in_hbm()] * (2 * heads + len(pieces)),
        out_specs=(whole_in_vmem(), whole_in_vmem()),
        out_shape=(
            jax.ShapeDtypeStruct((heads, turns, tokens, HEAD_DIM), dtype),
            jax.ShapeDtypeStruct((heads, 2, turns, tokens, HEAD_DIM), dtype),
        ),
        scratch_shapes=[
            pltpu.VMEM((slabs // joint, joint, CORES, depth, heads * columns), dtype),
            pltpu.VMEM((slabs // joint, turns * tokens, joint * features), dtype),
            pltpu.SemaphoreType.DMA((slabs, heads, 2)),
            pltpu.SemaphoreType.DMA((most, turns)),
        ],
        compiler_params=pltpu.CompilerParams(vmem_limit_bytes=VMEM_BYTES),
        name="project_heads",
    )(places, gains, *weights_own, *weights_other, *pieces)


def attend(first_head, heads, key_slots, counts, query_slots, group_most, parts):
    _, blocks, most = key_slots.shape
    groups = group_most.shape[1]
    together = blocks // groups
    scale = 1.0 / math.sqrt(HEAD_DIM)
    dtype = parts[0][4].dtype
    arrays = [array for part in parts for array in part[4:]]

    def body(slots_ref, counts_ref, from_ref, most_ref, *refs):
        out_ref, query_table, table, sems = refs[len(arrays) :]
        copies = []
        for at, (head, size, block, span, _, _, _) in enumerate(parts):
            query_part, own_part, other_part = refs[3 * at : 3 * at + 3]
            rows = pl.ds(head, size)
            copies.append(
                pltpu.make_async_copy(
                    query_part, query_table.at[rows, pl.ds(block, span)], sems.at[at, 0]
                )
            )
            for side, ref in enumerate((own_part, other_part)):
                place = pl.ds(side * blocks + block, span)
                copies.append(
                    pltpu.make_async_copy(ref, table.at[rows, :, place], sems.at[at, 1 + side])
                )
        for copy in copies:
            copy.start()
        for copy in copies:
            copy.wait()

        def run(head, group, listed, batch):
            for first in range(0, together, batch):
                spots = [group * together + at for at in range(first, min(first + batch, together))]
                slots = [[slots_ref[first_head + head, at, entry] for entry in range(listed)] for at in spots]
                scores = []
                for at, listing in zip(spots, slots):
                    keys = jnp.concatenate([table[head, 0, slot] for slot in listing], axis=0)
                    scores.append(
                        lax.dot_general(
                            query_table[head, from_ref[at]],
                            keys,
                            (((1,), (1,)), ((), ())),
                            preferred_element_type=jnp.float32,
                        )
                    )
                column = lax.broadcasted_iota(jnp.int32, (1, listed * BLOCK), 1)
                scores = [
                    jnp.where(column < counts_ref[first_head + head, at] * BLOCK, one * scale, -jnp.inf)
                    for at, one in zip(spots, scores)
                ]
                highest = [jnp.max(one, axis=1, keepdims=True) for one in scores]
                raised = [jnp.exp(one - top) for one, top in zip(scores, highest)]
                inverse = [1.0 / jnp.sum(one, axis=1, keepdims=True) for one in raised]
                weights = [(one * by).astype(dtype) for one, by in zip(raised, inverse)]
                mixed = []
                for one, listing in zip(weights, slots):
                    values = jnp.concatenate([table[head, 1, slot] for slot in listing], axis=0)
                    mixed.append(jnp.dot(one, values, preferred_element_type=jnp.float32))
                for at, one in enumerate(mixed):
                    out_ref[group, head, first + at] = one.astype(dtype)

        def step(at, carry):
            head, group = at // groups, at % groups
            few = most_ref[first_head + head, group] <= most // 2

            @pl.when(few)
            def _():
                run(head, group, most // 2, 6)

            @pl.when(jnp.logical_not(few))
            def _():
                run(head, group, most, 3)

            return carry

        lax.fori_loop(0, heads * groups, step, 0)

    return pl.pallas_call(
        body,
        in_specs=[in_smem()] * 4 + [in_hbm()] * len(arrays),
        out_specs=whole_in_vmem(),
        out_shape=jax.ShapeDtypeStruct((groups, heads, together, BLOCK, HEAD_DIM), dtype),
        scratch_shapes=[
            pltpu.VMEM((heads, blocks, BLOCK, HEAD_DIM), dtype),
            pltpu.VMEM((heads, 2, CORES * blocks, BLOCK, HEAD_DIM), dtype),
            pltpu.SemaphoreType.DMA((len(parts), 3)),
        ],
        compiler_params=pltpu.CompilerParams(vmem_limit_bytes=VMEM_BYTES),
        name="attend",
    )(key_slots, counts, query_slots, group_most, *arrays)


def out_blocks(which, sign, attended, place, out_weight, blocks, dtypes, before=None, skip=0):
    groups, heads, tokens, _ = attended.shape
    depth, features = out_weight.shape
    width = features // blocks
    wanted = which.shape[0]
    rows = heads * HEAD_DIM
    weight = out_weight.reshape(groups, depth // groups, features)
    stacked = len(dtypes) == 1 and wanted > 1

    def body(which_ref, sign_ref, mixed_ref, weight_ref, *refs):
        out_refs = refs if before is None else refs[1:]
        joined = jnp.concatenate(
            [mixed_ref[group, head] for group in range(groups) for head in range(heads)], axis=1
        )
        total = jnp.dot(
            joined,
            weight_ref[...].reshape(groups * rows, width),
            preferred_element_type=jnp.float32,
        )
        total = total * sign_ref[0].astype(jnp.float32)
        if before is not None:
            total = total + refs[0][0]
        if stacked:
            out_refs[0][0] = total.astype(dtypes[0])
        else:
            for at in range(wanted):

                @pl.when(pl.program_id(0) == at)
                def _(at=at):
                    out_refs[at][...] = total.astype(dtypes[at])

    in_specs = [
        pl.BlockSpec(attended.shape, lambda i, w, s: (0, 0, 0, 0)),
        pl.BlockSpec((groups, rows, width), lambda i, w, s: (0, place, w[i])),
    ]
    operands = [attended, weight]
    if before is not None:
        in_specs.append(pl.BlockSpec((1, tokens, width), lambda i, w, s: (i + skip, 0, 0)))
        operands.append(before)
    if stacked:
        out_specs = [pl.BlockSpec((1, tokens, width), lambda i, w, s: (i, 0, 0))]
        out_shape = [jax.ShapeDtypeStruct((wanted, tokens, width), dtypes[0])]
    else:
        out_specs = [pl.BlockSpec((tokens, width), lambda i, w, s: (0, 0))] * wanted
        out_shape = [jax.ShapeDtypeStruct((tokens, width), dtype) for dtype in dtypes]
    return pl.pallas_call(
        body,
        grid_spec=pltpu.PrefetchScalarGridSpec(
            num_scalar_prefetch=2, grid=(wanted,), in_specs=in_specs, out_specs=out_specs
        ),
        out_shape=out_shape,
        compiler_params=pltpu.CompilerParams(vmem_limit_bytes=VMEM_BYTES),
        name="out_blocks",
    )(which, sign, *operands)


def finish(own, sign, attended, place, out_weight, blocks, before, far_attended, far_weight, received):
    groups, heads, tokens, _ = attended.shape
    depth, features = out_weight.shape
    width = features // blocks
    rows = heads * HEAD_DIM
    weight = out_weight.reshape(groups, depth // groups, features)
    tile = 2 * HEAD_DIM
    steps = width // tile
    last = before.shape[0] - 1

    def body(own_ref, sign_ref, mixed_ref, weight_ref, far_ref, far_weight_ref, before_ref, *refs):
        def product(rows_ref, columns_ref):
            joined = jnp.concatenate(
                [rows_ref[group, head] for group in range(groups) for head in range(heads)], axis=1
            )
            columns = columns_ref[...].reshape(groups * rows, tile)
            return jnp.dot(joined, columns, preferred_element_type=jnp.float32)

        total = product(mixed_ref, weight_ref) - product(far_ref, far_weight_ref)
        total = total * sign_ref[0].astype(jnp.float32) + before_ref[0]
        for ref in refs[:-1]:
            total = total + ref[...].astype(jnp.float32)
        refs[-1][...] = total

    whole = pl.BlockSpec(attended.shape, lambda i, w, s: (0, 0, 0, 0))
    part = pl.BlockSpec((tokens, tile), lambda i, w, s: (0, i))
    return pl.pallas_call(
        body,
        grid_spec=pltpu.PrefetchScalarGridSpec(
            num_scalar_prefetch=2,
            grid=(steps,),
            in_specs=[
                whole,
                pl.BlockSpec((groups, rows, tile), lambda i, w, s: (0, place, w[0] * steps + i)),
                whole,
                pl.BlockSpec((groups, rows, tile), lambda i, w, s: (0, 0, i)),
                pl.BlockSpec((1, tokens, tile), lambda i, w, s: (last, 0, i)),
            ]
            + [part] * len(received),
            out_specs=part,
        ),
        out_shape=jax.ShapeDtypeStruct((tokens, width), jnp.float32),
        compiler_params=pltpu.CompilerParams(vmem_limit_bytes=VMEM_BYTES),
        name="finish",
    )(own, sign, attended, weight, far_attended, far_weight, before, *received)


def chunk_sizes(heads):
    last = heads // 3 if heads % 3 == 0 else 1
    return [heads - last, last] if heads > last else [heads]


def per_device_by_heads(
    hidden_rows,
    gen_weight,
    noise,
    timesteps,
    qkv_weight,
    out_weight,
    qk_gain,
    block_keys,
    block_count,
):
    role, head = lax.axis_index("role"), lax.axis_index("head")
    chip, core = lax.axis_index("chip"), lax.axis_index("core")
    chips = lax.axis_size("chip")
    local_heads, local_blocks, most = block_keys.shape
    heads = local_heads // chips
    tokens = hidden_rows.shape[0]
    width = hidden_rows.shape[1]
    features = gen_weight.shape[1]
    all_blocks = chips * local_blocks
    swap = [(0, 1), (1, 0)]
    far_swap = [(0, 3), (1, 2), (2, 1), (3, 0)]
    ring = [(at, (at + 1) % chips) for at in range(chips)]

    def turn_of(other):
        return (chip - other) % chips

    def exchange(array):
        return lax.all_to_all(array, "chip", split_axis=0, concat_axis=0, tiled=True)

    weight_here = qkv_weight[0]
    depth = weight_here.shape[0]
    wide = 3 * HEAD_DIM
    lists = jnp.concatenate([block_keys, block_count[:, :, None]], axis=2)
    lists = lists.reshape(chips, -1).astype(jnp.bfloat16)
    listed = lists.shape[1]
    spare = -(-listed // (16 * wide)) * 16
    lists = jnp.pad(lists, ((0, 0), (0, spare * wide - listed))).reshape(chips, spare, wide)
    cuts = [
        cut_columns(weight_here, chips, at, lists if at == 0 else None) for at in range(heads)
    ]
    hidden_rows, cuts[0] = lax.optimization_barrier((hidden_rows, cuts[0]))
    weights_own = [exchange(cuts[0])]
    weights_other = []

    mine = role * lax.axis_size("head") + head
    generated = jnp.dot(hidden_rows, gen_weight, preferred_element_type=jnp.float32)
    generated = lax.reduce_precision(generated, 8, 7)
    angle_blocks = (timesteps.astype(jnp.float32) * (math.pi / 2000.0))[:, None, None]
    noise_here = lax.dynamic_slice_in_dim(noise, mine * features, features, axis=1)
    noisy = jnp.cos(angle_blocks) * generated.reshape(local_blocks, BLOCK, features)
    noisy = noisy + jnp.sin(angle_blocks) * noise_here.astype(jnp.float32).reshape(
        local_blocks, BLOCK, features
    )
    squares = jnp.sum(noisy * noisy, axis=-1)
    squares = squares + lax.ppermute(squares, "role", swap)
    squares = squares + lax.ppermute(squares, "head", swap)
    normed = (noisy * lax.rsqrt(squares / width + 1e-06)[:, :, None]).astype(jnp.bfloat16)
    normed = normed.reshape(tokens, features)

    def tables_of(lists):
        lists = lists.reshape(chips, spare * wide)[:, :listed].astype(jnp.int32)
        lists = lists.reshape(chips, heads, local_blocks, most + 1).transpose(1, 0, 2, 3)
        lists = lists.reshape(heads, all_blocks, most + 1)
        owner = lists[:, :, :most] // local_blocks
        turn = turn_of(owner // CORES)
        far = (owner % CORES != core).astype(jnp.int32)
        key_slots = far * all_blocks + turn * local_blocks + lists[:, :, :most] % local_blocks
        counts = lists[:, :, most]
        group_most = jnp.max(counts.reshape(heads, chips, local_blocks), axis=2)
        spot = jnp.arange(all_blocks, dtype=jnp.int32)
        query_slots = turn_of(spot // local_blocks)
        query_slots = query_slots * local_blocks + spot % local_blocks

        return key_slots, counts, query_slots, group_most

    sides = lax.axis_size("head")
    peers = jnp.stack(
        [
            role * sides + head,
            (1 - role) * sides + head,
            role * sides + 1 - head,
            (1 - role) * sides + 1 - head,
        ]
    ).astype(jnp.int32)
    places = jnp.concatenate([peers, core[None].astype(jnp.int32)])
    gains = lax.dynamic_slice_in_dim(qk_gain[0], chip * heads, heads, axis=1)

    chunks = chunk_sizes(heads)
    spans = [slice(sum(chunks[:at]), sum(chunks[: at + 1])) for at in range(len(chunks))]
    parts = [[] for _ in chunks]

    def project(chunk, first, size, begin, some, places):
        at = spans[chunk].start + first
        span = slice(at, at + size)
        query, kv = project_heads(
            places, gains[:, span], some, depth, weights_own[span], weights_other[span]
        )
        here = len(some) * local_blocks
        kv = kv.reshape(size, 2, here, BLOCK, HEAD_DIM)
        kv_other = lax.ppermute(kv, "core", swap)
        query = query.reshape(size, here, BLOCK, HEAD_DIM)
        parts[chunk].append((first, size, begin * local_blocks, here, query, kv, kv_other))
        return lax.optimization_barrier((places, kv))[0]

    half = tokens // 2
    rounds = []
    straight = None
    held_places = places
    shard = normed
    for phase in range(chips + 1):
        step = phase + 1
        sent = {}
        if phase < chips:
            sent["role"] = lax.ppermute(shard, "role", swap)
            sent["head"] = lax.ppermute(shard, "head", swap)
        if straight is not None:
            sent["first"] = lax.ppermute(straight[2][:half], "role", swap)
            sent["second"] = lax.ppermute(straight[1][half:], "head", swap)
        if step < chips:
            sent["next"] = lax.ppermute(shard, "chip", ring)
        if phase == 0:
            sent["weights"] = weights_own.pop()
            sent["cuts"] = cuts[1:]
        if phase == 1:
            sent["places"] = places
            sent["gains"] = gains
        if step == chips:
            weights_other.append(lax.ppermute(weights_own[0], "core", swap))
            early = list(rounds)
            tables = tables_of(weights_own[0][:, depth:])
            held_places, tables = lax.optimization_barrier((held_places, tables))
            sent["places"] = project(0, 0, 1, 0, early, held_places)
        if step > chips and chunks[0] > 1:
            weights_other.append(lax.ppermute(weights_own[1], "core", swap))
            sent["places"] = project(0, 1, 1, 0, early, held_places)
        sent, shard = lax.optimization_barrier((sent, shard))
        if phase == 0:
            weights_own.append(sent["weights"])
            cuts[1:] = sent["cuts"]
        if phase == 1:
            gains = sent["gains"]
        if straight is not None:
            rounds.append(straight + (sent["first"], sent["second"]))
        held_places = sent.get("places", held_places)
        if phase < chips:
            straight = (shard, sent["role"], sent["head"])
        if step < chips:
            shard = sent["next"]
        if chips - 2 <= phase and len(weights_own) < heads:
            held, _ = lax.optimization_barrier((cuts[len(weights_own)], sent))
            weights_own.append(exchange(held))
    while len(weights_own) < heads:
        weights_own.append(exchange(cuts[len(weights_own)]))
    for at in range(len(weights_other), heads - 1):
        weights_other.append(lax.ppermute(weights_own[at], "core", swap))

    sign = (2 * role - 1).astype(jnp.int32)[None]
    blocks = sides * lax.axis_size("role")
    which = jnp.stack([peers[3], peers[2], peers[1], peers[0]])
    out_here = out_weight[0]
    out_width = out_here.shape[1] // blocks
    place = spans[-1].start // chunks[-1]

    attended = []
    received = []
    for chunk, size in enumerate(chunks):
        last = chunk == len(chunks) - 1
        if chunk == 0:
            for at in range(min(size, 2), size):
                held_places = project(0, at, 1, 0, early, held_places)
            held_places = project(0, 0, size, len(early), rounds[len(early) :], held_places)
            for at in range(len(weights_other), heads):
                weights_own[at], held_places = lax.optimization_barrier(
                    (weights_own[at], held_places)
                )
                weights_other.append(lax.ppermute(weights_own[at], "core", swap))
            corner, held_places = lax.optimization_barrier((which[0] * out_width, held_places))
            far_weight = lax.dynamic_slice(
                out_here.reshape(chips, heads * HEAD_DIM, -1),
                (0, spans[-1].start * HEAD_DIM, corner),
                (chips, chunks[-1] * HEAD_DIM, out_width),
            )
            far_weight = lax.ppermute(far_weight, ("role", "head"), far_swap)
        else:
            held_places = project(chunk, 0, size, 0, rounds, held_places)
        if last:
            for earlier in range(len(attended)):
                (diagonal,) = out_blocks(
                    which[:1], sign, attended[earlier], spans[earlier].start // chunks[earlier],
                    out_here, blocks, (jnp.bfloat16,),
                )
                tables, diagonal, far_weight = lax.optimization_barrier(
                    (tables, diagonal, far_weight)
                )
                received.append(lax.ppermute(diagonal, ("role", "head"), far_swap))
        mixed = attend(spans[chunk].start, size, *tables, parts[chunk])
        held_places, mixed = lax.optimization_barrier((held_places, mixed))
        mixed = mixed.reshape(chips, size, tokens, HEAD_DIM)
        if attended:
            mixed, attended = lax.optimization_barrier((mixed, attended))
        attended.append(exchange(mixed))

    before = None
    for chunk, size in enumerate(chunks[:-1]):
        before = out_blocks(
            which[1:], sign, attended[chunk], spans[chunk].start // size, out_here, blocks,
            (jnp.float32,), before,
        )[0]
    far_attended = lax.ppermute(attended[-1], ("role", "head"), far_swap)
    over_head, over_role = out_blocks(
        which[1:3], sign, attended[-1], place, out_here, blocks, (jnp.bfloat16, jnp.bfloat16), before
    )
    received.append(lax.ppermute(over_head, "head", swap))
    received.append(lax.ppermute(over_role, "role", swap))
    return finish(
        which[3:], sign, attended[-1], place, out_here, blocks, before, far_attended, far_weight,
        received,
    )


def splits_heads(mesh, qkv_weight, hidden_rows):
    role, seq, head = (mesh.shape[name] for name in ("role", "seq", "head"))
    if role != 2 or head != 2 or seq % CORES != 0:
        return False
    chips = seq // CORES
    heads = qkv_weight.shape[2] // (3 * HEAD_DIM * head)
    width = hidden_rows.shape[1]
    tokens = hidden_rows.shape[0] // seq
    return (
        heads % chips == 0
        and heads // chips > 1
        and chips == role * head
        and width % (role * head * 256) == 0
        and width % (seq * 16) == 0
        and tokens % (2 * BLOCK) == 0
        and hidden_rows.shape[0] // BLOCK <= 256
    )


def solution(mesh):
    def call(*arrays):
        if splits_heads(mesh, arrays[4], arrays[0]):
            per_device = per_device_by_heads
            seq = ("chip", "core")
            shape = mesh.devices.shape
            names = mesh.axis_names
            at = names.index("seq")
            layout = Mesh(
                mesh.devices.reshape(shape[:at] + (shape[at] // CORES, CORES) + shape[at + 1 :]),
                names[:at] + seq + names[at + 1 :],
            )
        else:
            per_device = per_device_by_tokens
            seq = "seq"
            layout = mesh
        placed = (
            P(seq, None),
            P(None, ("role", "head")),
            P(seq, None),
            P(seq),
            P("role", seq, "head"),
            P("role", "head", None),
            P("role", None, "head"),
            P("head", seq, None),
            P("head", seq),
        )
        return jax.shard_map(
            per_device,
            mesh=layout,
            in_specs=placed,
            out_specs=P(seq, ("role", "head")),
            check_vma=False,
        )(*arrays)

    return call
```

```python
import math

import jax
import jax.numpy as jnp
from jax import lax
from jax.experimental import pallas as pl
from jax.experimental.pallas import tpu as pltpu
from jax.sharding import Mesh
from jax.sharding import PartitionSpec as P

HEAD_DIM = 128
BLOCK = 64
KMAX = 8
CAP = 2


def rms_rows(values):
    return values * lax.rsqrt(jnp.mean(values * values, axis=-1, keepdims=True) + 1e-06)


def block_attention(queries, key_table, value_table, key_list, key_count):
    picked_keys = key_table[key_list]
    picked_values = value_table[key_list]
    scale = 1.0 / math.sqrt(HEAD_DIM)
    scores = (
        jnp.einsum("nqe,nkbe->nqkb", queries, picked_keys, preferred_element_type=jnp.float32)
        * scale
    )
    live = lax.broadcasted_iota(jnp.int32, (key_list.shape[0], KMAX), 1) < key_count[:, None]
    scores = jnp.where(live[:, None, :, None], scores, -jnp.inf)
    highest = jnp.max(scores, axis=(2, 3), keepdims=True)
    raised = jnp.exp(scores - highest)
    summed = jnp.sum(raised, axis=(2, 3), keepdims=True)
    weights = (raised / summed).astype(jnp.bfloat16)
    mixed = jnp.einsum("nqkb,nkbe->nqe", weights, picked_values, preferred_element_type=jnp.float32)
    return mixed.astype(jnp.bfloat16)


def pick_blocks(table, wanted):
    return table[wanted]


def per_device_by_tokens(
    hidden_rows,
    gen_weight,
    noise,
    timesteps,
    qkv_weight,
    out_weight,
    qk_gain,
    block_keys,
    block_count,
):
    generated = jnp.dot(hidden_rows, gen_weight, preferred_element_type=jnp.float32).astype(
        jnp.bfloat16
    )
    forked = lax.all_gather(generated, ("role", "head"), axis=1, tiled=True)
    row_count = forked.shape[0]
    width = forked.shape[1]
    local_blocks = timesteps.shape[0]
    angle_blocks = (timesteps.astype(jnp.float32) * (math.pi / 2000.0))[:, None, None]
    noisy = jnp.cos(angle_blocks) * forked.astype(jnp.float32).reshape(local_blocks, BLOCK, width)
    noisy = noisy + jnp.sin(angle_blocks) * noise.astype(jnp.float32).reshape(
        local_blocks, BLOCK, width
    )
    normed = rms_rows(noisy).reshape(row_count, width).astype(jnp.bfloat16)
    weight_here = qkv_weight[0]
    projected = jnp.dot(
        normed,
        lax.all_gather(weight_here, "seq", axis=0, tiled=True),
        preferred_element_type=jnp.float32,
    )
    heads_here = projected.shape[1] // (3 * HEAD_DIM)
    head_parts = projected.reshape(row_count, heads_here, 3, HEAD_DIM)
    gain_here = qk_gain[0]
    queries = (rms_rows(head_parts[:, :, 0]) * gain_here[0][None, :, None]).astype(jnp.bfloat16)
    key_local = (rms_rows(head_parts[:, :, 1]) * gain_here[1][None, :, None]).astype(jnp.bfloat16)
    value_local = head_parts[:, :, 2].astype(jnp.bfloat16)
    query_table = queries.reshape(local_blocks, BLOCK, heads_here, HEAD_DIM).transpose(2, 0, 1, 3)
    shard_count = lax.axis_size("seq")
    shard_here = lax.axis_index("seq")
    all_blocks = shard_count * local_blocks
    key_heads = key_local.reshape(local_blocks, BLOCK, heads_here, HEAD_DIM).transpose(2, 0, 1, 3)
    value_heads = value_local.reshape(local_blocks, BLOCK, heads_here, HEAD_DIM).transpose(
        2, 0, 1, 3
    )
    block_ids = lax.broadcasted_iota(jnp.int32, (1, 1, 1, all_blocks), 3)
    matches = block_keys[:, :, :, None] == block_ids
    remote = block_ids // local_blocks != shard_here
    needed = jnp.any(jnp.logical_and(matches, remote), axis=(1, 2))
    needed = needed.reshape(heads_here, shard_count, local_blocks)
    slot_of = jnp.cumsum(needed.astype(jnp.int32), axis=2) - 1
    slot_ids = lax.broadcasted_iota(jnp.int32, (1, 1, 1, CAP), 3)
    within_ids = lax.broadcasted_iota(jnp.int32, (1, 1, local_blocks, 1), 2)
    chosen_slot = jnp.logical_and(needed[..., None], slot_of[..., None] == slot_ids)
    requests = jnp.sum(jnp.where(chosen_slot, within_ids, 0), axis=2)
    asked = lax.all_to_all(
        requests.transpose(1, 0, 2), "seq", split_axis=0, concat_axis=0, tiled=True
    )
    sent_keys = jax.vmap(pick_blocks, in_axes=(0, 1), out_axes=1)(key_heads, asked)
    sent_values = jax.vmap(pick_blocks, in_axes=(0, 1), out_axes=1)(value_heads, asked)
    got_keys, got_values = (
        lax.all_to_all(sent_keys, "seq", split_axis=0, concat_axis=0, tiled=True),
        lax.all_to_all(sent_values, "seq", split_axis=0, concat_axis=0, tiled=True),
    )
    fetched_keys = got_keys.transpose(1, 0, 2, 3, 4).reshape(
        heads_here, shard_count * CAP, BLOCK, HEAD_DIM
    )
    fetched_values = got_values.transpose(1, 0, 2, 3, 4).reshape(
        heads_here, shard_count * CAP, BLOCK, HEAD_DIM
    )
    key_table = jnp.concatenate([key_heads, fetched_keys], axis=1)
    value_table = jnp.concatenate([value_heads, fetched_values], axis=1)
    local_ids = lax.broadcasted_iota(jnp.int32, (1, shard_count, local_blocks), 2)
    owner_grid = lax.broadcasted_iota(jnp.int32, (1, shard_count, local_blocks), 1)
    position = jnp.where(
        owner_grid == shard_here, local_ids, local_blocks + owner_grid * CAP + slot_of
    )
    position = position.reshape(heads_here, all_blocks)
    key_lists = jnp.sum(jnp.where(matches, position[:, None, None, :], 0), axis=3)
    attended = jax.vmap(block_attention)(
        query_table, key_table, value_table, key_lists, block_count
    )
    attended = attended.transpose(1, 2, 0, 3).reshape(row_count, heads_here * HEAD_DIM)
    contribution = jnp.dot(attended, out_weight[0], preferred_element_type=jnp.float32)
    signed = (2.0 * lax.axis_index("role").astype(jnp.float32) - 1.0) * contribution
    return lax.psum_scatter(
        signed.astype(jnp.bfloat16), ("role", "head"), scatter_dimension=1, tiled=True
    ).astype(jnp.float32)


VMEM_BYTES = 56 * 1024 * 1024
CORES = 2


def whole_in_vmem():
    return pl.BlockSpec(memory_space=pltpu.VMEM)


def in_hbm():
    return pl.BlockSpec(memory_space=pl.ANY)


def in_smem():
    return pl.BlockSpec(memory_space=pltpu.SMEM)


def cut_columns(weight, chips, head, extra=None):
    rows, columns = weight.shape
    wide = 3 * HEAD_DIM
    chip_heads = columns // (chips * wide)
    more = 0 if extra is None else extra.shape[1]

    def body(weight_ref, *refs):
        out_ref = refs[-1]
        out_ref[0, :rows] = weight_ref[...]
        if more:
            out_ref[0, rows:] = refs[0][0]

    in_specs = [pl.BlockSpec((rows, wide), lambda chip: (0, chip * chip_heads + head))]
    operands = [weight]
    if more:
        in_specs.append(pl.BlockSpec((1, more, wide), lambda chip: (chip, 0, 0)))
        operands.append(extra)
    return pl.pallas_call(
        body,
        grid=(chips,),
        in_specs=in_specs,
        out_specs=pl.BlockSpec((1, rows + more, wide), lambda chip: (chip, 0, 0)),
        out_shape=jax.ShapeDtypeStruct((chips, rows + more, wide), weight.dtype),
        name="cut_columns",
    )(*operands)


def project_heads(places, gains, rounds, depth, weights_own, weights_other):
    heads = len(weights_own)
    slabs, _, columns = weights_own[0].shape
    tokens, features = rounds[0][0].shape
    pieces = [piece for one in rounds for piece in one]
    turns = len(rounds)
    most = max(len(one) for one in rounds)
    joint = 2 if slabs % 2 == 0 else 1
    dtype = weights_own[0].dtype

    def body(places_ref, gains_ref, *refs):
        own_refs, other_refs = refs[:heads], refs[heads : 2 * heads]
        piece_refs = refs[2 * heads : 2 * heads + len(pieces)]
        query_ref, kv_ref = refs[2 * heads + len(pieces) : 2 * heads + len(pieces) + 2]
        table, rows, weight_sems, row_sems = refs[2 * heads + len(pieces) + 2 :]
        core = places_ref[slabs]
        copies = []
        for slab in range(slabs):
            here = []
            for head in range(heads):
                for side, ref in enumerate((own_refs[head], other_refs[head])):
                    place = core if side == 0 else 1 - core
                    here.append(
                        pltpu.make_async_copy(
                            ref.at[places_ref[slab], pl.ds(0, depth)],
                            table.at[
                                slab // joint,
                                slab % joint,
                                place,
                                :,
                                pl.ds(head * columns, columns),
                            ],
                            weight_sems.at[slab, head, side],
                        )
                    )
            at = 0
            for turn in range(turns):
                first = turn * tokens
                for which in range(len(rounds[turn])):
                    if min(which, slabs - 1) == slab:
                        count = rounds[turn][which].shape[0]
                        here.append(
                            pltpu.make_async_copy(
                                piece_refs[at],
                                rows.at[
                                    slab // joint,
                                    pl.ds(first, count),
                                    pl.ds(slab % joint * features, features),
                                ],
                                row_sems.at[which, turn],
                            )
                        )
                        first += count
                    at += 1
            for copy in here:
                copy.start()
            copies.append(here)
        total = None
        for group in range(slabs // joint):
            for slab in range(group * joint, (group + 1) * joint):
                for copy in copies[slab]:
                    copy.wait()
            part = jnp.dot(
                rows[group],
                table[group].reshape(joint * CORES * depth, heads * columns),
                preferred_element_type=jnp.float32,
            )
            total = part if total is None else total + part
        for turn in range(turns):
            here = total[turn * tokens : (turn + 1) * tokens]
            for head in range(heads):
                at = head * columns
                for which in range(2):
                    block = here[:, at + which * HEAD_DIM : at + (which + 1) * HEAD_DIM]
                    normal = (rms_rows(block) * gains_ref[which, head]).astype(dtype)
                    if which == 0:
                        query_ref[head, turn] = normal
                    else:
                        kv_ref[head, 0, turn] = normal
                block = here[:, at + 2 * HEAD_DIM : at + 3 * HEAD_DIM]
                kv_ref[head, 1, turn] = block.astype(dtype)

    return pl.pallas_call(
        body,
        in_specs=[in_smem(), in_smem()] + [in_hbm()] * (2 * heads + len(pieces)),
        out_specs=(whole_in_vmem(), whole_in_vmem()),
        out_shape=(
            jax.ShapeDtypeStruct((heads, turns, tokens, HEAD_DIM), dtype),
            jax.ShapeDtypeStruct((heads, 2, turns, tokens, HEAD_DIM), dtype),
        ),
        scratch_shapes=[
            pltpu.VMEM((slabs // joint, joint, CORES, depth, heads * columns), dtype),
            pltpu.VMEM((slabs // joint, turns * tokens, joint * features), dtype),
            pltpu.SemaphoreType.DMA((slabs, heads, 2)),
            pltpu.SemaphoreType.DMA((most, turns)),
        ],
        compiler_params=pltpu.CompilerParams(vmem_limit_bytes=VMEM_BYTES),
        name="project_heads",
    )(places, gains, *weights_own, *weights_other, *pieces)


def attend(first_head, heads, key_slots, counts, query_slots, group_most, parts):
    _, blocks, most = key_slots.shape
    groups = group_most.shape[1]
    together = blocks // groups
    scale = 1.0 / math.sqrt(HEAD_DIM)
    dtype = parts[0][4].dtype
    arrays = [array for part in parts for array in part[4:]]

    def body(slots_ref, counts_ref, from_ref, most_ref, *refs):
        out_ref, query_table, table, sems = refs[len(arrays) :]
        copies = []
        for at, (head, size, block, span, _, _, _) in enumerate(parts):
            query_part, own_part, other_part = refs[3 * at : 3 * at + 3]
            rows = pl.ds(head, size)
            copies.append(
                pltpu.make_async_copy(
                    query_part, query_table.at[rows, pl.ds(block, span)], sems.at[at, 0]
                )
            )
            for side, ref in enumerate((own_part, other_part)):
                place = pl.ds(side * blocks + block, span)
                copies.append(
                    pltpu.make_async_copy(ref, table.at[rows, :, place], sems.at[at, 1 + side])
                )
        for copy in copies:
            copy.start()
        for copy in copies:
            copy.wait()

        def run(head, group, listed, batch):
            for first in range(0, together, batch):
                spots = [group * together + at for at in range(first, min(first + batch, together))]
                slots = [[slots_ref[first_head + head, at, entry] for entry in range(listed)] for at in spots]
                scores = []
                for at, listing in zip(spots, slots):
                    keys = jnp.concatenate([table[head, 0, slot] for slot in listing], axis=0)
                    scores.append(
                        lax.dot_general(
                            query_table[head, from_ref[at]],
                            keys,
                            (((1,), (1,)), ((), ())),
                            preferred_element_type=jnp.float32,
                        )
                    )
                column = lax.broadcasted_iota(jnp.int32, (1, listed * BLOCK), 1)
                scores = [
                    jnp.where(column < counts_ref[first_head + head, at] * BLOCK, one * scale, -jnp.inf)
                    for at, one in zip(spots, scores)
                ]
                highest = [jnp.max(one, axis=1, keepdims=True) for one in scores]
                raised = [jnp.exp(one - top) for one, top in zip(scores, highest)]
                inverse = [1.0 / jnp.sum(one, axis=1, keepdims=True) for one in raised]
                weights = [(one * by).astype(dtype) for one, by in zip(raised, inverse)]
                mixed = []
                for one, listing in zip(weights, slots):
                    values = jnp.concatenate([table[head, 1, slot] for slot in listing], axis=0)
                    mixed.append(jnp.dot(one, values, preferred_element_type=jnp.float32))
                for at, one in enumerate(mixed):
                    out_ref[group, head, first + at] = one.astype(dtype)

        def step(at, carry):
            head, group = at // groups, at % groups
            few = most_ref[first_head + head, group] <= most // 2

            @pl.when(few)
            def _():
                run(head, group, most // 2, 6)

            @pl.when(jnp.logical_not(few))
            def _():
                run(head, group, most, 3)

            return carry

        lax.fori_loop(0, heads * groups, step, 0)

    return pl.pallas_call(
        body,
        in_specs=[in_smem()] * 4 + [in_hbm()] * len(arrays),
        out_specs=whole_in_vmem(),
        out_shape=jax.ShapeDtypeStruct((groups, heads, together, BLOCK, HEAD_DIM), dtype),
        scratch_shapes=[
            pltpu.VMEM((heads, blocks, BLOCK, HEAD_DIM), dtype),
            pltpu.VMEM((heads, 2, CORES * blocks, BLOCK, HEAD_DIM), dtype),
            pltpu.SemaphoreType.DMA((len(parts), 3)),
        ],
        compiler_params=pltpu.CompilerParams(vmem_limit_bytes=VMEM_BYTES),
        name="attend",
    )(key_slots, counts, query_slots, group_most, *arrays)


def out_blocks(which, sign, attended, place, out_weight, blocks, dtypes, before=None, skip=0):
    groups, heads, tokens, _ = attended.shape
    depth, features = out_weight.shape
    width = features // blocks
    wanted = which.shape[0]
    rows = heads * HEAD_DIM
    weight = out_weight.reshape(groups, depth // groups, features)
    stacked = len(dtypes) == 1 and wanted > 1

    def body(which_ref, sign_ref, mixed_ref, weight_ref, *refs):
        out_refs = refs if before is None else refs[1:]
        joined = jnp.concatenate(
            [mixed_ref[group, head] for group in range(groups) for head in range(heads)], axis=1
        )
        total = jnp.dot(
            joined,
            weight_ref[...].reshape(groups * rows, width),
            preferred_element_type=jnp.float32,
        )
        total = total * sign_ref[0].astype(jnp.float32)
        if before is not None:
            total = total + refs[0][0].astype(jnp.float32)
        if stacked:
            out_refs[0][0] = total.astype(dtypes[0])
        else:
            for at in range(wanted):

                @pl.when(pl.program_id(0) == at)
                def _(at=at):
                    out_refs[at][...] = total.astype(dtypes[at])

    in_specs = [
        pl.BlockSpec(attended.shape, lambda i, w, s: (0, 0, 0, 0)),
        pl.BlockSpec((groups, rows, width), lambda i, w, s: (0, place, w[i])),
    ]
    operands = [attended, weight]
    if before is not None:
        in_specs.append(pl.BlockSpec((1, tokens, width), lambda i, w, s: (i + skip, 0, 0)))
        operands.append(before)
    if stacked:
        out_specs = [pl.BlockSpec((1, tokens, width), lambda i, w, s: (i, 0, 0))]
        out_shape = [jax.ShapeDtypeStruct((wanted, tokens, width), dtypes[0])]
    else:
        out_specs = [pl.BlockSpec((tokens, width), lambda i, w, s: (0, 0))] * wanted
        out_shape = [jax.ShapeDtypeStruct((tokens, width), dtype) for dtype in dtypes]
    return pl.pallas_call(
        body,
        grid_spec=pltpu.PrefetchScalarGridSpec(
            num_scalar_prefetch=2, grid=(wanted,), in_specs=in_specs, out_specs=out_specs
        ),
        out_shape=out_shape,
        compiler_params=pltpu.CompilerParams(vmem_limit_bytes=VMEM_BYTES),
        name="out_blocks",
    )(which, sign, *operands)


def chunk_sizes(heads):
    last = heads // 3 if heads % 3 == 0 else 1
    return [heads - last, last] if heads > last else [heads]


def per_device_by_heads(
    hidden_rows,
    gen_weight,
    noise,
    timesteps,
    qkv_weight,
    out_weight,
    qk_gain,
    block_keys,
    block_count,
):
    role, head = lax.axis_index("role"), lax.axis_index("head")
    chip, core = lax.axis_index("chip"), lax.axis_index("core")
    chips = lax.axis_size("chip")
    local_heads, local_blocks, most = block_keys.shape
    heads = local_heads // chips
    tokens = hidden_rows.shape[0]
    width = hidden_rows.shape[1]
    features = gen_weight.shape[1]
    all_blocks = chips * local_blocks
    swap = [(0, 1), (1, 0)]
    far_swap = [(0, 3), (1, 2), (2, 1), (3, 0)]
    ring = [(at, (at + 1) % chips) for at in range(chips)]

    def turn_of(other):
        return (chip - other) % chips

    def exchange(array):
        return lax.all_to_all(array, "chip", split_axis=0, concat_axis=0, tiled=True)

    weight_here = qkv_weight[0]
    depth = weight_here.shape[0]
    wide = 3 * HEAD_DIM
    lists = jnp.concatenate([block_keys, block_count[:, :, None]], axis=2)
    lists = lists.reshape(chips, -1).astype(jnp.bfloat16)
    listed = lists.shape[1]
    spare = -(-listed // (16 * wide)) * 16
    lists = jnp.pad(lists, ((0, 0), (0, spare * wide - listed))).reshape(chips, spare, wide)
    cuts = [
        cut_columns(weight_here, chips, at, lists if at == 0 else None) for at in range(heads)
    ]
    hidden_rows, cuts[0] = lax.optimization_barrier((hidden_rows, cuts[0]))
    weights_own = [exchange(cuts[0])]
    weights_other = []

    mine = role * lax.axis_size("head") + head
    generated = jnp.dot(hidden_rows, gen_weight, preferred_element_type=jnp.float32)
    generated = lax.reduce_precision(generated, 8, 7)
    angle_blocks = (timesteps.astype(jnp.float32) * (math.pi / 2000.0))[:, None, None]
    noise_here = lax.dynamic_slice_in_dim(noise, mine * features, features, axis=1)
    noisy = jnp.cos(angle_blocks) * generated.reshape(local_blocks, BLOCK, features)
    noisy = noisy + jnp.sin(angle_blocks) * noise_here.astype(jnp.float32).reshape(
        local_blocks, BLOCK, features
    )
    squares = jnp.sum(noisy * noisy, axis=-1)
    squares = squares + lax.ppermute(squares, "role", swap)
    squares = squares + lax.ppermute(squares, "head", swap)
    normed = (noisy * lax.rsqrt(squares / width + 1e-06)[:, :, None]).astype(jnp.bfloat16)
    normed = normed.reshape(tokens, features)

    def tables_of(lists):
        lists = lists.reshape(chips, spare * wide)[:, :listed].astype(jnp.int32)
        lists = lists.reshape(chips, heads, local_blocks, most + 1).transpose(1, 0, 2, 3)
        lists = lists.reshape(heads, all_blocks, most + 1)
        owner = lists[:, :, :most] // local_blocks
        turn = turn_of(owner // CORES)
        far = (owner % CORES != core).astype(jnp.int32)
        key_slots = far * all_blocks + turn * local_blocks + lists[:, :, :most] % local_blocks
        counts = lists[:, :, most]
        group_most = jnp.max(counts.reshape(heads, chips, local_blocks), axis=2)
        spot = jnp.arange(all_blocks, dtype=jnp.int32)
        query_slots = turn_of(spot // local_blocks)
        query_slots = query_slots * local_blocks + spot % local_blocks

        return key_slots, counts, query_slots, group_most

    sides = lax.axis_size("head")
    peers = jnp.stack(
        [
            role * sides + head,
            (1 - role) * sides + head,
            role * sides + 1 - head,
            (1 - role) * sides + 1 - head,
        ]
    ).astype(jnp.int32)
    places = jnp.concatenate([peers, core[None].astype(jnp.int32)])
    gains = lax.dynamic_slice_in_dim(qk_gain[0], chip * heads, heads, axis=1)

    chunks = chunk_sizes(heads)
    spans = [slice(sum(chunks[:at]), sum(chunks[: at + 1])) for at in range(len(chunks))]
    parts = [[] for _ in chunks]

    def project(chunk, first, size, begin, some, places):
        at = spans[chunk].start + first
        span = slice(at, at + size)
        query, kv = project_heads(
            places, gains[:, span], some, depth, weights_own[span], weights_other[span]
        )
        here = len(some) * local_blocks
        kv = kv.reshape(size, 2, here, BLOCK, HEAD_DIM)
        kv_other = lax.ppermute(kv, "core", swap)
        query = query.reshape(size, here, BLOCK, HEAD_DIM)
        parts[chunk].append((first, size, begin * local_blocks, here, query, kv, kv_other))
        return lax.optimization_barrier((places, kv))[0]

    half = tokens // 2
    rounds = []
    straight = None
    held_places = places
    shard = normed
    for phase in range(chips + 1):
        step = phase + 1
        sent = {}
        if phase < chips:
            sent["role"] = lax.ppermute(shard, "role", swap)
            sent["head"] = lax.ppermute(shard, "head", swap)
        if straight is not None:
            sent["first"] = lax.ppermute(straight[2][:half], "role", swap)
            sent["second"] = lax.ppermute(straight[1][half:], "head", swap)
        if step < chips:
            sent["next"] = lax.ppermute(shard, "chip", ring)
        if phase == 0:
            sent["weights"] = weights_own.pop()
            sent["cuts"] = cuts[1:]
        if phase == 1:
            sent["places"] = places
            sent["gains"] = gains
        if step == chips:
            weights_other.append(lax.ppermute(weights_own[0], "core", swap))
            early = list(rounds)
            tables = tables_of(weights_own[0][:, depth:])
            held_places, tables = lax.optimization_barrier((held_places, tables))
            sent["places"] = project(0, 0, 1, 0, early, held_places)
        if step > chips and chunks[0] > 1:
            weights_other.append(lax.ppermute(weights_own[1], "core", swap))
            sent["places"] = project(0, 1, 1, 0, early, held_places)
        sent, shard = lax.optimization_barrier((sent, shard))
        if phase == 0:
            weights_own.append(sent["weights"])
            cuts[1:] = sent["cuts"]
        if phase == 1:
            gains = sent["gains"]
        if straight is not None:
            rounds.append(straight + (sent["first"], sent["second"]))
        held_places = sent.get("places", held_places)
        if phase < chips:
            straight = (shard, sent["role"], sent["head"])
        if step < chips:
            shard = sent["next"]
        if chips - 2 <= phase and len(weights_own) < heads:
            held, _ = lax.optimization_barrier((cuts[len(weights_own)], sent))
            weights_own.append(exchange(held))
    while len(weights_own) < heads:
        weights_own.append(exchange(cuts[len(weights_own)]))
    for at in range(len(weights_other), heads - 1):
        weights_other.append(lax.ppermute(weights_own[at], "core", swap))

    sign = (2 * role - 1).astype(jnp.int32)[None]
    blocks = sides * lax.axis_size("role")
    which = jnp.stack([peers[3], peers[2], peers[1], peers[0]])
    out_here = out_weight[0]
    out_width = out_here.shape[1] // blocks
    place = spans[-1].start // chunks[-1]

    attended = []
    received = []
    for chunk, size in enumerate(chunks):
        last = chunk == len(chunks) - 1
        if chunk == 0:
            for at in range(min(size, 2), size):
                held_places = project(0, at, 1, 0, early, held_places)
            held_places = project(0, 0, size, len(early), rounds[len(early) :], held_places)
        else:
            held_places = project(chunk, 0, size, 0, rounds, held_places)
        if last:
            for earlier in range(len(attended)):
                (diagonal,) = out_blocks(
                    which[:1], sign, attended[earlier], spans[earlier].start // chunks[earlier],
                    out_here, blocks, (jnp.bfloat16,),
                )
                tables, diagonal, far_weight = lax.optimization_barrier(
                    (tables, diagonal, far_weight)
                )
                received.append(lax.ppermute(diagonal, ("role", "head"), far_swap))
        mixed = attend(spans[chunk].start, size, *tables, parts[chunk])
        held_places, mixed = lax.optimization_barrier((held_places, mixed))
        if chunk == 0:
            for at in range(len(weights_other), heads):
                weights_own[at], held_places = lax.optimization_barrier(
                    (weights_own[at], held_places)
                )
                weights_other.append(lax.ppermute(weights_own[at], "core", swap))
            corner, held_places = lax.optimization_barrier((which[0] * out_width, held_places))
            far_weight = lax.dynamic_slice(
                out_here.reshape(chips, heads * HEAD_DIM, -1),
                (0, spans[-1].start * HEAD_DIM, corner),
                (chips, chunks[-1] * HEAD_DIM, out_width),
            )
            far_weight = lax.ppermute(far_weight, ("role", "head"), far_swap)
        mixed = mixed.reshape(chips, size, tokens, HEAD_DIM)
        if attended:
            mixed, attended = lax.optimization_barrier((mixed, attended))
        attended.append(exchange(mixed))

    def contributions(wanted, dtypes, before=None):
        for chunk, size in enumerate(chunks[:-1]):
            before = jnp.stack(
                out_blocks(
                    wanted, sign, attended[chunk], spans[chunk].start // size, out_here, blocks,
                    (jnp.float32,), before,
                )
            ).reshape(-1, tokens, out_width)
        return out_blocks(wanted, sign, attended[-1], place, out_here, blocks, dtypes, before)

    far_attended = lax.ppermute(attended[-1], ("role", "head"), far_swap)
    over_head, over_role = contributions(which[1:3], (jnp.bfloat16, jnp.bfloat16))
    received.append(lax.ppermute(over_head, "head", swap))
    received.append(lax.ppermute(over_role, "role", swap))
    (far,) = out_blocks(
        jnp.zeros_like(which[:1]), -sign, far_attended, 0, far_weight.reshape(-1, out_width), 1,
        (jnp.float32,), received[0][None],
    )
    (own,) = contributions(which[3:], (jnp.float32,), far[None])
    total = received[1].astype(jnp.float32)
    for one in received[2:]:
        total = total + one.astype(jnp.float32)
    return own + total


def splits_heads(mesh, qkv_weight, hidden_rows):
    role, seq, head = (mesh.shape[name] for name in ("role", "seq", "head"))
    if role != 2 or head != 2 or seq % CORES != 0:
        return False
    chips = seq // CORES
    heads = qkv_weight.shape[2] // (3 * HEAD_DIM * head)
    width = hidden_rows.shape[1]
    tokens = hidden_rows.shape[0] // seq
    return (
        heads % chips == 0
        and heads // chips > 1
        and chips == role * head
        and width % (role * head * 256) == 0
        and width % (seq * 16) == 0
        and tokens % (2 * BLOCK) == 0
        and hidden_rows.shape[0] // BLOCK <= 256
    )


def solution(mesh):
    def call(*arrays):
        if splits_heads(mesh, arrays[4], arrays[0]):
            per_device = per_device_by_heads
            seq = ("chip", "core")
            shape = mesh.devices.shape
            names = mesh.axis_names
            at = names.index("seq")
            layout = Mesh(
                mesh.devices.reshape(shape[:at] + (shape[at] // CORES, CORES) + shape[at + 1 :]),
                names[:at] + seq + names[at + 1 :],
            )
        else:
            per_device = per_device_by_tokens
            seq = "seq"
            layout = mesh
        placed = (
            P(seq, None),
            P(None, ("role", "head")),
            P(seq, None),
            P(seq),
            P("role", seq, "head"),
            P("role", "head", None),
            P("role", None, "head"),
            P("head", seq, None),
            P("head", seq),
        )
        return jax.shard_map(
            per_device,
            mesh=layout,
            in_specs=placed,
            out_specs=P(seq, ("role", "head")),
            check_vma=False,
        )(*arrays)

    return call
```

```python
import math

import jax
import jax.numpy as jnp
from jax import lax
from jax.experimental import pallas as pl
from jax.experimental.pallas import tpu as pltpu
from jax.sharding import Mesh
from jax.sharding import PartitionSpec as P

HEAD_DIM = 128
BLOCK = 64
KMAX = 8
CAP = 2


def rms_rows(values):
    return values * lax.rsqrt(jnp.mean(values * values, axis=-1, keepdims=True) + 1e-06)


def block_attention(queries, key_table, value_table, key_list, key_count):
    picked_keys = key_table[key_list]
    picked_values = value_table[key_list]
    scale = 1.0 / math.sqrt(HEAD_DIM)
    scores = (
        jnp.einsum("nqe,nkbe->nqkb", queries, picked_keys, preferred_element_type=jnp.float32)
        * scale
    )
    live = lax.broadcasted_iota(jnp.int32, (key_list.shape[0], KMAX), 1) < key_count[:, None]
    scores = jnp.where(live[:, None, :, None], scores, -jnp.inf)
    highest = jnp.max(scores, axis=(2, 3), keepdims=True)
    raised = jnp.exp(scores - highest)
    summed = jnp.sum(raised, axis=(2, 3), keepdims=True)
    weights = (raised / summed).astype(jnp.bfloat16)
    mixed = jnp.einsum("nqkb,nkbe->nqe", weights, picked_values, preferred_element_type=jnp.float32)
    return mixed.astype(jnp.bfloat16)


def pick_blocks(table, wanted):
    return table[wanted]


def per_device_by_tokens(
    hidden_rows,
    gen_weight,
    noise,
    timesteps,
    qkv_weight,
    out_weight,
    qk_gain,
    block_keys,
    block_count,
):
    generated = jnp.dot(hidden_rows, gen_weight, preferred_element_type=jnp.float32).astype(
        jnp.bfloat16
    )
    forked = lax.all_gather(generated, ("role", "head"), axis=1, tiled=True)
    row_count = forked.shape[0]
    width = forked.shape[1]
    local_blocks = timesteps.shape[0]
    angle_blocks = (timesteps.astype(jnp.float32) * (math.pi / 2000.0))[:, None, None]
    noisy = jnp.cos(angle_blocks) * forked.astype(jnp.float32).reshape(local_blocks, BLOCK, width)
    noisy = noisy + jnp.sin(angle_blocks) * noise.astype(jnp.float32).reshape(
        local_blocks, BLOCK, width
    )
    normed = rms_rows(noisy).reshape(row_count, width).astype(jnp.bfloat16)
    weight_here = qkv_weight[0]
    projected = jnp.dot(
        normed,
        lax.all_gather(weight_here, "seq", axis=0, tiled=True),
        preferred_element_type=jnp.float32,
    )
    heads_here = projected.shape[1] // (3 * HEAD_DIM)
    head_parts = projected.reshape(row_count, heads_here, 3, HEAD_DIM)
    gain_here = qk_gain[0]
    queries = (rms_rows(head_parts[:, :, 0]) * gain_here[0][None, :, None]).astype(jnp.bfloat16)
    key_local = (rms_rows(head_parts[:, :, 1]) * gain_here[1][None, :, None]).astype(jnp.bfloat16)
    value_local = head_parts[:, :, 2].astype(jnp.bfloat16)
    query_table = queries.reshape(local_blocks, BLOCK, heads_here, HEAD_DIM).transpose(2, 0, 1, 3)
    shard_count = lax.axis_size("seq")
    shard_here = lax.axis_index("seq")
    all_blocks = shard_count * local_blocks
    key_heads = key_local.reshape(local_blocks, BLOCK, heads_here, HEAD_DIM).transpose(2, 0, 1, 3)
    value_heads = value_local.reshape(local_blocks, BLOCK, heads_here, HEAD_DIM).transpose(
        2, 0, 1, 3
    )
    block_ids = lax.broadcasted_iota(jnp.int32, (1, 1, 1, all_blocks), 3)
    matches = block_keys[:, :, :, None] == block_ids
    remote = block_ids // local_blocks != shard_here
    needed = jnp.any(jnp.logical_and(matches, remote), axis=(1, 2))
    needed = needed.reshape(heads_here, shard_count, local_blocks)
    slot_of = jnp.cumsum(needed.astype(jnp.int32), axis=2) - 1
    slot_ids = lax.broadcasted_iota(jnp.int32, (1, 1, 1, CAP), 3)
    within_ids = lax.broadcasted_iota(jnp.int32, (1, 1, local_blocks, 1), 2)
    chosen_slot = jnp.logical_and(needed[..., None], slot_of[..., None] == slot_ids)
    requests = jnp.sum(jnp.where(chosen_slot, within_ids, 0), axis=2)
    asked = lax.all_to_all(
        requests.transpose(1, 0, 2), "seq", split_axis=0, concat_axis=0, tiled=True
    )
    sent_keys = jax.vmap(pick_blocks, in_axes=(0, 1), out_axes=1)(key_heads, asked)
    sent_values = jax.vmap(pick_blocks, in_axes=(0, 1), out_axes=1)(value_heads, asked)
    got_keys, got_values = (
        lax.all_to_all(sent_keys, "seq", split_axis=0, concat_axis=0, tiled=True),
        lax.all_to_all(sent_values, "seq", split_axis=0, concat_axis=0, tiled=True),
    )
    fetched_keys = got_keys.transpose(1, 0, 2, 3, 4).reshape(
        heads_here, shard_count * CAP, BLOCK, HEAD_DIM
    )
    fetched_values = got_values.transpose(1, 0, 2, 3, 4).reshape(
        heads_here, shard_count * CAP, BLOCK, HEAD_DIM
    )
    key_table = jnp.concatenate([key_heads, fetched_keys], axis=1)
    value_table = jnp.concatenate([value_heads, fetched_values], axis=1)
    local_ids = lax.broadcasted_iota(jnp.int32, (1, shard_count, local_blocks), 2)
    owner_grid = lax.broadcasted_iota(jnp.int32, (1, shard_count, local_blocks), 1)
    position = jnp.where(
        owner_grid == shard_here, local_ids, local_blocks + owner_grid * CAP + slot_of
    )
    position = position.reshape(heads_here, all_blocks)
    key_lists = jnp.sum(jnp.where(matches, position[:, None, None, :], 0), axis=3)
    attended = jax.vmap(block_attention)(
        query_table, key_table, value_table, key_lists, block_count
    )
    attended = attended.transpose(1, 2, 0, 3).reshape(row_count, heads_here * HEAD_DIM)
    contribution = jnp.dot(attended, out_weight[0], preferred_element_type=jnp.float32)
    signed = (2.0 * lax.axis_index("role").astype(jnp.float32) - 1.0) * contribution
    return lax.psum_scatter(
        signed.astype(jnp.bfloat16), ("role", "head"), scatter_dimension=1, tiled=True
    ).astype(jnp.float32)


VMEM_BYTES = 56 * 1024 * 1024
CORES = 2


def whole_in_vmem():
    return pl.BlockSpec(memory_space=pltpu.VMEM)


def in_hbm():
    return pl.BlockSpec(memory_space=pl.ANY)


def in_smem():
    return pl.BlockSpec(memory_space=pltpu.SMEM)


def cut_columns(weight, chips, head, extra=None):
    rows, columns = weight.shape
    wide = 3 * HEAD_DIM
    chip_heads = columns // (chips * wide)
    more = 0 if extra is None else extra.shape[1]

    def body(weight_ref, *refs):
        out_ref = refs[-1]
        out_ref[0, :rows] = weight_ref[...]
        if more:
            out_ref[0, rows:] = refs[0][0]

    in_specs = [pl.BlockSpec((rows, wide), lambda chip: (0, chip * chip_heads + head))]
    operands = [weight]
    if more:
        in_specs.append(pl.BlockSpec((1, more, wide), lambda chip: (chip, 0, 0)))
        operands.append(extra)
    return pl.pallas_call(
        body,
        grid=(chips,),
        in_specs=in_specs,
        out_specs=pl.BlockSpec((1, rows + more, wide), lambda chip: (chip, 0, 0)),
        out_shape=jax.ShapeDtypeStruct((chips, rows + more, wide), weight.dtype),
        name="cut_columns",
    )(*operands)


def project_heads(places, gains, rounds, depth, weights_own, weights_other):
    heads = len(weights_own)
    slabs, _, columns = weights_own[0].shape
    tokens, features = rounds[0][0].shape
    pieces = [piece for one in rounds for piece in one]
    turns = len(rounds)
    most = max(len(one) for one in rounds)
    joint = 2 if slabs % 2 == 0 else 1
    dtype = weights_own[0].dtype

    def body(places_ref, gains_ref, *refs):
        own_refs, other_refs = refs[:heads], refs[heads : 2 * heads]
        piece_refs = refs[2 * heads : 2 * heads + len(pieces)]
        query_ref, kv_ref = refs[2 * heads + len(pieces) : 2 * heads + len(pieces) + 2]
        table, rows, weight_sems, row_sems = refs[2 * heads + len(pieces) + 2 :]
        core = places_ref[slabs]
        copies = []
        for slab in range(slabs):
            here = []
            for head in range(heads):
                for side, ref in enumerate((own_refs[head], other_refs[head])):
                    place = core if side == 0 else 1 - core
                    here.append(
                        pltpu.make_async_copy(
                            ref.at[places_ref[slab], pl.ds(0, depth)],
                            table.at[
                                slab // joint,
                                slab % joint,
                                place,
                                :,
                                pl.ds(head * columns, columns),
                            ],
                            weight_sems.at[slab, head, side],
                        )
                    )
            at = 0
            for turn in range(turns):
                first = turn * tokens
                for which in range(len(rounds[turn])):
                    if min(which, slabs - 1) == slab:
                        count = rounds[turn][which].shape[0]
                        here.append(
                            pltpu.make_async_copy(
                                piece_refs[at],
                                rows.at[
                                    slab // joint,
                                    pl.ds(first, count),
                                    pl.ds(slab % joint * features, features),
                                ],
                                row_sems.at[which, turn],
                            )
                        )
                        first += count
                    at += 1
            for copy in here:
                copy.start()
            copies.append(here)
        total = None
        for group in range(slabs // joint):
            for slab in range(group * joint, (group + 1) * joint):
                for copy in copies[slab]:
                    copy.wait()
            part = jnp.dot(
                rows[group],
                table[group].reshape(joint * CORES * depth, heads * columns),
                preferred_element_type=jnp.float32,
            )
            total = part if total is None else total + part
        for turn in range(turns):
            here = total[turn * tokens : (turn + 1) * tokens]
            for head in range(heads):
                at = head * columns
                for which in range(2):
                    block = here[:, at + which * HEAD_DIM : at + (which + 1) * HEAD_DIM]
                    normal = (rms_rows(block) * gains_ref[which, head]).astype(dtype)
                    if which == 0:
                        query_ref[head, turn] = normal
                    else:
                        kv_ref[head, 0, turn] = normal
                block = here[:, at + 2 * HEAD_DIM : at + 3 * HEAD_DIM]
                kv_ref[head, 1, turn] = block.astype(dtype)

    return pl.pallas_call(
        body,
        in_specs=[in_smem(), in_smem()] + [in_hbm()] * (2 * heads + len(pieces)),
        out_specs=(whole_in_vmem(), whole_in_vmem()),
        out_shape=(
            jax.ShapeDtypeStruct((heads, turns, tokens, HEAD_DIM), dtype),
            jax.ShapeDtypeStruct((heads, 2, turns, tokens, HEAD_DIM), dtype),
        ),
        scratch_shapes=[
            pltpu.VMEM((slabs // joint, joint, CORES, depth, heads * columns), dtype),
            pltpu.VMEM((slabs // joint, turns * tokens, joint * features), dtype),
            pltpu.SemaphoreType.DMA((slabs, heads, 2)),
            pltpu.SemaphoreType.DMA((most, turns)),
        ],
        compiler_params=pltpu.CompilerParams(vmem_limit_bytes=VMEM_BYTES),
        name="project_heads",
    )(places, gains, *weights_own, *weights_other, *pieces)


def attend(first_head, heads, key_slots, counts, query_slots, group_most, parts):
    _, blocks, most = key_slots.shape
    groups = group_most.shape[1]
    together = blocks // groups
    scale = 1.0 / math.sqrt(HEAD_DIM)
    dtype = parts[0][4].dtype
    arrays = [array for part in parts for array in part[4:]]

    def body(slots_ref, counts_ref, from_ref, most_ref, *refs):
        out_ref, query_table, table, sems = refs[len(arrays) :]
        copies = []
        for at, (head, size, block, span, _, _, _) in enumerate(parts):
            query_part, own_part, other_part = refs[3 * at : 3 * at + 3]
            rows = pl.ds(head, size)
            copies.append(
                pltpu.make_async_copy(
                    query_part, query_table.at[rows, pl.ds(block, span)], sems.at[at, 0]
                )
            )
            for side, ref in enumerate((own_part, other_part)):
                place = pl.ds(side * blocks + block, span)
                copies.append(
                    pltpu.make_async_copy(ref, table.at[rows, :, place], sems.at[at, 1 + side])
                )
        for copy in copies:
            copy.start()
        for copy in copies:
            copy.wait()

        def run(head, group, listed, batch):
            for first in range(0, together, batch):
                spots = [group * together + at for at in range(first, min(first + batch, together))]
                slots = [[slots_ref[first_head + head, at, entry] for entry in range(listed)] for at in spots]
                scores = []
                for at, listing in zip(spots, slots):
                    keys = jnp.concatenate([table[head, 0, slot] for slot in listing], axis=0)
                    scores.append(
                        lax.dot_general(
                            query_table[head, from_ref[at]],
                            keys,
                            (((1,), (1,)), ((), ())),
                            preferred_element_type=jnp.float32,
                        )
                    )
                column = lax.broadcasted_iota(jnp.int32, (1, listed * BLOCK), 1)
                scores = [
                    jnp.where(column < counts_ref[first_head + head, at] * BLOCK, one * scale, -jnp.inf)
                    for at, one in zip(spots, scores)
                ]
                highest = [jnp.max(one, axis=1, keepdims=True) for one in scores]
                raised = [jnp.exp(one - top) for one, top in zip(scores, highest)]
                inverse = [1.0 / jnp.sum(one, axis=1, keepdims=True) for one in raised]
                weights = [(one * by).astype(dtype) for one, by in zip(raised, inverse)]
                mixed = []
                for one, listing in zip(weights, slots):
                    values = jnp.concatenate([table[head, 1, slot] for slot in listing], axis=0)
                    mixed.append(jnp.dot(one, values, preferred_element_type=jnp.float32))
                for at, one in enumerate(mixed):
                    out_ref[group, head, first + at] = one.astype(dtype)

        def step(at, carry):
            head, group = at // groups, at % groups
            few = most_ref[first_head + head, group] <= most // 2

            @pl.when(few)
            def _():
                run(head, group, most // 2, 6)

            @pl.when(jnp.logical_not(few))
            def _():
                run(head, group, most, 3)

            return carry

        lax.fori_loop(0, heads * groups, step, 0)

    return pl.pallas_call(
        body,
        in_specs=[in_smem()] * 4 + [in_hbm()] * len(arrays),
        out_specs=whole_in_vmem(),
        out_shape=jax.ShapeDtypeStruct((groups, heads, together, BLOCK, HEAD_DIM), dtype),
        scratch_shapes=[
            pltpu.VMEM((heads, blocks, BLOCK, HEAD_DIM), dtype),
            pltpu.VMEM((heads, 2, CORES * blocks, BLOCK, HEAD_DIM), dtype),
            pltpu.SemaphoreType.DMA((len(parts), 3)),
        ],
        compiler_params=pltpu.CompilerParams(vmem_limit_bytes=VMEM_BYTES),
        name="attend",
    )(key_slots, counts, query_slots, group_most, *arrays)


def out_blocks(which, sign, attended, place, out_weight, blocks, dtypes, before=None, skip=0):
    groups, heads, tokens, _ = attended.shape
    depth, features = out_weight.shape
    width = features // blocks
    wanted = which.shape[0]
    rows = heads * HEAD_DIM
    weight = out_weight.reshape(groups, depth // groups, features)
    stacked = len(dtypes) == 1 and wanted > 1

    def body(which_ref, sign_ref, mixed_ref, weight_ref, *refs):
        out_refs = refs if before is None else refs[1:]
        joined = jnp.concatenate(
            [mixed_ref[group, head] for group in range(groups) for head in range(heads)], axis=1
        )
        total = jnp.dot(
            joined,
            weight_ref[...].reshape(groups * rows, width),
            preferred_element_type=jnp.float32,
        )
        total = total * sign_ref[0].astype(jnp.float32)
        if before is not None:
            total = total + refs[0][0].astype(jnp.float32)
        if stacked:
            out_refs[0][0] = total.astype(dtypes[0])
        else:
            for at in range(wanted):

                @pl.when(pl.program_id(0) == at)
                def _(at=at):
                    out_refs[at][...] = total.astype(dtypes[at])

    in_specs = [
        pl.BlockSpec(attended.shape, lambda i, w, s: (0, 0, 0, 0)),
        pl.BlockSpec((groups, rows, width), lambda i, w, s: (0, place, w[i])),
    ]
    operands = [attended, weight]
    if before is not None:
        in_specs.append(pl.BlockSpec((1, tokens, width), lambda i, w, s: (i + skip, 0, 0)))
        operands.append(before)
    if stacked:
        out_specs = [pl.BlockSpec((1, tokens, width), lambda i, w, s: (i, 0, 0))]
        out_shape = [jax.ShapeDtypeStruct((wanted, tokens, width), dtypes[0])]
    else:
        out_specs = [pl.BlockSpec((tokens, width), lambda i, w, s: (0, 0))] * wanted
        out_shape = [jax.ShapeDtypeStruct((tokens, width), dtype) for dtype in dtypes]
    return pl.pallas_call(
        body,
        grid_spec=pltpu.PrefetchScalarGridSpec(
            num_scalar_prefetch=2, grid=(wanted,), in_specs=in_specs, out_specs=out_specs
        ),
        out_shape=out_shape,
        compiler_params=pltpu.CompilerParams(vmem_limit_bytes=VMEM_BYTES),
        name="out_blocks",
    )(which, sign, *operands)


def chunk_sizes(heads):
    last = heads // 3 if heads % 3 == 0 else 1
    return [heads - last, last] if heads > last else [heads]


def per_device_by_heads(
    hidden_rows,
    gen_weight,
    noise,
    timesteps,
    qkv_weight,
    out_weight,
    qk_gain,
    block_keys,
    block_count,
):
    role, head = lax.axis_index("role"), lax.axis_index("head")
    chip, core = lax.axis_index("chip"), lax.axis_index("core")
    chips = lax.axis_size("chip")
    local_heads, local_blocks, most = block_keys.shape
    heads = local_heads // chips
    tokens = hidden_rows.shape[0]
    width = hidden_rows.shape[1]
    features = gen_weight.shape[1]
    all_blocks = chips * local_blocks
    swap = [(0, 1), (1, 0)]
    far_swap = [(0, 3), (1, 2), (2, 1), (3, 0)]
    ring = [(at, (at + 1) % chips) for at in range(chips)]

    def turn_of(other):
        return (chip - other) % chips

    def exchange(array):
        return lax.all_to_all(array, "chip", split_axis=0, concat_axis=0, tiled=True)

    weight_here = qkv_weight[0]
    depth = weight_here.shape[0]
    wide = 3 * HEAD_DIM
    lists = jnp.concatenate([block_keys, block_count[:, :, None]], axis=2)
    lists = lists.reshape(chips, -1).astype(jnp.bfloat16)
    listed = lists.shape[1]
    spare = -(-listed // (16 * wide)) * 16
    lists = jnp.pad(lists, ((0, 0), (0, spare * wide - listed))).reshape(chips, spare, wide)
    cuts = [
        cut_columns(weight_here, chips, at, lists if at == 0 else None) for at in range(heads)
    ]
    hidden_rows, cuts[0] = lax.optimization_barrier((hidden_rows, cuts[0]))
    weights_own = [exchange(cuts[0])]
    weights_other = []

    mine = role * lax.axis_size("head") + head
    generated = jnp.dot(hidden_rows, gen_weight, preferred_element_type=jnp.float32)
    generated = lax.reduce_precision(generated, 8, 7)
    angle_blocks = (timesteps.astype(jnp.float32) * (math.pi / 2000.0))[:, None, None]
    noise_here = lax.dynamic_slice_in_dim(noise, mine * features, features, axis=1)
    noisy = jnp.cos(angle_blocks) * generated.reshape(local_blocks, BLOCK, features)
    noisy = noisy + jnp.sin(angle_blocks) * noise_here.astype(jnp.float32).reshape(
        local_blocks, BLOCK, features
    )
    squares = jnp.sum(noisy * noisy, axis=-1)
    squares = squares + lax.ppermute(squares, "role", swap)
    squares = squares + lax.ppermute(squares, "head", swap)
    normed = (noisy * lax.rsqrt(squares / width + 1e-06)[:, :, None]).astype(jnp.bfloat16)
    normed = normed.reshape(tokens, features)

    def tables_of(lists):
        lists = lists.reshape(chips, spare * wide)[:, :listed].astype(jnp.int32)
        lists = lists.reshape(chips, heads, local_blocks, most + 1).transpose(1, 0, 2, 3)
        lists = lists.reshape(heads, all_blocks, most + 1)
        owner = lists[:, :, :most] // local_blocks
        turn = turn_of(owner // CORES)
        far = (owner % CORES != core).astype(jnp.int32)
        key_slots = far * all_blocks + turn * local_blocks + lists[:, :, :most] % local_blocks
        counts = lists[:, :, most]
        group_most = jnp.max(counts.reshape(heads, chips, local_blocks), axis=2)
        spot = jnp.arange(all_blocks, dtype=jnp.int32)
        query_slots = turn_of(spot // local_blocks)
        query_slots = query_slots * local_blocks + spot % local_blocks

        return key_slots, counts, query_slots, group_most

    sides = lax.axis_size("head")
    peers = jnp.stack(
        [
            role * sides + head,
            (1 - role) * sides + head,
            role * sides + 1 - head,
            (1 - role) * sides + 1 - head,
        ]
    ).astype(jnp.int32)
    places = jnp.concatenate([peers, core[None].astype(jnp.int32)])
    gains = lax.dynamic_slice_in_dim(qk_gain[0], chip * heads, heads, axis=1)

    chunks = chunk_sizes(heads)
    spans = [slice(sum(chunks[:at]), sum(chunks[: at + 1])) for at in range(len(chunks))]
    parts = [[] for _ in chunks]

    def project(chunk, first, size, begin, some, places):
        at = spans[chunk].start + first
        span = slice(at, at + size)
        query, kv = project_heads(
            places, gains[:, span], some, depth, weights_own[span], weights_other[span]
        )
        here = len(some) * local_blocks
        kv = kv.reshape(size, 2, here, BLOCK, HEAD_DIM)
        kv_other = lax.ppermute(kv, "core", swap)
        query = query.reshape(size, here, BLOCK, HEAD_DIM)
        parts[chunk].append((first, size, begin * local_blocks, here, query, kv, kv_other))
        return lax.optimization_barrier((places, kv))[0]

    sign = (2 * role - 1).astype(jnp.int32)[None]
    blocks = sides * lax.axis_size("role")
    which = jnp.stack([peers[3], peers[2], peers[1], peers[0]])
    out_here = out_weight[0]
    out_width = out_here.shape[1] // blocks
    place = spans[-1].start // chunks[-1]

    half = tokens // 2
    rounds = []
    straight = None
    held_places = places
    shard = normed
    for phase in range(chips + 1):
        step = phase + 1
        sent = {}
        if phase < chips:
            sent["role"] = lax.ppermute(shard, "role", swap)
            sent["head"] = lax.ppermute(shard, "head", swap)
        if straight is not None:
            sent["first"] = lax.ppermute(straight[2][:half], "role", swap)
            sent["second"] = lax.ppermute(straight[1][half:], "head", swap)
        if step < chips:
            sent["next"] = lax.ppermute(shard, "chip", ring)
        if phase == 0:
            sent["weights"] = weights_own.pop()
            sent["cuts"] = cuts[1:]
        if phase == 1:
            sent["places"] = places
            sent["gains"] = gains
            sent["corner"] = lax.dynamic_slice(
                out_here.reshape(chips, heads * HEAD_DIM, -1),
                (0, spans[-1].start * HEAD_DIM, which[0] * out_width),
                (chips, chunks[-1] * HEAD_DIM, out_width),
            )
        if step == chips:
            weights_other.append(lax.ppermute(weights_own[0], "core", swap))
            early = list(rounds)
            tables = tables_of(weights_own[0][:, depth:])
            held_places, tables = lax.optimization_barrier((held_places, tables))
            sent["places"] = project(0, 0, 1, 0, early, held_places)
        if step > chips and chunks[0] > 1:
            weights_other.append(lax.ppermute(weights_own[1], "core", swap))
            sent["places"] = project(0, 1, 1, 0, early, held_places)
        sent, shard = lax.optimization_barrier((sent, shard))
        if phase == 0:
            weights_own.append(sent["weights"])
            cuts[1:] = sent["cuts"]
        if phase == 1:
            gains, corner = sent["gains"], sent["corner"]
        if straight is not None:
            rounds.append(straight + (sent["first"], sent["second"]))
        held_places = sent.get("places", held_places)
        if phase < chips:
            straight = (shard, sent["role"], sent["head"])
        if step < chips:
            shard = sent["next"]
        if chips - 2 <= phase and len(weights_own) < heads:
            held, _ = lax.optimization_barrier((cuts[len(weights_own)], sent))
            weights_own.append(exchange(held))
    while len(weights_own) < heads:
        weights_own.append(exchange(cuts[len(weights_own)]))
    for at in range(len(weights_other), heads - 1):
        weights_other.append(lax.ppermute(weights_own[at], "core", swap))

    corner, held_places = lax.optimization_barrier((corner, held_places))
    far_weight = lax.ppermute(corner, ("role", "head"), far_swap)
    attended = []
    received = []
    for chunk, size in enumerate(chunks):
        last = chunk == len(chunks) - 1
        if chunk == 0:
            for at in range(min(size, 2), size):
                held_places = project(0, at, 1, 0, early, held_places)
            held_places = project(0, 0, size, len(early), rounds[len(early) :], held_places)
        else:
            held_places = project(chunk, 0, size, 0, rounds, held_places)
        if last:
            for earlier in range(len(attended)):
                (diagonal,) = out_blocks(
                    which[:1], sign, attended[earlier], spans[earlier].start // chunks[earlier],
                    out_here, blocks, (jnp.bfloat16,),
                )
                tables, diagonal, far_weight = lax.optimization_barrier(
                    (tables, diagonal, far_weight)
                )
                received.append(lax.ppermute(diagonal, ("role", "head"), far_swap))
        mixed = attend(spans[chunk].start, size, *tables, parts[chunk])
        held_places, mixed = lax.optimization_barrier((held_places, mixed))
        if chunk == 0:
            for at in range(len(weights_other), heads):
                weights_own[at], held_places = lax.optimization_barrier(
                    (weights_own[at], held_places)
                )
                weights_other.append(lax.ppermute(weights_own[at], "core", swap))
        mixed = mixed.reshape(chips, size, tokens, HEAD_DIM)
        if attended:
            mixed, attended = lax.optimization_barrier((mixed, attended))
        attended.append(exchange(mixed))

    def contributions(wanted, dtypes, before=None):
        for chunk, size in enumerate(chunks[:-1]):
            before = jnp.stack(
                out_blocks(
                    wanted, sign, attended[chunk], spans[chunk].start // size, out_here, blocks,
                    (jnp.float32,), before,
                )
            ).reshape(-1, tokens, out_width)
        wanted, _ = lax.optimization_barrier((wanted, received[0]))
        return out_blocks(wanted, sign, attended[-1], place, out_here, blocks, dtypes, before)

    far_attended = lax.ppermute(attended[-1], ("role", "head"), far_swap)
    over_head, over_role = contributions(which[1:3], (jnp.bfloat16, jnp.bfloat16))
    (over_head, over_role), far_attended = lax.optimization_barrier(
        ((over_head, over_role), far_attended)
    )
    received.append(lax.ppermute(over_head, "head", swap))
    received.append(lax.ppermute(over_role, "role", swap))
    (far,) = out_blocks(
        jnp.zeros_like(which[:1]), -sign, far_attended, 0, far_weight.reshape(-1, out_width), 1,
        (jnp.float32,), received[0][None],
    )
    (own,) = contributions(which[3:], (jnp.float32,), far[None])
    total = received[1].astype(jnp.float32)
    for one in received[2:]:
        total = total + one.astype(jnp.float32)
    return own + total


def splits_heads(mesh, qkv_weight, hidden_rows):
    role, seq, head = (mesh.shape[name] for name in ("role", "seq", "head"))
    if role != 2 or head != 2 or seq % CORES != 0:
        return False
    chips = seq // CORES
    heads = qkv_weight.shape[2] // (3 * HEAD_DIM * head)
    width = hidden_rows.shape[1]
    tokens = hidden_rows.shape[0] // seq
    return (
        heads % chips == 0
        and heads // chips > 1
        and chips == role * head
        and width % (role * head * 256) == 0
        and width % (seq * 16) == 0
        and tokens % (2 * BLOCK) == 0
        and hidden_rows.shape[0] // BLOCK <= 256
    )


def solution(mesh):
    def call(*arrays):
        if splits_heads(mesh, arrays[4], arrays[0]):
            per_device = per_device_by_heads
            seq = ("chip", "core")
            shape = mesh.devices.shape
            names = mesh.axis_names
            at = names.index("seq")
            layout = Mesh(
                mesh.devices.reshape(shape[:at] + (shape[at] // CORES, CORES) + shape[at + 1 :]),
                names[:at] + seq + names[at + 1 :],
            )
        else:
            per_device = per_device_by_tokens
            seq = "seq"
            layout = mesh
        placed = (
            P(seq, None),
            P(None, ("role", "head")),
            P(seq, None),
            P(seq),
            P("role", seq, "head"),
            P("role", "head", None),
            P("role", None, "head"),
            P("head", seq, None),
            P("head", seq),
        )
        return jax.shard_map(
            per_device,
            mesh=layout,
            in_specs=placed,
            out_specs=P(seq, ("role", "head")),
            check_vma=False,
        )(*arrays)

    return call
```

```python
import math

import jax
import jax.numpy as jnp
from jax import lax
from jax.experimental import pallas as pl
from jax.experimental.pallas import tpu as pltpu
from jax.sharding import Mesh
from jax.sharding import PartitionSpec as P

HEAD_DIM = 128
BLOCK = 64
KMAX = 8
CAP = 2


def rms_rows(values):
    return values * lax.rsqrt(jnp.mean(values * values, axis=-1, keepdims=True) + 1e-06)


def block_attention(queries, key_table, value_table, key_list, key_count):
    picked_keys = key_table[key_list]
    picked_values = value_table[key_list]
    scale = 1.0 / math.sqrt(HEAD_DIM)
    scores = (
        jnp.einsum("nqe,nkbe->nqkb", queries, picked_keys, preferred_element_type=jnp.float32)
        * scale
    )
    live = lax.broadcasted_iota(jnp.int32, (key_list.shape[0], KMAX), 1) < key_count[:, None]
    scores = jnp.where(live[:, None, :, None], scores, -jnp.inf)
    highest = jnp.max(scores, axis=(2, 3), keepdims=True)
    raised = jnp.exp(scores - highest)
    summed = jnp.sum(raised, axis=(2, 3), keepdims=True)
    weights = (raised / summed).astype(jnp.bfloat16)
    mixed = jnp.einsum("nqkb,nkbe->nqe", weights, picked_values, preferred_element_type=jnp.float32)
    return mixed.astype(jnp.bfloat16)


def pick_blocks(table, wanted):
    return table[wanted]


def per_device_by_tokens(
    hidden_rows,
    gen_weight,
    noise,
    timesteps,
    qkv_weight,
    out_weight,
    qk_gain,
    block_keys,
    block_count,
):
    generated = jnp.dot(hidden_rows, gen_weight, preferred_element_type=jnp.float32).astype(
        jnp.bfloat16
    )
    forked = lax.all_gather(generated, ("role", "head"), axis=1, tiled=True)
    row_count = forked.shape[0]
    width = forked.shape[1]
    local_blocks = timesteps.shape[0]
    angle_blocks = (timesteps.astype(jnp.float32) * (math.pi / 2000.0))[:, None, None]
    noisy = jnp.cos(angle_blocks) * forked.astype(jnp.float32).reshape(local_blocks, BLOCK, width)
    noisy = noisy + jnp.sin(angle_blocks) * noise.astype(jnp.float32).reshape(
        local_blocks, BLOCK, width
    )
    normed = rms_rows(noisy).reshape(row_count, width).astype(jnp.bfloat16)
    weight_here = qkv_weight[0]
    projected = jnp.dot(
        normed,
        lax.all_gather(weight_here, "seq", axis=0, tiled=True),
        preferred_element_type=jnp.float32,
    )
    heads_here = projected.shape[1] // (3 * HEAD_DIM)
    head_parts = projected.reshape(row_count, heads_here, 3, HEAD_DIM)
    gain_here = qk_gain[0]
    queries = (rms_rows(head_parts[:, :, 0]) * gain_here[0][None, :, None]).astype(jnp.bfloat16)
    key_local = (rms_rows(head_parts[:, :, 1]) * gain_here[1][None, :, None]).astype(jnp.bfloat16)
    value_local = head_parts[:, :, 2].astype(jnp.bfloat16)
    query_table = queries.reshape(local_blocks, BLOCK, heads_here, HEAD_DIM).transpose(2, 0, 1, 3)
    shard_count = lax.axis_size("seq")
    shard_here = lax.axis_index("seq")
    all_blocks = shard_count * local_blocks
    key_heads = key_local.reshape(local_blocks, BLOCK, heads_here, HEAD_DIM).transpose(2, 0, 1, 3)
    value_heads = value_local.reshape(local_blocks, BLOCK, heads_here, HEAD_DIM).transpose(
        2, 0, 1, 3
    )
    block_ids = lax.broadcasted_iota(jnp.int32, (1, 1, 1, all_blocks), 3)
    matches = block_keys[:, :, :, None] == block_ids
    remote = block_ids // local_blocks != shard_here
    needed = jnp.any(jnp.logical_and(matches, remote), axis=(1, 2))
    needed = needed.reshape(heads_here, shard_count, local_blocks)
    slot_of = jnp.cumsum(needed.astype(jnp.int32), axis=2) - 1
    slot_ids = lax.broadcasted_iota(jnp.int32, (1, 1, 1, CAP), 3)
    within_ids = lax.broadcasted_iota(jnp.int32, (1, 1, local_blocks, 1), 2)
    chosen_slot = jnp.logical_and(needed[..., None], slot_of[..., None] == slot_ids)
    requests = jnp.sum(jnp.where(chosen_slot, within_ids, 0), axis=2)
    asked = lax.all_to_all(
        requests.transpose(1, 0, 2), "seq", split_axis=0, concat_axis=0, tiled=True
    )
    sent_keys = jax.vmap(pick_blocks, in_axes=(0, 1), out_axes=1)(key_heads, asked)
    sent_values = jax.vmap(pick_blocks, in_axes=(0, 1), out_axes=1)(value_heads, asked)
    got_keys, got_values = (
        lax.all_to_all(sent_keys, "seq", split_axis=0, concat_axis=0, tiled=True),
        lax.all_to_all(sent_values, "seq", split_axis=0, concat_axis=0, tiled=True),
    )
    fetched_keys = got_keys.transpose(1, 0, 2, 3, 4).reshape(
        heads_here, shard_count * CAP, BLOCK, HEAD_DIM
    )
    fetched_values = got_values.transpose(1, 0, 2, 3, 4).reshape(
        heads_here, shard_count * CAP, BLOCK, HEAD_DIM
    )
    key_table = jnp.concatenate([key_heads, fetched_keys], axis=1)
    value_table = jnp.concatenate([value_heads, fetched_values], axis=1)
    local_ids = lax.broadcasted_iota(jnp.int32, (1, shard_count, local_blocks), 2)
    owner_grid = lax.broadcasted_iota(jnp.int32, (1, shard_count, local_blocks), 1)
    position = jnp.where(
        owner_grid == shard_here, local_ids, local_blocks + owner_grid * CAP + slot_of
    )
    position = position.reshape(heads_here, all_blocks)
    key_lists = jnp.sum(jnp.where(matches, position[:, None, None, :], 0), axis=3)
    attended = jax.vmap(block_attention)(
        query_table, key_table, value_table, key_lists, block_count
    )
    attended = attended.transpose(1, 2, 0, 3).reshape(row_count, heads_here * HEAD_DIM)
    contribution = jnp.dot(attended, out_weight[0], preferred_element_type=jnp.float32)
    signed = (2.0 * lax.axis_index("role").astype(jnp.float32) - 1.0) * contribution
    return lax.psum_scatter(
        signed.astype(jnp.bfloat16), ("role", "head"), scatter_dimension=1, tiled=True
    ).astype(jnp.float32)


VMEM_BYTES = 56 * 1024 * 1024
CORES = 2


def whole_in_vmem():
    return pl.BlockSpec(memory_space=pltpu.VMEM)


def in_hbm():
    return pl.BlockSpec(memory_space=pl.ANY)


def in_smem():
    return pl.BlockSpec(memory_space=pltpu.SMEM)


def cut_columns(weight, chips, head, extra=None):
    rows, columns = weight.shape
    wide = 3 * HEAD_DIM
    chip_heads = columns // (chips * wide)
    more = 0 if extra is None else extra.shape[1]

    def body(weight_ref, *refs):
        out_ref = refs[-1]
        out_ref[0, :rows] = weight_ref[...]
        if more:
            out_ref[0, rows:] = refs[0][0]

    in_specs = [pl.BlockSpec((rows, wide), lambda chip: (0, chip * chip_heads + head))]
    operands = [weight]
    if more:
        in_specs.append(pl.BlockSpec((1, more, wide), lambda chip: (chip, 0, 0)))
        operands.append(extra)
    return pl.pallas_call(
        body,
        grid=(chips,),
        in_specs=in_specs,
        out_specs=pl.BlockSpec((1, rows + more, wide), lambda chip: (chip, 0, 0)),
        out_shape=jax.ShapeDtypeStruct((chips, rows + more, wide), weight.dtype),
        name="cut_columns",
    )(*operands)


def project_heads(places, gains, rounds, depth, weights_own, weights_other):
    heads = len(weights_own)
    slabs, _, columns = weights_own[0].shape
    tokens, features = rounds[0][0].shape
    pieces = [piece for one in rounds for piece in one]
    turns = len(rounds)
    most = max(len(one) for one in rounds)
    joint = 2 if slabs % 2 == 0 else 1
    dtype = weights_own[0].dtype

    def body(places_ref, gains_ref, *refs):
        own_refs, other_refs = refs[:heads], refs[heads : 2 * heads]
        piece_refs = refs[2 * heads : 2 * heads + len(pieces)]
        query_ref, kv_ref = refs[2 * heads + len(pieces) : 2 * heads + len(pieces) + 2]
        table, rows, weight_sems, row_sems = refs[2 * heads + len(pieces) + 2 :]
        core = places_ref[slabs]
        copies = []
        for slab in range(slabs):
            here = []
            for head in range(heads):
                for side, ref in enumerate((own_refs[head], other_refs[head])):
                    place = core if side == 0 else 1 - core
                    here.append(
                        pltpu.make_async_copy(
                            ref.at[places_ref[slab], pl.ds(0, depth)],
                            table.at[
                                slab // joint,
                                slab % joint,
                                place,
                                :,
                                pl.ds(head * columns, columns),
                            ],
                            weight_sems.at[slab, head, side],
                        )
                    )
            at = 0
            for turn in range(turns):
                first = turn * tokens
                for which in range(len(rounds[turn])):
                    if min(which, slabs - 1) == slab:
                        count = rounds[turn][which].shape[0]
                        here.append(
                            pltpu.make_async_copy(
                                piece_refs[at],
                                rows.at[
                                    slab // joint,
                                    pl.ds(first, count),
                                    pl.ds(slab % joint * features, features),
                                ],
                                row_sems.at[which, turn],
                            )
                        )
                        first += count
                    at += 1
            for copy in here:
                copy.start()
            copies.append(here)
        total = None
        for group in range(slabs // joint):
            for slab in range(group * joint, (group + 1) * joint):
                for copy in copies[slab]:
                    copy.wait()
            part = jnp.dot(
                rows[group],
                table[group].reshape(joint * CORES * depth, heads * columns),
                preferred_element_type=jnp.float32,
            )
            total = part if total is None else total + part
        for turn in range(turns):
            here = total[turn * tokens : (turn + 1) * tokens]
            for head in range(heads):
                at = head * columns
                for which in range(2):
                    block = here[:, at + which * HEAD_DIM : at + (which + 1) * HEAD_DIM]
                    normal = (rms_rows(block) * gains_ref[which, head]).astype(dtype)
                    if which == 0:
                        query_ref[head, turn] = normal
                    else:
                        kv_ref[head, 0, turn] = normal
                block = here[:, at + 2 * HEAD_DIM : at + 3 * HEAD_DIM]
                kv_ref[head, 1, turn] = block.astype(dtype)

    return pl.pallas_call(
        body,
        in_specs=[in_smem(), in_smem()] + [in_hbm()] * (2 * heads + len(pieces)),
        out_specs=(whole_in_vmem(), whole_in_vmem()),
        out_shape=(
            jax.ShapeDtypeStruct((heads, turns, tokens, HEAD_DIM), dtype),
            jax.ShapeDtypeStruct((heads, 2, turns, tokens, HEAD_DIM), dtype),
        ),
        scratch_shapes=[
            pltpu.VMEM((slabs // joint, joint, CORES, depth, heads * columns), dtype),
            pltpu.VMEM((slabs // joint, turns * tokens, joint * features), dtype),
            pltpu.SemaphoreType.DMA((slabs, heads, 2)),
            pltpu.SemaphoreType.DMA((most, turns)),
        ],
        compiler_params=pltpu.CompilerParams(vmem_limit_bytes=VMEM_BYTES),
        name="project_heads",
    )(places, gains, *weights_own, *weights_other, *pieces)


def attend(first_head, heads, key_slots, counts, query_slots, group_most, parts):
    _, blocks, most = key_slots.shape
    groups = group_most.shape[1]
    together = blocks // groups
    scale = 1.0 / math.sqrt(HEAD_DIM)
    dtype = parts[0][4].dtype
    arrays = [array for part in parts for array in part[4:]]

    def body(slots_ref, counts_ref, from_ref, most_ref, *refs):
        out_ref, query_table, table, sems = refs[len(arrays) :]
        copies = []
        for at, (head, size, block, span, _, _, _) in enumerate(parts):
            query_part, own_part, other_part = refs[3 * at : 3 * at + 3]
            rows = pl.ds(head, size)
            copies.append(
                pltpu.make_async_copy(
                    query_part, query_table.at[rows, pl.ds(block, span)], sems.at[at, 0]
                )
            )
            for side, ref in enumerate((own_part, other_part)):
                place = pl.ds(side * blocks + block, span)
                copies.append(
                    pltpu.make_async_copy(ref, table.at[rows, :, place], sems.at[at, 1 + side])
                )
        for copy in copies:
            copy.start()
        for copy in copies:
            copy.wait()

        def run(head, group, listed, batch):
            for first in range(0, together, batch):
                spots = [group * together + at for at in range(first, min(first + batch, together))]
                slots = [[slots_ref[first_head + head, at, entry] for entry in range(listed)] for at in spots]
                scores = []
                for at, listing in zip(spots, slots):
                    keys = jnp.concatenate([table[head, 0, slot] for slot in listing], axis=0)
                    scores.append(
                        lax.dot_general(
                            query_table[head, from_ref[at]],
                            keys,
                            (((1,), (1,)), ((), ())),
                            preferred_element_type=jnp.float32,
                        )
                    )
                column = lax.broadcasted_iota(jnp.int32, (1, listed * BLOCK), 1)
                scores = [
                    jnp.where(column < counts_ref[first_head + head, at] * BLOCK, one * scale, -jnp.inf)
                    for at, one in zip(spots, scores)
                ]
                highest = [jnp.max(one, axis=1, keepdims=True) for one in scores]
                raised = [jnp.exp(one - top) for one, top in zip(scores, highest)]
                inverse = [1.0 / jnp.sum(one, axis=1, keepdims=True) for one in raised]
                weights = [(one * by).astype(dtype) for one, by in zip(raised, inverse)]
                mixed = []
                for one, listing in zip(weights, slots):
                    values = jnp.concatenate([table[head, 1, slot] for slot in listing], axis=0)
                    mixed.append(jnp.dot(one, values, preferred_element_type=jnp.float32))
                for at, one in enumerate(mixed):
                    out_ref[group, head, first + at] = one.astype(dtype)

        def step(at, carry):
            head, group = at // groups, at % groups
            few = most_ref[first_head + head, group] <= most // 2

            @pl.when(few)
            def _():
                run(head, group, most // 2, 6)

            @pl.when(jnp.logical_not(few))
            def _():
                run(head, group, most, 3)

            return carry

        lax.fori_loop(0, heads * groups, step, 0)

    return pl.pallas_call(
        body,
        in_specs=[in_smem()] * 4 + [in_hbm()] * len(arrays),
        out_specs=whole_in_vmem(),
        out_shape=jax.ShapeDtypeStruct((groups, heads, together, BLOCK, HEAD_DIM), dtype),
        scratch_shapes=[
            pltpu.VMEM((heads, blocks, BLOCK, HEAD_DIM), dtype),
            pltpu.VMEM((heads, 2, CORES * blocks, BLOCK, HEAD_DIM), dtype),
            pltpu.SemaphoreType.DMA((len(parts), 3)),
        ],
        compiler_params=pltpu.CompilerParams(vmem_limit_bytes=VMEM_BYTES),
        name="attend",
    )(key_slots, counts, query_slots, group_most, *arrays)


def out_blocks(which, sign, attended, place, out_weight, blocks, dtypes, before=None, skip=0):
    groups, heads, tokens, _ = attended.shape
    depth, features = out_weight.shape
    width = features // blocks
    wanted = which.shape[0]
    rows = heads * HEAD_DIM
    weight = out_weight.reshape(groups, depth // groups, features)
    stacked = len(dtypes) == 1 and wanted > 1

    def body(which_ref, sign_ref, mixed_ref, weight_ref, *refs):
        out_refs = refs if before is None else refs[1:]
        joined = jnp.concatenate(
            [mixed_ref[group, head] for group in range(groups) for head in range(heads)], axis=1
        )
        total = jnp.dot(
            joined,
            weight_ref[...].reshape(groups * rows, width),
            preferred_element_type=jnp.float32,
        )
        total = total * sign_ref[0].astype(jnp.float32)
        if before is not None:
            total = total + refs[0][0].astype(jnp.float32)
        if stacked:
            out_refs[0][0] = total.astype(dtypes[0])
        else:
            for at in range(wanted):

                @pl.when(pl.program_id(0) == at)
                def _(at=at):
                    out_refs[at][...] = total.astype(dtypes[at])

    in_specs = [
        pl.BlockSpec(attended.shape, lambda i, w, s: (0, 0, 0, 0)),
        pl.BlockSpec((groups, rows, width), lambda i, w, s: (0, place, w[i])),
    ]
    operands = [attended, weight]
    if before is not None:
        in_specs.append(pl.BlockSpec((1, tokens, width), lambda i, w, s: (i + skip, 0, 0)))
        operands.append(before)
    if stacked:
        out_specs = [pl.BlockSpec((1, tokens, width), lambda i, w, s: (i, 0, 0))]
        out_shape = [jax.ShapeDtypeStruct((wanted, tokens, width), dtypes[0])]
    else:
        out_specs = [pl.BlockSpec((tokens, width), lambda i, w, s: (0, 0))] * wanted
        out_shape = [jax.ShapeDtypeStruct((tokens, width), dtype) for dtype in dtypes]
    return pl.pallas_call(
        body,
        grid_spec=pltpu.PrefetchScalarGridSpec(
            num_scalar_prefetch=2, grid=(wanted,), in_specs=in_specs, out_specs=out_specs
        ),
        out_shape=out_shape,
        compiler_params=pltpu.CompilerParams(vmem_limit_bytes=VMEM_BYTES),
        name="out_blocks",
    )(which, sign, *operands)


def chunk_sizes(heads):
    last = heads // 3 if heads % 3 == 0 else 1
    return [heads - last, last] if heads > last else [heads]


def per_device_by_heads(
    hidden_rows,
    gen_weight,
    noise,
    timesteps,
    qkv_weight,
    out_weight,
    qk_gain,
    block_keys,
    block_count,
):
    role, head = lax.axis_index("role"), lax.axis_index("head")
    chip, core = lax.axis_index("chip"), lax.axis_index("core")
    chips = lax.axis_size("chip")
    local_heads, local_blocks, most = block_keys.shape
    heads = local_heads // chips
    tokens = hidden_rows.shape[0]
    width = hidden_rows.shape[1]
    features = gen_weight.shape[1]
    all_blocks = chips * local_blocks
    swap = [(0, 1), (1, 0)]
    far_swap = [(0, 3), (1, 2), (2, 1), (3, 0)]
    ring = [(at, (at + 1) % chips) for at in range(chips)]

    def turn_of(other):
        return (chip - other) % chips

    def exchange(array):
        return lax.all_to_all(array, "chip", split_axis=0, concat_axis=0, tiled=True)

    weight_here = qkv_weight[0]
    depth = weight_here.shape[0]
    wide = 3 * HEAD_DIM
    lists = jnp.concatenate([block_keys, block_count[:, :, None]], axis=2)
    lists = lists.reshape(chips, -1).astype(jnp.bfloat16)
    listed = lists.shape[1]
    spare = -(-listed // (16 * wide)) * 16
    lists = jnp.pad(lists, ((0, 0), (0, spare * wide - listed))).reshape(chips, spare, wide)
    cuts = [
        cut_columns(weight_here, chips, at, lists if at == 0 else None) for at in range(heads)
    ]
    hidden_rows, cuts[0] = lax.optimization_barrier((hidden_rows, cuts[0]))
    weights_own = [exchange(cuts[0])]
    weights_other = []

    mine = role * lax.axis_size("head") + head
    generated = jnp.dot(hidden_rows, gen_weight, preferred_element_type=jnp.float32)
    generated = lax.reduce_precision(generated, 8, 7)
    angle_blocks = (timesteps.astype(jnp.float32) * (math.pi / 2000.0))[:, None, None]
    noise_here = lax.dynamic_slice_in_dim(noise, mine * features, features, axis=1)
    noisy = jnp.cos(angle_blocks) * generated.reshape(local_blocks, BLOCK, features)
    noisy = noisy + jnp.sin(angle_blocks) * noise_here.astype(jnp.float32).reshape(
        local_blocks, BLOCK, features
    )
    squares = jnp.sum(noisy * noisy, axis=-1)
    squares = squares + lax.ppermute(squares, "role", swap)
    squares = squares + lax.ppermute(squares, "head", swap)
    normed = (noisy * lax.rsqrt(squares / width + 1e-06)[:, :, None]).astype(jnp.bfloat16)
    normed = normed.reshape(tokens, features)

    def tables_of(lists):
        lists = lists.reshape(chips, spare * wide)[:, :listed].astype(jnp.int32)
        lists = lists.reshape(chips, heads, local_blocks, most + 1).transpose(1, 0, 2, 3)
        lists = lists.reshape(heads, all_blocks, most + 1)
        owner = lists[:, :, :most] // local_blocks
        turn = turn_of(owner // CORES)
        far = (owner % CORES != core).astype(jnp.int32)
        key_slots = far * all_blocks + turn * local_blocks + lists[:, :, :most] % local_blocks
        counts = lists[:, :, most]
        group_most = jnp.max(counts.reshape(heads, chips, local_blocks), axis=2)
        spot = jnp.arange(all_blocks, dtype=jnp.int32)
        query_slots = turn_of(spot // local_blocks)
        query_slots = query_slots * local_blocks + spot % local_blocks

        return key_slots, counts, query_slots, group_most

    sides = lax.axis_size("head")
    peers = jnp.stack(
        [
            role * sides + head,
            (1 - role) * sides + head,
            role * sides + 1 - head,
            (1 - role) * sides + 1 - head,
        ]
    ).astype(jnp.int32)
    places = jnp.concatenate([peers, core[None].astype(jnp.int32)])
    gains = lax.dynamic_slice_in_dim(qk_gain[0], chip * heads, heads, axis=1)

    chunks = chunk_sizes(heads)
    spans = [slice(sum(chunks[:at]), sum(chunks[: at + 1])) for at in range(len(chunks))]
    parts = [[] for _ in chunks]

    def project(chunk, first, size, begin, some, places):
        at = spans[chunk].start + first
        span = slice(at, at + size)
        query, kv = project_heads(
            places, gains[:, span], some, depth, weights_own[span], weights_other[span]
        )
        here = len(some) * local_blocks
        kv = kv.reshape(size, 2, here, BLOCK, HEAD_DIM)
        kv_other = lax.ppermute(kv, "core", swap)
        query = query.reshape(size, here, BLOCK, HEAD_DIM)
        parts[chunk].append((first, size, begin * local_blocks, here, query, kv, kv_other))
        return lax.optimization_barrier((places, kv))[0]

    sign = (2 * role - 1).astype(jnp.int32)[None]
    blocks = sides * lax.axis_size("role")
    which = jnp.stack([peers[3], peers[2], peers[1], peers[0]])
    out_here = out_weight[0]
    out_width = out_here.shape[1] // blocks
    place = spans[-1].start // chunks[-1]

    half = tokens // 2
    rounds = []
    straight = None
    held_places = places
    shard = normed
    for phase in range(chips + 1):
        step = phase + 1
        sent = {}
        if phase < chips:
            sent["role"] = lax.ppermute(shard, "role", swap)
            sent["head"] = lax.ppermute(shard, "head", swap)
        if straight is not None:
            sent["first"] = lax.ppermute(straight[2][:half], "role", swap)
            sent["second"] = lax.ppermute(straight[1][half:], "head", swap)
        if step < chips:
            sent["next"] = lax.ppermute(shard, "chip", ring)
        if phase == 0:
            sent["weights"] = weights_own.pop()
            sent["cuts"] = cuts[1:]
        if phase == 1:
            sent["places"] = places
            sent["gains"] = gains
            sent["corner"] = lax.dynamic_slice(
                out_here.reshape(chips, heads * HEAD_DIM, -1),
                (0, spans[-1].start * HEAD_DIM, which[0] * out_width),
                (chips, chunks[-1] * HEAD_DIM, out_width),
            )
        if step == chips:
            weights_other.append(lax.ppermute(weights_own[0], "core", swap))
            early = list(rounds)
            tables = tables_of(weights_own[0][:, depth:])
            held_places, tables = lax.optimization_barrier((held_places, tables))
            sent["places"] = project(0, 0, 1, 0, early, held_places)
        if step > chips and chunks[0] > 1:
            weights_other.append(lax.ppermute(weights_own[1], "core", swap))
            sent["places"] = project(0, 1, 1, 0, early, held_places)
        sent, shard = lax.optimization_barrier((sent, shard))
        if phase == 0:
            weights_own.append(sent["weights"])
            cuts[1:] = sent["cuts"]
        if phase == 1:
            gains, corner = sent["gains"], sent["corner"]
        if straight is not None:
            rounds.append(straight + (sent["first"], sent["second"]))
        held_places = sent.get("places", held_places)
        if phase < chips:
            straight = (shard, sent["role"], sent["head"])
        if step < chips:
            shard = sent["next"]
        if chips - 2 <= phase and len(weights_own) < heads:
            held, _ = lax.optimization_barrier((cuts[len(weights_own)], sent))
            weights_own.append(exchange(held))
    while len(weights_own) < heads:
        weights_own.append(exchange(cuts[len(weights_own)]))
    for at in range(len(weights_other), heads - 1):
        weights_other.append(lax.ppermute(weights_own[at], "core", swap))

    corner, held_places = lax.optimization_barrier((corner, held_places))
    far_weight = lax.ppermute(corner, ("role", "head"), far_swap)
    attended = []
    received = []
    for chunk, size in enumerate(chunks):
        last = chunk == len(chunks) - 1
        if chunk == 0:
            for at in range(min(size, 2), size):
                held_places = project(0, at, 1, 0, early, held_places)
            held_places = project(0, 0, size, len(early), rounds[len(early) :], held_places)
        else:
            held_places = project(chunk, 0, size, 0, rounds, held_places)
        if last:
            for earlier in range(len(attended)):
                (diagonal,) = out_blocks(
                    which[:1], sign, attended[earlier], spans[earlier].start // chunks[earlier],
                    out_here, blocks, (jnp.bfloat16,),
                )
                tables, diagonal, far_weight = lax.optimization_barrier(
                    (tables, diagonal, far_weight)
                )
                received.append(lax.ppermute(diagonal, ("role", "head"), far_swap))
        mixed = attend(spans[chunk].start, size, *tables, parts[chunk])
        held_places, mixed = lax.optimization_barrier((held_places, mixed))
        if chunk == 0:
            for at in range(len(weights_other), heads):
                weights_own[at], held_places = lax.optimization_barrier(
                    (weights_own[at], held_places)
                )
                weights_other.append(lax.ppermute(weights_own[at], "core", swap))
        mixed = mixed.reshape(chips, size, tokens, HEAD_DIM)
        if attended:
            mixed, attended = lax.optimization_barrier((mixed, attended))
        attended.append(exchange(mixed))

    def earlier_share(wanted, before=None):
        for chunk, size in enumerate(chunks[:-1]):
            before = jnp.stack(
                out_blocks(
                    wanted, sign, attended[chunk], spans[chunk].start // size, out_here, blocks,
                    (jnp.float32,), before,
                )
            ).reshape(-1, tokens, out_width)
        return before

    leaving = earlier_share(which[1:3])
    attended[-1], leaving = lax.optimization_barrier((attended[-1], leaving))
    far_attended = lax.ppermute(attended[-1], ("role", "head"), far_swap)
    wanted, _ = lax.optimization_barrier((which[1:3], received[0]))
    over_head, over_role = out_blocks(
        wanted, sign, attended[-1], place, out_here, blocks, (jnp.bfloat16, jnp.bfloat16), leaving
    )
    (over_head, over_role), far_attended = lax.optimization_barrier(
        ((over_head, over_role), far_attended)
    )
    received.append(lax.ppermute(over_head, "head", swap))
    received.append(lax.ppermute(over_role, "role", swap))
    (far,) = out_blocks(
        jnp.zeros_like(which[:1]), -sign, far_attended, 0, far_weight.reshape(-1, out_width), 1,
        (jnp.float32,), received[0][None],
    )
    (own,) = out_blocks(
        which[3:], sign, attended[-1], place, out_here, blocks, (jnp.float32,),
        earlier_share(which[3:], far[None]),
    )
    total = received[1].astype(jnp.float32)
    for one in received[2:]:
        total = total + one.astype(jnp.float32)
    return own + total


def splits_heads(mesh, qkv_weight, hidden_rows):
    role, seq, head = (mesh.shape[name] for name in ("role", "seq", "head"))
    if role != 2 or head != 2 or seq % CORES != 0:
        return False
    chips = seq // CORES
    heads = qkv_weight.shape[2] // (3 * HEAD_DIM * head)
    width = hidden_rows.shape[1]
    tokens = hidden_rows.shape[0] // seq
    return (
        heads % chips == 0
        and heads // chips > 1
        and chips == role * head
        and width % (role * head * 256) == 0
        and width % (seq * 16) == 0
        and tokens % (2 * BLOCK) == 0
        and hidden_rows.shape[0] // BLOCK <= 256
    )


def solution(mesh):
    def call(*arrays):
        if splits_heads(mesh, arrays[4], arrays[0]):
            per_device = per_device_by_heads
            seq = ("chip", "core")
            shape = mesh.devices.shape
            names = mesh.axis_names
            at = names.index("seq")
            layout = Mesh(
                mesh.devices.reshape(shape[:at] + (shape[at] // CORES, CORES) + shape[at + 1 :]),
                names[:at] + seq + names[at + 1 :],
            )
        else:
            per_device = per_device_by_tokens
            seq = "seq"
            layout = mesh
        placed = (
            P(seq, None),
            P(None, ("role", "head")),
            P(seq, None),
            P(seq),
            P("role", seq, "head"),
            P("role", "head", None),
            P("role", None, "head"),
            P("head", seq, None),
            P("head", seq),
        )
        return jax.shard_map(
            per_device,
            mesh=layout,
            in_specs=placed,
            out_specs=P(seq, ("role", "head")),
            check_vma=False,
        )(*arrays)

    return call
```

```python
import math

import jax
import jax.numpy as jnp
from jax import lax
from jax.experimental import pallas as pl
from jax.experimental.pallas import tpu as pltpu
from jax.sharding import Mesh
from jax.sharding import PartitionSpec as P

HEAD_DIM = 128
BLOCK = 64
KMAX = 8
CAP = 2


def rms_rows(values):
    return values * lax.rsqrt(jnp.mean(values * values, axis=-1, keepdims=True) + 1e-06)


def block_attention(queries, key_table, value_table, key_list, key_count):
    picked_keys = key_table[key_list]
    picked_values = value_table[key_list]
    scale = 1.0 / math.sqrt(HEAD_DIM)
    scores = (
        jnp.einsum("nqe,nkbe->nqkb", queries, picked_keys, preferred_element_type=jnp.float32)
        * scale
    )
    live = lax.broadcasted_iota(jnp.int32, (key_list.shape[0], KMAX), 1) < key_count[:, None]
    scores = jnp.where(live[:, None, :, None], scores, -jnp.inf)
    highest = jnp.max(scores, axis=(2, 3), keepdims=True)
    raised = jnp.exp(scores - highest)
    summed = jnp.sum(raised, axis=(2, 3), keepdims=True)
    weights = (raised / summed).astype(jnp.bfloat16)
    mixed = jnp.einsum("nqkb,nkbe->nqe", weights, picked_values, preferred_element_type=jnp.float32)
    return mixed.astype(jnp.bfloat16)


def pick_blocks(table, wanted):
    return table[wanted]


def per_device_by_tokens(
    hidden_rows,
    gen_weight,
    noise,
    timesteps,
    qkv_weight,
    out_weight,
    qk_gain,
    block_keys,
    block_count,
):
    generated = jnp.dot(hidden_rows, gen_weight, preferred_element_type=jnp.float32).astype(
        jnp.bfloat16
    )
    forked = lax.all_gather(generated, ("role", "head"), axis=1, tiled=True)
    row_count = forked.shape[0]
    width = forked.shape[1]
    local_blocks = timesteps.shape[0]
    angle_blocks = (timesteps.astype(jnp.float32) * (math.pi / 2000.0))[:, None, None]
    noisy = jnp.cos(angle_blocks) * forked.astype(jnp.float32).reshape(local_blocks, BLOCK, width)
    noisy = noisy + jnp.sin(angle_blocks) * noise.astype(jnp.float32).reshape(
        local_blocks, BLOCK, width
    )
    normed = rms_rows(noisy).reshape(row_count, width).astype(jnp.bfloat16)
    weight_here = qkv_weight[0]
    projected = jnp.dot(
        normed,
        lax.all_gather(weight_here, "seq", axis=0, tiled=True),
        preferred_element_type=jnp.float32,
    )
    heads_here = projected.shape[1] // (3 * HEAD_DIM)
    head_parts = projected.reshape(row_count, heads_here, 3, HEAD_DIM)
    gain_here = qk_gain[0]
    queries = (rms_rows(head_parts[:, :, 0]) * gain_here[0][None, :, None]).astype(jnp.bfloat16)
    key_local = (rms_rows(head_parts[:, :, 1]) * gain_here[1][None, :, None]).astype(jnp.bfloat16)
    value_local = head_parts[:, :, 2].astype(jnp.bfloat16)
    query_table = queries.reshape(local_blocks, BLOCK, heads_here, HEAD_DIM).transpose(2, 0, 1, 3)
    shard_count = lax.axis_size("seq")
    shard_here = lax.axis_index("seq")
    all_blocks = shard_count * local_blocks
    key_heads = key_local.reshape(local_blocks, BLOCK, heads_here, HEAD_DIM).transpose(2, 0, 1, 3)
    value_heads = value_local.reshape(local_blocks, BLOCK, heads_here, HEAD_DIM).transpose(
        2, 0, 1, 3
    )
    block_ids = lax.broadcasted_iota(jnp.int32, (1, 1, 1, all_blocks), 3)
    matches = block_keys[:, :, :, None] == block_ids
    remote = block_ids // local_blocks != shard_here
    needed = jnp.any(jnp.logical_and(matches, remote), axis=(1, 2))
    needed = needed.reshape(heads_here, shard_count, local_blocks)
    slot_of = jnp.cumsum(needed.astype(jnp.int32), axis=2) - 1
    slot_ids = lax.broadcasted_iota(jnp.int32, (1, 1, 1, CAP), 3)
    within_ids = lax.broadcasted_iota(jnp.int32, (1, 1, local_blocks, 1), 2)
    chosen_slot = jnp.logical_and(needed[..., None], slot_of[..., None] == slot_ids)
    requests = jnp.sum(jnp.where(chosen_slot, within_ids, 0), axis=2)
    asked = lax.all_to_all(
        requests.transpose(1, 0, 2), "seq", split_axis=0, concat_axis=0, tiled=True
    )
    sent_keys = jax.vmap(pick_blocks, in_axes=(0, 1), out_axes=1)(key_heads, asked)
    sent_values = jax.vmap(pick_blocks, in_axes=(0, 1), out_axes=1)(value_heads, asked)
    got_keys, got_values = (
        lax.all_to_all(sent_keys, "seq", split_axis=0, concat_axis=0, tiled=True),
        lax.all_to_all(sent_values, "seq", split_axis=0, concat_axis=0, tiled=True),
    )
    fetched_keys = got_keys.transpose(1, 0, 2, 3, 4).reshape(
        heads_here, shard_count * CAP, BLOCK, HEAD_DIM
    )
    fetched_values = got_values.transpose(1, 0, 2, 3, 4).reshape(
        heads_here, shard_count * CAP, BLOCK, HEAD_DIM
    )
    key_table = jnp.concatenate([key_heads, fetched_keys], axis=1)
    value_table = jnp.concatenate([value_heads, fetched_values], axis=1)
    local_ids = lax.broadcasted_iota(jnp.int32, (1, shard_count, local_blocks), 2)
    owner_grid = lax.broadcasted_iota(jnp.int32, (1, shard_count, local_blocks), 1)
    position = jnp.where(
        owner_grid == shard_here, local_ids, local_blocks + owner_grid * CAP + slot_of
    )
    position = position.reshape(heads_here, all_blocks)
    key_lists = jnp.sum(jnp.where(matches, position[:, None, None, :], 0), axis=3)
    attended = jax.vmap(block_attention)(
        query_table, key_table, value_table, key_lists, block_count
    )
    attended = attended.transpose(1, 2, 0, 3).reshape(row_count, heads_here * HEAD_DIM)
    contribution = jnp.dot(attended, out_weight[0], preferred_element_type=jnp.float32)
    signed = (2.0 * lax.axis_index("role").astype(jnp.float32) - 1.0) * contribution
    return lax.psum_scatter(
        signed.astype(jnp.bfloat16), ("role", "head"), scatter_dimension=1, tiled=True
    ).astype(jnp.float32)


VMEM_BYTES = 56 * 1024 * 1024
CORES = 2


def whole_in_vmem():
    return pl.BlockSpec(memory_space=pltpu.VMEM)


def in_hbm():
    return pl.BlockSpec(memory_space=pl.ANY)


def in_smem():
    return pl.BlockSpec(memory_space=pltpu.SMEM)


def cut_columns(weight, chips, head, extra=None):
    rows, columns = weight.shape
    wide = 3 * HEAD_DIM
    chip_heads = columns // (chips * wide)
    more = 0 if extra is None else extra.shape[1]

    def body(weight_ref, *refs):
        out_ref = refs[-1]
        out_ref[0, :rows] = weight_ref[...]
        if more:
            out_ref[0, rows:] = refs[0][0]

    in_specs = [pl.BlockSpec((rows, wide), lambda chip: (0, chip * chip_heads + head))]
    operands = [weight]
    if more:
        in_specs.append(pl.BlockSpec((1, more, wide), lambda chip: (chip, 0, 0)))
        operands.append(extra)
    return pl.pallas_call(
        body,
        grid=(chips,),
        in_specs=in_specs,
        out_specs=pl.BlockSpec((1, rows + more, wide), lambda chip: (chip, 0, 0)),
        out_shape=jax.ShapeDtypeStruct((chips, rows + more, wide), weight.dtype),
        name="cut_columns",
    )(*operands)


def project_heads(places, gains, rounds, depth, weights_own, weights_other):
    heads = len(weights_own)
    slabs, _, columns = weights_own[0].shape
    tokens, features = rounds[0][0].shape
    pieces = [piece for one in rounds for piece in one]
    turns = len(rounds)
    most = max(len(one) for one in rounds)
    joint = 2 if slabs % 2 == 0 else 1
    dtype = weights_own[0].dtype

    def body(places_ref, gains_ref, *refs):
        own_refs, other_refs = refs[:heads], refs[heads : 2 * heads]
        piece_refs = refs[2 * heads : 2 * heads + len(pieces)]
        query_ref, kv_ref = refs[2 * heads + len(pieces) : 2 * heads + len(pieces) + 2]
        table, rows, weight_sems, row_sems = refs[2 * heads + len(pieces) + 2 :]
        core = places_ref[slabs]
        copies = []
        for slab in range(slabs):
            here = []
            for head in range(heads):
                for side, ref in enumerate((own_refs[head], other_refs[head])):
                    place = core if side == 0 else 1 - core
                    here.append(
                        pltpu.make_async_copy(
                            ref.at[places_ref[slab], pl.ds(0, depth)],
                            table.at[
                                slab // joint,
                                slab % joint,
                                place,
                                :,
                                pl.ds(head * columns, columns),
                            ],
                            weight_sems.at[slab, head, side],
                        )
                    )
            at = 0
            for turn in range(turns):
                first = turn * tokens
                for which in range(len(rounds[turn])):
                    if min(which, slabs - 1) == slab:
                        count = rounds[turn][which].shape[0]
                        here.append(
                            pltpu.make_async_copy(
                                piece_refs[at],
                                rows.at[
                                    slab // joint,
                                    pl.ds(first, count),
                                    pl.ds(slab % joint * features, features),
                                ],
                                row_sems.at[which, turn],
                            )
                        )
                        first += count
                    at += 1
            for copy in here:
                copy.start()
            copies.append(here)
        total = None
        for group in range(slabs // joint):
            for slab in range(group * joint, (group + 1) * joint):
                for copy in copies[slab]:
                    copy.wait()
            part = jnp.dot(
                rows[group],
                table[group].reshape(joint * CORES * depth, heads * columns),
                preferred_element_type=jnp.float32,
            )
            total = part if total is None else total + part
        for turn in range(turns):
            here = total[turn * tokens : (turn + 1) * tokens]
            for head in range(heads):
                at = head * columns
                for which in range(2):
                    block = here[:, at + which * HEAD_DIM : at + (which + 1) * HEAD_DIM]
                    normal = (rms_rows(block) * gains_ref[which, head]).astype(dtype)
                    if which == 0:
                        query_ref[head, turn] = normal
                    else:
                        kv_ref[head, 0, turn] = normal
                block = here[:, at + 2 * HEAD_DIM : at + 3 * HEAD_DIM]
                kv_ref[head, 1, turn] = block.astype(dtype)

    return pl.pallas_call(
        body,
        in_specs=[in_smem(), in_smem()] + [in_hbm()] * (2 * heads + len(pieces)),
        out_specs=(whole_in_vmem(), whole_in_vmem()),
        out_shape=(
            jax.ShapeDtypeStruct((heads, turns, tokens, HEAD_DIM), dtype),
            jax.ShapeDtypeStruct((heads, 2, turns, tokens, HEAD_DIM), dtype),
        ),
        scratch_shapes=[
            pltpu.VMEM((slabs // joint, joint, CORES, depth, heads * columns), dtype),
            pltpu.VMEM((slabs // joint, turns * tokens, joint * features), dtype),
            pltpu.SemaphoreType.DMA((slabs, heads, 2)),
            pltpu.SemaphoreType.DMA((most, turns)),
        ],
        compiler_params=pltpu.CompilerParams(vmem_limit_bytes=VMEM_BYTES),
        name="project_heads",
    )(places, gains, *weights_own, *weights_other, *pieces)


def attend(first_head, heads, key_slots, counts, query_slots, group_most, parts):
    _, blocks, most = key_slots.shape
    groups = group_most.shape[1]
    together = blocks // groups
    scale = 1.0 / math.sqrt(HEAD_DIM)
    dtype = parts[0][4].dtype
    arrays = [array for part in parts for array in part[4:]]

    def body(slots_ref, counts_ref, from_ref, most_ref, *refs):
        out_ref, query_table, table, sems = refs[len(arrays) :]
        copies = []
        for at, (head, size, block, span, _, _, _) in enumerate(parts):
            query_part, own_part, other_part = refs[3 * at : 3 * at + 3]
            rows = pl.ds(head, size)
            copies.append(
                pltpu.make_async_copy(
                    query_part, query_table.at[rows, pl.ds(block, span)], sems.at[at, 0]
                )
            )
            for side, ref in enumerate((own_part, other_part)):
                place = pl.ds(side * blocks + block, span)
                copies.append(
                    pltpu.make_async_copy(ref, table.at[rows, :, place], sems.at[at, 1 + side])
                )
        for copy in copies:
            copy.start()
        for copy in copies:
            copy.wait()

        def run(head, group, listed, batch):
            for first in range(0, together, batch):
                spots = [group * together + at for at in range(first, min(first + batch, together))]
                slots = [[slots_ref[first_head + head, at, entry] for entry in range(listed)] for at in spots]
                scores = []
                for at, listing in zip(spots, slots):
                    keys = jnp.concatenate([table[head, 0, slot] for slot in listing], axis=0)
                    scores.append(
                        lax.dot_general(
                            query_table[head, from_ref[at]],
                            keys,
                            (((1,), (1,)), ((), ())),
                            preferred_element_type=jnp.float32,
                        )
                    )
                column = lax.broadcasted_iota(jnp.int32, (1, listed * BLOCK), 1)
                scores = [
                    jnp.where(column < counts_ref[first_head + head, at] * BLOCK, one * scale, -jnp.inf)
                    for at, one in zip(spots, scores)
                ]
                highest = [jnp.max(one, axis=1, keepdims=True) for one in scores]
                raised = [jnp.exp(one - top) for one, top in zip(scores, highest)]
                inverse = [1.0 / jnp.sum(one, axis=1, keepdims=True) for one in raised]
                weights = [(one * by).astype(dtype) for one, by in zip(raised, inverse)]
                mixed = []
                for one, listing in zip(weights, slots):
                    values = jnp.concatenate([table[head, 1, slot] for slot in listing], axis=0)
                    mixed.append(jnp.dot(one, values, preferred_element_type=jnp.float32))
                for at, one in enumerate(mixed):
                    out_ref[group, head, first + at] = one.astype(dtype)

        def step(at, carry):
            head, group = at // groups, at % groups
            few = most_ref[first_head + head, group] <= most // 2

            @pl.when(few)
            def _():
                run(head, group, most // 2, 6)

            @pl.when(jnp.logical_not(few))
            def _():
                run(head, group, most, 6)

            return carry

        lax.fori_loop(0, heads * groups, step, 0)

    return pl.pallas_call(
        body,
        in_specs=[in_smem()] * 4 + [in_hbm()] * len(arrays),
        out_specs=whole_in_vmem(),
        out_shape=jax.ShapeDtypeStruct((groups, heads, together, BLOCK, HEAD_DIM), dtype),
        scratch_shapes=[
            pltpu.VMEM((heads, blocks, BLOCK, HEAD_DIM), dtype),
            pltpu.VMEM((heads, 2, CORES * blocks, BLOCK, HEAD_DIM), dtype),
            pltpu.SemaphoreType.DMA((len(parts), 3)),
        ],
        compiler_params=pltpu.CompilerParams(vmem_limit_bytes=VMEM_BYTES),
        name="attend",
    )(key_slots, counts, query_slots, group_most, *arrays)


def out_blocks(which, sign, attended, place, out_weight, blocks, dtypes, before=None, skip=0):
    groups, heads, tokens, _ = attended.shape
    depth, features = out_weight.shape
    width = features // blocks
    wanted = which.shape[0]
    rows = heads * HEAD_DIM
    weight = out_weight.reshape(groups, depth // groups, features)
    stacked = len(dtypes) == 1 and wanted > 1

    def body(which_ref, sign_ref, mixed_ref, weight_ref, *refs):
        out_refs = refs if before is None else refs[1:]
        joined = jnp.concatenate(
            [mixed_ref[group, head] for group in range(groups) for head in range(heads)], axis=1
        )
        total = jnp.dot(
            joined,
            weight_ref[...].reshape(groups * rows, width),
            preferred_element_type=jnp.float32,
        )
        total = total * sign_ref[0].astype(jnp.float32)
        if before is not None:
            total = total + refs[0][0].astype(jnp.float32)
        if stacked:
            out_refs[0][0] = total.astype(dtypes[0])
        else:
            for at in range(wanted):

                @pl.when(pl.program_id(0) == at)
                def _(at=at):
                    out_refs[at][...] = total.astype(dtypes[at])

    in_specs = [
        pl.BlockSpec(attended.shape, lambda i, w, s: (0, 0, 0, 0)),
        pl.BlockSpec((groups, rows, width), lambda i, w, s: (0, place, w[i])),
    ]
    operands = [attended, weight]
    if before is not None:
        in_specs.append(pl.BlockSpec((1, tokens, width), lambda i, w, s: (i + skip, 0, 0)))
        operands.append(before)
    if stacked:
        out_specs = [pl.BlockSpec((1, tokens, width), lambda i, w, s: (i, 0, 0))]
        out_shape = [jax.ShapeDtypeStruct((wanted, tokens, width), dtypes[0])]
    else:
        out_specs = [pl.BlockSpec((tokens, width), lambda i, w, s: (0, 0))] * wanted
        out_shape = [jax.ShapeDtypeStruct((tokens, width), dtype) for dtype in dtypes]
    return pl.pallas_call(
        body,
        grid_spec=pltpu.PrefetchScalarGridSpec(
            num_scalar_prefetch=2, grid=(wanted,), in_specs=in_specs, out_specs=out_specs
        ),
        out_shape=out_shape,
        compiler_params=pltpu.CompilerParams(vmem_limit_bytes=VMEM_BYTES),
        name="out_blocks",
    )(which, sign, *operands)


def chunk_sizes(heads):
    last = heads // 3 if heads % 3 == 0 else 1
    return [heads - last, last] if heads > last else [heads]


def per_device_by_heads(
    hidden_rows,
    gen_weight,
    noise,
    timesteps,
    qkv_weight,
    out_weight,
    qk_gain,
    block_keys,
    block_count,
):
    role, head = lax.axis_index("role"), lax.axis_index("head")
    chip, core = lax.axis_index("chip"), lax.axis_index("core")
    chips = lax.axis_size("chip")
    local_heads, local_blocks, most = block_keys.shape
    heads = local_heads // chips
    tokens = hidden_rows.shape[0]
    width = hidden_rows.shape[1]
    features = gen_weight.shape[1]
    all_blocks = chips * local_blocks
    swap = [(0, 1), (1, 0)]
    far_swap = [(0, 3), (1, 2), (2, 1), (3, 0)]
    ring = [(at, (at + 1) % chips) for at in range(chips)]

    def turn_of(other):
        return (chip - other) % chips

    def exchange(array):
        return lax.all_to_all(array, "chip", split_axis=0, concat_axis=0, tiled=True)

    weight_here = qkv_weight[0]
    depth = weight_here.shape[0]
    wide = 3 * HEAD_DIM
    lists = jnp.concatenate([block_keys, block_count[:, :, None]], axis=2)
    lists = lists.reshape(chips, -1).astype(jnp.bfloat16)
    listed = lists.shape[1]
    spare = -(-listed // (16 * wide)) * 16
    lists = jnp.pad(lists, ((0, 0), (0, spare * wide - listed))).reshape(chips, spare, wide)
    cuts = [
        cut_columns(weight_here, chips, at, lists if at == 0 else None) for at in range(heads)
    ]
    hidden_rows, cuts[0] = lax.optimization_barrier((hidden_rows, cuts[0]))
    weights_own = [exchange(cuts[0])]
    weights_other = []

    mine = role * lax.axis_size("head") + head
    generated = jnp.dot(hidden_rows, gen_weight, preferred_element_type=jnp.float32)
    generated = lax.reduce_precision(generated, 8, 7)
    angle_blocks = (timesteps.astype(jnp.float32) * (math.pi / 2000.0))[:, None, None]
    noise_here = lax.dynamic_slice_in_dim(noise, mine * features, features, axis=1)
    noisy = jnp.cos(angle_blocks) * generated.reshape(local_blocks, BLOCK, features)
    noisy = noisy + jnp.sin(angle_blocks) * noise_here.astype(jnp.float32).reshape(
        local_blocks, BLOCK, features
    )
    squares = jnp.sum(noisy * noisy, axis=-1)
    squares = squares + lax.ppermute(squares, "role", swap)
    squares = squares + lax.ppermute(squares, "head", swap)
    normed = (noisy * lax.rsqrt(squares / width + 1e-06)[:, :, None]).astype(jnp.bfloat16)
    normed = normed.reshape(tokens, features)

    def tables_of(lists):
        lists = lists.reshape(chips, spare * wide)[:, :listed].astype(jnp.int32)
        lists = lists.reshape(chips, heads, local_blocks, most + 1).transpose(1, 0, 2, 3)
        lists = lists.reshape(heads, all_blocks, most + 1)
        owner = lists[:, :, :most] // local_blocks
        turn = turn_of(owner // CORES)
        far = (owner % CORES != core).astype(jnp.int32)
        key_slots = far * all_blocks + turn * local_blocks + lists[:, :, :most] % local_blocks
        counts = lists[:, :, most]
        group_most = jnp.max(counts.reshape(heads, chips, local_blocks), axis=2)
        spot = jnp.arange(all_blocks, dtype=jnp.int32)
        query_slots = turn_of(spot // local_blocks)
        query_slots = query_slots * local_blocks + spot % local_blocks

        return key_slots, counts, query_slots, group_most

    sides = lax.axis_size("head")
    peers = jnp.stack(
        [
            role * sides + head,
            (1 - role) * sides + head,
            role * sides + 1 - head,
            (1 - role) * sides + 1 - head,
        ]
    ).astype(jnp.int32)
    places = jnp.concatenate([peers, core[None].astype(jnp.int32)])
    gains = lax.dynamic_slice_in_dim(qk_gain[0], chip * heads, heads, axis=1)

    chunks = chunk_sizes(heads)
    spans = [slice(sum(chunks[:at]), sum(chunks[: at + 1])) for at in range(len(chunks))]
    parts = [[] for _ in chunks]

    def project(chunk, first, size, begin, some, places):
        at = spans[chunk].start + first
        span = slice(at, at + size)
        query, kv = project_heads(
            places, gains[:, span], some, depth, weights_own[span], weights_other[span]
        )
        here = len(some) * local_blocks
        kv = kv.reshape(size, 2, here, BLOCK, HEAD_DIM)
        kv_other = lax.ppermute(kv, "core", swap)
        query = query.reshape(size, here, BLOCK, HEAD_DIM)
        parts[chunk].append((first, size, begin * local_blocks, here, query, kv, kv_other))
        return lax.optimization_barrier((places, kv))[0]

    sign = (2 * role - 1).astype(jnp.int32)[None]
    blocks = sides * lax.axis_size("role")
    which = jnp.stack([peers[3], peers[2], peers[1], peers[0]])
    out_here = out_weight[0]
    out_width = out_here.shape[1] // blocks
    place = spans[-1].start // chunks[-1]

    half = tokens // 2
    rounds = []
    straight = None
    held_places = places
    shard = normed
    for phase in range(chips + 1):
        step = phase + 1
        sent = {}
        if phase < chips:
            sent["role"] = lax.ppermute(shard, "role", swap)
            sent["head"] = lax.ppermute(shard, "head", swap)
        if straight is not None:
            sent["first"] = lax.ppermute(straight[2][:half], "role", swap)
            sent["second"] = lax.ppermute(straight[1][half:], "head", swap)
        if step < chips:
            sent["next"] = lax.ppermute(shard, "chip", ring)
        if phase == 0:
            sent["weights"] = weights_own.pop()
            sent["cuts"] = cuts[1:]
        if phase == 1:
            sent["places"] = places
            sent["gains"] = gains
            sent["corner"] = lax.dynamic_slice(
                out_here.reshape(chips, heads * HEAD_DIM, -1),
                (0, spans[-1].start * HEAD_DIM, which[0] * out_width),
                (chips, chunks[-1] * HEAD_DIM, out_width),
            )
        if step == chips:
            weights_other.append(lax.ppermute(weights_own[0], "core", swap))
            early = list(rounds)
            tables = tables_of(weights_own[0][:, depth:])
            held_places, tables = lax.optimization_barrier((held_places, tables))
            sent["places"] = project(0, 0, 1, 0, early, held_places)
        if step > chips and chunks[0] > 1:
            weights_other.append(lax.ppermute(weights_own[1], "core", swap))
            sent["places"] = project(0, 1, 1, 0, early, held_places)
        sent, shard = lax.optimization_barrier((sent, shard))
        if phase == 0:
            weights_own.append(sent["weights"])
            cuts[1:] = sent["cuts"]
        if phase == 1:
            gains, corner = sent["gains"], sent["corner"]
        if straight is not None:
            rounds.append(straight + (sent["first"], sent["second"]))
        held_places = sent.get("places", held_places)
        if phase < chips:
            straight = (shard, sent["role"], sent["head"])
        if step < chips:
            shard = sent["next"]
        if chips - 2 <= phase and len(weights_own) < heads:
            held, _ = lax.optimization_barrier((cuts[len(weights_own)], sent))
            weights_own.append(exchange(held))
    while len(weights_own) < heads:
        weights_own.append(exchange(cuts[len(weights_own)]))
    for at in range(len(weights_other), heads - 1):
        weights_other.append(lax.ppermute(weights_own[at], "core", swap))

    corner, held_places = lax.optimization_barrier((corner, held_places))
    far_weight = lax.ppermute(corner, ("role", "head"), far_swap)
    attended = []
    received = []
    for chunk, size in enumerate(chunks):
        last = chunk == len(chunks) - 1
        if chunk == 0:
            for at in range(min(size, 2), size):
                held_places = project(0, at, 1, 0, early, held_places)
            held_places = project(0, 0, size, len(early), rounds[len(early) :], held_places)
        else:
            held_places, far_weight = lax.optimization_barrier((held_places, far_weight))
            held_places = project(chunk, 0, size, 0, rounds, held_places)
        if last:
            for earlier in range(len(attended)):
                (diagonal,) = out_blocks(
                    which[:1], sign, attended[earlier], spans[earlier].start // chunks[earlier],
                    out_here, blocks, (jnp.bfloat16,),
                )
                tables, diagonal, far_weight = lax.optimization_barrier(
                    (tables, diagonal, far_weight)
                )
                received.append(lax.ppermute(diagonal, ("role", "head"), far_swap))
        mixed = attend(spans[chunk].start, size, *tables, parts[chunk])
        held_places, mixed = lax.optimization_barrier((held_places, mixed))
        if chunk == 0:
            for at in range(len(weights_other), heads):
                weights_own[at], held_places = lax.optimization_barrier(
                    (weights_own[at], held_places)
                )
                weights_other.append(lax.ppermute(weights_own[at], "core", swap))
        mixed = mixed.reshape(chips, size, tokens, HEAD_DIM)
        if attended:
            mixed, attended = lax.optimization_barrier((mixed, attended))
        attended.append(exchange(mixed))

    def earlier_share(wanted, before=None):
        for chunk, size in enumerate(chunks[:-1]):
            before = jnp.stack(
                out_blocks(
                    wanted, sign, attended[chunk], spans[chunk].start // size, out_here, blocks,
                    (jnp.float32,), before,
                )
            ).reshape(-1, tokens, out_width)
        return before

    leaving = earlier_share(which[1:3])
    attended[-1], leaving = lax.optimization_barrier((attended[-1], leaving))
    far_attended = lax.ppermute(attended[-1], ("role", "head"), far_swap)
    wanted, _ = lax.optimization_barrier((which[1:3], received[0]))
    over_head, over_role = out_blocks(
        wanted, sign, attended[-1], place, out_here, blocks, (jnp.bfloat16, jnp.bfloat16), leaving
    )
    (over_head, over_role), far_attended = lax.optimization_barrier(
        ((over_head, over_role), far_attended)
    )
    received.append(lax.ppermute(over_head, "head", swap))
    received.append(lax.ppermute(over_role, "role", swap))
    (far,) = out_blocks(
        jnp.zeros_like(which[:1]), -sign, far_attended, 0, far_weight.reshape(-1, out_width), 1,
        (jnp.float32,), received[0][None],
    )
    (own,) = out_blocks(
        which[3:], sign, attended[-1], place, out_here, blocks, (jnp.float32,),
        earlier_share(which[3:], far[None]),
    )
    total = received[1].astype(jnp.float32)
    for one in received[2:]:
        total = total + one.astype(jnp.float32)
    return own + total


def splits_heads(mesh, qkv_weight, hidden_rows):
    role, seq, head = (mesh.shape[name] for name in ("role", "seq", "head"))
    if role != 2 or head != 2 or seq % CORES != 0:
        return False
    chips = seq // CORES
    heads = qkv_weight.shape[2] // (3 * HEAD_DIM * head)
    width = hidden_rows.shape[1]
    tokens = hidden_rows.shape[0] // seq
    return (
        heads % chips == 0
        and heads // chips > 1
        and chips == role * head
        and width % (role * head * 256) == 0
        and width % (seq * 16) == 0
        and tokens % (2 * BLOCK) == 0
        and hidden_rows.shape[0] // BLOCK <= 256
    )


def solution(mesh):
    def call(*arrays):
        if splits_heads(mesh, arrays[4], arrays[0]):
            per_device = per_device_by_heads
            seq = ("chip", "core")
            shape = mesh.devices.shape
            names = mesh.axis_names
            at = names.index("seq")
            layout = Mesh(
                mesh.devices.reshape(shape[:at] + (shape[at] // CORES, CORES) + shape[at + 1 :]),
                names[:at] + seq + names[at + 1 :],
            )
        else:
            per_device = per_device_by_tokens
            seq = "seq"
            layout = mesh
        placed = (
            P(seq, None),
            P(None, ("role", "head")),
            P(seq, None),
            P(seq),
            P("role", seq, "head"),
            P("role", "head", None),
            P("role", None, "head"),
            P("head", seq, None),
            P("head", seq),
        )
        return jax.shard_map(
            per_device,
            mesh=layout,
            in_specs=placed,
            out_specs=P(seq, ("role", "head")),
            check_vma=False,
        )(*arrays)

    return call
```

```python
import math

import jax
import jax.numpy as jnp
from jax import lax
from jax.experimental import pallas as pl
from jax.experimental.pallas import tpu as pltpu
from jax.sharding import Mesh
from jax.sharding import PartitionSpec as P

HEAD_DIM = 128
BLOCK = 64
KMAX = 8
CAP = 2


def rms_rows(values):
    return values * lax.rsqrt(jnp.mean(values * values, axis=-1, keepdims=True) + 1e-06)


def block_attention(queries, key_table, value_table, key_list, key_count):
    picked_keys = key_table[key_list]
    picked_values = value_table[key_list]
    scale = 1.0 / math.sqrt(HEAD_DIM)
    scores = (
        jnp.einsum("nqe,nkbe->nqkb", queries, picked_keys, preferred_element_type=jnp.float32)
        * scale
    )
    live = lax.broadcasted_iota(jnp.int32, (key_list.shape[0], KMAX), 1) < key_count[:, None]
    scores = jnp.where(live[:, None, :, None], scores, -jnp.inf)
    highest = jnp.max(scores, axis=(2, 3), keepdims=True)
    raised = jnp.exp(scores - highest)
    summed = jnp.sum(raised, axis=(2, 3), keepdims=True)
    weights = (raised / summed).astype(jnp.bfloat16)
    mixed = jnp.einsum("nqkb,nkbe->nqe", weights, picked_values, preferred_element_type=jnp.float32)
    return mixed.astype(jnp.bfloat16)


def pick_blocks(table, wanted):
    return table[wanted]


def per_device_by_tokens(
    hidden_rows,
    gen_weight,
    noise,
    timesteps,
    qkv_weight,
    out_weight,
    qk_gain,
    block_keys,
    block_count,
):
    generated = jnp.dot(hidden_rows, gen_weight, preferred_element_type=jnp.float32).astype(
        jnp.bfloat16
    )
    forked = lax.all_gather(generated, ("role", "head"), axis=1, tiled=True)
    row_count = forked.shape[0]
    width = forked.shape[1]
    local_blocks = timesteps.shape[0]
    angle_blocks = (timesteps.astype(jnp.float32) * (math.pi / 2000.0))[:, None, None]
    noisy = jnp.cos(angle_blocks) * forked.astype(jnp.float32).reshape(local_blocks, BLOCK, width)
    noisy = noisy + jnp.sin(angle_blocks) * noise.astype(jnp.float32).reshape(
        local_blocks, BLOCK, width
    )
    normed = rms_rows(noisy).reshape(row_count, width).astype(jnp.bfloat16)
    weight_here = qkv_weight[0]
    projected = jnp.dot(
        normed,
        lax.all_gather(weight_here, "seq", axis=0, tiled=True),
        preferred_element_type=jnp.float32,
    )
    heads_here = projected.shape[1] // (3 * HEAD_DIM)
    head_parts = projected.reshape(row_count, heads_here, 3, HEAD_DIM)
    gain_here = qk_gain[0]
    queries = (rms_rows(head_parts[:, :, 0]) * gain_here[0][None, :, None]).astype(jnp.bfloat16)
    key_local = (rms_rows(head_parts[:, :, 1]) * gain_here[1][None, :, None]).astype(jnp.bfloat16)
    value_local = head_parts[:, :, 2].astype(jnp.bfloat16)
    query_table = queries.reshape(local_blocks, BLOCK, heads_here, HEAD_DIM).transpose(2, 0, 1, 3)
    shard_count = lax.axis_size("seq")
    shard_here = lax.axis_index("seq")
    all_blocks = shard_count * local_blocks
    key_heads = key_local.reshape(local_blocks, BLOCK, heads_here, HEAD_DIM).transpose(2, 0, 1, 3)
    value_heads = value_local.reshape(local_blocks, BLOCK, heads_here, HEAD_DIM).transpose(
        2, 0, 1, 3
    )
    block_ids = lax.broadcasted_iota(jnp.int32, (1, 1, 1, all_blocks), 3)
    matches = block_keys[:, :, :, None] == block_ids
    remote = block_ids // local_blocks != shard_here
    needed = jnp.any(jnp.logical_and(matches, remote), axis=(1, 2))
    needed = needed.reshape(heads_here, shard_count, local_blocks)
    slot_of = jnp.cumsum(needed.astype(jnp.int32), axis=2) - 1
    slot_ids = lax.broadcasted_iota(jnp.int32, (1, 1, 1, CAP), 3)
    within_ids = lax.broadcasted_iota(jnp.int32, (1, 1, local_blocks, 1), 2)
    chosen_slot = jnp.logical_and(needed[..., None], slot_of[..., None] == slot_ids)
    requests = jnp.sum(jnp.where(chosen_slot, within_ids, 0), axis=2)
    asked = lax.all_to_all(
        requests.transpose(1, 0, 2), "seq", split_axis=0, concat_axis=0, tiled=True
    )
    sent_keys = jax.vmap(pick_blocks, in_axes=(0, 1), out_axes=1)(key_heads, asked)
    sent_values = jax.vmap(pick_blocks, in_axes=(0, 1), out_axes=1)(value_heads, asked)
    got_keys, got_values = (
        lax.all_to_all(sent_keys, "seq", split_axis=0, concat_axis=0, tiled=True),
        lax.all_to_all(sent_values, "seq", split_axis=0, concat_axis=0, tiled=True),
    )
    fetched_keys = got_keys.transpose(1, 0, 2, 3, 4).reshape(
        heads_here, shard_count * CAP, BLOCK, HEAD_DIM
    )
    fetched_values = got_values.transpose(1, 0, 2, 3, 4).reshape(
        heads_here, shard_count * CAP, BLOCK, HEAD_DIM
    )
    key_table = jnp.concatenate([key_heads, fetched_keys], axis=1)
    value_table = jnp.concatenate([value_heads, fetched_values], axis=1)
    local_ids = lax.broadcasted_iota(jnp.int32, (1, shard_count, local_blocks), 2)
    owner_grid = lax.broadcasted_iota(jnp.int32, (1, shard_count, local_blocks), 1)
    position = jnp.where(
        owner_grid == shard_here, local_ids, local_blocks + owner_grid * CAP + slot_of
    )
    position = position.reshape(heads_here, all_blocks)
    key_lists = jnp.sum(jnp.where(matches, position[:, None, None, :], 0), axis=3)
    attended = jax.vmap(block_attention)(
        query_table, key_table, value_table, key_lists, block_count
    )
    attended = attended.transpose(1, 2, 0, 3).reshape(row_count, heads_here * HEAD_DIM)
    contribution = jnp.dot(attended, out_weight[0], preferred_element_type=jnp.float32)
    signed = (2.0 * lax.axis_index("role").astype(jnp.float32) - 1.0) * contribution
    return lax.psum_scatter(
        signed.astype(jnp.bfloat16), ("role", "head"), scatter_dimension=1, tiled=True
    ).astype(jnp.float32)


VMEM_BYTES = 56 * 1024 * 1024
CORES = 2


def whole_in_vmem():
    return pl.BlockSpec(memory_space=pltpu.VMEM)


def in_hbm():
    return pl.BlockSpec(memory_space=pl.ANY)


def in_smem():
    return pl.BlockSpec(memory_space=pltpu.SMEM)


def cut_columns(weight, chips, head, extra=None):
    rows, columns = weight.shape
    wide = 3 * HEAD_DIM
    chip_heads = columns // (chips * wide)
    more = 0 if extra is None else extra.shape[1]

    def body(weight_ref, *refs):
        out_ref = refs[-1]
        out_ref[0, :rows] = weight_ref[...]
        if more:
            out_ref[0, rows:] = refs[0][0]

    in_specs = [pl.BlockSpec((rows, wide), lambda chip: (0, chip * chip_heads + head))]
    operands = [weight]
    if more:
        in_specs.append(pl.BlockSpec((1, more, wide), lambda chip: (chip, 0, 0)))
        operands.append(extra)
    return pl.pallas_call(
        body,
        grid=(chips,),
        in_specs=in_specs,
        out_specs=pl.BlockSpec((1, rows + more, wide), lambda chip: (chip, 0, 0)),
        out_shape=jax.ShapeDtypeStruct((chips, rows + more, wide), weight.dtype),
        name="cut_columns",
    )(*operands)


def project_heads(places, gains, rounds, depth, weights_own, weights_other):
    heads = len(weights_own)
    slabs, _, columns = weights_own[0].shape
    tokens, features = rounds[0][0].shape
    pieces = [piece for one in rounds for piece in one]
    turns = len(rounds)
    most = max(len(one) for one in rounds)
    joint = 2 if slabs % 2 == 0 else 1
    dtype = weights_own[0].dtype

    def body(places_ref, gains_ref, *refs):
        own_refs, other_refs = refs[:heads], refs[heads : 2 * heads]
        piece_refs = refs[2 * heads : 2 * heads + len(pieces)]
        query_ref, kv_ref = refs[2 * heads + len(pieces) : 2 * heads + len(pieces) + 2]
        table, rows, weight_sems, row_sems = refs[2 * heads + len(pieces) + 2 :]
        core = places_ref[slabs]
        copies = []
        for slab in range(slabs):
            here = []
            for head in range(heads):
                for side, ref in enumerate((own_refs[head], other_refs[head])):
                    place = core if side == 0 else 1 - core
                    here.append(
                        pltpu.make_async_copy(
                            ref.at[places_ref[slab], pl.ds(0, depth)],
                            table.at[
                                slab // joint,
                                slab % joint,
                                place,
                                :,
                                pl.ds(head * columns, columns),
                            ],
                            weight_sems.at[slab, head, side],
                        )
                    )
            at = 0
            for turn in range(turns):
                first = turn * tokens
                for which in range(len(rounds[turn])):
                    if min(which, slabs - 1) == slab:
                        count = rounds[turn][which].shape[0]
                        here.append(
                            pltpu.make_async_copy(
                                piece_refs[at],
                                rows.at[
                                    slab // joint,
                                    pl.ds(first, count),
                                    pl.ds(slab % joint * features, features),
                                ],
                                row_sems.at[which, turn],
                            )
                        )
                        first += count
                    at += 1
            for copy in here:
                copy.start()
            copies.append(here)
        total = None
        for group in range(slabs // joint):
            for slab in range(group * joint, (group + 1) * joint):
                for copy in copies[slab]:
                    copy.wait()
            part = jnp.dot(
                rows[group],
                table[group].reshape(joint * CORES * depth, heads * columns),
                preferred_element_type=jnp.float32,
            )
            total = part if total is None else total + part
        for turn in range(turns):
            here = total[turn * tokens : (turn + 1) * tokens]
            for head in range(heads):
                at = head * columns
                for which in range(2):
                    block = here[:, at + which * HEAD_DIM : at + (which + 1) * HEAD_DIM]
                    normal = (rms_rows(block) * gains_ref[which, head]).astype(dtype)
                    if which == 0:
                        query_ref[head, turn] = normal
                    else:
                        kv_ref[head, 0, turn] = normal
                block = here[:, at + 2 * HEAD_DIM : at + 3 * HEAD_DIM]
                kv_ref[head, 1, turn] = block.astype(dtype)

    return pl.pallas_call(
        body,
        in_specs=[in_smem(), in_smem()] + [in_hbm()] * (2 * heads + len(pieces)),
        out_specs=(whole_in_vmem(), whole_in_vmem()),
        out_shape=(
            jax.ShapeDtypeStruct((heads, turns, tokens, HEAD_DIM), dtype),
            jax.ShapeDtypeStruct((heads, 2, turns, tokens, HEAD_DIM), dtype),
        ),
        scratch_shapes=[
            pltpu.VMEM((slabs // joint, joint, CORES, depth, heads * columns), dtype),
            pltpu.VMEM((slabs // joint, turns * tokens, joint * features), dtype),
            pltpu.SemaphoreType.DMA((slabs, heads, 2)),
            pltpu.SemaphoreType.DMA((most, turns)),
        ],
        compiler_params=pltpu.CompilerParams(vmem_limit_bytes=VMEM_BYTES),
        name="project_heads",
    )(places, gains, *weights_own, *weights_other, *pieces)


def attend(first_head, heads, key_slots, counts, query_slots, group_most, parts):
    _, blocks, most = key_slots.shape
    groups = group_most.shape[1]
    together = blocks // groups
    scale = 1.0 / math.sqrt(HEAD_DIM)
    dtype = parts[0][4].dtype
    arrays = [array for part in parts for array in part[4:]]

    def body(slots_ref, counts_ref, from_ref, most_ref, *refs):
        out_ref, query_table, table, sems = refs[len(arrays) :]
        copies = []
        for at, (head, size, block, span, _, _, _) in enumerate(parts):
            query_part, own_part, other_part = refs[3 * at : 3 * at + 3]
            rows = pl.ds(head, size)
            copies.append(
                pltpu.make_async_copy(
                    query_part, query_table.at[rows, pl.ds(block, span)], sems.at[at, 0]
                )
            )
            for side, ref in enumerate((own_part, other_part)):
                place = pl.ds(side * blocks + block, span)
                copies.append(
                    pltpu.make_async_copy(ref, table.at[rows, :, place], sems.at[at, 1 + side])
                )
        for copy in copies:
            copy.start()
        for copy in copies:
            copy.wait()

        def run(head, group, listed, batch):
            for first in range(0, together, batch):
                spots = [group * together + at for at in range(first, min(first + batch, together))]
                slots = [[slots_ref[first_head + head, at, entry] for entry in range(listed)] for at in spots]
                scores = []
                for at, listing in zip(spots, slots):
                    keys = jnp.concatenate([table[head, 0, slot] for slot in listing], axis=0)
                    scores.append(
                        lax.dot_general(
                            query_table[head, from_ref[at]],
                            keys,
                            (((1,), (1,)), ((), ())),
                            preferred_element_type=jnp.float32,
                        )
                    )
                column = lax.broadcasted_iota(jnp.int32, (1, listed * BLOCK), 1)
                scores = [
                    jnp.where(column < counts_ref[first_head + head, at] * BLOCK, one * scale, -jnp.inf)
                    for at, one in zip(spots, scores)
                ]
                highest = [jnp.max(one, axis=1, keepdims=True) for one in scores]
                raised = [jnp.exp(one - top) for one, top in zip(scores, highest)]
                inverse = [1.0 / jnp.sum(one, axis=1, keepdims=True) for one in raised]
                weights = [(one * by).astype(dtype) for one, by in zip(raised, inverse)]
                mixed = []
                for one, listing in zip(weights, slots):
                    values = jnp.concatenate([table[head, 1, slot] for slot in listing], axis=0)
                    mixed.append(jnp.dot(one, values, preferred_element_type=jnp.float32))
                for at, one in enumerate(mixed):
                    out_ref[group, head, first + at] = one.astype(dtype)

        def step(at, carry):
            head, group = at // groups, at % groups
            few = most_ref[first_head + head, group] <= most // 2

            @pl.when(few)
            def _():
                run(head, group, most // 2, 6)

            @pl.when(jnp.logical_not(few))
            def _():
                run(head, group, most, 6)

            return carry

        lax.fori_loop(0, heads * groups, step, 0)

    return pl.pallas_call(
        body,
        in_specs=[in_smem()] * 4 + [in_hbm()] * len(arrays),
        out_specs=whole_in_vmem(),
        out_shape=jax.ShapeDtypeStruct((groups, heads, together, BLOCK, HEAD_DIM), dtype),
        scratch_shapes=[
            pltpu.VMEM((heads, blocks, BLOCK, HEAD_DIM), dtype),
            pltpu.VMEM((heads, 2, CORES * blocks, BLOCK, HEAD_DIM), dtype),
            pltpu.SemaphoreType.DMA((len(parts), 3)),
        ],
        compiler_params=pltpu.CompilerParams(vmem_limit_bytes=VMEM_BYTES),
        name="attend",
    )(key_slots, counts, query_slots, group_most, *arrays)


def out_blocks(which, sign, attended, place, out_weight, blocks, dtypes, before=None, skip=0):
    groups, heads, tokens, _ = attended.shape
    depth, features = out_weight.shape
    width = features // blocks
    wanted = which.shape[0]
    rows = heads * HEAD_DIM
    weight = out_weight.reshape(groups, depth // groups, features)
    stacked = len(dtypes) == 1 and wanted > 1

    def body(which_ref, sign_ref, mixed_ref, weight_ref, *refs):
        out_refs = refs if before is None else refs[1:]
        joined = jnp.concatenate(
            [mixed_ref[group, head] for group in range(groups) for head in range(heads)], axis=1
        )
        total = jnp.dot(
            joined,
            weight_ref[...].reshape(groups * rows, width),
            preferred_element_type=jnp.float32,
        )
        total = total * sign_ref[0].astype(jnp.float32)
        if before is not None:
            total = total + refs[0][0].astype(jnp.float32)
        if stacked:
            out_refs[0][0] = total.astype(dtypes[0])
        else:
            for at in range(wanted):

                @pl.when(pl.program_id(0) == at)
                def _(at=at):
                    out_refs[at][...] = total.astype(dtypes[at])

    in_specs = [
        pl.BlockSpec(attended.shape, lambda i, w, s: (0, 0, 0, 0)),
        pl.BlockSpec((groups, rows, width), lambda i, w, s: (0, place, w[i])),
    ]
    operands = [attended, weight]
    if before is not None:
        in_specs.append(pl.BlockSpec((1, tokens, width), lambda i, w, s: (i + skip, 0, 0)))
        operands.append(before)
    if stacked:
        out_specs = [pl.BlockSpec((1, tokens, width), lambda i, w, s: (i, 0, 0))]
        out_shape = [jax.ShapeDtypeStruct((wanted, tokens, width), dtypes[0])]
    else:
        out_specs = [pl.BlockSpec((tokens, width), lambda i, w, s: (0, 0))] * wanted
        out_shape = [jax.ShapeDtypeStruct((tokens, width), dtype) for dtype in dtypes]
    return pl.pallas_call(
        body,
        grid_spec=pltpu.PrefetchScalarGridSpec(
            num_scalar_prefetch=2, grid=(wanted,), in_specs=in_specs, out_specs=out_specs
        ),
        out_shape=out_shape,
        compiler_params=pltpu.CompilerParams(vmem_limit_bytes=VMEM_BYTES),
        name="out_blocks",
    )(which, sign, *operands)


def chunk_sizes(heads):
    last = heads // 3 if heads % 3 == 0 else 1
    return [heads - last, last] if heads > last else [heads]


def per_device_by_heads(
    hidden_rows,
    gen_weight,
    noise,
    timesteps,
    qkv_weight,
    out_weight,
    qk_gain,
    block_keys,
    block_count,
):
    role, head = lax.axis_index("role"), lax.axis_index("head")
    chip, core = lax.axis_index("chip"), lax.axis_index("core")
    chips = lax.axis_size("chip")
    local_heads, local_blocks, most = block_keys.shape
    heads = local_heads // chips
    tokens = hidden_rows.shape[0]
    width = hidden_rows.shape[1]
    features = gen_weight.shape[1]
    all_blocks = chips * local_blocks
    swap = [(0, 1), (1, 0)]
    far_swap = [(0, 3), (1, 2), (2, 1), (3, 0)]
    ring = [(at, (at + 1) % chips) for at in range(chips)]

    def turn_of(other):
        return (chip - other) % chips

    def exchange(array):
        return lax.all_to_all(array, "chip", split_axis=0, concat_axis=0, tiled=True)

    weight_here = qkv_weight[0]
    depth = weight_here.shape[0]
    wide = 3 * HEAD_DIM
    lists = jnp.concatenate([block_keys, block_count[:, :, None]], axis=2)
    lists = lists.reshape(chips, -1).astype(jnp.bfloat16)
    listed = lists.shape[1]
    spare = -(-listed // (16 * wide)) * 16
    lists = jnp.pad(lists, ((0, 0), (0, spare * wide - listed))).reshape(chips, spare, wide)
    cuts = [
        cut_columns(weight_here, chips, at, lists if at == 0 else None) for at in range(heads)
    ]
    hidden_rows, cuts[0] = lax.optimization_barrier((hidden_rows, cuts[0]))
    weights_own = [exchange(cuts[0])]
    weights_other = []

    mine = role * lax.axis_size("head") + head
    generated = jnp.dot(hidden_rows, gen_weight, preferred_element_type=jnp.float32)
    generated = lax.reduce_precision(generated, 8, 7)
    angle_blocks = (timesteps.astype(jnp.float32) * (math.pi / 2000.0))[:, None, None]
    noise_here = lax.dynamic_slice_in_dim(noise, mine * features, features, axis=1)
    noisy = jnp.cos(angle_blocks) * generated.reshape(local_blocks, BLOCK, features)
    noisy = noisy + jnp.sin(angle_blocks) * noise_here.astype(jnp.float32).reshape(
        local_blocks, BLOCK, features
    )
    squares = jnp.sum(noisy * noisy, axis=-1)
    squares = squares + lax.ppermute(squares, "role", swap)
    squares = squares + lax.ppermute(squares, "head", swap)
    normed = (noisy * lax.rsqrt(squares / width + 1e-06)[:, :, None]).astype(jnp.bfloat16)
    normed = normed.reshape(tokens, features)

    def tables_of(lists):
        lists = lists.reshape(chips, spare * wide)[:, :listed].astype(jnp.int32)
        lists = lists.reshape(chips, heads, local_blocks, most + 1).transpose(1, 0, 2, 3)
        lists = lists.reshape(heads, all_blocks, most + 1)
        owner = lists[:, :, :most] // local_blocks
        turn = turn_of(owner // CORES)
        far = (owner % CORES != core).astype(jnp.int32)
        key_slots = far * all_blocks + turn * local_blocks + lists[:, :, :most] % local_blocks
        counts = lists[:, :, most]
        group_most = jnp.max(counts.reshape(heads, chips, local_blocks), axis=2)
        spot = jnp.arange(all_blocks, dtype=jnp.int32)
        query_slots = turn_of(spot // local_blocks)
        query_slots = query_slots * local_blocks + spot % local_blocks

        return key_slots, counts, query_slots, group_most

    sides = lax.axis_size("head")
    peers = jnp.stack(
        [
            role * sides + head,
            (1 - role) * sides + head,
            role * sides + 1 - head,
            (1 - role) * sides + 1 - head,
        ]
    ).astype(jnp.int32)
    places = jnp.concatenate([peers, core[None].astype(jnp.int32)])
    gains = lax.dynamic_slice_in_dim(qk_gain[0], chip * heads, heads, axis=1)

    chunks = chunk_sizes(heads)
    spans = [slice(sum(chunks[:at]), sum(chunks[: at + 1])) for at in range(len(chunks))]
    parts = [[] for _ in chunks]

    def project(chunk, first, size, begin, some, places):
        at = spans[chunk].start + first
        span = slice(at, at + size)
        query, kv = project_heads(
            places, gains[:, span], some, depth, weights_own[span], weights_other[span]
        )
        here = len(some) * local_blocks
        kv = kv.reshape(size, 2, here, BLOCK, HEAD_DIM)
        kv_other = lax.ppermute(kv, "core", swap)
        query = query.reshape(size, here, BLOCK, HEAD_DIM)
        parts[chunk].append((first, size, begin * local_blocks, here, query, kv, kv_other))
        return lax.optimization_barrier((places, kv))[0]

    sign = (2 * role - 1).astype(jnp.int32)[None]
    blocks = sides * lax.axis_size("role")
    which = jnp.stack([peers[3], peers[2], peers[1], peers[0]])
    out_here = out_weight[0]
    out_width = out_here.shape[1] // blocks
    place = spans[-1].start // chunks[-1]

    half = tokens // 2
    rounds = []
    straight = None
    held_places = places
    shard = normed
    for phase in range(chips + 1):
        step = phase + 1
        sent = {}
        if phase < chips:
            sent["role"] = lax.ppermute(shard, "role", swap)
            sent["head"] = lax.ppermute(shard, "head", swap)
        if straight is not None:
            sent["first"] = lax.ppermute(straight[2][:half], "role", swap)
            sent["second"] = lax.ppermute(straight[1][half:], "head", swap)
        if step < chips:
            sent["next"] = lax.ppermute(shard, "chip", ring)
        if phase == 0:
            sent["weights"] = weights_own.pop()
            sent["cuts"] = cuts[1:]
        if phase == 1:
            sent["places"] = places
            sent["gains"] = gains
            sent["corner"] = lax.dynamic_slice(
                out_here.reshape(chips, heads * HEAD_DIM, -1),
                (0, spans[-1].start * HEAD_DIM, which[0] * out_width),
                (chips, chunks[-1] * HEAD_DIM, out_width),
            )
        if step == chips:
            weights_other.append(lax.ppermute(weights_own[0], "core", swap))
            early = list(rounds)
            tables = tables_of(weights_own[0][:, depth:])
            held_places, tables = lax.optimization_barrier((held_places, tables))
            sent["places"] = project(0, 0, 1, 0, early, held_places)
        if step > chips and chunks[0] > 1:
            weights_other.append(lax.ppermute(weights_own[1], "core", swap))
            sent["places"] = project(0, 1, 1, 0, early, held_places)
        sent, shard = lax.optimization_barrier((sent, shard))
        if phase == 0:
            weights_own.append(sent["weights"])
            cuts[1:] = sent["cuts"]
        if phase == 1:
            gains, corner = sent["gains"], sent["corner"]
        if straight is not None:
            rounds.append(straight + (sent["first"], sent["second"]))
        held_places = sent.get("places", held_places)
        if phase < chips:
            straight = (shard, sent["role"], sent["head"])
        if step < chips:
            shard = sent["next"]
        if chips - 2 <= phase and len(weights_own) < heads:
            held, _ = lax.optimization_barrier((cuts[len(weights_own)], sent))
            weights_own.append(exchange(held))
    while len(weights_own) < heads:
        weights_own.append(exchange(cuts[len(weights_own)]))
    for at in range(len(weights_other), heads - 1):
        weights_other.append(lax.ppermute(weights_own[at], "core", swap))

    corner, held_places = lax.optimization_barrier((corner, held_places))
    far_weight = lax.ppermute(corner, ("role", "head"), far_swap)
    attended = []
    received = []
    for chunk, size in enumerate(chunks):
        last = chunk == len(chunks) - 1
        if chunk == 0:
            for at in range(min(size, 2), size):
                held_places = project(0, at, 1, 0, early, held_places)
            held_places = project(0, 0, size, len(early), rounds[len(early) :], held_places)
        else:
            held_places = project(chunk, 0, size, 0, rounds, held_places)
        if last:
            for earlier in range(len(attended)):
                (diagonal,) = out_blocks(
                    which[:1], sign, attended[earlier], spans[earlier].start // chunks[earlier],
                    out_here, blocks, (jnp.bfloat16,),
                )
                tables, diagonal, far_weight = lax.optimization_barrier(
                    (tables, diagonal, far_weight)
                )
                received.append(lax.ppermute(diagonal, ("role", "head"), far_swap))
        mixed = attend(spans[chunk].start, size, *tables, parts[chunk])
        held_places, mixed = lax.optimization_barrier((held_places, mixed))
        if chunk == 0:
            for at in range(len(weights_other), heads):
                weights_own[at], held_places = lax.optimization_barrier(
                    (weights_own[at], held_places)
                )
                weights_other.append(lax.ppermute(weights_own[at], "core", swap))
        mixed = mixed.reshape(chips, size, tokens, HEAD_DIM)
        if attended:
            mixed, attended = lax.optimization_barrier((mixed, attended))
        attended.append(exchange(mixed))

    def earlier_share(wanted, before=None):
        for chunk, size in enumerate(chunks[:-1]):
            before = jnp.stack(
                out_blocks(
                    wanted, sign, attended[chunk], spans[chunk].start // size, out_here, blocks,
                    (jnp.float32,), before,
                )
            ).reshape(-1, tokens, out_width)
        return before

    leaving = earlier_share(which[1:3])
    attended[-1], leaving = lax.optimization_barrier((attended[-1], leaving))
    far_attended = lax.ppermute(attended[-1], ("role", "head"), far_swap)
    wanted, _ = lax.optimization_barrier((which[1:3], received[0]))
    over_head, over_role = out_blocks(
        wanted, sign, attended[-1], place, out_here, blocks, (jnp.bfloat16, jnp.bfloat16), leaving
    )
    (over_head, over_role), far_attended = lax.optimization_barrier(
        ((over_head, over_role), far_attended)
    )
    received.append(lax.ppermute(over_head, "head", swap))
    received.append(lax.ppermute(over_role, "role", swap))
    (far,) = out_blocks(
        jnp.zeros_like(which[:1]), -sign, far_attended, 0, far_weight.reshape(-1, out_width), 1,
        (jnp.float32,), received[0][None],
    )
    (own,) = out_blocks(
        which[3:], sign, attended[-1], place, out_here, blocks, (jnp.float32,),
        earlier_share(which[3:], far[None]),
    )
    total = received[1].astype(jnp.float32)
    for one in received[2:]:
        total = total + one.astype(jnp.float32)
    return own + total


def splits_heads(mesh, qkv_weight, hidden_rows):
    role, seq, head = (mesh.shape[name] for name in ("role", "seq", "head"))
    if role != 2 or head != 2 or seq % CORES != 0:
        return False
    chips = seq // CORES
    heads = qkv_weight.shape[2] // (3 * HEAD_DIM * head)
    width = hidden_rows.shape[1]
    tokens = hidden_rows.shape[0] // seq
    return (
        heads % chips == 0
        and heads // chips > 1
        and chips == role * head
        and width % (role * head * 256) == 0
        and width % (seq * 16) == 0
        and tokens % (2 * BLOCK) == 0
        and hidden_rows.shape[0] // BLOCK <= 256
    )


def solution(mesh):
    def call(*arrays):
        if splits_heads(mesh, arrays[4], arrays[0]):
            per_device = per_device_by_heads
            seq = ("chip", "core")
            shape = mesh.devices.shape
            names = mesh.axis_names
            at = names.index("seq")
            layout = Mesh(
                mesh.devices.reshape(shape[:at] + (shape[at] // CORES, CORES) + shape[at + 1 :]),
                names[:at] + seq + names[at + 1 :],
            )
        else:
            per_device = per_device_by_tokens
            seq = "seq"
            layout = mesh
        placed = (
            P(seq, None),
            P(None, ("role", "head")),
            P(seq, None),
            P(seq),
            P("role", seq, "head"),
            P("role", "head", None),
            P("role", None, "head"),
            P("head", seq, None),
            P("head", seq),
        )
        return jax.shard_map(
            per_device,
            mesh=layout,
            in_specs=placed,
            out_specs=P(seq, ("role", "head")),
            check_vma=False,
        )(*arrays)

    return call
```

```python
import math

import jax
import jax.numpy as jnp
from jax import lax
from jax.experimental import pallas as pl
from jax.experimental.pallas import tpu as pltpu
from jax.sharding import Mesh
from jax.sharding import PartitionSpec as P

HEAD_DIM = 128
BLOCK = 64
KMAX = 8
CAP = 2


def rms_rows(values):
    return values * lax.rsqrt(jnp.mean(values * values, axis=-1, keepdims=True) + 1e-06)


def block_attention(queries, key_table, value_table, key_list, key_count):
    picked_keys = key_table[key_list]
    picked_values = value_table[key_list]
    scale = 1.0 / math.sqrt(HEAD_DIM)
    scores = (
        jnp.einsum("nqe,nkbe->nqkb", queries, picked_keys, preferred_element_type=jnp.float32)
        * scale
    )
    live = lax.broadcasted_iota(jnp.int32, (key_list.shape[0], KMAX), 1) < key_count[:, None]
    scores = jnp.where(live[:, None, :, None], scores, -jnp.inf)
    highest = jnp.max(scores, axis=(2, 3), keepdims=True)
    raised = jnp.exp(scores - highest)
    summed = jnp.sum(raised, axis=(2, 3), keepdims=True)
    weights = (raised / summed).astype(jnp.bfloat16)
    mixed = jnp.einsum("nqkb,nkbe->nqe", weights, picked_values, preferred_element_type=jnp.float32)
    return mixed.astype(jnp.bfloat16)


def pick_blocks(table, wanted):
    return table[wanted]


def per_device_by_tokens(
    hidden_rows,
    gen_weight,
    noise,
    timesteps,
    qkv_weight,
    out_weight,
    qk_gain,
    block_keys,
    block_count,
):
    generated = jnp.dot(hidden_rows, gen_weight, preferred_element_type=jnp.float32).astype(
        jnp.bfloat16
    )
    forked = lax.all_gather(generated, ("role", "head"), axis=1, tiled=True)
    row_count = forked.shape[0]
    width = forked.shape[1]
    local_blocks = timesteps.shape[0]
    angle_blocks = (timesteps.astype(jnp.float32) * (math.pi / 2000.0))[:, None, None]
    noisy = jnp.cos(angle_blocks) * forked.astype(jnp.float32).reshape(local_blocks, BLOCK, width)
    noisy = noisy + jnp.sin(angle_blocks) * noise.astype(jnp.float32).reshape(
        local_blocks, BLOCK, width
    )
    normed = rms_rows(noisy).reshape(row_count, width).astype(jnp.bfloat16)
    weight_here = qkv_weight[0]
    projected = jnp.dot(
        normed,
        lax.all_gather(weight_here, "seq", axis=0, tiled=True),
        preferred_element_type=jnp.float32,
    )
    heads_here = projected.shape[1] // (3 * HEAD_DIM)
    head_parts = projected.reshape(row_count, heads_here, 3, HEAD_DIM)
    gain_here = qk_gain[0]
    queries = (rms_rows(head_parts[:, :, 0]) * gain_here[0][None, :, None]).astype(jnp.bfloat16)
    key_local = (rms_rows(head_parts[:, :, 1]) * gain_here[1][None, :, None]).astype(jnp.bfloat16)
    value_local = head_parts[:, :, 2].astype(jnp.bfloat16)
    query_table = queries.reshape(local_blocks, BLOCK, heads_here, HEAD_DIM).transpose(2, 0, 1, 3)
    shard_count = lax.axis_size("seq")
    shard_here = lax.axis_index("seq")
    all_blocks = shard_count * local_blocks
    key_heads = key_local.reshape(local_blocks, BLOCK, heads_here, HEAD_DIM).transpose(2, 0, 1, 3)
    value_heads = value_local.reshape(local_blocks, BLOCK, heads_here, HEAD_DIM).transpose(
        2, 0, 1, 3
    )
    block_ids = lax.broadcasted_iota(jnp.int32, (1, 1, 1, all_blocks), 3)
    matches = block_keys[:, :, :, None] == block_ids
    remote = block_ids // local_blocks != shard_here
    needed = jnp.any(jnp.logical_and(matches, remote), axis=(1, 2))
    needed = needed.reshape(heads_here, shard_count, local_blocks)
    slot_of = jnp.cumsum(needed.astype(jnp.int32), axis=2) - 1
    slot_ids = lax.broadcasted_iota(jnp.int32, (1, 1, 1, CAP), 3)
    within_ids = lax.broadcasted_iota(jnp.int32, (1, 1, local_blocks, 1), 2)
    chosen_slot = jnp.logical_and(needed[..., None], slot_of[..., None] == slot_ids)
    requests = jnp.sum(jnp.where(chosen_slot, within_ids, 0), axis=2)
    asked = lax.all_to_all(
        requests.transpose(1, 0, 2), "seq", split_axis=0, concat_axis=0, tiled=True
    )
    sent_keys = jax.vmap(pick_blocks, in_axes=(0, 1), out_axes=1)(key_heads, asked)
    sent_values = jax.vmap(pick_blocks, in_axes=(0, 1), out_axes=1)(value_heads, asked)
    got_keys, got_values = (
        lax.all_to_all(sent_keys, "seq", split_axis=0, concat_axis=0, tiled=True),
        lax.all_to_all(sent_values, "seq", split_axis=0, concat_axis=0, tiled=True),
    )
    fetched_keys = got_keys.transpose(1, 0, 2, 3, 4).reshape(
        heads_here, shard_count * CAP, BLOCK, HEAD_DIM
    )
    fetched_values = got_values.transpose(1, 0, 2, 3, 4).reshape(
        heads_here, shard_count * CAP, BLOCK, HEAD_DIM
    )
    key_table = jnp.concatenate([key_heads, fetched_keys], axis=1)
    value_table = jnp.concatenate([value_heads, fetched_values], axis=1)
    local_ids = lax.broadcasted_iota(jnp.int32, (1, shard_count, local_blocks), 2)
    owner_grid = lax.broadcasted_iota(jnp.int32, (1, shard_count, local_blocks), 1)
    position = jnp.where(
        owner_grid == shard_here, local_ids, local_blocks + owner_grid * CAP + slot_of
    )
    position = position.reshape(heads_here, all_blocks)
    key_lists = jnp.sum(jnp.where(matches, position[:, None, None, :], 0), axis=3)
    attended = jax.vmap(block_attention)(
        query_table, key_table, value_table, key_lists, block_count
    )
    attended = attended.transpose(1, 2, 0, 3).reshape(row_count, heads_here * HEAD_DIM)
    contribution = jnp.dot(attended, out_weight[0], preferred_element_type=jnp.float32)
    signed = (2.0 * lax.axis_index("role").astype(jnp.float32) - 1.0) * contribution
    return lax.psum_scatter(
        signed.astype(jnp.bfloat16), ("role", "head"), scatter_dimension=1, tiled=True
    ).astype(jnp.float32)


VMEM_BYTES = 56 * 1024 * 1024
CORES = 2


def whole_in_vmem():
    return pl.BlockSpec(memory_space=pltpu.VMEM)


def in_hbm():
    return pl.BlockSpec(memory_space=pl.ANY)


def in_smem():
    return pl.BlockSpec(memory_space=pltpu.SMEM)


def cut_columns(weight, chips, head, extra=None):
    rows, columns = weight.shape
    wide = 3 * HEAD_DIM
    chip_heads = columns // (chips * wide)
    more = 0 if extra is None else extra.shape[1]

    def body(weight_ref, *refs):
        out_ref = refs[-1]
        out_ref[0, :rows] = weight_ref[...]
        if more:
            out_ref[0, rows:] = refs[0][0]

    in_specs = [pl.BlockSpec((rows, wide), lambda chip: (0, chip * chip_heads + head))]
    operands = [weight]
    if more:
        in_specs.append(pl.BlockSpec((1, more, wide), lambda chip: (chip, 0, 0)))
        operands.append(extra)
    return pl.pallas_call(
        body,
        grid=(chips,),
        in_specs=in_specs,
        out_specs=pl.BlockSpec((1, rows + more, wide), lambda chip: (chip, 0, 0)),
        out_shape=jax.ShapeDtypeStruct((chips, rows + more, wide), weight.dtype),
        name="cut_columns",
    )(*operands)


def project_heads(places, gains, rounds, depth, weights_own, weights_other):
    heads = len(weights_own)
    slabs, _, columns = weights_own[0].shape
    tokens, features = rounds[0][0].shape
    pieces = [piece for one in rounds for piece in one]
    turns = len(rounds)
    most = max(len(one) for one in rounds)
    joint = 2 if slabs % 2 == 0 else 1
    dtype = weights_own[0].dtype

    def body(places_ref, gains_ref, *refs):
        own_refs, other_refs = refs[:heads], refs[heads : 2 * heads]
        piece_refs = refs[2 * heads : 2 * heads + len(pieces)]
        query_ref, kv_ref = refs[2 * heads + len(pieces) : 2 * heads + len(pieces) + 2]
        table, rows, weight_sems, row_sems = refs[2 * heads + len(pieces) + 2 :]
        core = places_ref[slabs]
        copies = []
        for slab in range(slabs):
            here = []
            for head in range(heads):
                for side, ref in enumerate((own_refs[head], other_refs[head])):
                    place = core if side == 0 else 1 - core
                    here.append(
                        pltpu.make_async_copy(
                            ref.at[places_ref[slab], pl.ds(0, depth)],
                            table.at[
                                slab // joint,
                                slab % joint,
                                place,
                                :,
                                pl.ds(head * columns, columns),
                            ],
                            weight_sems.at[slab, head, side],
                        )
                    )
            at = 0
            for turn in range(turns):
                first = turn * tokens
                for which in range(len(rounds[turn])):
                    if min(which, slabs - 1) == slab:
                        count = rounds[turn][which].shape[0]
                        here.append(
                            pltpu.make_async_copy(
                                piece_refs[at],
                                rows.at[
                                    slab // joint,
                                    pl.ds(first, count),
                                    pl.ds(slab % joint * features, features),
                                ],
                                row_sems.at[which, turn],
                            )
                        )
                        first += count
                    at += 1
            for copy in here:
                copy.start()
            copies.append(here)
        total = None
        for group in range(slabs // joint):
            for slab in range(group * joint, (group + 1) * joint):
                for copy in copies[slab]:
                    copy.wait()
            part = jnp.dot(
                rows[group],
                table[group].reshape(joint * CORES * depth, heads * columns),
                preferred_element_type=jnp.float32,
            )
            total = part if total is None else total + part
        for turn in range(turns):
            here = total[turn * tokens : (turn + 1) * tokens]
            for head in range(heads):
                at = head * columns
                for which in range(2):
                    block = here[:, at + which * HEAD_DIM : at + (which + 1) * HEAD_DIM]
                    normal = (rms_rows(block) * gains_ref[which, head]).astype(dtype)
                    if which == 0:
                        query_ref[head, turn] = normal
                    else:
                        kv_ref[head, 0, turn] = normal
                block = here[:, at + 2 * HEAD_DIM : at + 3 * HEAD_DIM]
                kv_ref[head, 1, turn] = block.astype(dtype)

    return pl.pallas_call(
        body,
        in_specs=[in_smem(), in_smem()] + [in_hbm()] * (2 * heads + len(pieces)),
        out_specs=(whole_in_vmem(), whole_in_vmem()),
        out_shape=(
            jax.ShapeDtypeStruct((heads, turns, tokens, HEAD_DIM), dtype),
            jax.ShapeDtypeStruct((heads, 2, turns, tokens, HEAD_DIM), dtype),
        ),
        scratch_shapes=[
            pltpu.VMEM((slabs // joint, joint, CORES, depth, heads * columns), dtype),
            pltpu.VMEM((slabs // joint, turns * tokens, joint * features), dtype),
            pltpu.SemaphoreType.DMA((slabs, heads, 2)),
            pltpu.SemaphoreType.DMA((most, turns)),
        ],
        compiler_params=pltpu.CompilerParams(vmem_limit_bytes=VMEM_BYTES),
        name="project_heads",
    )(places, gains, *weights_own, *weights_other, *pieces)


def attend(first_head, heads, key_slots, counts, query_slots, group_most, parts):
    _, blocks, most = key_slots.shape
    groups = group_most.shape[1]
    together = blocks // groups
    scale = 1.0 / math.sqrt(HEAD_DIM)
    dtype = parts[0][4].dtype
    arrays = [array for part in parts for array in part[4:]]

    def body(slots_ref, counts_ref, from_ref, most_ref, *refs):
        out_ref, query_table, table, sems = refs[len(arrays) :]
        copies = []
        for at, (head, size, block, span, _, _, _) in enumerate(parts):
            query_part, own_part, other_part = refs[3 * at : 3 * at + 3]
            rows = pl.ds(head, size)
            copies.append(
                pltpu.make_async_copy(
                    query_part, query_table.at[rows, pl.ds(block, span)], sems.at[at, 0]
                )
            )
            for side, ref in enumerate((own_part, other_part)):
                place = pl.ds(side * blocks + block, span)
                copies.append(
                    pltpu.make_async_copy(ref, table.at[rows, :, place], sems.at[at, 1 + side])
                )
        for copy in copies:
            copy.start()
        for copy in copies:
            copy.wait()

        def run(head, group, listed, batch):
            for first in range(0, together, batch):
                spots = [group * together + at for at in range(first, min(first + batch, together))]
                slots = [[slots_ref[first_head + head, at, entry] for entry in range(listed)] for at in spots]
                scores = []
                for at, listing in zip(spots, slots):
                    keys = jnp.concatenate([table[head, 0, slot] for slot in listing], axis=0)
                    scores.append(
                        lax.dot_general(
                            query_table[head, from_ref[at]],
                            keys,
                            (((1,), (1,)), ((), ())),
                            preferred_element_type=jnp.float32,
                        )
                    )
                column = lax.broadcasted_iota(jnp.int32, (1, listed * BLOCK), 1)
                scores = [
                    jnp.where(column < counts_ref[first_head + head, at] * BLOCK, one * scale, -jnp.inf)
                    for at, one in zip(spots, scores)
                ]
                highest = [jnp.max(one, axis=1, keepdims=True) for one in scores]
                raised = [jnp.exp(one - top) for one, top in zip(scores, highest)]
                inverse = [1.0 / jnp.sum(one, axis=1, keepdims=True) for one in raised]
                weights = [(one * by).astype(dtype) for one, by in zip(raised, inverse)]
                mixed = []
                for one, listing in zip(weights, slots):
                    values = jnp.concatenate([table[head, 1, slot] for slot in listing], axis=0)
                    mixed.append(jnp.dot(one, values, preferred_element_type=jnp.float32))
                for at, one in enumerate(mixed):
                    out_ref[group, head, first + at] = one.astype(dtype)

        def step(at, carry):
            head, group = at // groups, at % groups
            few = most_ref[first_head + head, group] <= most // 2

            @pl.when(few)
            def _():
                run(head, group, most // 2, 6)

            @pl.when(jnp.logical_not(few))
            def _():
                run(head, group, most, 6)

            return carry

        lax.fori_loop(0, heads * groups, step, 0)

    return pl.pallas_call(
        body,
        in_specs=[in_smem()] * 4 + [in_hbm()] * len(arrays),
        out_specs=whole_in_vmem(),
        out_shape=jax.ShapeDtypeStruct((groups, heads, together, BLOCK, HEAD_DIM), dtype),
        scratch_shapes=[
            pltpu.VMEM((heads, blocks, BLOCK, HEAD_DIM), dtype),
            pltpu.VMEM((heads, 2, CORES * blocks, BLOCK, HEAD_DIM), dtype),
            pltpu.SemaphoreType.DMA((len(parts), 3)),
        ],
        compiler_params=pltpu.CompilerParams(vmem_limit_bytes=VMEM_BYTES),
        name="attend",
    )(key_slots, counts, query_slots, group_most, *arrays)


def out_blocks(which, sign, attended, place, out_weight, blocks, dtypes, before=None, skip=0):
    groups, heads, tokens, _ = attended.shape
    depth, features = out_weight.shape
    width = features // blocks
    wanted = which.shape[0]
    rows = heads * HEAD_DIM
    weight = out_weight.reshape(groups, depth // groups, features)
    stacked = len(dtypes) == 1 and wanted > 1

    def body(which_ref, sign_ref, mixed_ref, weight_ref, *refs):
        out_refs = refs if before is None else refs[1:]
        joined = jnp.concatenate(
            [mixed_ref[group, head] for group in range(groups) for head in range(heads)], axis=1
        )
        total = jnp.dot(
            joined,
            weight_ref[...].reshape(groups * rows, width),
            preferred_element_type=jnp.float32,
        )
        total = total * sign_ref[0].astype(jnp.float32)
        if before is not None:
            total = total + refs[0][0].astype(jnp.float32)
        if stacked:
            out_refs[0][0] = total.astype(dtypes[0])
        else:
            for at in range(wanted):

                @pl.when(pl.program_id(0) == at)
                def _(at=at):
                    out_refs[at][...] = total.astype(dtypes[at])

    in_specs = [
        pl.BlockSpec(attended.shape, lambda i, w, s: (0, 0, 0, 0)),
        pl.BlockSpec((groups, rows, width), lambda i, w, s: (0, place, w[i])),
    ]
    operands = [attended, weight]
    if before is not None:
        in_specs.append(pl.BlockSpec((1, tokens, width), lambda i, w, s: (i + skip, 0, 0)))
        operands.append(before)
    if stacked:
        out_specs = [pl.BlockSpec((1, tokens, width), lambda i, w, s: (i, 0, 0))]
        out_shape = [jax.ShapeDtypeStruct((wanted, tokens, width), dtypes[0])]
    else:
        out_specs = [pl.BlockSpec((tokens, width), lambda i, w, s: (0, 0))] * wanted
        out_shape = [jax.ShapeDtypeStruct((tokens, width), dtype) for dtype in dtypes]
    return pl.pallas_call(
        body,
        grid_spec=pltpu.PrefetchScalarGridSpec(
            num_scalar_prefetch=2, grid=(wanted,), in_specs=in_specs, out_specs=out_specs
        ),
        out_shape=out_shape,
        compiler_params=pltpu.CompilerParams(vmem_limit_bytes=VMEM_BYTES),
        name="out_blocks",
    )(which, sign, *operands)


def chunk_sizes(heads):
    last = heads // 3 if heads % 3 == 0 else 1
    return [heads - last, last] if heads > last else [heads]


def per_device_by_heads(
    hidden_rows,
    gen_weight,
    noise,
    timesteps,
    qkv_weight,
    out_weight,
    qk_gain,
    block_keys,
    block_count,
):
    role, head = lax.axis_index("role"), lax.axis_index("head")
    chip, core = lax.axis_index("chip"), lax.axis_index("core")
    chips = lax.axis_size("chip")
    local_heads, local_blocks, most = block_keys.shape
    heads = local_heads // chips
    tokens = hidden_rows.shape[0]
    width = hidden_rows.shape[1]
    features = gen_weight.shape[1]
    all_blocks = chips * local_blocks
    swap = [(0, 1), (1, 0)]
    far_swap = [(0, 3), (1, 2), (2, 1), (3, 0)]
    ring = [(at, (at + 1) % chips) for at in range(chips)]

    def turn_of(other):
        return (chip - other) % chips

    def exchange(array):
        return lax.all_to_all(array, "chip", split_axis=0, concat_axis=0, tiled=True)

    weight_here = qkv_weight[0]
    depth = weight_here.shape[0]
    wide = 3 * HEAD_DIM
    lists = jnp.concatenate([block_keys, block_count[:, :, None]], axis=2)
    lists = lists.reshape(chips, -1).astype(jnp.bfloat16)
    listed = lists.shape[1]
    spare = -(-listed // (16 * wide)) * 16
    lists = jnp.pad(lists, ((0, 0), (0, spare * wide - listed))).reshape(chips, spare, wide)
    cuts = [
        cut_columns(weight_here, chips, at, lists if at == 0 else None) for at in range(heads)
    ]
    hidden_rows, cuts[0] = lax.optimization_barrier((hidden_rows, cuts[0]))
    weights_own = [exchange(cuts[0])]
    weights_other = []

    mine = role * lax.axis_size("head") + head
    generated = jnp.dot(hidden_rows, gen_weight, preferred_element_type=jnp.float32)
    generated = lax.reduce_precision(generated, 8, 7)
    angle_blocks = (timesteps.astype(jnp.float32) * (math.pi / 2000.0))[:, None, None]
    noise_here = lax.dynamic_slice_in_dim(noise, mine * features, features, axis=1)
    noisy = jnp.cos(angle_blocks) * generated.reshape(local_blocks, BLOCK, features)
    noisy = noisy + jnp.sin(angle_blocks) * noise_here.astype(jnp.float32).reshape(
        local_blocks, BLOCK, features
    )
    squares = jnp.sum(noisy * noisy, axis=-1)
    squares = squares + lax.ppermute(squares, "role", swap)
    squares = squares + lax.ppermute(squares, "head", swap)
    normed = (noisy * lax.rsqrt(squares / width + 1e-06)[:, :, None]).astype(jnp.bfloat16)
    normed = normed.reshape(tokens, features)

    def tables_of(lists):
        lists = lists.reshape(chips, spare * wide)[:, :listed].astype(jnp.int32)
        lists = lists.reshape(chips, heads, local_blocks, most + 1).transpose(1, 0, 2, 3)
        lists = lists.reshape(heads, all_blocks, most + 1)
        owner = lists[:, :, :most] // local_blocks
        turn = turn_of(owner // CORES)
        far = (owner % CORES != core).astype(jnp.int32)
        key_slots = far * all_blocks + turn * local_blocks + lists[:, :, :most] % local_blocks
        counts = lists[:, :, most]
        group_most = jnp.max(counts.reshape(heads, chips, local_blocks), axis=2)
        spot = jnp.arange(all_blocks, dtype=jnp.int32)
        query_slots = turn_of(spot // local_blocks)
        query_slots = query_slots * local_blocks + spot % local_blocks

        return key_slots, counts, query_slots, group_most

    sides = lax.axis_size("head")
    peers = jnp.stack(
        [
            role * sides + head,
            (1 - role) * sides + head,
            role * sides + 1 - head,
            (1 - role) * sides + 1 - head,
        ]
    ).astype(jnp.int32)
    places = jnp.concatenate([peers, core[None].astype(jnp.int32)])
    gains = lax.dynamic_slice_in_dim(qk_gain[0], chip * heads, heads, axis=1)

    chunks = chunk_sizes(heads)
    spans = [slice(sum(chunks[:at]), sum(chunks[: at + 1])) for at in range(len(chunks))]
    parts = [[] for _ in chunks]

    def project(chunk, first, size, begin, some, places):
        at = spans[chunk].start + first
        span = slice(at, at + size)
        query, kv = project_heads(
            places, gains[:, span], some, depth, weights_own[span], weights_other[span]
        )
        here = len(some) * local_blocks
        kv = kv.reshape(size, 2, here, BLOCK, HEAD_DIM)
        kv_other = lax.ppermute(kv, "core", swap)
        query = query.reshape(size, here, BLOCK, HEAD_DIM)
        parts[chunk].append((first, size, begin * local_blocks, here, query, kv, kv_other))
        return lax.optimization_barrier((places, kv))[0]

    sign = (2 * role - 1).astype(jnp.int32)[None]
    blocks = sides * lax.axis_size("role")
    which = jnp.stack([peers[3], peers[2], peers[1], peers[0]])
    out_here = out_weight[0]
    out_width = out_here.shape[1] // blocks
    place = spans[-1].start // chunks[-1]

    half = tokens // 2
    rounds = []
    straight = None
    held_places = places
    shard = normed
    for phase in range(chips + 1):
        step = phase + 1
        sent = {}
        if phase < chips:
            sent["role"] = lax.ppermute(shard, "role", swap)
            sent["head"] = lax.ppermute(shard, "head", swap)
        if straight is not None:
            sent["first"] = lax.ppermute(straight[2][:half], "role", swap)
            sent["second"] = lax.ppermute(straight[1][half:], "head", swap)
        if step < chips:
            sent["next"] = lax.ppermute(shard, "chip", ring)
        if phase == 0:
            sent["cuts"] = cuts[1:]
        if phase == 1:
            sent["weights"] = weights_own.pop()
            sent["places"] = places
            sent["gains"] = gains
            sent["corner"] = lax.dynamic_slice(
                out_here.reshape(chips, heads * HEAD_DIM, -1),
                (0, spans[-1].start * HEAD_DIM, which[0] * out_width),
                (chips, chunks[-1] * HEAD_DIM, out_width),
            )
        if step == chips:
            weights_other.append(lax.ppermute(weights_own[0], "core", swap))
            early = list(rounds)
            tables = tables_of(weights_own[0][:, depth:])
            held_places, tables = lax.optimization_barrier((held_places, tables))
            sent["places"] = project(0, 0, 1, 0, early, held_places)
        if step > chips and chunks[0] > 1:
            weights_other.append(lax.ppermute(weights_own[1], "core", swap))
            sent["places"] = project(0, 1, 1, 0, early, held_places)
        sent, shard = lax.optimization_barrier((sent, shard))
        if phase == 0:
            cuts[1:] = sent["cuts"]
        if phase == 1:
            weights_own.append(sent["weights"])
            gains, corner = sent["gains"], sent["corner"]
        if straight is not None:
            rounds.append(straight + (sent["first"], sent["second"]))
        held_places = sent.get("places", held_places)
        if phase < chips:
            straight = (shard, sent["role"], sent["head"])
        if step < chips:
            shard = sent["next"]
        if chips - 2 <= phase and len(weights_own) < heads:
            held, _ = lax.optimization_barrier((cuts[len(weights_own)], sent))
            weights_own.append(exchange(held))
    while len(weights_own) < heads:
        weights_own.append(exchange(cuts[len(weights_own)]))
    for at in range(len(weights_other), heads - 1):
        weights_other.append(lax.ppermute(weights_own[at], "core", swap))

    corner, held_places = lax.optimization_barrier((corner, held_places))
    far_weight = lax.ppermute(corner, ("role", "head"), far_swap)
    attended = []
    received = []
    for chunk, size in enumerate(chunks):
        last = chunk == len(chunks) - 1
        if chunk == 0:
            for at in range(min(size, 2), size):
                held_places = project(0, at, 1, 0, early, held_places)
            held_places = project(0, 0, size, len(early), rounds[len(early) :], held_places)
        else:
            held_places = project(chunk, 0, size, 0, rounds, held_places)
        if last:
            for earlier in range(len(attended)):
                (diagonal,) = out_blocks(
                    which[:1], sign, attended[earlier], spans[earlier].start // chunks[earlier],
                    out_here, blocks, (jnp.bfloat16,),
                )
                tables, diagonal, far_weight = lax.optimization_barrier(
                    (tables, diagonal, far_weight)
                )
                received.append(lax.ppermute(diagonal, ("role", "head"), far_swap))
        mixed = attend(spans[chunk].start, size, *tables, parts[chunk])
        held_places, mixed = lax.optimization_barrier((held_places, mixed))
        if chunk == 0:
            for at in range(len(weights_other), heads):
                weights_own[at], held_places = lax.optimization_barrier(
                    (weights_own[at], held_places)
                )
                weights_other.append(lax.ppermute(weights_own[at], "core", swap))
        mixed = mixed.reshape(chips, size, tokens, HEAD_DIM)
        if attended:
            mixed, attended = lax.optimization_barrier((mixed, attended))
        attended.append(exchange(mixed))

    def earlier_share(wanted, before=None):
        for chunk, size in enumerate(chunks[:-1]):
            before = jnp.stack(
                out_blocks(
                    wanted, sign, attended[chunk], spans[chunk].start // size, out_here, blocks,
                    (jnp.float32,), before,
                )
            ).reshape(-1, tokens, out_width)
        return before

    leaving = earlier_share(which[1:3])
    attended[-1], leaving = lax.optimization_barrier((attended[-1], leaving))
    far_attended = lax.ppermute(attended[-1], ("role", "head"), far_swap)
    wanted, _ = lax.optimization_barrier((which[1:3], received[0]))
    over_head, over_role = out_blocks(
        wanted, sign, attended[-1], place, out_here, blocks, (jnp.bfloat16, jnp.bfloat16), leaving
    )
    (over_head, over_role), far_attended = lax.optimization_barrier(
        ((over_head, over_role), far_attended)
    )
    received.append(lax.ppermute(over_head, "head", swap))
    received.append(lax.ppermute(over_role, "role", swap))
    (far,) = out_blocks(
        jnp.zeros_like(which[:1]), -sign, far_attended, 0, far_weight.reshape(-1, out_width), 1,
        (jnp.float32,), received[0][None],
    )
    (own,) = out_blocks(
        which[3:], sign, attended[-1], place, out_here, blocks, (jnp.float32,),
        earlier_share(which[3:], far[None]),
    )
    total = received[1].astype(jnp.float32)
    for one in received[2:]:
        total = total + one.astype(jnp.float32)
    return own + total


def splits_heads(mesh, qkv_weight, hidden_rows):
    role, seq, head = (mesh.shape[name] for name in ("role", "seq", "head"))
    if role != 2 or head != 2 or seq % CORES != 0:
        return False
    chips = seq // CORES
    heads = qkv_weight.shape[2] // (3 * HEAD_DIM * head)
    width = hidden_rows.shape[1]
    tokens = hidden_rows.shape[0] // seq
    return (
        heads % chips == 0
        and heads // chips > 1
        and chips == role * head
        and width % (role * head * 256) == 0
        and width % (seq * 16) == 0
        and tokens % (2 * BLOCK) == 0
        and hidden_rows.shape[0] // BLOCK <= 256
    )


def solution(mesh):
    def call(*arrays):
        if splits_heads(mesh, arrays[4], arrays[0]):
            per_device = per_device_by_heads
            seq = ("chip", "core")
            shape = mesh.devices.shape
            names = mesh.axis_names
            at = names.index("seq")
            layout = Mesh(
                mesh.devices.reshape(shape[:at] + (shape[at] // CORES, CORES) + shape[at + 1 :]),
                names[:at] + seq + names[at + 1 :],
            )
        else:
            per_device = per_device_by_tokens
            seq = "seq"
            layout = mesh
        placed = (
            P(seq, None),
            P(None, ("role", "head")),
            P(seq, None),
            P(seq),
            P("role", seq, "head"),
            P("role", "head", None),
            P("role", None, "head"),
            P("head", seq, None),
            P("head", seq),
        )
        return jax.shard_map(
            per_device,
            mesh=layout,
            in_specs=placed,
            out_specs=P(seq, ("role", "head")),
            check_vma=False,
        )(*arrays)

    return call
```
